32 devices in a mesh: grp: 2 (over y), blk: 4 (over z), term: 2 (over x), sub: 2 (over core).
Axes of the slice: x: 2, y: 2, z: 4, core: 2. Of those that a mesh axis runs over, the one named last changes fastest.
Arguments:
- amplitudes: float32 [128, 128, 3, 128], P(('grp', 'blk'), 'sub'), parts along dimension 0, may hold values from -6 to 6
- left_operators: float32 [32, 64, 128, 128], P(('grp', 'term'), 'blk', 'sub'), parts along dimension 0, may hold values from -0.125 to 0.125
- right_operators: float32 [32, 64, 128, 128], P(('grp', 'term'), 'blk'), parts along dimension 0, may hold values from -0.5 to 0.5
- term_kind: int32 [32], P(('grp', 'term')), parts along dimension 0, may hold values 0 or 1
- partner: int32 [128], P(('grp', 'blk')), parts along dimension 0, may hold values from 0 to 63, as said below
- left_diag: float32 [128, 128], P(('grp', 'blk'), 'sub'), parts along dimension 0, may hold values from 0.5 to 8
- right_diag: float32 [128, 128], P(('grp', 'blk')), parts along dimension 0, may hold values from 0.5 to 8
Outputs:
- sigma_second: float32 [128, 128, 3, 128], P(('grp', 'blk'), 'sub'), parts along dimension 0
- correction: float32 [128, 128, 3, 128], P(('grp', 'blk'), 'sub'), parts along dimension 0
The draws below stay inside these ranges and needn't reach their ends.
There are 2 independent parts, one for each index of `grp`. The reference program is written for one: setup_inputs(seed, part) draws one part's arguments, and reference() takes and returns one part's arrays. A program takes and returns all parts, laid end to end along the dimension named above; each array names one. Nothing has to cross between parts.
Inputs may be any that keep to these rules, and one draw needn't show every extreme that they name: partner is a permutation of the sectors. Sector 16 p + j goes to sector 16 ((p + c_j) mod 4) + pi_j, where c and pi (a permutation of 0 to 15) are the same for every p, and each value of c_j mod 4 occurs exactly 16 / 4 times.
All inputs are finite; a program needn't handle non-finite values. No bound on the sum of `term_kind` on one device may be relied on, other than what follows from the above.
Results may differ from the reference program's by a relative error of at most 0.0003.
Values sent between devices are 32-bit elements; how exact they have to be, the bound alone decides.
No kernel may reach another device: no remote copies, remote signals or barrier semaphores. Data moves between devices by JAX's collectives and lax.ppermute only.
A program may use at most 64 MiB of HBM per device.

```python
import math
import jax
import jax.numpy as jnp
from jax import lax

B = 128
R = 3
SEC_DEV = 16
NSEC = 64
K = 16
N_BLK = 4


def draw_partner(key, part):
    key = jax.random.fold_in(key, 11)
    first_key, second_key = jax.random.split(key)
    offsets = jax.random.permutation(first_key, SEC_DEV) % N_BLK
    within = jax.random.permutation(second_key, SEC_DEV)
    devices = jnp.arange(N_BLK)[:, None]
    table = (devices + offsets[None, :]) % N_BLK * SEC_DEV + within[None, :]
    return table.reshape(-1).astype(jnp.int32)


def place_ends(values, stream_key, least, largest):
    shape = values.shape
    spot = [jax.random.randint(jax.random.fold_in(stream_key, axis), (), 0, shape[axis]) for axis in range(len(shape))]
    values = values.at[tuple(spot)].set(least)
    longest = shape.index(max(shape))
    spot[longest] = (spot[longest] + 1) % shape[longest]
    return values.at[tuple(spot)].set(largest)


def block_scale(key, dims, shards, least, top_value):
    def one(axis_at, blocks):
        heights = jax.random.uniform(jax.random.fold_in(jax.random.fold_in(key, 6), axis_at), (blocks,), jnp.float32, least / len(shards), top_value / len(shards))
        return jnp.repeat(jnp.exp(heights), dims[axis_at] // blocks).reshape((-1,) + (1,) * (len(dims) - axis_at - 1))

    factor_of = one(*shards[0])
    for cut in shards[1:]:
        factor_of = factor_of * one(*cut)
    return factor_of


def gaussian(key, extent, scale, bound, pieces=(), held_as=jnp.bfloat16):
    entries = scale * jax.random.normal(key, extent, jnp.float32)
    if pieces:
        entries = entries * block_scale(key, extent, pieces, -0.22, 0.18)
    return jnp.clip(entries, -bound, bound).astype(held_as)


def setup_inputs(seed: int = 0, part: int = 0) -> dict:
    key_of = jax.random.split(jax.random.key(seed), 8)
    part_keys = jax.random.split(jax.random.fold_in(key_of[7], part), 8)
    amplitudes = gaussian(part_keys[0], (NSEC, B, R, B), 1.0, 6.0, ((0, 4), (1, 2)), jnp.float32)
    left_operators = gaussian(part_keys[1], (K, NSEC, B, B), (B * K) ** -0.5, 0.125, ((0, 2), (1, 4), (2, 2)), jnp.float32)
    right_operators = gaussian(part_keys[2], (K, NSEC, B, B), B ** -0.5, 0.5, ((0, 2), (1, 4)), jnp.float32)
    term_kind = place_ends((jax.random.randint(part_keys[3], (K,), 0, 2) < 1).astype(jnp.int32), jax.random.fold_in(part_keys[3], 1), 0, 1)
    partner = draw_partner(jax.random.fold_in(jax.random.fold_in(key_of[7], part), 71), part)
    left_diag = jnp.clip(jnp.exp(math.log(8.0) - 2.7725887 * jax.random.uniform(part_keys[5], (NSEC, B), jnp.float32) ** block_scale(part_keys[5], (NSEC, B), ((0, 4), (1, 2)), -0.2, 0.2)), 0.5, 8.0)
    right_diag = jnp.clip(jnp.exp(math.log(8.0) - 2.7725887 * jax.random.uniform(part_keys[6], (NSEC, B), jnp.float32) ** block_scale(part_keys[6], (NSEC, B), ((0, 4),), -0.2, 0.2)), 0.5, 8.0)
    return dict(amplitudes=amplitudes, left_operators=left_operators, right_operators=right_operators, term_kind=term_kind, partner=partner, left_diag=left_diag, right_diag=right_diag)


def apply_hamiltonian(vector, left_operators, right_operators, term_kind, partner, hdiag):

    def one_term(carry, inputs):
        left_block, right_block, kind = inputs
        middle = jnp.einsum('soi,sirc->sorc', left_block, vector, precision=lax.Precision.HIGHEST)
        result = jnp.einsum('sorc,sdc->sord', middle, right_block, precision=lax.Precision.HIGHEST)
        moved = jnp.zeros_like(result).at[partner].set(result)
        return (carry + jnp.where(kind == 1, moved, result), None)
    start = jnp.zeros(vector.shape, jnp.float32)
    total, _ = lax.scan(one_term, start, (left_operators, right_operators, term_kind))
    return total + hdiag * vector

def reference(amplitudes, left_operators, right_operators, term_kind, partner, left_diag, right_diag):
    hdiag = left_diag[:, :, None, None] + right_diag[:, None, None, :]
    sigma_first = apply_hamiltonian(amplitudes, left_operators, right_operators, term_kind, partner, hdiag)
    correlation = lax.optimization_barrier(jnp.sum(amplitudes * sigma_first, axis=(0, 1, 3)))
    weight = lax.optimization_barrier(jnp.sum(amplitudes * amplitudes, axis=(0, 1, 3)))
    theta = (correlation / weight)[None, None, :, None]
    raw = (sigma_first - theta * amplitudes) / jnp.maximum(jnp.abs(hdiag - theta), 1.0)
    scale = lax.rsqrt(lax.optimization_barrier(jnp.mean(raw * raw, axis=(0, 1, 3))) + 1e-06)
    correction = raw * scale[None, None, :, None]
    sigma_second = apply_hamiltonian(correction, left_operators, right_operators, term_kind, partner, hdiag)
    return (sigma_second, correction)
```

```python
import functools

import jax
import jax.numpy as jnp
from jax import lax
from jax.experimental import pallas as pl
from jax.experimental.pallas import tpu as pltpu
from jax.sharding import PartitionSpec as P

LIMIT = 48 * 1024 * 1024
WHOLE = pl.BlockSpec(memory_space=pltpu.VMEM)
SCALARS = pl.BlockSpec(memory_space=pltpu.SMEM)
ANY = pl.BlockSpec(memory_space=pl.ANY)


def power_of_two(size):
    return size & (size - 1) == 0


def flip(value, axis, bit):
    size = lax.axis_size(axis)
    return lax.ppermute(value, axis, [(i, i ^ bit) for i in range(size)])


def small_sum(value, axis):
    size = lax.axis_size(axis)
    if not power_of_two(size):
        return lax.psum(value, axis)
    if size == 4:
        one, two, three = (flip(value, axis, bit) for bit in (1, 2, 3))
        return (value + one) + (two + three)
    bit = 1
    while bit < size:
        value = value + flip(value, axis, bit)
        bit *= 2
    return value


def halves(value):
    high = value.astype(jnp.bfloat16)
    low = (value - high.astype(jnp.float32)).astype(jnp.bfloat16)
    return high, low


def table_kernel(devices, partner_ref, kind_ref, table_ref, used):
    count, terms = partner_ref.shape[0], kind_ref.shape[0]
    per = count // devices
    me = lax.axis_index("blk")
    for c in range(devices):
        used[c] = 0

    def place(j, carry):
        where_to = partner_ref[j]
        owner = lax.div(where_to, count)
        offset = lax.rem(owner - me + devices, devices)
        at = offset * per + used[offset]
        used[offset] = used[offset] + 1
        table_ref[at] = j
        table_ref[count + at] = where_to - owner * count
        table_ref[2 * count + j] = at
        return carry

    lax.fori_loop(0, count, place, 0)
    for k in range(terms):
        table_ref[3 * count + k] = kind_ref[k]
    table_ref[3 * count + terms] = lax.axis_index("sub")


def make_table(partner, term_kind):
    devices = lax.axis_size("blk")
    length = 3 * partner.shape[0] + term_kind.shape[0] + 1
    return pl.pallas_call(
        functools.partial(table_kernel, devices),
        out_shape=jax.ShapeDtypeStruct((length,), jnp.int32),
        in_specs=[SCALARS, SCALARS],
        out_specs=SCALARS,
        scratch_shapes=[pltpu.SMEM((devices,), jnp.int32)],
    )(partner, term_kind)


def sector_kernel(count, terms, table, l_ref, r_ref, own_ref, other_ref, *rest):
    moved_ref, kept_ref, lhs, high_rhs, low_rhs = rest[-5:]
    roots, rows, width = own_ref.shape[1:]
    first = table[3 * count + terms] == 0
    own, other = own_ref[0], other_ref[0]
    top = jnp.where(first, own, other)
    bottom = jnp.where(first, other, own)
    vector = jnp.concatenate(
        [jnp.concatenate([half[r] for r in range(roots)], axis=1) for half in (top, bottom)], axis=0
    )
    wide = jnp.concatenate(halves(vector), axis=1)
    left = l_ref[:, 0].reshape(terms * rows, 2 * rows)
    both = jnp.dot(
        jnp.concatenate(halves(left), axis=1),
        jnp.concatenate([wide, wide], axis=0),
        preferred_element_type=jnp.float32,
    )
    span = roots * width
    middle_high, middle_low = halves(both[:, :span] + both[:, span:])
    for k in range(terms):
        lanes = slice(k * width, (k + 1) * width)
        for r in range(roots):
            part = (slice(k * rows, (k + 1) * rows), slice(r * width, (r + 1) * width))
            lhs[r * rows : (r + 1) * rows, lanes] = middle_high[part]
            lhs[(roots + r) * rows : (roots + r + 1) * rows, lanes] = middle_low[part]
    blank = jnp.zeros((width, width), jnp.bfloat16)
    for k in range(terms):
        lanes = slice(k * width, (k + 1) * width)
        kind = table[3 * count + k]
        used = pl.ds(pl.multiple_of((1 - kind) * width, width), width)
        unused = pl.ds(pl.multiple_of(kind * width, width), width)
        high, low = halves(r_ref[k, 0])
        high_rhs[used, lanes] = high
        high_rhs[unused, lanes] = blank
        low_rhs[used, lanes] = low
        low_rhs[unused, lanes] = blank
    dims = (((1,), (1,)), ((), ()))
    tall = lax.dot_general(lhs[...], high_rhs[...], dims, preferred_element_type=jnp.float32)
    short = lax.dot_general(
        lhs[: roots * rows], low_rhs[...], dims, preferred_element_type=jnp.float32
    )
    result = tall[: roots * rows] + tall[roots * rows :] + short
    moved_ref[0] = result[:, :width].reshape(roots, rows, width)
    kept_ref[0] = result[:, width:].reshape(roots, rows, width)


def sectors(table, base, size, left, right, own, other, kept, ordered):
    terms, count, rows, _ = left.shape
    roots, width = own.shape[1], own.shape[3]

    def source(i, table):
        return table[base + i]

    def held(i, table):
        return base + i if ordered else table[base + i]

    def vector_at(i, table):
        return (held(i, table), 0, 0, 0)

    block = (1, roots, rows, width)
    in_specs = [
        pl.BlockSpec((terms, 1, rows, 2 * rows), lambda i, t: (0, source(i, t), 0, 0)),
        pl.BlockSpec((terms, 1, width, width), lambda i, t: (0, source(i, t), 0, 0)),
        pl.BlockSpec(block, vector_at),
        pl.BlockSpec(block, vector_at),
    ]
    args = [left, right, own, other]
    aliases = {}
    if kept is not None:
        in_specs.append(ANY)
        args.append(kept)
        aliases = {5: 1}
    flops = size * terms * rows * width * roots * width * 4 * 3
    return pl.pallas_call(
        functools.partial(sector_kernel, count, terms),
        out_shape=[
            jax.ShapeDtypeStruct((size,) + block[1:], jnp.float32),
            jax.ShapeDtypeStruct((count,) + block[1:], jnp.float32),
        ],
        grid_spec=pltpu.PrefetchScalarGridSpec(
            num_scalar_prefetch=1,
            grid=(size,),
            in_specs=in_specs,
            out_specs=[
                pl.BlockSpec(block, lambda i, t: (i, 0, 0, 0)),
                pl.BlockSpec(block, lambda i, t: (source(i, t), 0, 0, 0)),
            ],
            scratch_shapes=[
                pltpu.VMEM((2 * roots * rows, terms * width), jnp.bfloat16),
                pltpu.VMEM((2 * width, terms * width), jnp.bfloat16),
                pltpu.VMEM((2 * width, terms * width), jnp.bfloat16),
            ],
        ),
        input_output_aliases=aliases,
        compiler_params=pltpu.CompilerParams(vmem_limit_bytes=LIMIT),
        cost_estimate=pl.CostEstimate(
            flops=flops, bytes_accessed=size * terms * 3 * rows * width * 4, transcendentals=0
        ),
        name="sectors",
    )(table, *args)


def gather_kernel(share, with_inner, table, kept_ref, arrived_ref, vector_ref, diag_ref, sum_ref, *rest):
    vector = vector_ref[0]
    total = kept_ref[0] + arrived_ref[0] + (share * diag_ref[0])[None] * vector
    sum_ref[0] = total
    if with_inner:
        inner_ref = rest[0]

        @pl.when(pl.program_id(0) == 0)
        def _():
            inner_ref[...] = jnp.zeros_like(inner_ref)

        for r in range(vector.shape[0]):
            inner_ref[r : r + 1] += jnp.sum(vector[r] * total[r], axis=0, keepdims=True)


def combine(table, base, size, kept, arrived, vector, diag, share, ordered, with_inner):
    count, roots, rows, width = kept.shape
    block = (1, roots, rows, width)

    def slot(i, table):
        return table[count + base + i]

    def held(i, table):
        return table[2 * count + slot(i, table)] if ordered else slot(i, table)

    out_shape = [jax.ShapeDtypeStruct((size,) + block[1:], jnp.float32)]
    out_specs = [pl.BlockSpec(block, lambda i, t: (i, 0, 0, 0))]
    if with_inner:
        out_shape.append(jax.ShapeDtypeStruct((8, width), jnp.float32))
        out_specs.append(pl.BlockSpec((8, width), lambda i, t: (0, 0)))
    out = pl.pallas_call(
        functools.partial(gather_kernel, share, with_inner),
        out_shape=out_shape,
        grid_spec=pltpu.PrefetchScalarGridSpec(
            num_scalar_prefetch=1,
            grid=(size,),
            in_specs=[
                pl.BlockSpec(block, lambda i, t: (slot(i, t), 0, 0, 0)),
                pl.BlockSpec(block, lambda i, t: (i, 0, 0, 0)),
                pl.BlockSpec(block, lambda i, t: (held(i, t), 0, 0, 0)),
                pl.BlockSpec((1, rows, width), lambda i, t: (slot(i, t), 0, 0)),
            ],
            out_specs=out_specs,
        ),
        compiler_params=pltpu.CompilerParams(vmem_limit_bytes=LIMIT),
        cost_estimate=pl.CostEstimate(
            flops=size * roots * rows * width * 4,
            bytes_accessed=size * roots * rows * width * 16,
            transcendentals=0,
        ),
        name="combine",
    )(table, kept, arrived, vector, diag)
    return out if with_inner else (out[0], None)


def correct_kernel(pieces, table, weight_ref, inner_ref, vector_ref, diag_ref, *rest):
    parts, (raw_ref, squares_ref) = rest[:-2], rest[-2:]
    count, roots, rows, width = vector_ref.shape
    theta = jnp.sum(inner_ref[...], axis=1, keepdims=True) / jnp.sum(
        weight_ref[...], axis=1, keepdims=True
    )
    squares = [jnp.zeros((1, width), jnp.float32) for _ in range(roots)]
    for piece, (base, size) in enumerate(pieces):
        mine, theirs = parts[2 * piece], parts[2 * piece + 1]
        for i in range(size):
            slot = table[count + base + i]
            place = table[2 * count + slot]
            diag = diag_ref[slot]
            for r in range(roots):
                shift = theta[r : r + 1]
                sigma = mine[i, r] + theirs[i, r]
                raw = (sigma - shift * vector_ref[slot, r]) / jnp.maximum(jnp.abs(diag - shift), 1.0)
                raw_ref[place, r] = raw
                squares[r] = squares[r] + jnp.sum(raw * raw, axis=0, keepdims=True)
    squares_ref[...] = jnp.zeros_like(squares_ref)
    for r in range(roots):
        squares_ref[r : r + 1] = squares[r]


def correct(table, pieces, weight, inner, vector, diag, parts):
    return pl.pallas_call(
        functools.partial(correct_kernel, pieces),
        out_shape=[
            jax.ShapeDtypeStruct(vector.shape, jnp.float32),
            jax.ShapeDtypeStruct(weight.shape, jnp.float32),
        ],
        in_specs=[SCALARS] + [WHOLE] * (4 + len(parts)),
        out_specs=[WHOLE, WHOLE],
        compiler_params=pltpu.CompilerParams(vmem_limit_bytes=LIMIT),
        name="correct",
    )(table, weight, inner, vector, diag, *parts)


def scale_of(squares_ref, count):
    return lax.rsqrt(jnp.sum(squares_ref[...], axis=1, keepdims=True) / count + 1e-06)


def scaled_kernel(count, table, squares_ref, raw_ref, out_ref):
    scale = scale_of(squares_ref, count)
    for r in range(raw_ref.shape[1]):
        out_ref[0, r] = raw_ref[0, r] * scale[r : r + 1]


def scaled(table, squares, raw, count):
    slots, roots, rows, width = raw.shape
    block = (1, roots, rows, width)
    return pl.pallas_call(
        functools.partial(scaled_kernel, count),
        out_shape=jax.ShapeDtypeStruct(raw.shape, jnp.float32),
        grid_spec=pltpu.PrefetchScalarGridSpec(
            num_scalar_prefetch=1,
            grid=(slots,),
            in_specs=[
                pl.BlockSpec(squares.shape, lambda i, t: (0, 0)),
                pl.BlockSpec(block, lambda i, t: (t[2 * slots + i], 0, 0, 0)),
            ],
            out_specs=pl.BlockSpec(block, lambda i, t: (i, 0, 0, 0)),
        ),
        compiler_params=pltpu.CompilerParams(vmem_limit_bytes=LIMIT),
        name="scaled",
    )(table, squares, raw)


def finish_kernel(count, table, squares_ref, mine_ref, theirs_ref, *rest):
    out_ref = rest[-1]
    scale = scale_of(squares_ref, count)
    for r in range(mine_ref.shape[1]):
        out_ref[0, r] = (mine_ref[0, r] + theirs_ref[0, r]) * scale[r : r + 1]


def finish(table, base, squares, mine, theirs, out, slots, count):
    size, roots, rows, width = mine.shape
    block = (1, roots, rows, width)
    in_specs = [
        pl.BlockSpec(squares.shape, lambda i, t: (0, 0)),
        pl.BlockSpec(block, lambda i, t: (i, 0, 0, 0)),
        pl.BlockSpec(block, lambda i, t: (i, 0, 0, 0)),
    ]
    args, aliases = [squares, mine, theirs], {}
    if out is not None:
        in_specs.append(ANY)
        args.append(out)
        aliases = {4: 0}
    return pl.pallas_call(
        functools.partial(finish_kernel, count),
        out_shape=jax.ShapeDtypeStruct((slots,) + block[1:], jnp.float32),
        grid_spec=pltpu.PrefetchScalarGridSpec(
            num_scalar_prefetch=1,
            grid=(size,),
            in_specs=in_specs,
            out_specs=pl.BlockSpec(block, lambda i, t: (t[slots + base + i], 0, 0, 0)),
        ),
        input_output_aliases=aliases,
        compiler_params=pltpu.CompilerParams(vmem_limit_bytes=LIMIT),
        name="finish",
    )(table, *args)


def add_over_term(value):
    size = lax.axis_size("term")
    if size == 1 or not power_of_two(size):
        return lax.psum(value, "term"), jnp.zeros_like(value)
    bit = 1
    while 2 * bit < size:
        value = value + flip(value, "term", bit)
        bit *= 2
    return value, flip(value, "term", bit)


def shards(amplitudes, left, right, term_kind, partner, left_diag, right_diag):
    devices, terms_over = lax.axis_size("blk"), lax.axis_size("term")
    vector = jnp.transpose(amplitudes, (0, 2, 1, 3))
    slots, roots, rows, width = vector.shape
    per = slots // devices
    count = slots * devices * rows * lax.axis_size("sub") * width
    table = make_table(partner, term_kind)
    diag = left_diag[:, :, None] + right_diag[:, None, :]

    moving = [c for c in range(1, devices) if 2 * c != devices]
    moving.sort(key=lambda c: min(c, devices - c))
    moving = [(c, c * per, per) for c in moving]
    if devices % 2 == 0:
        c, cut = devices // 2, (per + 1) // 2
        moving.append((c, c * per, cut))
        if per > cut:
            moving.append((c, c * per + cut, per - cut))
    staying = (0, 0, per)
    order = [staying] + moving
    spans = [(base, size) for _, base, size in order]

    def sub_pair(value):
        return lax.ppermute(value, "sub", [(0, 1), (1, 0)])

    def partials(own, ordered, with_inner):
        other = sub_pair(own)
        kept, outgoing = None, {}
        for piece in moving + [staying]:
            outgoing[piece], kept = sectors(
                table, piece[1], piece[2], left, right, own, other, kept, ordered
            )
        sums, inners, arrivals = [], [], []
        for at, piece in enumerate(order):
            c, base, size = piece
            arrived = outgoing[piece]
            if c:
                if len(arrivals) >= 2:
                    arrived, _ = lax.optimization_barrier((arrived, arrivals[-2]))
                arrived = lax.ppermute(
                    arrived, "blk", [(p, (p + c) % devices) for p in range(devices)]
                )
                arrivals.append(arrived)
            mine, inner = combine(
                table, base, size, kept, arrived, own, diag, 1.0 / terms_over, ordered, with_inner
            )
            sums += list(add_over_term(mine))
            inners.append(inner)
        return sums, inners

    weight = jnp.sum(vector * vector, axis=(0, 2))
    weight = jnp.pad(weight, ((0, 8 - roots), (0, 0)), constant_values=1.0)
    weight = small_sum(small_sum(weight, "sub"), "blk")
    sums, inners = partials(vector, False, True)
    inner = sum(inners[1:], inners[0])
    for axis in ("sub", "term", "blk"):
        inner = small_sum(inner, axis)
    raw, squares = correct(table, spans, weight, inner, vector, diag, sums)
    for axis in ("sub", "blk"):
        squares = small_sum(squares, axis)
    sums, _ = partials(raw, True, False)
    correction = scaled(table, squares, raw, count)
    sigma = None
    for piece, (base, size) in enumerate(spans):
        sigma = finish(
            table, base, squares, sums[2 * piece], sums[2 * piece + 1], sigma, slots, count
        )
    return jnp.transpose(sigma, (0, 2, 1, 3)), jnp.transpose(correction, (0, 2, 1, 3))


def solution(mesh):
    return jax.shard_map(
        shards,
        mesh=mesh,
        in_specs=(
            P(("grp", "blk"), "sub", None, None),
            P(("grp", "term"), "blk", "sub", None),
            P(("grp", "term"), "blk", None, None),
            P(("grp", "term")),
            P(("grp", "blk")),
            P(("grp", "blk"), "sub"),
            P(("grp", "blk"), None),
        ),
        out_specs=(P(("grp", "blk"), "sub", None, None), P(("grp", "blk"), "sub", None, None)),
        check_vma=False,
    )
```

```python
import functools

import jax
import jax.numpy as jnp
from jax import lax
from jax.experimental import pallas as pl
from jax.experimental.pallas import tpu as pltpu
from jax.sharding import PartitionSpec as P

LIMIT = 48 * 1024 * 1024
SMALL = 24 * 1024 * 1024
FREE = pl.CostEstimate(flops=0, bytes_accessed=0, transcendentals=0)
WHOLE = pl.BlockSpec(memory_space=pltpu.VMEM)
SCALARS = pl.BlockSpec(memory_space=pltpu.SMEM)
ANY = pl.BlockSpec(memory_space=pl.ANY)


def power_of_two(size):
    return size & (size - 1) == 0


def flip(value, axis, bit):
    size = lax.axis_size(axis)
    return lax.ppermute(value, axis, [(i, i ^ bit) for i in range(size)])


def small_sum(value, axis):
    size = lax.axis_size(axis)
    if not power_of_two(size):
        return lax.psum(value, axis)
    if size == 4:
        one, two, three = (flip(value, axis, bit) for bit in (1, 2, 3))
        return (value + one) + (two + three)
    bit = 1
    while bit < size:
        value = value + flip(value, axis, bit)
        bit *= 2
    return value


def halves(value):
    high = value.astype(jnp.bfloat16)
    low = (value - high.astype(jnp.float32)).astype(jnp.bfloat16)
    return high, low


def table_kernel(devices, partner_ref, kind_ref, table_ref, used):
    count, terms = partner_ref.shape[0], kind_ref.shape[0]
    per = count // devices
    me = lax.axis_index("blk")
    for c in range(devices):
        used[c] = 0

    def place(j, carry):
        where_to = partner_ref[j]
        owner = lax.div(where_to, count)
        offset = lax.rem(owner - me + devices, devices)
        at = offset * per + used[offset]
        used[offset] = used[offset] + 1
        table_ref[at] = j
        table_ref[count + at] = where_to - owner * count
        table_ref[2 * count + j] = at
        return carry

    lax.fori_loop(0, count, place, 0)
    for k in range(terms):
        table_ref[3 * count + k] = kind_ref[k]
    table_ref[3 * count + terms] = lax.axis_index("sub")


def make_table(partner, term_kind):
    devices = lax.axis_size("blk")
    length = 3 * partner.shape[0] + term_kind.shape[0] + 1
    return pl.pallas_call(
        functools.partial(table_kernel, devices),
        out_shape=jax.ShapeDtypeStruct((length,), jnp.int32),
        in_specs=[SCALARS, SCALARS],
        out_specs=SCALARS,
        scratch_shapes=[pltpu.SMEM((devices,), jnp.int32)],
    )(partner, term_kind)


def sector(table, count, terms, l_ref, r_ref, own_ref, other_ref, lhs, high_rhs, low_rhs):
    roots, rows, width = own_ref.shape[1:]
    first = table[3 * count + terms] == 0
    own, other = own_ref[0], other_ref[0]
    top = jnp.where(first, own, other)
    bottom = jnp.where(first, other, own)
    left = l_ref[:, 0].reshape(terms * rows, 2 * rows)
    left = jnp.concatenate(halves(left), axis=1)
    for r in range(roots):
        wide = jnp.concatenate(halves(jnp.concatenate([top[r], bottom[r]], axis=0)), axis=1)
        both = jnp.dot(
            left, jnp.concatenate([wide, wide], axis=0), preferred_element_type=jnp.float32
        )
        high, low = halves(both[:, :width] + both[:, width:])
        for k in range(terms):
            lanes = slice(k * width, (k + 1) * width)
            part = slice(k * rows, (k + 1) * rows)
            lhs[r * rows : (r + 1) * rows, lanes] = high[part]
            lhs[(roots + r) * rows : (roots + r + 1) * rows, lanes] = low[part]
    for k in range(terms):
        lanes = slice(k * width, (k + 1) * width)
        kind = table[3 * count + k]
        used = pl.ds(pl.multiple_of((1 - kind) * width, width), width)
        high, low = halves(r_ref[k, 0])
        high_rhs[used, lanes] = high
        low_rhs[used, lanes] = low
    dims = (((1,), (1,)), ((), ()))
    tall = lax.dot_general(lhs[...], high_rhs[...], dims, preferred_element_type=jnp.float32)
    short = lax.dot_general(
        lhs[: roots * rows], low_rhs[...], dims, preferred_element_type=jnp.float32
    )
    result = tall[: roots * rows] + tall[roots * rows :] + short
    return result.reshape(roots, rows, 2 * width)


def sector_kernel(count, terms, unroll, starts, table, *refs):
    inputs, scratch = refs[: 4 * unroll], refs[-3 * unroll :]
    outputs = refs[-3 * unroll - len(starts) : -3 * unroll]
    moved_refs, kept_ref = outputs[:-1], outputs[-1]
    width = kept_ref.shape[3]
    step = pl.program_id(0)

    @pl.when(step == 0)
    def _():
        for ref in scratch:
            if ref.shape[0] == 2 * width:
                ref[...] = jnp.zeros_like(ref)

    results = [
        sector(table, count, terms, *inputs[4 * u : 4 * u + 4], *scratch[3 * u : 3 * u + 3])
        for u in range(unroll)
    ]
    for u in range(unroll):
        kept_ref[u] = results[u][:, :, width:]
    for ref, begin, end in zip(moved_refs, starts, starts[1:]):

        @pl.when((step >= begin) & (step < end))
        def _(ref=ref):
            for u in range(unroll):
                ref[u] = results[u][:, :, :width]


def sectors(table, pieces, left, right, own, other, kept, ordered):
    terms, count, rows, _ = left.shape
    roots, width = own.shape[1], own.shape[3]
    unroll = 2 if all(base % 2 == 0 and size % 2 == 0 for base, size in pieces) else 1
    starts = [0]
    for _, size in pieces:
        starts.append(starts[-1] + size // unroll)

    def place(i):
        at = pieces[0][0] // unroll + i
        for begin, (base, _) in zip(starts[1:], pieces[1:]):
            at = jnp.where(i >= begin, base // unroll + i - begin, at)
        return at

    def specs(u):
        def source(i, table):
            return table[unroll * place(i) + u]

        def held(i, table):
            return (unroll * place(i) + u if ordered else source(i, table), 0, 0, 0)

        return [
            pl.BlockSpec((terms, 1, rows, 2 * rows), lambda i, t: (0, source(i, t), 0, 0)),
            pl.BlockSpec((terms, 1, width, width), lambda i, t: (0, source(i, t), 0, 0)),
            pl.BlockSpec((1, roots, rows, width), held),
            pl.BlockSpec((1, roots, rows, width), held),
        ]

    def moved_spec(begin, end):
        return pl.BlockSpec(block, lambda i, t: (jnp.clip(i - begin, 0, end - begin - 1), 0, 0, 0))

    block = (unroll, roots, rows, width)
    in_specs = [spec for u in range(unroll) for spec in specs(u)]
    args = [left, right, own, other] * unroll
    aliases = {}
    if kept is not None:
        in_specs.append(ANY)
        args.append(kept)
        aliases = {4 * unroll + 1: len(pieces)}
    out = pl.pallas_call(
        functools.partial(sector_kernel, count, terms, unroll, starts),
        out_shape=[
            jax.ShapeDtypeStruct((size,) + block[1:], jnp.float32)
            for size in [size for _, size in pieces] + [count]
        ],
        grid_spec=pltpu.PrefetchScalarGridSpec(
            num_scalar_prefetch=1,
            grid=(starts[-1],),
            in_specs=in_specs,
            out_specs=[moved_spec(begin, end) for begin, end in zip(starts, starts[1:])]
            + [pl.BlockSpec(block, lambda i, t: (place(i), 0, 0, 0))],
            scratch_shapes=[
                pltpu.VMEM((2 * roots * rows, terms * width), jnp.bfloat16),
                pltpu.VMEM((2 * width, terms * width), jnp.bfloat16),
                pltpu.VMEM((2 * width, terms * width), jnp.bfloat16),
            ]
            * unroll,
        ),
        input_output_aliases=aliases,
        compiler_params=pltpu.CompilerParams(vmem_limit_bytes=LIMIT),
        cost_estimate=FREE,
        name="sectors",
    )(table, *args)
    return out[:-1], out[-1]


def gather_kernel(share, with_inner, table, kept_ref, arrived_ref, vector_ref, diag_ref, sum_ref, *rest):
    vector = vector_ref[0]
    total = kept_ref[0] + arrived_ref[0] + (share * diag_ref[0])[None] * vector
    sum_ref[0] = total
    if with_inner:
        inner_ref = rest[0]
        roots = vector.shape[0]

        @pl.when(pl.program_id(0) == 0)
        def _():
            inner_ref[...] = jnp.zeros_like(inner_ref)

        for r in range(roots):
            inner_ref[r : r + 1] += jnp.sum(vector[r] * total[r], axis=0, keepdims=True)
            inner_ref[roots + r : roots + r + 1] += share * jnp.sum(
                vector[r] * vector[r], axis=0, keepdims=True
            )


def combine(table, base, size, kept, arrived, vector, diag, share, ordered, with_inner):
    count, roots, rows, width = kept.shape
    block = (1, roots, rows, width)

    def slot(i, table):
        return table[count + base + i]

    def place(i, table):
        return table[2 * count + slot(i, table)]

    def held(i, table):
        return place(i, table) if ordered else slot(i, table)

    out_shape = [jax.ShapeDtypeStruct((size,) + block[1:], jnp.float32)]
    out_specs = [pl.BlockSpec(block, lambda i, t: (i, 0, 0, 0))]
    if with_inner:
        out_shape.append(jax.ShapeDtypeStruct((8, width), jnp.float32))
        out_specs.append(pl.BlockSpec((8, width), lambda i, t: (0, 0)))
    out = pl.pallas_call(
        functools.partial(gather_kernel, share, with_inner),
        out_shape=out_shape,
        grid_spec=pltpu.PrefetchScalarGridSpec(
            num_scalar_prefetch=1,
            grid=(size,),
            in_specs=[
                pl.BlockSpec(block, lambda i, t: (place(i, t), 0, 0, 0)),
                pl.BlockSpec(block, lambda i, t: (i, 0, 0, 0)),
                pl.BlockSpec(block, lambda i, t: (held(i, t), 0, 0, 0)),
                pl.BlockSpec((1, rows, width), lambda i, t: (slot(i, t), 0, 0)),
            ],
            out_specs=out_specs,
        ),
        compiler_params=pltpu.CompilerParams(vmem_limit_bytes=SMALL),
        cost_estimate=FREE,
        name="combine",
    )(table, kept, arrived, vector, diag)
    return out if with_inner else (out[0], None)


def correct_kernel(pieces, table, inner_ref, vector_ref, diag_ref, *rest):
    parts, (raw_ref, squares_ref) = rest[:-2], rest[-2:]
    count, roots, rows, width = vector_ref.shape
    inner = jnp.sum(inner_ref[...], axis=1, keepdims=True)
    theta = inner[:roots] / inner[roots : 2 * roots]
    squares = [jnp.zeros((1, width), jnp.float32) for _ in range(roots)]
    for piece, (base, size) in enumerate(pieces):
        mine, theirs = parts[2 * piece], parts[2 * piece + 1]
        for i in range(size):
            slot = table[count + base + i]
            place = table[2 * count + slot]
            diag = diag_ref[slot]
            for r in range(roots):
                shift = theta[r : r + 1]
                sigma = mine[i, r] + theirs[i, r]
                raw = (sigma - shift * vector_ref[slot, r]) / jnp.maximum(jnp.abs(diag - shift), 1.0)
                raw_ref[place, r] = raw
                squares[r] = squares[r] + jnp.sum(raw * raw, axis=0, keepdims=True)
    squares_ref[...] = jnp.zeros_like(squares_ref)
    for r in range(roots):
        squares_ref[r : r + 1] = squares[r]


def correct(table, pieces, inner, vector, diag, parts):
    return pl.pallas_call(
        functools.partial(correct_kernel, pieces),
        out_shape=[
            jax.ShapeDtypeStruct(vector.shape, jnp.float32),
            jax.ShapeDtypeStruct(inner.shape, jnp.float32),
        ],
        in_specs=[SCALARS] + [WHOLE] * (3 + len(parts)),
        out_specs=[WHOLE, WHOLE],
        compiler_params=pltpu.CompilerParams(vmem_limit_bytes=SMALL),
        cost_estimate=FREE,
        name="correct",
    )(table, inner, vector, diag, *parts)


def scaled_kernel(table, scale_ref, raw_ref, out_ref):
    for r in range(raw_ref.shape[1]):
        out_ref[0, r] = raw_ref[0, r] * scale_ref[r : r + 1]


def scaled(table, scale, raw):
    slots, roots, rows, width = raw.shape
    block = (1, roots, rows, width)
    return pl.pallas_call(
        scaled_kernel,
        out_shape=jax.ShapeDtypeStruct(raw.shape, jnp.float32),
        grid_spec=pltpu.PrefetchScalarGridSpec(
            num_scalar_prefetch=1,
            grid=(slots,),
            in_specs=[
                pl.BlockSpec(scale.shape, lambda i, t: (0, 0)),
                pl.BlockSpec(block, lambda i, t: (t[2 * slots + i], 0, 0, 0)),
            ],
            out_specs=pl.BlockSpec(block, lambda i, t: (i, 0, 0, 0)),
        ),
        compiler_params=pltpu.CompilerParams(vmem_limit_bytes=SMALL),
        cost_estimate=FREE,
        name="scaled",
    )(table, scale, raw)


def finish_kernel(table, scale_ref, mine_ref, theirs_ref, *rest):
    out_ref = rest[-1]
    for r in range(mine_ref.shape[1]):
        out_ref[0, r] = (mine_ref[0, r] + theirs_ref[0, r]) * scale_ref[r : r + 1]


def finish(table, base, scale, mine, theirs, out, slots):
    size, roots, rows, width = mine.shape
    block = (1, roots, rows, width)
    in_specs = [
        pl.BlockSpec(scale.shape, lambda i, t: (0, 0)),
        pl.BlockSpec(block, lambda i, t: (i, 0, 0, 0)),
        pl.BlockSpec(block, lambda i, t: (i, 0, 0, 0)),
    ]
    args, aliases = [scale, mine, theirs], {}
    if out is not None:
        in_specs.append(ANY)
        args.append(out)
        aliases = {4: 0}
    return pl.pallas_call(
        finish_kernel,
        out_shape=jax.ShapeDtypeStruct((slots,) + block[1:], jnp.float32),
        grid_spec=pltpu.PrefetchScalarGridSpec(
            num_scalar_prefetch=1,
            grid=(size,),
            in_specs=in_specs,
            out_specs=pl.BlockSpec(block, lambda i, t: (t[slots + base + i], 0, 0, 0)),
        ),
        input_output_aliases=aliases,
        compiler_params=pltpu.CompilerParams(vmem_limit_bytes=SMALL),
        cost_estimate=FREE,
        name="finish",
    )(table, *args)


def add_over_term(value):
    size = lax.axis_size("term")
    if size == 1 or not power_of_two(size):
        return lax.psum(value, "term"), jnp.zeros_like(value)
    bit = 1
    while 2 * bit < size:
        value = value + flip(value, "term", bit)
        bit *= 2
    return value, flip(value, "term", bit)


def shards(amplitudes, left, right, term_kind, partner, left_diag, right_diag):
    devices, terms_over = lax.axis_size("blk"), lax.axis_size("term")
    vector = jnp.transpose(amplitudes, (0, 2, 1, 3))
    slots, roots, rows, width = vector.shape
    per = slots // devices
    count = slots * devices * rows * lax.axis_size("sub") * width
    table = make_table(partner, term_kind)
    diag = left_diag[:, :, None] + right_diag[:, None, :]

    cuts = [(0, per // 2), (per // 2, per - per // 2)] if per > 1 else [(0, per)]
    moving = []
    for c in range(1, (devices + 1) // 2):
        for start, size in cuts:
            moving += [(c, c * per + start, size), (devices - c, (devices - c) * per + start, size)]
    if devices % 2 == 0 and devices > 1:
        c = devices // 2
        moving += [(c, c * per + start, size) for start, size in cuts]
    order = [(0, 0, per)] + moving
    spans = [(base, size) for _, base, size in order]
    batches = [order[1:3], order[3:] + order[:1]]

    def after(value, *others):
        return lax.optimization_barrier((value,) + others)[0]

    def relay(value, c):
        return lax.ppermute(value, "blk", [(p, (p + c) % devices) for p in range(devices)])

    def partials(own, ordered, with_inner):
        other = lax.ppermute(own, "sub", [(0, 1), (1, 0)])
        kept, outgoing = None, {}
        for batch in batches:
            if batch:
                parts, kept = sectors(
                    table, [piece[1:] for piece in batch], left, right, own, other, kept, ordered
                )
                outgoing.update(zip(batch, parts))
        sums, inners, arrivals, exchanged = [], [], [], []
        for piece in order:
            c, base, size = piece
            arrived = outgoing[piece]
            if not c:
                early = []
                for first in batches[0]:
                    early.append(relay(outgoing[first], first[0]))
                arrived = after(arrived, *early)
                arrivals += early
            elif piece not in batches[0]:
                arrived = relay(after(arrived, arrivals[-2]), c)
                arrivals.append(arrived)
            else:
                arrived = arrivals[batches[0].index(piece)]
            mine, inner = combine(
                table, base, size, kept, arrived, own, diag, 1.0 / terms_over, ordered, with_inner
            )
            if len(exchanged) >= 2:
                mine = after(mine, exchanged[-2])
            mine, theirs = add_over_term(mine)
            sums += [mine, theirs]
            exchanged.append(theirs)
            inners.append(inner)
        return sums, inners, kept, exchanged

    sums, inners, _, exchanged = partials(vector, False, True)
    inner = sum(inners[1:], inners[0])
    if len(exchanged) >= 4:
        inner = after(inner, exchanged[-3])
    inner = small_sum(small_sum(inner, ("term", "sub")), "blk")
    raw, squares = correct(table, spans, inner, vector, diag, sums)
    sums, _, kept, _ = partials(raw, True, False)
    squares = small_sum(small_sum(after(squares, kept), "sub"), "blk")
    scale = lax.rsqrt(jnp.sum(squares, axis=1, keepdims=True) / count + 1e-06)
    scale = jnp.broadcast_to(scale, squares.shape)
    correction = scaled(table, scale, raw)
    sigma = None
    for piece, (base, size) in enumerate(spans):
        sigma = finish(
            table, base, scale, sums[2 * piece], sums[2 * piece + 1], sigma, slots
        )
    return jnp.transpose(sigma, (0, 2, 1, 3)), jnp.transpose(correction, (0, 2, 1, 3))


def solution(mesh):
    return jax.shard_map(
        shards,
        mesh=mesh,
        in_specs=(
            P(("grp", "blk"), "sub", None, None),
            P(("grp", "term"), "blk", "sub", None),
            P(("grp", "term"), "blk", None, None),
            P(("grp", "term")),
            P(("grp", "blk")),
            P(("grp", "blk"), "sub"),
            P(("grp", "blk"), None),
        ),
        out_specs=(P(("grp", "blk"), "sub", None, None), P(("grp", "blk"), "sub", None, None)),
        check_vma=False,
    )
```

```python
import functools

import jax
import jax.numpy as jnp
from jax import lax
from jax.experimental import pallas as pl
from jax.experimental.pallas import tpu as pltpu
from jax.sharding import PartitionSpec as P

TAG = 8
LIMIT = 48 * 1024 * 1024
SMALL = 24 * 1024 * 1024
FREE = pl.CostEstimate(flops=0, bytes_accessed=0, transcendentals=0)
WHOLE = pl.BlockSpec(memory_space=pltpu.VMEM)
SCALARS = pl.BlockSpec(memory_space=pltpu.SMEM)
ANY = pl.BlockSpec(memory_space=pl.ANY)


def power_of_two(size):
    return size & (size - 1) == 0


def flip(value, axis, bit):
    size = lax.axis_size(axis)
    return lax.ppermute(value, axis, [(i, i ^ bit) for i in range(size)])


def small_sum(value, axis):
    size = lax.axis_size(axis)
    if not power_of_two(size):
        return lax.psum(value, axis)
    if size == 4:
        one, two, three = (flip(value, axis, bit) for bit in (1, 2, 3))
        return (value + one) + (two + three)
    bit = 1
    while bit < size:
        value = value + flip(value, axis, bit)
        bit *= 2
    return value


def halves(value):
    high = value.astype(jnp.bfloat16)
    low = (value - high.astype(jnp.float32)).astype(jnp.bfloat16)
    return high, low


def table_kernel(devices, partner_ref, kind_ref, table_ref, used):
    count, terms = partner_ref.shape[0], kind_ref.shape[0]
    per = count // devices
    me = lax.axis_index("blk")
    for c in range(devices):
        used[c] = 0

    def place(j, carry):
        where_to = partner_ref[j]
        owner = lax.div(where_to, count)
        offset = lax.rem(owner - me + devices, devices)
        at = offset * per + used[offset]
        used[offset] = used[offset] + 1
        table_ref[at] = j
        table_ref[count + at] = where_to - owner * count
        table_ref[2 * count + j] = at
        return carry

    lax.fori_loop(0, count, place, 0)
    for k in range(terms):
        table_ref[3 * count + k] = kind_ref[k]
    table_ref[3 * count + terms] = lax.axis_index("sub")


def make_table(partner, term_kind):
    devices = lax.axis_size("blk")
    length = 3 * partner.shape[0] + term_kind.shape[0] + 1
    return pl.pallas_call(
        functools.partial(table_kernel, devices),
        out_shape=jax.ShapeDtypeStruct((length,), jnp.int32),
        in_specs=[SCALARS, SCALARS],
        out_specs=SCALARS,
        scratch_shapes=[pltpu.SMEM((devices,), jnp.int32)],
    )(partner, term_kind)


def sector(table, count, terms, l_ref, r_ref, own_ref, other_ref, lhs, high_rhs, low_rhs):
    rows, width = l_ref.shape[2], r_ref.shape[3]
    roots = own_ref.shape[0] // rows
    first = table[3 * count + terms] == 0
    own, other = own_ref[...], other_ref[...]
    top = jnp.where(first, own, other)
    bottom = jnp.where(first, other, own)
    left = l_ref[:, 0].reshape(terms * rows, 2 * rows)
    left = jnp.concatenate(halves(left), axis=1)
    for r in range(roots):
        at = slice(r * rows, (r + 1) * rows)
        wide = jnp.concatenate(halves(jnp.concatenate([top[at], bottom[at]], axis=0)), axis=1)
        both = jnp.dot(
            left, jnp.concatenate([wide, wide], axis=0), preferred_element_type=jnp.float32
        )
        high, low = halves(both[:, :width] + both[:, width:])
        for k in range(terms):
            lanes = slice(k * width, (k + 1) * width)
            part = slice(k * rows, (k + 1) * rows)
            lhs[r * rows : (r + 1) * rows, lanes] = high[part]
            lhs[(roots + r) * rows : (roots + r + 1) * rows, lanes] = low[part]
    for k in range(terms):
        lanes = slice(k * width, (k + 1) * width)
        kind = table[3 * count + k]
        used = pl.ds(pl.multiple_of((1 - kind) * width, width), width)
        high, low = halves(r_ref[k, 0])
        high_rhs[used, lanes] = high
        low_rhs[used, lanes] = low
    dims = (((1,), (1,)), ((), ()))
    tall = lax.dot_general(lhs[...], high_rhs[...], dims, preferred_element_type=jnp.float32)
    short = lax.dot_general(
        lhs[: roots * rows], low_rhs[...], dims, preferred_element_type=jnp.float32
    )
    return tall[: roots * rows] + tall[roots * rows :] + short


def sector_kernel(count, terms, unroll, starts, tags, table, *refs):
    inputs, scratch = refs[: 4 * unroll], refs[-3 * unroll :]
    outputs = refs[-3 * unroll - len(starts) : -3 * unroll]
    tag_refs = refs[4 * unroll : 4 * unroll + 2]
    moved_refs, kept_ref = outputs[:-1], outputs[-1]
    width = kept_ref.shape[1]
    height = kept_ref.shape[0] // unroll
    step = pl.program_id(0)

    @pl.when(step == 0)
    def _():
        for ref in scratch:
            if ref.shape[0] == 2 * width:
                ref[...] = jnp.zeros_like(ref)
        if any(tags):
            tag = tag_refs[0][...] + tag_refs[1][...]
            for ref, begin, end, tagged in zip(moved_refs, starts, starts[1:], tags):
                if tagged:
                    ref[(end - begin) * unroll * height :] = tag

    results = [
        sector(table, count, terms, *inputs[4 * u : 4 * u + 4], *scratch[3 * u : 3 * u + 3])
        for u in range(unroll)
    ]
    for u in range(unroll):
        kept_ref[u * height : (u + 1) * height] = results[u][:, width:]
    for ref, begin, end in zip(moved_refs, starts, starts[1:]):

        @pl.when((step >= begin) & (step < end))
        def _(ref=ref, begin=begin):
            for u in range(unroll):
                at = pl.multiple_of(((step - begin) * unroll + u) * height, height)
                ref[pl.ds(at, height)] = results[u][:, :width]


def place_of(i, pieces):
    at, begin = pieces[0][0] + i, 0
    for (_, size), (base, _) in zip(pieces, pieces[1:]):
        begin += size
        at = jnp.where(i >= begin, base + i - begin, at)
    return at


def sectors(table, pieces, tags, left, right, own, other, kept, ordered):
    terms, count, rows, width = left.shape
    height = own.shape[0] // TAG * TAG // count // rows * rows
    roots = height // rows
    unroll = 2 if all(base % 2 == 0 and size % 2 == 0 for base, size in pieces) else 1
    units = [(base // unroll, size // unroll) for base, size in pieces]
    starts = [0]
    for _, size in units:
        starts.append(starts[-1] + size)

    def specs(u):
        def source(i, table):
            return table[unroll * place_of(i, units) + u]

        def held(i, table):
            return (unroll * place_of(i, units) + u if ordered else source(i, table), 0)

        return [
            pl.BlockSpec((terms, 1, rows, width), lambda i, t: (0, source(i, t), 0, 0)),
            pl.BlockSpec((terms, 1, width, width), lambda i, t: (0, source(i, t), 0, 0)),
            pl.BlockSpec((height, width), held),
            pl.BlockSpec((height, width), held),
        ]

    in_specs = [spec for u in range(unroll) for spec in specs(u)]
    args = [left, right, own, other] * unroll
    if any(tags):
        in_specs += [pl.BlockSpec((TAG, width), lambda i, t: (count * height // TAG, 0))] * 2
        args += [own, other]
    aliases = {}
    if kept is not None:
        in_specs.append(ANY)
        args.append(kept)
        aliases = {len(args): len(pieces)}
    shapes = [(size * height + TAG * tagged, width) for (_, size), tagged in zip(pieces, tags)]
    out = pl.pallas_call(
        functools.partial(sector_kernel, count, terms, unroll, starts, tags),
        out_shape=[
            jax.ShapeDtypeStruct(shape, jnp.float32)
            for shape in shapes + [(count * height, width)]
        ],
        grid_spec=pltpu.PrefetchScalarGridSpec(
            num_scalar_prefetch=1,
            grid=(starts[-1],),
            in_specs=in_specs,
            out_specs=[pl.BlockSpec(shape, lambda i, t: (0, 0)) for shape in shapes]
            + [pl.BlockSpec((unroll * height, width), lambda i, t: (place_of(i, units), 0))],
            scratch_shapes=[
                pltpu.VMEM((2 * height, terms * width), jnp.bfloat16),
                pltpu.VMEM((2 * width, terms * width), jnp.bfloat16),
                pltpu.VMEM((2 * width, terms * width), jnp.bfloat16),
            ]
            * unroll,
        ),
        input_output_aliases=aliases,
        compiler_params=pltpu.CompilerParams(vmem_limit_bytes=LIMIT),
        cost_estimate=FREE,
        name="sectors",
    )(table, *args)
    return out[:-1], out[-1]


def combine_kernel(share, starts, with_inner, table, kept_ref, vector_ref, diag_ref, *refs):
    arrived_refs, sum_ref = refs[: len(starts)], refs[len(starts)]
    rows = diag_ref.shape[1]
    roots = vector_ref.shape[0] // rows
    step = pl.program_id(0)
    arrived = arrived_refs[0][...]
    for ref, begin in zip(arrived_refs[1:], starts[1:]):
        arrived = jnp.where(step >= begin, ref[...], arrived)
    diag = share * diag_ref[0]
    if with_inner:
        inner_ref = refs[-1]

        @pl.when(step == 0)
        def _():
            inner_ref[...] = jnp.zeros_like(inner_ref)

    for r in range(roots):
        at = slice(r * rows, (r + 1) * rows)
        vector = vector_ref[at]
        total = kept_ref[at] + arrived[at] + diag * vector
        sum_ref[at] = total
        if with_inner:
            inner_ref[r : r + 1] += jnp.sum(vector * total, axis=0, keepdims=True)
            inner_ref[roots + r : roots + r + 1] += share * jnp.sum(
                vector * vector, axis=0, keepdims=True
            )


def combine(table, pieces, kept, arrived, vector, diag, share, ordered, with_inner):
    count, rows, width = diag.shape
    height = kept.shape[0] // count
    starts = [0]
    for _, size in pieces:
        starts.append(starts[-1] + size)

    def slot(i, table):
        return table[count + place_of(i, pieces)]

    def place(i, table):
        return table[2 * count + slot(i, table)]

    def held(i, table):
        return (place(i, table) if ordered else slot(i, table), 0)

    def arrived_spec(begin, end):
        return pl.BlockSpec((height, width), lambda i, t: (jnp.clip(i - begin, 0, end - begin - 1), 0))

    block = (height, width)
    out_shape = [jax.ShapeDtypeStruct((starts[-1] * height, width), jnp.float32)]
    out_specs = [pl.BlockSpec(block, lambda i, t: (i, 0))]
    if with_inner:
        out_shape.append(jax.ShapeDtypeStruct((TAG, width), jnp.float32))
        out_specs.append(pl.BlockSpec((TAG, width), lambda i, t: (0, 0)))
    out = pl.pallas_call(
        functools.partial(combine_kernel, share, starts[:-1], with_inner),
        out_shape=out_shape,
        grid_spec=pltpu.PrefetchScalarGridSpec(
            num_scalar_prefetch=1,
            grid=(starts[-1],),
            in_specs=[
                pl.BlockSpec(block, lambda i, t: (place(i, t), 0)),
                pl.BlockSpec(block, held),
                pl.BlockSpec((1, rows, width), lambda i, t: (slot(i, t), 0, 0)),
            ]
            + [arrived_spec(begin, end) for begin, end in zip(starts, starts[1:])],
            out_specs=out_specs,
        ),
        compiler_params=pltpu.CompilerParams(vmem_limit_bytes=SMALL),
        cost_estimate=FREE,
        name="combine",
    )(table, kept, vector, diag, *arrived)
    return out if with_inner else (out[0], None)


def correct_kernel(groups, table, inner_ref, vector_ref, diag_ref, *rest):
    parts, raw_ref = rest[:-1], rest[-1]
    count, rows, width = diag_ref.shape
    height = vector_ref.shape[0] // count
    roots = height // rows
    inner = jnp.sum(inner_ref[...], axis=1, keepdims=True)
    theta = inner[:roots] / inner[roots : 2 * roots]
    squares = [jnp.zeros((1, width), jnp.float32) for _ in range(roots)]
    for at, pieces in enumerate(groups):
        mine, theirs = parts[2 * at], parts[2 * at + 1]
        row = 0
        for base, size in pieces:
            for i in range(size):
                slot = table[count + base + i]
                held = slot * height
                place = table[2 * count + slot] * height
                diag = diag_ref[slot]
                for r in range(roots):
                    shift = theta[r : r + 1]
                    sigma = mine[row : row + rows] + theirs[row : row + rows]
                    vector = vector_ref[pl.ds(pl.multiple_of(held + r * rows, rows), rows)]
                    raw = (sigma - shift * vector) / jnp.maximum(jnp.abs(diag - shift), 1.0)
                    raw_ref[pl.ds(pl.multiple_of(place + r * rows, rows), rows)] = raw
                    squares[r] = squares[r] + jnp.sum(raw * raw, axis=0, keepdims=True)
                    row += rows
    raw_ref[count * height :] = jnp.concatenate(
        squares + [jnp.zeros((TAG - roots, width), jnp.float32)], axis=0
    )


def correct(table, groups, inner, vector, diag, parts):
    return pl.pallas_call(
        functools.partial(correct_kernel, groups),
        out_shape=jax.ShapeDtypeStruct((vector.shape[0] + TAG, vector.shape[1]), jnp.float32),
        in_specs=[SCALARS] + [WHOLE] * (3 + len(parts)),
        out_specs=WHOLE,
        compiler_params=pltpu.CompilerParams(vmem_limit_bytes=SMALL),
        cost_estimate=FREE,
        name="correct",
    )(table, inner, vector, diag, *parts)


def scaled_kernel(rows, table, scale_ref, raw_ref, out_ref):
    for r in range(raw_ref.shape[0] // rows):
        at = slice(r * rows, (r + 1) * rows)
        out_ref[at] = raw_ref[at] * scale_ref[r : r + 1]


def scaled(table, scale, raw, count, rows):
    height, width = raw.shape[0] // count // rows * rows, raw.shape[1]
    return pl.pallas_call(
        functools.partial(scaled_kernel, rows),
        out_shape=jax.ShapeDtypeStruct((count * height, width), jnp.float32),
        grid_spec=pltpu.PrefetchScalarGridSpec(
            num_scalar_prefetch=1,
            grid=(count,),
            in_specs=[
                pl.BlockSpec(scale.shape, lambda i, t: (0, 0)),
                pl.BlockSpec((height, width), lambda i, t: (t[2 * count + i], 0)),
            ],
            out_specs=pl.BlockSpec((height, width), lambda i, t: (i, 0)),
        ),
        compiler_params=pltpu.CompilerParams(vmem_limit_bytes=SMALL),
        cost_estimate=FREE,
        name="scaled",
    )(table, scale, raw)


def finish_kernel(rows, table, scale_ref, mine_ref, theirs_ref, *rest):
    out_ref = rest[-1]
    for r in range(mine_ref.shape[0] // rows):
        at = slice(r * rows, (r + 1) * rows)
        out_ref[at] = (mine_ref[at] + theirs_ref[at]) * scale_ref[r : r + 1]


def finish(table, pieces, scale, mine, theirs, out, count, rows):
    size = sum(size for _, size in pieces)
    height, width = mine.shape[0] // size, mine.shape[1]
    block = (height, width)
    in_specs = [
        pl.BlockSpec(scale.shape, lambda i, t: (0, 0)),
        pl.BlockSpec(block, lambda i, t: (i, 0)),
        pl.BlockSpec(block, lambda i, t: (i, 0)),
    ]
    args, aliases = [scale, mine, theirs], {}
    if out is not None:
        in_specs.append(ANY)
        args.append(out)
        aliases = {4: 0}
    return pl.pallas_call(
        functools.partial(finish_kernel, rows),
        out_shape=jax.ShapeDtypeStruct((count * height, width), jnp.float32),
        grid_spec=pltpu.PrefetchScalarGridSpec(
            num_scalar_prefetch=1,
            grid=(size,),
            in_specs=in_specs,
            out_specs=pl.BlockSpec(block, lambda i, t: (t[count + place_of(i, pieces)], 0)),
        ),
        input_output_aliases=aliases,
        compiler_params=pltpu.CompilerParams(vmem_limit_bytes=SMALL),
        cost_estimate=FREE,
        name="finish",
    )(table, *args)


def add_over_term(value):
    size = lax.axis_size("term")
    if size == 1 or not power_of_two(size):
        return lax.psum(value, "term"), jnp.zeros_like(value)
    bit = 1
    while 2 * bit < size:
        value = value + flip(value, "term", bit)
        bit *= 2
    return value, flip(value, "term", bit)


def after(value, *others):
    return lax.optimization_barrier((value,) + others)[0]


def shards(amplitudes, left, right, term_kind, partner, left_diag, right_diag):
    devices, terms_over = lax.axis_size("blk"), lax.axis_size("term")
    slots, rows, roots, width = amplitudes.shape
    per = slots // devices
    elements = slots * devices * rows * lax.axis_size("sub") * width
    vector = jnp.transpose(amplitudes, (0, 2, 1, 3)).reshape(slots * roots * rows, width)
    table = make_table(partner, term_kind)
    diag = left_diag[:, :, None] + right_diag[:, None, :]

    cuts = [(0, per // 2), (per // 2, per - per // 2)] if per > 1 else [(0, per)]
    staying, moving = (0, 0, per), []
    for c in range(1, (devices + 1) // 2):
        for start, size in cuts:
            moving += [(c, c * per + start, size), (devices - c, (devices - c) * per + start, size)]
    groups = [[staying] + moving[:2]] + [moving[i : i + 2] for i in range(2, len(moving), 2)]
    if devices % 2 == 0:
        c = devices // 2
        opposite = [(c, c * per + start, size) for start, size in cuts]
        groups += [[piece] for piece in opposite]
        moving += opposite
    batches = [moving[:2], moving[2:] + [staying]]

    def spans(pieces):
        return [piece[1:] for piece in pieces]

    def relay(value, c):
        return lax.ppermute(value, "blk", [(p, (p + c) % devices) for p in range(devices)])

    def partials(own, second):
        other = lax.ppermute(own, "sub", [(0, 1), (1, 0)])
        kept, outgoing = None, {}
        for batch in batches:
            parts, kept = sectors(
                table,
                spans(batch),
                [second and piece[0] > 0 for piece in batch],
                left,
                right,
                own,
                other,
                kept,
                second,
            )
            outgoing.update(zip(batch, parts))
        arrived, sums, inners = {}, [], []
        for at, piece in enumerate(moving):
            value = outgoing[piece]
            if at >= 2:
                value = after(value, arrived[moving[at - 2]])
            arrived[piece] = relay(value, piece[0])
        arrived[staying] = after(outgoing[staying], *[arrived[piece] for piece in moving[:2]])
        for group in groups:
            mine, inner = combine(
                table,
                spans(group),
                kept,
                [arrived[piece] for piece in group],
                own,
                diag,
                1.0 / terms_over,
                second,
                not second,
            )
            if len(sums) >= 4:
                mine = after(mine, sums[-3])
            sums += add_over_term(mine)
            inners.append(inner)
        return sums, inners, arrived, other

    sums, inners, _, _ = partials(vector, False)
    inner = sum(inners[1:], inners[0])
    for axis in ("sub", "blk", "term"):
        inner = small_sum(inner, axis)
    raw = correct(table, [spans(group) for group in groups], inner, vector, diag, sums)
    sums, _, arrived, other = partials(raw, True)
    squares = raw[-TAG:] + other[-TAG:]
    seen = set()
    for piece in moving:
        if piece[0] not in seen:
            seen.add(piece[0])
            squares = squares + arrived[piece][-TAG:]
    scale = lax.rsqrt(jnp.sum(squares, axis=1, keepdims=True) / elements + 1e-06)
    scale = jnp.broadcast_to(scale, squares.shape)
    correction = scaled(table, scale, raw, slots, rows)
    sigma = None
    for at, group in enumerate(groups):
        sigma = finish(
            table, spans(group), scale, sums[2 * at], sums[2 * at + 1], sigma, slots, rows
        )
    return tuple(
        jnp.transpose(value.reshape(slots, roots, rows, width), (0, 2, 1, 3))
        for value in (sigma, correction)
    )


def solution(mesh):
    return jax.shard_map(
        shards,
        mesh=mesh,
        in_specs=(
            P(("grp", "blk"), "sub", None, None),
            P(("grp", "term"), "blk", "sub", None),
            P(("grp", "term"), "blk", None, None),
            P(("grp", "term")),
            P(("grp", "blk")),
            P(("grp", "blk"), "sub"),
            P(("grp", "blk"), None),
        ),
        out_specs=(P(("grp", "blk"), "sub", None, None), P(("grp", "blk"), "sub", None, None)),
        check_vma=False,
    )
```

```python
import functools

import jax
import jax.numpy as jnp
from jax import lax
from jax.experimental import pallas as pl
from jax.experimental.pallas import tpu as pltpu
from jax.sharding import PartitionSpec as P

TAG = 8
LIMIT = 48 * 1024 * 1024
SMALL = 24 * 1024 * 1024
FREE = pl.CostEstimate(flops=0, bytes_accessed=0, transcendentals=0)
WHOLE = pl.BlockSpec(memory_space=pltpu.VMEM)
SCALARS = pl.BlockSpec(memory_space=pltpu.SMEM)
ANY = pl.BlockSpec(memory_space=pl.ANY)


def power_of_two(size):
    return size & (size - 1) == 0


def flip(value, axis, bit):
    size = lax.axis_size(axis)
    return lax.ppermute(value, axis, [(i, i ^ bit) for i in range(size)])


def small_sum(value, axis):
    size = lax.axis_size(axis)
    if not power_of_two(size):
        return lax.psum(value, axis)
    if size == 4:
        one, two, three = (flip(value, axis, bit) for bit in (1, 2, 3))
        return (value + one) + (two + three)
    bit = 1
    while bit < size:
        value = value + flip(value, axis, bit)
        bit *= 2
    return value


def halves(value):
    high = value.astype(jnp.bfloat16)
    low = (value - high.astype(jnp.float32)).astype(jnp.bfloat16)
    return high, low


def table_kernel(devices, partner_ref, kind_ref, table_ref, used):
    count, terms = partner_ref.shape[0], kind_ref.shape[0]
    per = count // devices
    me = lax.axis_index("blk")
    for c in range(devices):
        used[c] = 0

    def place(j, carry):
        where_to = partner_ref[j]
        owner = lax.div(where_to, count)
        offset = lax.rem(owner - me + devices, devices)
        at = offset * per + used[offset]
        used[offset] = used[offset] + 1
        table_ref[at] = j
        table_ref[count + at] = where_to - owner * count
        table_ref[2 * count + j] = at
        return carry

    lax.fori_loop(0, count, place, 0)
    for k in range(terms):
        table_ref[3 * count + k] = kind_ref[k]
    table_ref[3 * count + terms] = lax.axis_index("sub")


def make_table(partner, term_kind):
    devices = lax.axis_size("blk")
    length = 3 * partner.shape[0] + term_kind.shape[0] + 1
    return pl.pallas_call(
        functools.partial(table_kernel, devices),
        out_shape=jax.ShapeDtypeStruct((length,), jnp.int32),
        in_specs=[SCALARS, SCALARS],
        out_specs=SCALARS,
        scratch_shapes=[pltpu.SMEM((devices,), jnp.int32)],
    )(partner, term_kind)


def sector(table, count, terms, joined, l_ref, r_ref, own_ref, other_ref, lhs, high_rhs, low_rhs):
    rows, width = l_ref.shape[2], r_ref.shape[3]
    roots = own_ref.shape[0] // rows
    first = table[3 * count + terms] == 0
    own, other = own_ref[...], other_ref[...]
    top = jnp.where(first, own, other)
    bottom = jnp.where(first, other, own)
    left = l_ref[:, 0].reshape(terms * rows, 2 * rows)
    left = jnp.concatenate(halves(left), axis=1)
    wide = []
    for r in range(roots):
        at = slice(r * rows, (r + 1) * rows)
        one = jnp.concatenate(halves(jnp.concatenate([top[at], bottom[at]], axis=0)), axis=1)
        wide.append(jnp.concatenate([one, one], axis=0))
    if joined:
        every = jnp.dot(left, jnp.concatenate(wide, axis=1), preferred_element_type=jnp.float32)
    for r in range(roots):
        if joined:
            both = every[:, 2 * r * width : 2 * (r + 1) * width]
        else:
            both = jnp.dot(left, wide[r], preferred_element_type=jnp.float32)
        high, low = halves(both[:, :width] + both[:, width:])
        for k in range(terms):
            lanes = slice(k * width, (k + 1) * width)
            part = slice(k * rows, (k + 1) * rows)
            lhs[r * rows : (r + 1) * rows, lanes] = high[part]
            lhs[(roots + r) * rows : (roots + r + 1) * rows, lanes] = low[part]
    for k in range(terms):
        lanes = slice(k * width, (k + 1) * width)
        kind = table[3 * count + k]
        used = pl.ds(pl.multiple_of((1 - kind) * width, width), width)
        high, low = halves(r_ref[k, 0])
        high_rhs[used, lanes] = high
        low_rhs[used, lanes] = low
    dims = (((1,), (1,)), ((), ()))
    tall = lax.dot_general(lhs[...], high_rhs[...], dims, preferred_element_type=jnp.float32)
    short = lax.dot_general(
        lhs[: roots * rows], low_rhs[...], dims, preferred_element_type=jnp.float32
    )
    return tall[: roots * rows] + tall[roots * rows :] + short


def sector_kernel(count, terms, unroll, joined, starts, tags, table, *refs):
    inputs, scratch = refs[: 4 * unroll], refs[-3 * unroll :]
    outputs = refs[-3 * unroll - len(starts) : -3 * unroll]
    tag_refs = refs[4 * unroll : 4 * unroll + 2]
    moved_refs, kept_ref = outputs[:-1], outputs[-1]
    width = kept_ref.shape[1]
    height = kept_ref.shape[0] // unroll
    step = pl.program_id(0)

    @pl.when(step == 0)
    def _():
        for ref in scratch:
            if ref.shape[0] == 2 * width:
                ref[...] = jnp.zeros_like(ref)
        if any(tags):
            tag = tag_refs[0][...] + tag_refs[1][...]
            for ref, begin, end, tagged in zip(moved_refs, starts, starts[1:], tags):
                if tagged:
                    ref[(end - begin) * unroll * height :] = tag

    results = [
        sector(table, count, terms, joined, *inputs[4 * u : 4 * u + 4], *scratch[3 * u : 3 * u + 3])
        for u in range(unroll)
    ]
    for u in range(unroll):
        kept_ref[u * height : (u + 1) * height] = results[u][:, width:]
    for ref, begin, end in zip(moved_refs, starts, starts[1:]):

        @pl.when((step >= begin) & (step < end))
        def _(ref=ref, begin=begin):
            for u in range(unroll):
                at = pl.multiple_of(((step - begin) * unroll + u) * height, height)
                ref[pl.ds(at, height)] = results[u][:, :width]


def place_of(i, pieces):
    at, begin = pieces[0][0] + i, 0
    for (_, size), (base, _) in zip(pieces, pieces[1:]):
        begin += size
        at = jnp.where(i >= begin, base + i - begin, at)
    return at


def sectors(table, pieces, tags, left, right, own, other, kept, ordered):
    terms, count, rows, width = left.shape
    height = own.shape[0] // TAG * TAG // count // rows * rows
    roots = height // rows
    unroll = 2 if all(base % 2 == 0 and size % 2 == 0 for base, size in pieces) else 1
    units = [(base // unroll, size // unroll) for base, size in pieces]
    starts = [0]
    for _, size in units:
        starts.append(starts[-1] + size)

    def specs(u):
        def source(i, table):
            return table[unroll * place_of(i, units) + u]

        def held(i, table):
            return (unroll * place_of(i, units) + u if ordered else source(i, table), 0)

        return [
            pl.BlockSpec((terms, 1, rows, width), lambda i, t: (0, source(i, t), 0, 0)),
            pl.BlockSpec((terms, 1, width, width), lambda i, t: (0, source(i, t), 0, 0)),
            pl.BlockSpec((height, width), held),
            pl.BlockSpec((height, width), held),
        ]

    in_specs = [spec for u in range(unroll) for spec in specs(u)]
    args = [left, right, own, other] * unroll
    if any(tags):
        in_specs += [pl.BlockSpec((TAG, width), lambda i, t: (count * height // TAG, 0))] * 2
        args += [own, other]
    aliases = {}
    if kept is not None:
        in_specs.append(ANY)
        args.append(kept)
        aliases = {len(args): len(pieces)}
    shapes = [(size * height + TAG * tagged, width) for (_, size), tagged in zip(pieces, tags)]
    out = pl.pallas_call(
        functools.partial(sector_kernel, count, terms, unroll, not ordered, starts, tags),
        out_shape=[
            jax.ShapeDtypeStruct(shape, jnp.float32)
            for shape in shapes + [(count * height, width)]
        ],
        grid_spec=pltpu.PrefetchScalarGridSpec(
            num_scalar_prefetch=1,
            grid=(starts[-1],),
            in_specs=in_specs,
            out_specs=[pl.BlockSpec(shape, lambda i, t: (0, 0)) for shape in shapes]
            + [pl.BlockSpec((unroll * height, width), lambda i, t: (place_of(i, units), 0))],
            scratch_shapes=[
                pltpu.VMEM((2 * height, terms * width), jnp.bfloat16),
                pltpu.VMEM((2 * width, terms * width), jnp.bfloat16),
                pltpu.VMEM((2 * width, terms * width), jnp.bfloat16),
            ]
            * unroll,
        ),
        input_output_aliases=aliases,
        compiler_params=pltpu.CompilerParams(vmem_limit_bytes=LIMIT),
        cost_estimate=FREE,
        name="sectors",
    )(table, *args)
    return out[:-1], out[-1]


def combine_kernel(share, starts, with_inner, table, kept_ref, vector_ref, diag_ref, *refs):
    arrived_refs, sum_ref = refs[: len(starts)], refs[-2 if with_inner else -1]
    height = vector_ref.shape[0]
    before = refs[len(starts) : -2] if with_inner else ()
    rows = diag_ref.shape[1]
    roots = vector_ref.shape[0] // rows
    step = pl.program_id(0)
    arrived = arrived_refs[0][...]
    for ref, begin in zip(arrived_refs[1:], starts[1:]):
        arrived = jnp.where(step >= begin, ref[...], arrived)
    diag = share * diag_ref[0]
    if with_inner:
        inner_ref = refs[-1]

        @pl.when(step == 0)
        def _():
            inner_ref[...] = sum((ref[...] for ref in before), jnp.zeros_like(inner_ref))

    for r in range(roots):
        at = slice(r * rows, (r + 1) * rows)
        vector = vector_ref[at]
        total = kept_ref[at] + arrived[at] + diag * vector
        if before:
            sum_ref[pl.ds(pl.multiple_of(step * height + r * rows, rows), rows)] = total
        else:
            sum_ref[at] = total
        if with_inner:
            inner_ref[r : r + 1] += jnp.sum(vector * total, axis=0, keepdims=True)
            inner_ref[roots + r : roots + r + 1] += share * jnp.sum(
                vector * vector, axis=0, keepdims=True
            )
    if before:
        sum_ref[sum_ref.shape[0] - TAG :] = inner_ref[...]


def combine(table, pieces, kept, arrived, vector, diag, share, ordered, with_inner, before):
    count, rows, width = diag.shape
    height = kept.shape[0] // count
    starts = [0]
    for _, size in pieces:
        starts.append(starts[-1] + size)

    def slot(i, table):
        return table[count + place_of(i, pieces)]

    def place(i, table):
        return table[2 * count + slot(i, table)]

    def held(i, table):
        return (place(i, table) if ordered else slot(i, table), 0)

    def arrived_spec(begin, end):
        return pl.BlockSpec((height, width), lambda i, t: (jnp.clip(i - begin, 0, end - begin - 1), 0))

    block = (height, width)
    whole = (starts[-1] * height + TAG * bool(before), width)
    out_shape = [jax.ShapeDtypeStruct(whole, jnp.float32)]
    out_specs = [pl.BlockSpec(whole if before else block, lambda i, t: (0 if before else i, 0))]
    if with_inner:
        out_shape.append(jax.ShapeDtypeStruct((TAG, width), jnp.float32))
        out_specs.append(pl.BlockSpec((TAG, width), lambda i, t: (0, 0)))
    out = pl.pallas_call(
        functools.partial(combine_kernel, share, starts[:-1], with_inner),
        out_shape=out_shape,
        grid_spec=pltpu.PrefetchScalarGridSpec(
            num_scalar_prefetch=1,
            grid=(starts[-1],),
            in_specs=[
                pl.BlockSpec(block, lambda i, t: (place(i, t), 0)),
                pl.BlockSpec(block, held),
                pl.BlockSpec((1, rows, width), lambda i, t: (slot(i, t), 0, 0)),
            ]
            + [arrived_spec(begin, end) for begin, end in zip(starts, starts[1:])]
            + [pl.BlockSpec((TAG, width), lambda i, t: (0, 0))] * len(before),
            out_specs=out_specs,
        ),
        compiler_params=pltpu.CompilerParams(vmem_limit_bytes=SMALL),
        cost_estimate=FREE,
        name="combine",
    )(table, kept, vector, diag, *arrived, *before)
    return out if with_inner else (out[0], None)


def correct_kernel(groups, table, inner_ref, vector_ref, diag_ref, *rest):
    parts, raw_ref = rest[:-1], rest[-1]
    count, rows, width = diag_ref.shape
    height = vector_ref.shape[0] // count
    roots = height // rows
    inner = jnp.sum(inner_ref[...], axis=1, keepdims=True)
    theta = inner[:roots] / inner[roots : 2 * roots]
    squares = [jnp.zeros((1, width), jnp.float32) for _ in range(roots)]
    for at, pieces in enumerate(groups):
        mine, theirs = parts[2 * at], parts[2 * at + 1]
        row = 0
        for base, size in pieces:
            for i in range(size):
                slot = table[count + base + i]
                held = slot * height
                place = table[2 * count + slot] * height
                diag = diag_ref[slot]
                for r in range(roots):
                    shift = theta[r : r + 1]
                    sigma = mine[row : row + rows] + theirs[row : row + rows]
                    vector = vector_ref[pl.ds(pl.multiple_of(held + r * rows, rows), rows)]
                    raw = (sigma - shift * vector) / jnp.maximum(jnp.abs(diag - shift), 1.0)
                    raw_ref[pl.ds(pl.multiple_of(place + r * rows, rows), rows)] = raw
                    squares[r] = squares[r] + jnp.sum(raw * raw, axis=0, keepdims=True)
                    row += rows
    raw_ref[count * height :] = jnp.concatenate(
        squares + [jnp.zeros((TAG - roots, width), jnp.float32)], axis=0
    )


def correct(table, groups, inner, vector, diag, parts):
    return pl.pallas_call(
        functools.partial(correct_kernel, groups),
        out_shape=jax.ShapeDtypeStruct((vector.shape[0] + TAG, vector.shape[1]), jnp.float32),
        in_specs=[SCALARS] + [WHOLE] * (3 + len(parts)),
        out_specs=WHOLE,
        compiler_params=pltpu.CompilerParams(vmem_limit_bytes=SMALL),
        cost_estimate=FREE,
        name="correct",
    )(table, inner, vector, diag, *parts)


def scatter(held, out_ref, sems, rows_of):
    height = held.shape[0] // len(rows_of)
    copies = []
    for i, make in enumerate(rows_of):
        at = slice(i * height, (i + 1) * height)
        row = make(at)
        copies.append(
            pltpu.make_async_copy(
                held.at[at], out_ref.at[pl.ds(pl.multiple_of(row, height), height)], sems.at[i]
            )
        )
        copies[-1].start()
    for copy in copies:
        copy.wait()


def scaled_kernel(count, rows, table, scale_ref, raw_ref, out_ref, held, sems):
    height = held.shape[0] // count

    def make(i, at):
        place = pl.multiple_of(table[2 * count + i] * height, height)
        for r in range(height // rows):
            part = raw_ref[pl.ds(place + r * rows, rows)]
            held[at.start + r * rows : at.start + (r + 1) * rows] = part * scale_ref[r : r + 1]
        return i * height

    scatter(held, out_ref, sems, [functools.partial(make, i) for i in range(count)])


def scaled(table, scale, raw, count, rows):
    height, width = raw.shape[0] // count // rows * rows, raw.shape[1]
    return pl.pallas_call(
        functools.partial(scaled_kernel, count, rows),
        out_shape=jax.ShapeDtypeStruct((count * height, width), jnp.float32),
        in_specs=[SCALARS, WHOLE, WHOLE],
        out_specs=ANY,
        scratch_shapes=[
            pltpu.VMEM((count * height, width), jnp.float32),
            pltpu.SemaphoreType.DMA((count,)),
        ],
        compiler_params=pltpu.CompilerParams(vmem_limit_bytes=SMALL),
        cost_estimate=FREE,
        name="scaled",
    )(table, scale, raw)


def finish_kernel(count, rows, places, table, scale_ref, mine_ref, theirs_ref, *rest):
    out_ref, held, sems = rest[-3:]
    height = held.shape[0] // len(places)

    def make(place, at):
        for r in range(height // rows):
            part = slice(at.start + r * rows, at.start + (r + 1) * rows)
            held[part] = (mine_ref[part] + theirs_ref[part]) * scale_ref[r : r + 1]
        return table[count + place] * height

    scatter(held, out_ref, sems, [functools.partial(make, place) for place in places])


def finish(table, pieces, scale, mine, theirs, out, count, rows):
    places = [base + i for base, size in pieces for i in range(size)]
    height, width = mine.shape[0] // len(places), mine.shape[1]
    in_specs = [SCALARS, WHOLE, WHOLE, WHOLE]
    args, aliases = [table, scale, mine, theirs], {}
    if out is not None:
        in_specs.append(ANY)
        args.append(out)
        aliases = {4: 0}
    return pl.pallas_call(
        functools.partial(finish_kernel, count, rows, places),
        out_shape=jax.ShapeDtypeStruct((count * height, width), jnp.float32),
        in_specs=in_specs,
        out_specs=ANY,
        scratch_shapes=[
            pltpu.VMEM(mine.shape, jnp.float32),
            pltpu.SemaphoreType.DMA((len(places),)),
        ],
        input_output_aliases=aliases,
        compiler_params=pltpu.CompilerParams(vmem_limit_bytes=SMALL),
        cost_estimate=FREE,
        name="finish",
    )(*args)


def add_over_term(value):
    size = lax.axis_size("term")
    if size == 1 or not power_of_two(size):
        return lax.psum(value, "term"), jnp.zeros_like(value)
    bit = 1
    while 2 * bit < size:
        value = value + flip(value, "term", bit)
        bit *= 2
    return value, flip(value, "term", bit)


def after(*values):
    return lax.optimization_barrier(values)


def shards(amplitudes, left, right, term_kind, partner, left_diag, right_diag):
    devices, terms_over = lax.axis_size("blk"), lax.axis_size("term")
    slots, rows, roots, width = amplitudes.shape
    per = slots // devices
    elements = slots * devices * rows * lax.axis_size("sub") * width
    vector = jnp.transpose(amplitudes, (0, 2, 1, 3)).reshape(slots * roots * rows, width)
    table = make_table(partner, term_kind)
    diag = left_diag[:, :, None] + right_diag[:, None, :]

    cuts = [(0, per // 2), (per // 2, per - per // 2)] if per > 1 else [(0, per)]
    staying, moving = (0, 0, per), []
    for c in range(1, (devices + 1) // 2):
        for start, size in cuts:
            moving += [(c, c * per + start, size), (devices - c, (devices - c) * per + start, size)]
    groups = [[staying] + moving[:2]] + [moving[i : i + 2] for i in range(2, len(moving), 2)]
    if devices % 2 == 0:
        c = devices // 2
        opposite = [(c, c * per + start, size) for start, size in cuts]
        groups += [[piece] for piece in opposite]
        moving += opposite
    batches = [moving[:2], moving[2:] + [staying]]
    late = len(groups) > 2 and per > 1 and devices % 2 == 0

    def spans(pieces):
        return [piece[1:] for piece in pieces]

    def relay(value, c):
        return lax.ppermute(value, "blk", [(p, (p + c) % devices) for p in range(devices)])

    def partials(own, second, between):
        other = lax.ppermute(own, "sub", [(0, 1), (1, 0)])
        kept, outgoing = None, {}
        for batch in batches:
            parts, kept = sectors(
                table,
                spans(batch),
                [second and piece[0] > 0 for piece in batch],
                left,
                right,
                own,
                other,
                kept,
                second,
            )
            outgoing.update(zip(batch, parts))
        arrived, sums, inners, done = {}, [], [], ()
        for at, piece in enumerate(moving[:-1] if late else moving):
            value = outgoing[piece]
            if at >= 2:
                value = after(value, arrived[moving[at - 2]])[0]
                if 2 * piece[0] == devices:
                    value = after(value, arrived[moving[at - 1]])[0]
            arrived[piece] = relay(value, piece[0])
        arrived[staying] = after(outgoing[staying], *[arrived[piece] for piece in moving[:2]])[0]
        for group in groups:
            if late and group == groups[-1]:
                piece = group[0]
                arrived[piece] = relay(after(outgoing[piece], sums[-2])[0], piece[0])
                if between:
                    arrived[piece], *done = after(arrived[piece], *between(sums, arrived, other))
            first, *others = [arrived[piece] for piece in group]
            if sums:
                first = after(first, sums[-2])[0]
            last = group == groups[-1] and len(groups) > 1
            mine, inner = combine(
                table,
                spans(group),
                kept,
                [first] + others,
                own,
                diag,
                1.0 / terms_over,
                second,
                not second,
                inners if last and not second else (),
            )
            if len(sums) >= 4:
                mine = after(mine, sums[-1 if last else -3])[0]
            sums += add_over_term(mine)
            inners.append(inner)
        if between and not late:
            done = between(sums, arrived, other)
        return sums, inners, done

    sums, inners, _ = partials(vector, False, None)
    if len(groups) > 1:
        inner = sums[-2][-TAG:] + sums[-1][-TAG:]
    else:
        inner = small_sum(inners[0], "term")
    for axis in ("sub", "blk"):
        inner = small_sum(inner, axis)
    raw = correct(table, [spans(group) for group in groups], inner, vector, diag, sums)

    def add_finished(sigma, scale, sums, at):
        return finish(
            table, spans(groups[at]), scale, sums[2 * at], sums[2 * at + 1], sigma, slots, rows
        )

    def correction_and_more(sums, arrived, other):
        squares = raw[-TAG:] + other[-TAG:]
        first_of = {piece[0]: piece for piece in reversed(moving)}
        for c in sorted(first_of):
            squares = squares + arrived[first_of[c]][-TAG:]
        scale = lax.rsqrt(jnp.sum(squares, axis=1, keepdims=True) / elements + 1e-06)
        scale = jnp.broadcast_to(scale, squares.shape)
        return scaled(table, scale, raw, slots, rows), scale, add_finished(None, scale, sums, 0)

    sums, _, (correction, scale, sigma) = partials(raw, True, correction_and_more)
    for at in range(1, len(groups)):
        sigma = add_finished(sigma, scale, sums, at)
    return tuple(
        jnp.transpose(value.reshape(slots, roots, rows, width), (0, 2, 1, 3))
        for value in (sigma, correction)
    )


def solution(mesh):
    return jax.shard_map(
        shards,
        mesh=mesh,
        in_specs=(
            P(("grp", "blk"), "sub", None, None),
            P(("grp", "term"), "blk", "sub", None),
            P(("grp", "term"), "blk", None, None),
            P(("grp", "term")),
            P(("grp", "blk")),
            P(("grp", "blk"), "sub"),
            P(("grp", "blk"), None),
        ),
        out_specs=(P(("grp", "blk"), "sub", None, None), P(("grp", "blk"), "sub", None, None)),
        check_vma=False,
    )
```

```python
import functools

import jax
import jax.numpy as jnp
from jax import lax
from jax.experimental import pallas as pl
from jax.experimental.pallas import tpu as pltpu
from jax.sharding import PartitionSpec as P

TAG = 8
LIMIT = 48 * 1024 * 1024
SMALL = 24 * 1024 * 1024
FREE = pl.CostEstimate(flops=0, bytes_accessed=0, transcendentals=0)
WHOLE = pl.BlockSpec(memory_space=pltpu.VMEM)
SCALARS = pl.BlockSpec(memory_space=pltpu.SMEM)
ANY = pl.BlockSpec(memory_space=pl.ANY)


def power_of_two(size):
    return size & (size - 1) == 0


def flip(value, axis, bit):
    size = lax.axis_size(axis)
    return lax.ppermute(value, axis, [(i, i ^ bit) for i in range(size)])


def small_sum(value, axis):
    size = lax.axis_size(axis)
    if not power_of_two(size):
        return lax.psum(value, axis)
    if size == 4:
        one, two, three = (flip(value, axis, bit) for bit in (1, 2, 3))
        return (value + one) + (two + three)
    bit = 1
    while bit < size:
        value = value + flip(value, axis, bit)
        bit *= 2
    return value


def halves(value):
    high = value.astype(jnp.bfloat16)
    low = (value - high.astype(jnp.float32)).astype(jnp.bfloat16)
    return high, low


def table_kernel(devices, partner_ref, kind_ref, table_ref, used):
    count, terms = partner_ref.shape[0], kind_ref.shape[0]
    per = count // devices
    me = lax.axis_index("blk")
    for c in range(devices):
        used[c] = 0

    def place(j, carry):
        where_to = partner_ref[j]
        owner = lax.div(where_to, count)
        offset = lax.rem(owner - me + devices, devices)
        at = offset * per + used[offset]
        used[offset] = used[offset] + 1
        table_ref[at] = j
        table_ref[count + at] = where_to - owner * count
        table_ref[2 * count + j] = at
        return carry

    lax.fori_loop(0, count, place, 0)
    for k in range(terms):
        table_ref[3 * count + k] = kind_ref[k]
    table_ref[3 * count + terms] = lax.axis_index("sub")


def make_table(partner, term_kind):
    devices = lax.axis_size("blk")
    length = 3 * partner.shape[0] + term_kind.shape[0] + 1
    return pl.pallas_call(
        functools.partial(table_kernel, devices),
        out_shape=jax.ShapeDtypeStruct((length,), jnp.int32),
        in_specs=[SCALARS, SCALARS],
        out_specs=SCALARS,
        scratch_shapes=[pltpu.SMEM((devices,), jnp.int32)],
    )(partner, term_kind)


def sector(table, count, terms, turned, l_ref, r_ref, own_ref, other_ref, lhs, high_rhs, low_rhs):
    rows, width = l_ref.shape[2], r_ref.shape[3]
    roots = own_ref.shape[0] // rows
    first = table[3 * count + terms] == 0
    own, other = own_ref[...], other_ref[...]
    top = jnp.where(first, own, other)
    bottom = jnp.where(first, other, own)
    left = l_ref[:, 0].reshape(terms * rows, 2 * rows)
    left = jnp.concatenate(halves(left), axis=1)
    wide = []
    for r in range(roots):
        at = slice(r * rows, (r + 1) * rows)
        one = jnp.concatenate(halves(jnp.concatenate([top[at], bottom[at]], axis=0)), axis=1)
        wide.append(jnp.concatenate([one, one], axis=0))
    for r in range(roots):
        both = jnp.dot(left, wide[r], preferred_element_type=jnp.float32)
        high, low = halves(both[:, :width] + both[:, width:])
        for k in range(terms):
            lanes = slice(k * width, (k + 1) * width)
            part = slice(k * rows, (k + 1) * rows)
            lhs[r * rows : (r + 1) * rows, lanes] = high[part]
            lhs[(roots + r) * rows : (roots + r + 1) * rows, lanes] = low[part]
    for k in range(terms):
        lanes = slice(k * width, (k + 1) * width)
        kind = table[3 * count + k]
        used = pl.ds(pl.multiple_of((1 - kind) * width, width), width)
        high, low = halves(r_ref[k, 0].T if turned else r_ref[k, 0])
        to = (lanes, used) if turned else (used, lanes)
        high_rhs[to] = high
        low_rhs[to] = low
    dims = (((1,), (0 if turned else 1,)), ((), ()))
    tall = lax.dot_general(lhs[...], high_rhs[...], dims, preferred_element_type=jnp.float32)
    short = lax.dot_general(
        lhs[: roots * rows], low_rhs[...], dims, preferred_element_type=jnp.float32
    )
    return tall[: roots * rows] + tall[roots * rows :] + short


def sector_kernel(count, terms, unroll, turned, starts, tags, table, *refs):
    inputs, scratch = refs[: 4 * unroll], refs[-3 * unroll :]
    outputs = refs[-3 * unroll - len(starts) : -3 * unroll]
    tag_refs = refs[4 * unroll : 4 * unroll + 2]
    moved_refs, kept_ref = outputs[:-1], outputs[-1]
    width = kept_ref.shape[1]
    height = kept_ref.shape[0] // unroll
    step = pl.program_id(0)

    @pl.when(step == 0)
    def _():
        for at, ref in enumerate(scratch):
            if at % 3:
                ref[...] = jnp.zeros_like(ref)
        if any(tags):
            tag = tag_refs[0][...] + tag_refs[1][...]
            for ref, begin, end, tagged in zip(moved_refs, starts, starts[1:], tags):
                if tagged:
                    ref[(end - begin) * unroll * height :] = tag

    results = [
        sector(table, count, terms, turned, *inputs[4 * u : 4 * u + 4], *scratch[3 * u : 3 * u + 3])
        for u in range(unroll)
    ]
    for u in range(unroll):
        kept_ref[u * height : (u + 1) * height] = results[u][:, width:]
    for ref, begin, end in zip(moved_refs, starts, starts[1:]):

        @pl.when((step >= begin) & (step < end))
        def _(ref=ref, begin=begin):
            for u in range(unroll):
                at = pl.multiple_of(((step - begin) * unroll + u) * height, height)
                ref[pl.ds(at, height)] = results[u][:, :width]


def place_of(i, pieces):
    at, begin = pieces[0][0] + i, 0
    for (_, size), (base, _) in zip(pieces, pieces[1:]):
        begin += size
        at = jnp.where(i >= begin, base + i - begin, at)
    return at


def sectors(table, pieces, tags, left, right, own, other, kept, ordered):
    terms, count, rows, width = left.shape
    height = own.shape[0] // TAG * TAG // count // rows * rows
    roots = height // rows
    unroll = 2 if all(base % 2 == 0 and size % 2 == 0 for base, size in pieces) else 1
    units = [(base // unroll, size // unroll) for base, size in pieces]
    starts = [0]
    for _, size in units:
        starts.append(starts[-1] + size)

    def specs(u):
        def source(i, table):
            return table[unroll * place_of(i, units) + u]

        def held(i, table):
            return (unroll * place_of(i, units) + u if ordered else source(i, table), 0)

        return [
            pl.BlockSpec((terms, 1, rows, width), lambda i, t: (0, source(i, t), 0, 0)),
            pl.BlockSpec((terms, 1, width, width), lambda i, t: (0, source(i, t), 0, 0)),
            pl.BlockSpec((height, width), held),
            pl.BlockSpec((height, width), held),
        ]

    in_specs = [spec for u in range(unroll) for spec in specs(u)]
    args = [left, right, own, other] * unroll
    if any(tags):
        in_specs += [pl.BlockSpec((TAG, width), lambda i, t: (count * height // TAG, 0))] * 2
        args += [own, other]
    aliases = {}
    if kept is not None:
        in_specs.append(ANY)
        args.append(kept)
        aliases = {len(args): len(pieces)}
    rhs = (terms * width, 2 * width) if ordered else (2 * width, terms * width)
    shapes = [(size * height + TAG * tagged, width) for (_, size), tagged in zip(pieces, tags)]
    out = pl.pallas_call(
        functools.partial(sector_kernel, count, terms, unroll, ordered, starts, tags),
        out_shape=[
            jax.ShapeDtypeStruct(shape, jnp.float32)
            for shape in shapes + [(count * height, width)]
        ],
        grid_spec=pltpu.PrefetchScalarGridSpec(
            num_scalar_prefetch=1,
            grid=(starts[-1],),
            in_specs=in_specs,
            out_specs=[pl.BlockSpec(shape, lambda i, t: (0, 0)) for shape in shapes]
            + [pl.BlockSpec((unroll * height, width), lambda i, t: (place_of(i, units), 0))],
            scratch_shapes=[
                pltpu.VMEM((2 * height, terms * width), jnp.bfloat16),
                pltpu.VMEM(rhs, jnp.bfloat16),
                pltpu.VMEM(rhs, jnp.bfloat16),
            ]
            * unroll,
        ),
        input_output_aliases=aliases,
        compiler_params=pltpu.CompilerParams(vmem_limit_bytes=LIMIT),
        cost_estimate=FREE,
        name="sectors",
    )(table, *args)
    return out[:-1], out[-1]


def combine_kernel(share, starts, with_inner, table, kept_ref, vector_ref, diag_ref, *refs):
    arrived_refs, sum_ref = refs[: len(starts)], refs[-2 if with_inner else -1]
    height = vector_ref.shape[0]
    before = refs[len(starts) : -2] if with_inner else ()
    rows = diag_ref.shape[1]
    roots = vector_ref.shape[0] // rows
    step = pl.program_id(0)
    arrived = arrived_refs[0][...]
    for ref, begin in zip(arrived_refs[1:], starts[1:]):
        arrived = jnp.where(step >= begin, ref[...], arrived)
    diag = share * diag_ref[0]
    if with_inner:
        inner_ref = refs[-1]

        @pl.when(step == 0)
        def _():
            inner_ref[...] = sum((ref[...] for ref in before), jnp.zeros_like(inner_ref))

    for r in range(roots):
        at = slice(r * rows, (r + 1) * rows)
        vector = vector_ref[at]
        total = kept_ref[at] + arrived[at] + diag * vector
        if before:
            sum_ref[pl.ds(pl.multiple_of(step * height + r * rows, rows), rows)] = total
        else:
            sum_ref[at] = total
        if with_inner:
            inner_ref[r : r + 1] += jnp.sum(vector * total, axis=0, keepdims=True)
            inner_ref[roots + r : roots + r + 1] += share * jnp.sum(
                vector * vector, axis=0, keepdims=True
            )
    if before:
        sum_ref[sum_ref.shape[0] - TAG :] = inner_ref[...]


def combine(table, pieces, kept, arrived, vector, diag, share, ordered, with_inner, before):
    count, rows, width = diag.shape
    height = kept.shape[0] // count
    starts = [0]
    for _, size in pieces:
        starts.append(starts[-1] + size)

    def slot(i, table):
        return table[count + place_of(i, pieces)]

    def place(i, table):
        return table[2 * count + slot(i, table)]

    def held(i, table):
        return (place(i, table) if ordered else slot(i, table), 0)

    def arrived_spec(begin, end):
        return pl.BlockSpec((height, width), lambda i, t: (jnp.clip(i - begin, 0, end - begin - 1), 0))

    block = (height, width)
    whole = (starts[-1] * height + TAG * bool(before), width)
    out_shape = [jax.ShapeDtypeStruct(whole, jnp.float32)]
    out_specs = [pl.BlockSpec(whole if before else block, lambda i, t: (0 if before else i, 0))]
    if with_inner:
        out_shape.append(jax.ShapeDtypeStruct((TAG, width), jnp.float32))
        out_specs.append(pl.BlockSpec((TAG, width), lambda i, t: (0, 0)))
    out = pl.pallas_call(
        functools.partial(combine_kernel, share, starts[:-1], with_inner),
        out_shape=out_shape,
        grid_spec=pltpu.PrefetchScalarGridSpec(
            num_scalar_prefetch=1,
            grid=(starts[-1],),
            in_specs=[
                pl.BlockSpec(block, lambda i, t: (place(i, t), 0)),
                pl.BlockSpec(block, held),
                pl.BlockSpec((1, rows, width), lambda i, t: (slot(i, t), 0, 0)),
            ]
            + [arrived_spec(begin, end) for begin, end in zip(starts, starts[1:])]
            + [pl.BlockSpec((TAG, width), lambda i, t: (0, 0))] * len(before),
            out_specs=out_specs,
        ),
        compiler_params=pltpu.CompilerParams(vmem_limit_bytes=SMALL),
        cost_estimate=FREE,
        name="combine",
    )(table, kept, vector, diag, *arrived, *before)
    return out if with_inner else (out[0], None)


def correct_kernel(groups, table, inner_ref, vector_ref, diag_ref, *rest):
    parts, raw_ref = rest[:-1], rest[-1]
    count, rows, width = diag_ref.shape
    height = vector_ref.shape[0] // count
    roots = height // rows
    inner = jnp.sum(inner_ref[...], axis=1, keepdims=True)
    theta = inner[:roots] / inner[roots : 2 * roots]
    squares = [jnp.zeros((1, width), jnp.float32) for _ in range(roots)]
    for at, pieces in enumerate(groups):
        mine, theirs = parts[2 * at], parts[2 * at + 1]
        row = 0
        for base, size in pieces:
            for i in range(size):
                slot = table[count + base + i]
                held = slot * height
                place = table[2 * count + slot] * height
                diag = diag_ref[slot]
                for r in range(roots):
                    shift = theta[r : r + 1]
                    sigma = mine[row : row + rows] + theirs[row : row + rows]
                    vector = vector_ref[pl.ds(pl.multiple_of(held + r * rows, rows), rows)]
                    raw = (sigma - shift * vector) / jnp.maximum(jnp.abs(diag - shift), 1.0)
                    raw_ref[pl.ds(pl.multiple_of(place + r * rows, rows), rows)] = raw
                    squares[r] = squares[r] + jnp.sum(raw * raw, axis=0, keepdims=True)
                    row += rows
    raw_ref[count * height :] = jnp.concatenate(
        squares + [jnp.zeros((TAG - roots, width), jnp.float32)], axis=0
    )


def correct(table, groups, inner, vector, diag, parts):
    return pl.pallas_call(
        functools.partial(correct_kernel, groups),
        out_shape=jax.ShapeDtypeStruct((vector.shape[0] + TAG, vector.shape[1]), jnp.float32),
        in_specs=[SCALARS] + [WHOLE] * (3 + len(parts)),
        out_specs=WHOLE,
        compiler_params=pltpu.CompilerParams(vmem_limit_bytes=SMALL),
        cost_estimate=FREE,
        name="correct",
    )(table, inner, vector, diag, *parts)


def scatter(held, out_ref, sems, rows_of):
    height = held.shape[0] // len(rows_of)
    copies = []
    for i, make in enumerate(rows_of):
        at = slice(i * height, (i + 1) * height)
        row = make(at)
        copies.append(
            pltpu.make_async_copy(
                held.at[at], out_ref.at[pl.ds(pl.multiple_of(row, height), height)], sems.at[i]
            )
        )
        copies[-1].start()
    for copy in copies:
        copy.wait()


def scaled_kernel(count, rows, table, scale_ref, raw_ref, out_ref, held, sems):
    height = held.shape[0] // count

    def make(i, at):
        place = pl.multiple_of(table[2 * count + i] * height, height)
        for r in range(height // rows):
            part = raw_ref[pl.ds(place + r * rows, rows)]
            held[at.start + r * rows : at.start + (r + 1) * rows] = part * scale_ref[r : r + 1]
        return i * height

    scatter(held, out_ref, sems, [functools.partial(make, i) for i in range(count)])


def scaled(table, scale, raw, count, rows):
    height, width = raw.shape[0] // count // rows * rows, raw.shape[1]
    return pl.pallas_call(
        functools.partial(scaled_kernel, count, rows),
        out_shape=jax.ShapeDtypeStruct((count * height, width), jnp.float32),
        in_specs=[SCALARS, WHOLE, WHOLE],
        out_specs=ANY,
        scratch_shapes=[
            pltpu.VMEM((count * height, width), jnp.float32),
            pltpu.SemaphoreType.DMA((count,)),
        ],
        compiler_params=pltpu.CompilerParams(vmem_limit_bytes=SMALL),
        cost_estimate=FREE,
        name="scaled",
    )(table, scale, raw)


def finish_kernel(count, rows, places, table, scale_ref, mine_ref, theirs_ref, *rest):
    out_ref, held, sems = rest[-3:]
    height = held.shape[0] // len(places)

    def make(place, at):
        for r in range(height // rows):
            part = slice(at.start + r * rows, at.start + (r + 1) * rows)
            held[part] = (mine_ref[part] + theirs_ref[part]) * scale_ref[r : r + 1]
        return table[count + place] * height

    scatter(held, out_ref, sems, [functools.partial(make, place) for place in places])


def finish(table, pieces, scale, mine, theirs, out, count, rows):
    places = [base + i for base, size in pieces for i in range(size)]
    height, width = mine.shape[0] // len(places), mine.shape[1]
    in_specs = [SCALARS, WHOLE, WHOLE, WHOLE]
    args, aliases = [table, scale, mine, theirs], {}
    if out is not None:
        in_specs.append(ANY)
        args.append(out)
        aliases = {4: 0}
    return pl.pallas_call(
        functools.partial(finish_kernel, count, rows, places),
        out_shape=jax.ShapeDtypeStruct((count * height, width), jnp.float32),
        in_specs=in_specs,
        out_specs=ANY,
        scratch_shapes=[
            pltpu.VMEM(mine.shape, jnp.float32),
            pltpu.SemaphoreType.DMA((len(places),)),
        ],
        input_output_aliases=aliases,
        compiler_params=pltpu.CompilerParams(vmem_limit_bytes=SMALL),
        cost_estimate=FREE,
        name="finish",
    )(*args)


def add_over_term(value):
    size = lax.axis_size("term")
    if size == 1 or not power_of_two(size):
        return lax.psum(value, "term"), jnp.zeros_like(value)
    bit = 1
    while 2 * bit < size:
        value = value + flip(value, "term", bit)
        bit *= 2
    return value, flip(value, "term", bit)


def after(*values):
    return lax.optimization_barrier(values)


def shards(amplitudes, left, right, term_kind, partner, left_diag, right_diag):
    devices, terms_over = lax.axis_size("blk"), lax.axis_size("term")
    slots, rows, roots, width = amplitudes.shape
    per = slots // devices
    elements = slots * devices * rows * lax.axis_size("sub") * width
    vector = jnp.transpose(amplitudes, (0, 2, 1, 3)).reshape(slots * roots * rows, width)
    table = make_table(partner, term_kind)
    diag = left_diag[:, :, None] + right_diag[:, None, :]

    staying = (0, 0, per)
    pairs = [
        [(c, c * per, per), (devices - c, (devices - c) * per, per)]
        for c in range(1, (devices + 1) // 2)
    ]
    opposite = []
    if devices % 2 == 0:
        c = devices // 2
        cuts = [(0, per // 2), (per // 2, per - per // 2)] if per > 1 else [(0, per)]
        opposite = [(c, c * per + start, size) for start, size in cuts]
    groups = [[staying]] + pairs + [[piece] for piece in opposite]
    moving = [piece for group in groups[1:] for piece in group]
    batches = [moving[:2], moving[2:] + [staying]]
    late = len(opposite) == 2 and len(pairs) > 0

    def spans(pieces):
        return [piece[1:] for piece in pieces]

    def relay(value, c):
        return lax.ppermute(value, "blk", [(p, (p + c) % devices) for p in range(devices)])

    def partials(own, second, between):
        other = lax.ppermute(own, "sub", [(0, 1), (1, 0)])
        kept, outgoing = None, {}
        for batch in batches:
            parts, kept = sectors(
                table,
                spans(batch),
                [second and piece[0] > 0 for piece in batch],
                left,
                right,
                own,
                other,
                kept,
                second,
            )
            outgoing.update(zip(batch, parts))
        arrived, sums, inners, done = {}, [], [], ()
        for at, piece in enumerate(moving[:-1] if late else moving):
            value = outgoing[piece]
            if at >= 2:
                value = after(value, arrived[moving[at - 2]], arrived[moving[at - 1]])[0]
            arrived[piece] = relay(value, piece[0])
        arrived[staying] = outgoing[staying]
        for group in groups:
            if late and group == groups[-1]:
                piece = group[0]
                arrived[piece] = relay(after(outgoing[piece], sums[-2])[0], piece[0])
                if between:
                    arrived[piece], *done = after(arrived[piece], *between(sums, arrived, other))
            first, *others = [arrived[piece] for piece in group]
            if sums:
                first = after(first, sums[-2])[0]
            last = group == groups[-1] and len(groups) > 1
            mine, inner = combine(
                table,
                spans(group),
                kept,
                [first] + others,
                own,
                diag,
                1.0 / terms_over,
                second,
                not second,
                inners if last and not second else (),
            )
            if len(sums) == 2 or last:
                mine = after(mine, *sums[1::2][-2:])[0]
            sums += add_over_term(mine)
            inners.append(inner)
        if between and not late:
            done = between(sums, arrived, other)
        return sums, inners, done

    sums, inners, _ = partials(vector, False, None)
    if len(groups) > 1:
        inner = sums[-2][-TAG:] + sums[-1][-TAG:]
    else:
        inner = small_sum(inners[0], "term")
    for axis in ("sub", "blk"):
        inner = small_sum(inner, axis)
    raw = correct(table, [spans(group) for group in groups], inner, vector, diag, sums)

    def add_finished(sigma, scale, sums, at):
        return finish(
            table, spans(groups[at]), scale, sums[2 * at], sums[2 * at + 1], sigma, slots, rows
        )

    def correction_and_more(sums, arrived, other):
        squares = raw[-TAG:] + other[-TAG:]
        first_of = {piece[0]: piece for piece in reversed(moving)}
        for c in sorted(first_of):
            squares = squares + arrived[first_of[c]][-TAG:]
        scale = lax.rsqrt(jnp.sum(squares, axis=1, keepdims=True) / elements + 1e-06)
        scale = jnp.broadcast_to(scale, squares.shape)
        return scaled(table, scale, raw, slots, rows), scale, add_finished(None, scale, sums, 0)

    sums, _, (correction, scale, sigma) = partials(raw, True, correction_and_more)
    for at in range(1, len(groups)):
        sigma = add_finished(sigma, scale, sums, at)
    return tuple(
        jnp.transpose(value.reshape(slots, roots, rows, width), (0, 2, 1, 3))
        for value in (sigma, correction)
    )


def solution(mesh):
    return jax.shard_map(
        shards,
        mesh=mesh,
        in_specs=(
            P(("grp", "blk"), "sub", None, None),
            P(("grp", "term"), "blk", "sub", None),
            P(("grp", "term"), "blk", None, None),
            P(("grp", "term")),
            P(("grp", "blk")),
            P(("grp", "blk"), "sub"),
            P(("grp", "blk"), None),
        ),
        out_specs=(P(("grp", "blk"), "sub", None, None), P(("grp", "blk"), "sub", None, None)),
        check_vma=False,
    )
```

```python
import functools

import jax
import jax.numpy as jnp
from jax import lax
from jax.experimental import pallas as pl
from jax.experimental.pallas import tpu as pltpu
from jax.sharding import PartitionSpec as P

TAG = 8
LIMIT = 48 * 1024 * 1024
SMALL = 24 * 1024 * 1024
FREE = pl.CostEstimate(flops=0, bytes_accessed=0, transcendentals=0)
WHOLE = pl.BlockSpec(memory_space=pltpu.VMEM)
SCALARS = pl.BlockSpec(memory_space=pltpu.SMEM)
ANY = pl.BlockSpec(memory_space=pl.ANY)


def power_of_two(size):
    return size & (size - 1) == 0


def flip(value, axis, bit):
    size = lax.axis_size(axis)
    return lax.ppermute(value, axis, [(i, i ^ bit) for i in range(size)])


def small_sum(value, axis):
    size = lax.axis_size(axis)
    if not power_of_two(size):
        return lax.psum(value, axis)
    bit = 1
    while bit < size:
        value = value + flip(value, axis, bit)
        bit *= 2
    return value


def halves(value):
    high = value.astype(jnp.bfloat16)
    low = (value - high.astype(jnp.float32)).astype(jnp.bfloat16)
    return high, low


def table_kernel(devices, partner_ref, kind_ref, vector_ref, table_ref, copied_ref, used, sem):
    copy = pltpu.make_async_copy(vector_ref, copied_ref, sem)
    copy.start()
    count, terms = partner_ref.shape[0], kind_ref.shape[0]
    per = count // devices
    me = lax.axis_index("blk")
    for c in range(devices):
        used[c] = 0

    def place(j, carry):
        where_to = partner_ref[j]
        owner = lax.div(where_to, count)
        offset = lax.rem(owner - me + devices, devices)
        at = offset * per + used[offset]
        used[offset] = used[offset] + 1
        table_ref[at] = j
        table_ref[count + at] = where_to - owner * count
        table_ref[2 * count + j] = at
        return carry

    lax.fori_loop(0, count, place, 0)
    for k in range(terms):
        table_ref[3 * count + k] = kind_ref[k]
    table_ref[3 * count + terms] = lax.axis_index("sub")
    copy.wait()


def make_table(partner, term_kind, vector):
    devices = lax.axis_size("blk")
    length = 3 * partner.shape[0] + term_kind.shape[0] + 1
    return pl.pallas_call(
        functools.partial(table_kernel, devices),
        out_shape=[
            jax.ShapeDtypeStruct((length,), jnp.int32),
            jax.ShapeDtypeStruct(vector.shape, vector.dtype),
        ],
        in_specs=[SCALARS, SCALARS, ANY],
        out_specs=[SCALARS, ANY],
        scratch_shapes=[pltpu.SMEM((devices,), jnp.int32), pltpu.SemaphoreType.DMA],
        name="table",
    )(partner, term_kind, vector)


def sector(table, count, terms, l_ref, r_ref, own_ref, other_ref, lhs, high_rhs, low_rhs):
    rows, width = l_ref.shape[2], r_ref.shape[3]
    roots = own_ref.shape[0] // rows
    first = table[3 * count + terms] == 0
    own, other = own_ref[...], other_ref[...]
    top = jnp.where(first, own, other)
    bottom = jnp.where(first, other, own)
    left = l_ref[:, 0].reshape(terms * rows, 2 * rows)
    left = jnp.concatenate(halves(left), axis=1)
    wide = []
    for r in range(roots):
        at = slice(r * rows, (r + 1) * rows)
        one = jnp.concatenate(halves(jnp.concatenate([top[at], bottom[at]], axis=0)), axis=1)
        wide.append(jnp.concatenate([one, one], axis=0))
    for r in range(roots):
        both = jnp.dot(left, wide[r], preferred_element_type=jnp.float32)
        high, low = halves(both[:, :width] + both[:, width:])
        for k in range(terms):
            lanes = slice(k * width, (k + 1) * width)
            part = slice(k * rows, (k + 1) * rows)
            lhs[r * rows : (r + 1) * rows, lanes] = high[part]
            lhs[(roots + r) * rows : (roots + r + 1) * rows, lanes] = low[part]
    for k in range(terms):
        lanes = slice(k * width, (k + 1) * width)
        kind = table[3 * count + k]
        used = pl.ds(pl.multiple_of((1 - kind) * width, width), width)
        high, low = halves(r_ref[k, 0].T)
        high_rhs[lanes, used] = high
        low_rhs[lanes, used] = low
    tall = jnp.dot(lhs[...], high_rhs[...], preferred_element_type=jnp.float32)
    short = jnp.dot(lhs[: roots * rows], low_rhs[...], preferred_element_type=jnp.float32)
    return tall[: roots * rows] + tall[roots * rows :] + short


def sector_kernel(count, terms, unroll, starts, tags, table, *refs):
    inputs, scratch = refs[: 4 * unroll], refs[-3 * unroll :]
    outputs = refs[-3 * unroll - len(starts) : -3 * unroll]
    tag_refs = refs[4 * unroll : 4 * unroll + 2]
    moved_refs, kept_ref = outputs[:-1], outputs[-1]
    width = kept_ref.shape[1]
    height = kept_ref.shape[0] // unroll
    step = pl.program_id(0)

    @pl.when(step == 0)
    def _():
        for at, ref in enumerate(scratch):
            if at % 3:
                ref[...] = jnp.zeros_like(ref)
        if any(tags):
            tag = tag_refs[0][...] + tag_refs[1][...]
            for ref, begin, end, tagged in zip(moved_refs, starts, starts[1:], tags):
                if tagged:
                    ref[(end - begin) * height :] = tag

    results = [
        sector(table, count, terms, *inputs[4 * u : 4 * u + 4], *scratch[3 * u : 3 * u + 3])
        for u in range(unroll)
    ]
    for u in range(unroll):
        kept_ref[u * height : (u + 1) * height] = results[u][:, width:]
    for ref, begin, end in zip(moved_refs, starts, starts[1:]):
        for u in range(unroll):
            at = step * unroll + u - begin

            @pl.when((at >= 0) & (at < end - begin))
            def _(ref=ref, u=u, at=at):
                ref[pl.ds(pl.multiple_of(at * height, height), height)] = results[u][:, :width]


def place_of(i, pieces):
    at, begin = pieces[0][0] + i, 0
    for (_, size), (base, _) in zip(pieces, pieces[1:]):
        begin += size
        at = jnp.where(i >= begin, base + i - begin, at)
    return at


def sectors(table, pieces, tags, left, right, own, other, kept, ordered):
    terms, count, rows, width = left.shape
    height = own.shape[0] // TAG * TAG // count // rows * rows
    roots = height // rows
    starts = [0]
    for _, size in pieces:
        starts.append(starts[-1] + size)
    places = [base + i for base, size in pieces for i in range(size)]

    def fits(unroll):
        return len(places) % unroll == 0 and all(
            places[i] % unroll == 0
            and places[i : i + unroll] == list(range(places[i], places[i] + unroll))
            for i in range(0, len(places), unroll)
        )

    choices = (2, 1) if ordered or len(places) < 8 else (4, 2, 1)
    unroll = next(unroll for unroll in choices if fits(unroll))

    def specs(u):
        def source(i, table):
            return table[place_of(unroll * i + u, pieces)]

        def held(i, table):
            return (place_of(unroll * i + u, pieces) if ordered else source(i, table), 0)

        return [
            pl.BlockSpec((terms, 1, rows, width), lambda i, t: (0, source(i, t), 0, 0)),
            pl.BlockSpec((terms, 1, width, width), lambda i, t: (0, source(i, t), 0, 0)),
            pl.BlockSpec((height, width), held),
            pl.BlockSpec((height, width), held),
        ]

    in_specs = [spec for u in range(unroll) for spec in specs(u)]
    args = [left, right, own, other] * unroll
    if any(tags):
        in_specs += [pl.BlockSpec((TAG, width), lambda i, t: (count * height // TAG, 0))] * 2
        args += [own, other]
    aliases = {}
    if kept is not None:
        in_specs.append(ANY)
        args.append(kept)
        aliases = {len(args): len(pieces)}
    rhs = (terms * width, 2 * width)
    shapes = [(size * height + TAG * tagged, width) for (_, size), tagged in zip(pieces, tags)]
    out = pl.pallas_call(
        functools.partial(sector_kernel, count, terms, unroll, starts, tags),
        out_shape=[
            jax.ShapeDtypeStruct(shape, jnp.float32)
            for shape in shapes + [(count * height, width)]
        ],
        grid_spec=pltpu.PrefetchScalarGridSpec(
            num_scalar_prefetch=1,
            grid=(starts[-1] // unroll,),
            in_specs=in_specs,
            out_specs=[pl.BlockSpec(shape, lambda i, t: (0, 0)) for shape in shapes]
            + [
                pl.BlockSpec(
                    (unroll * height, width),
                    lambda i, t: (lax.div(place_of(unroll * i, pieces), unroll), 0),
                )
            ],
            scratch_shapes=[
                pltpu.VMEM((2 * height, terms * width), jnp.bfloat16),
                pltpu.VMEM(rhs, jnp.bfloat16),
                pltpu.VMEM(rhs, jnp.bfloat16),
            ]
            * unroll,
        ),
        input_output_aliases=aliases,
        compiler_params=pltpu.CompilerParams(vmem_limit_bytes=LIMIT),
        cost_estimate=FREE,
        name="sectors",
    )(table, *args)
    return out[:-1], out[-1]


def combine_kernel(share, starts, with_inner, table, kept_ref, vector_ref, diag_ref, *refs):
    arrived_refs, sum_ref = refs[: len(starts)], refs[-2 if with_inner else -1]
    height = vector_ref.shape[0]
    before = refs[len(starts) : -2] if with_inner else ()
    rows = diag_ref.shape[1]
    roots = vector_ref.shape[0] // rows
    step = pl.program_id(0)
    arrived = arrived_refs[0][...]
    for ref, begin in zip(arrived_refs[1:], starts[1:]):
        arrived = jnp.where(step >= begin, ref[...], arrived)
    diag = share * diag_ref[0]
    if with_inner:
        inner_ref = refs[-1]

        @pl.when(step == 0)
        def _():
            inner_ref[...] = sum((ref[...] for ref in before), jnp.zeros_like(inner_ref))

    for r in range(roots):
        at = slice(r * rows, (r + 1) * rows)
        vector = vector_ref[at]
        total = kept_ref[at] + arrived[at] + diag * vector
        if before:
            sum_ref[pl.ds(pl.multiple_of(step * height + r * rows, rows), rows)] = total
        else:
            sum_ref[at] = total
        if with_inner:
            inner_ref[r : r + 1] += jnp.sum(vector * total, axis=0, keepdims=True)
            inner_ref[roots + r : roots + r + 1] += share * jnp.sum(
                vector * vector, axis=0, keepdims=True
            )
    if before:
        sum_ref[sum_ref.shape[0] - TAG :] = inner_ref[...]


def combine(table, pieces, kept, arrived, vector, diag, share, ordered, with_inner, before):
    count, rows, width = diag.shape
    height = kept.shape[0] // count
    starts = [0]
    for _, size in pieces:
        starts.append(starts[-1] + size)

    def slot(i, table):
        return table[count + place_of(i, pieces)]

    def place(i, table):
        return table[2 * count + slot(i, table)]

    def held(i, table):
        return (place(i, table) if ordered else slot(i, table), 0)

    def arrived_spec(begin, end):
        return pl.BlockSpec((height, width), lambda i, t: (jnp.clip(i - begin, 0, end - begin - 1), 0))

    block = (height, width)
    whole = (starts[-1] * height + TAG * bool(before), width)
    out_shape = [jax.ShapeDtypeStruct(whole, jnp.float32)]
    out_specs = [pl.BlockSpec(whole if before else block, lambda i, t: (0 if before else i, 0))]
    if with_inner:
        out_shape.append(jax.ShapeDtypeStruct((TAG, width), jnp.float32))
        out_specs.append(pl.BlockSpec((TAG, width), lambda i, t: (0, 0)))
    out = pl.pallas_call(
        functools.partial(combine_kernel, share, starts[:-1], with_inner),
        out_shape=out_shape,
        grid_spec=pltpu.PrefetchScalarGridSpec(
            num_scalar_prefetch=1,
            grid=(starts[-1],),
            in_specs=[
                pl.BlockSpec(block, lambda i, t: (place(i, t), 0)),
                pl.BlockSpec(block, held),
                pl.BlockSpec((1, rows, width), lambda i, t: (slot(i, t), 0, 0)),
            ]
            + [arrived_spec(begin, end) for begin, end in zip(starts, starts[1:])]
            + [pl.BlockSpec((TAG, width), lambda i, t: (0, 0))] * len(before),
            out_specs=out_specs,
        ),
        compiler_params=pltpu.CompilerParams(vmem_limit_bytes=SMALL),
        cost_estimate=FREE,
        name="combine",
    )(table, kept, vector, diag, *arrived, *before)
    return out if with_inner else (out[0], None)


def correct_kernel(groups, table, inner_ref, vector_ref, diag_ref, *rest):
    parts, raw_ref = rest[:-1], rest[-1]
    count, rows, width = diag_ref.shape
    height = vector_ref.shape[0] // count
    roots = height // rows
    inner = jnp.sum(inner_ref[...], axis=1, keepdims=True)
    theta = inner[:roots] / inner[roots : 2 * roots]
    squares = [jnp.zeros((1, width), jnp.float32) for _ in range(roots)]
    for at, pieces in enumerate(groups):
        mine, theirs = parts[2 * at], parts[2 * at + 1]
        row = 0
        for base, size in pieces:
            for i in range(size):
                slot = table[count + base + i]
                held = slot * height
                place = table[2 * count + slot] * height
                diag = diag_ref[slot]
                for r in range(roots):
                    shift = theta[r : r + 1]
                    sigma = mine[row : row + rows] + theirs[row : row + rows]
                    vector = vector_ref[pl.ds(pl.multiple_of(held + r * rows, rows), rows)]
                    raw = (sigma - shift * vector) / jnp.maximum(jnp.abs(diag - shift), 1.0)
                    raw_ref[pl.ds(pl.multiple_of(place + r * rows, rows), rows)] = raw
                    squares[r] = squares[r] + jnp.sum(raw * raw, axis=0, keepdims=True)
                    row += rows
    raw_ref[count * height :] = jnp.concatenate(
        squares + [jnp.zeros((TAG - roots, width), jnp.float32)], axis=0
    )


def correct(table, groups, inner, vector, diag, parts):
    return pl.pallas_call(
        functools.partial(correct_kernel, groups),
        out_shape=jax.ShapeDtypeStruct((vector.shape[0] + TAG, vector.shape[1]), jnp.float32),
        in_specs=[SCALARS] + [WHOLE] * (3 + len(parts)),
        out_specs=WHOLE,
        compiler_params=pltpu.CompilerParams(vmem_limit_bytes=SMALL),
        cost_estimate=FREE,
        name="correct",
    )(table, inner, vector, diag, *parts)


def scatter(held, out_ref, sems, rows_of):
    height = held.shape[0] // len(rows_of)
    copies = []
    for i, make in enumerate(rows_of):
        at = slice(i * height, (i + 1) * height)
        row = make(at)
        copies.append(
            pltpu.make_async_copy(
                held.at[at], out_ref.at[pl.ds(pl.multiple_of(row, height), height)], sems.at[i]
            )
        )
        copies[-1].start()
    for copy in copies:
        copy.wait()


def scaled_kernel(count, rows, table, scale_ref, raw_ref, out_ref, held, sems):
    height = held.shape[0] // count

    def make(i, at):
        place = pl.multiple_of(table[2 * count + i] * height, height)
        for r in range(height // rows):
            part = raw_ref[pl.ds(place + r * rows, rows)]
            held[at.start + r * rows : at.start + (r + 1) * rows] = part * scale_ref[r : r + 1]
        return i * height

    scatter(held, out_ref, sems, [functools.partial(make, i) for i in range(count)])


def scaled(table, scale, raw, count, rows):
    height, width = raw.shape[0] // count // rows * rows, raw.shape[1]
    return pl.pallas_call(
        functools.partial(scaled_kernel, count, rows),
        out_shape=jax.ShapeDtypeStruct((count * height, width), jnp.float32),
        in_specs=[SCALARS, WHOLE, WHOLE],
        out_specs=ANY,
        scratch_shapes=[
            pltpu.VMEM((count * height, width), jnp.float32),
            pltpu.SemaphoreType.DMA((count,)),
        ],
        compiler_params=pltpu.CompilerParams(vmem_limit_bytes=SMALL),
        cost_estimate=FREE,
        name="scaled",
    )(table, scale, raw)


def finish_kernel(count, rows, places, table, scale_ref, mine_ref, theirs_ref, *rest):
    out_ref, held, sems = rest[-3:]
    height = held.shape[0] // len(places)

    def make(place, at):
        for r in range(height // rows):
            part = slice(at.start + r * rows, at.start + (r + 1) * rows)
            held[part] = (mine_ref[part] + theirs_ref[part]) * scale_ref[r : r + 1]
        return table[count + place] * height

    scatter(held, out_ref, sems, [functools.partial(make, place) for place in places])


def finish(table, pieces, scale, mine, theirs, out, count, rows):
    places = [base + i for base, size in pieces for i in range(size)]
    height, width = mine.shape[0] // len(places), mine.shape[1]
    in_specs = [SCALARS, WHOLE, WHOLE, WHOLE]
    args, aliases = [table, scale, mine, theirs], {}
    if out is not None:
        in_specs.append(ANY)
        args.append(out)
        aliases = {4: 0}
    return pl.pallas_call(
        functools.partial(finish_kernel, count, rows, places),
        out_shape=jax.ShapeDtypeStruct((count * height, width), jnp.float32),
        in_specs=in_specs,
        out_specs=ANY,
        scratch_shapes=[
            pltpu.VMEM(mine.shape, jnp.float32),
            pltpu.SemaphoreType.DMA((len(places),)),
        ],
        input_output_aliases=aliases,
        compiler_params=pltpu.CompilerParams(vmem_limit_bytes=SMALL),
        cost_estimate=FREE,
        name="finish",
    )(*args)


def add_over_term(value):
    size = lax.axis_size("term")
    if size == 1 or not power_of_two(size):
        return lax.psum(value, "term"), jnp.zeros_like(value)
    bit = 1
    while 2 * bit < size:
        value = value + flip(value, "term", bit)
        bit *= 2
    return value, flip(value, "term", bit)


def after(*values):
    return lax.optimization_barrier(values)


def shards(amplitudes, left, right, term_kind, partner, left_diag, right_diag):
    devices, terms_over = lax.axis_size("blk"), lax.axis_size("term")
    slots, rows, roots, width = amplitudes.shape
    per = slots // devices
    elements = slots * devices * rows * lax.axis_size("sub") * width
    vector = jnp.transpose(amplitudes, (0, 2, 1, 3)).reshape(slots * roots * rows, width)
    arriving = lax.ppermute(vector, "sub", [(0, 1), (1, 0)])
    table, vector = make_table(partner, term_kind, vector)
    diag = left_diag[:, :, None] + right_diag[:, None, :]

    staying = (0, 0, per)
    pairs = [
        [(c, c * per, per), (devices - c, (devices - c) * per, per)]
        for c in range(1, (devices + 1) // 2)
    ]
    opposite = []
    if devices % 2 == 0:
        c = devices // 2
        cuts = [(0, per // 2), (per // 2, per - per // 2)] if per > 1 else [(0, per)]
        opposite = [(c, c * per + start, size) for start, size in cuts]
    moving = [piece for pair in pairs for piece in pair] + opposite
    groups = [[piece] for piece in [staying] + moving]
    batches = [moving[:1], moving[1:] + [staying]]
    late = len(opposite) == 2 and len(pairs) > 0

    def spans(pieces):
        return [piece[1:] for piece in pieces]

    def relay(value, c):
        return lax.ppermute(value, "blk", [(p, (p + c) % devices) for p in range(devices)])

    def partials(own, second, between):
        other = lax.ppermute(own, "sub", [(0, 1), (1, 0)]) if second else arriving
        kept, outgoing = None, {}
        for batch in batches:
            parts, kept = sectors(
                table,
                spans(batch),
                [second and piece[0] > 0 for piece in batch],
                left,
                right,
                own,
                other,
                kept,
                second,
            )
            outgoing.update(zip(batch, parts))
        arrived, sums, inners, done = {}, [], [], ()
        for at, piece in enumerate(moving):
            value = outgoing[piece]
            if at >= 1:
                value = after(value, arrived[moving[at - 1]])[0]
            arrived[piece] = relay(value, piece[0])
        arrived[staying] = after(outgoing[staying], arrived[moving[0]])[0]
        for group in groups:
            if late and group == groups[-1] and between:
                piece = group[0]
                arrived[piece], *done = after(arrived[piece], *between(sums, arrived, other))
            first, *others = [arrived[piece] for piece in group]
            if sums:
                first = after(first, sums[-2])[0]
            last = group == groups[-1] and len(groups) > 1
            mine, inner = combine(
                table,
                spans(group),
                kept,
                [first] + others,
                own,
                diag,
                1.0 / terms_over,
                second,
                not second,
                inners if last and not second else (),
            )
            if last:
                mine = after(mine, *sums[1::2][-2:])[0]
            elif len(sums) >= 4:
                mine = after(mine, sums[-3])[0]
            sums += add_over_term(mine)
            inners.append(inner)
        if between and not late:
            done = between(sums, arrived, other)
        return sums, inners, done

    sums, inners, _ = partials(vector, False, None)
    if len(groups) > 1:
        inner = sums[-2][-TAG:] + sums[-1][-TAG:]
    else:
        inner = small_sum(inners[0], "term")
    for axis in ("sub", "blk"):
        inner = small_sum(inner, axis)
    raw = correct(table, [spans(group) for group in groups], inner, vector, diag, sums)

    def add_finished(sigma, scale, sums, at):
        return finish(
            table, spans(groups[at]), scale, sums[2 * at], sums[2 * at + 1], sigma, slots, rows
        )

    def correction_and_more(sums, arrived, other):
        squares = raw[-TAG:] + other[-TAG:]
        first_of = {piece[0]: piece for piece in reversed(moving)}
        for c in sorted(first_of):
            squares = squares + arrived[first_of[c]][-TAG:]
        scale = lax.rsqrt(jnp.sum(squares, axis=1, keepdims=True) / elements + 1e-06)
        scale = jnp.broadcast_to(scale, squares.shape)
        return scaled(table, scale, raw, slots, rows), scale, add_finished(None, scale, sums, 0)

    sums, _, (correction, scale, sigma) = partials(raw, True, correction_and_more)
    for at in range(1, len(groups)):
        sigma = add_finished(sigma, scale, sums, at)
    return tuple(
        jnp.transpose(value.reshape(slots, roots, rows, width), (0, 2, 1, 3))
        for value in (sigma, correction)
    )


def solution(mesh):
    return jax.shard_map(
        shards,
        mesh=mesh,
        in_specs=(
            P(("grp", "blk"), "sub", None, None),
            P(("grp", "term"), "blk", "sub", None),
            P(("grp", "term"), "blk", None, None),
            P(("grp", "term")),
            P(("grp", "blk")),
            P(("grp", "blk"), "sub"),
            P(("grp", "blk"), None),
        ),
        out_specs=(P(("grp", "blk"), "sub", None, None), P(("grp", "blk"), "sub", None, None)),
        check_vma=False,
    )
```

```python
import functools

import jax
import jax.numpy as jnp
from jax import lax
from jax.experimental import pallas as pl
from jax.experimental.pallas import tpu as pltpu
from jax.sharding import PartitionSpec as P

TAG = 8
LIMIT = 48 * 1024 * 1024
SMALL = 24 * 1024 * 1024
FREE = pl.CostEstimate(flops=0, bytes_accessed=0, transcendentals=0)
WHOLE = pl.BlockSpec(memory_space=pltpu.VMEM)
SCALARS = pl.BlockSpec(memory_space=pltpu.SMEM)
ANY = pl.BlockSpec(memory_space=pl.ANY)


def power_of_two(size):
    return size & (size - 1) == 0


def flip(value, axis, bit):
    size = lax.axis_size(axis)
    return lax.ppermute(value, axis, [(i, i ^ bit) for i in range(size)])


def small_sum(value, axis):
    size = lax.axis_size(axis)
    if not power_of_two(size):
        return lax.psum(value, axis)
    bit = 1
    while bit < size:
        value = value + flip(value, axis, bit)
        bit *= 2
    return value


def halves(value):
    high = value.astype(jnp.bfloat16)
    low = (value - high.astype(jnp.float32)).astype(jnp.bfloat16)
    return high, low


def table_kernel(devices, partner_ref, kind_ref, _, table_ref, used):
    count, terms = partner_ref.shape[0], kind_ref.shape[0]
    per = count // devices
    me = lax.axis_index("blk")
    for c in range(devices):
        used[c] = 0

    def place(j, carry):
        where_to = partner_ref[j]
        owner = lax.div(where_to, count)
        offset = lax.rem(owner - me + devices, devices)
        at = offset * per + used[offset]
        used[offset] = used[offset] + 1
        table_ref[at] = j
        table_ref[count + at] = where_to - owner * count
        table_ref[2 * count + j] = at
        return carry

    lax.fori_loop(0, count, place, 0)
    moving = sum(kind_ref[k] for k in range(terms))
    moving_pairs = lax.div(moving + 1, 2)
    before = (jnp.int32(0), 2 * moving_pairs)
    for k in range(terms):
        moves = kind_ref[k] == 1
        table_ref[3 * count + k] = jnp.where(moves, before[0], before[1])
        before = (jnp.where(moves, before[0] + 1, before[0]), jnp.where(moves, before[1], before[1] + 1))
    at = 3 * count + terms
    table_ref[at] = lax.axis_index("sub")
    table_ref[at + 1] = moving_pairs
    table_ref[at + 2] = moving_pairs + lax.div(terms - moving + 1, 2)
    table_ref[at + 3] = moving


def make_table(partner, term_kind, vector):
    devices = lax.axis_size("blk")
    length = 3 * partner.shape[0] + term_kind.shape[0] + 4
    return pl.pallas_call(
        functools.partial(table_kernel, devices),
        out_shape=jax.ShapeDtypeStruct((length,), jnp.int32),
        in_specs=[SCALARS, SCALARS, WHOLE],
        out_specs=SCALARS,
        scratch_shapes=[pltpu.SMEM((devices,), jnp.int32)],
        compiler_params=pltpu.CompilerParams(vmem_limit_bytes=SMALL),
        name="table",
    )(partner, term_kind, vector)


def add_pair(table, at, pair, lhs, rhs, total):
    height, width = total.shape[0] // 2, total.shape[1]
    deep = slice(2 * pair * width, 2 * (pair + 1) * width)
    both = jnp.dot(lhs[:, deep], rhs[deep], preferred_element_type=jnp.float32)
    result = both[:height, :width] + both[:height, width:] + both[height:, :width]
    kept = jnp.where(pair < table[at + 1], 0, height)
    into = pl.ds(pl.multiple_of(kept, height), height)
    total[into] = total[into] + result


def sector(table, count, terms, l_ref, r_ref, own_ref, other_ref, lhs, rhs, total):
    rows, width = l_ref.shape[2], r_ref.shape[3]
    roots = own_ref.shape[0] // rows
    first = table[3 * count + terms] == 0
    own, other = own_ref[...], other_ref[...]
    top = jnp.where(first, own, other)
    bottom = jnp.where(first, other, own)
    left = l_ref[:, 0].reshape(terms * rows, 2 * rows)
    left = jnp.concatenate(halves(left), axis=1)

    def lanes_of(k):
        return pl.ds(pl.multiple_of(table[3 * count + k] * width, width), width)

    for r in range(roots):
        at = slice(r * rows, (r + 1) * rows)
        wide = jnp.concatenate(halves(jnp.concatenate([top[at], bottom[at]], axis=0)), axis=1)
        both = jnp.dot(
            left, jnp.concatenate([wide, wide], axis=0), preferred_element_type=jnp.float32
        )
        high, low = halves(both[:, :width] + both[:, width:])
        for k in range(terms):
            part = slice(k * rows, (k + 1) * rows)
            lhs[r * rows : (r + 1) * rows, lanes_of(k)] = high[part]
            lhs[(roots + r) * rows : (roots + r + 1) * rows, lanes_of(k)] = low[part]
    for k in range(terms):
        high, low = halves(r_ref[k, 0].T)
        rhs[lanes_of(k), :width] = high
        rhs[lanes_of(k), width:] = low
    total[...] = jnp.zeros_like(total)
    for pair in range((terms + 1) // 2):
        add_pair(table, 3 * count + terms, pair, lhs, rhs, total)


def sector_kernel(count, terms, unroll, starts, tags, table, *refs):
    inputs, scratch = refs[: 4 * unroll], refs[-3 * unroll :]
    outputs = refs[-3 * unroll - len(starts) : -3 * unroll]
    tag_refs = refs[4 * unroll : 4 * unroll + 2]
    moved_refs, kept_ref = outputs[:-1], outputs[-1]
    width = kept_ref.shape[1]
    height = kept_ref.shape[0] // unroll
    step = pl.program_id(0)
    at = 3 * count + terms

    @pl.when(step == 0)
    def _():
        if any(tags):
            tag = tag_refs[0][...] + tag_refs[1][...]
            for ref, begin, end, tagged in zip(moved_refs, starts, starts[1:], tags):
                if tagged:
                    ref[(end - begin) * height :] = tag

    @pl.when((step == 0) & (lax.rem(table[at + 3], 2) + terms % 2 > 0))
    def _():
        empty = [jnp.where(lax.rem(table[at + 3], 2) == 1, table[at + 3], terms)]
        empty += range(terms, scratch[0].shape[1] // width)
        for u in range(unroll):
            lhs, rhs, _ = scratch[3 * u : 3 * u + 3]
            for one in empty:
                lanes = pl.ds(pl.multiple_of(one * width, width), width)
                lhs[:, lanes] = jnp.zeros((lhs.shape[0], width), lhs.dtype)
                rhs[lanes] = jnp.zeros((width, rhs.shape[1]), rhs.dtype)

    for u in range(unroll):
        sector(table, count, terms, *inputs[4 * u : 4 * u + 4], *scratch[3 * u : 3 * u + 3])
    if terms % 2 == 0:

        @pl.when(table[at + 2] > terms // 2)
        def _():
            for u in range(unroll):
                add_pair(table, at, terms // 2, *scratch[3 * u : 3 * u + 3])

    for u in range(unroll):
        kept_ref[u * height : (u + 1) * height] = scratch[3 * u + 2][height:]
    for ref, begin, end in zip(moved_refs, starts, starts[1:]):
        for u in range(unroll):
            to = step * unroll + u - begin

            @pl.when((to >= 0) & (to < end - begin))
            def _(ref=ref, u=u, to=to):
                into = pl.ds(pl.multiple_of(to * height, height), height)
                ref[into] = scratch[3 * u + 2][:height]


def place_of(i, pieces):
    at, begin = pieces[0][0] + i, 0
    for (_, size), (base, _) in zip(pieces, pieces[1:]):
        begin += size
        at = jnp.where(i >= begin, base + i - begin, at)
    return at


def sectors(table, pieces, tags, left, right, own, other, kept, origin, roots):
    terms, count, rows, width = left.shape
    height = roots * rows
    starts = [0]
    for _, size in pieces:
        starts.append(starts[-1] + size)
    places = [base + i for base, size in pieces for i in range(size)]

    def fits(unroll):
        return len(places) % unroll == 0 and all(
            places[i] % unroll == 0
            and places[i : i + unroll] == list(range(places[i], places[i] + unroll))
            for i in range(0, len(places), unroll)
        )

    unroll = next(unroll for unroll in (2, 1) if fits(unroll))

    def specs(u):
        def source(i, table):
            return table[place_of(unroll * i + u, pieces)]

        def held(i, table):
            at = source(i, table) if origin is None else place_of(unroll * i + u, pieces) - origin
            return (at, 0)

        return [
            pl.BlockSpec((terms, 1, rows, width), lambda i, t: (0, source(i, t), 0, 0)),
            pl.BlockSpec((terms, 1, width, width), lambda i, t: (0, source(i, t), 0, 0)),
            pl.BlockSpec((height, width), held),
            pl.BlockSpec((height, width), held),
        ]

    in_specs = [spec for u in range(unroll) for spec in specs(u)]
    args = [left, right, own, other] * unroll
    if any(tags):
        in_specs += [pl.BlockSpec((TAG, width), lambda i, t: (own.shape[0] // TAG - 1, 0))] * 2
        args += [own, other]
    aliases = {}
    if kept is not None:
        in_specs.append(ANY)
        args.append(kept)
        aliases = {len(args): len(pieces)}
    deep = (terms + 2 - terms % 2) * width
    shapes = [(size * height + TAG * tagged, width) for (_, size), tagged in zip(pieces, tags)]
    out = pl.pallas_call(
        functools.partial(sector_kernel, count, terms, unroll, starts, tags),
        out_shape=[
            jax.ShapeDtypeStruct(shape, jnp.float32)
            for shape in shapes + [(count * height, width)]
        ],
        grid_spec=pltpu.PrefetchScalarGridSpec(
            num_scalar_prefetch=1,
            grid=(starts[-1] // unroll,),
            in_specs=in_specs,
            out_specs=[pl.BlockSpec(shape, lambda i, t: (0, 0)) for shape in shapes]
            + [
                pl.BlockSpec(
                    (unroll * height, width),
                    lambda i, t: (lax.div(place_of(unroll * i, pieces), unroll), 0),
                )
            ],
            scratch_shapes=[
                pltpu.VMEM((2 * height, deep), jnp.bfloat16),
                pltpu.VMEM((deep, 2 * width), jnp.bfloat16),
                pltpu.VMEM((2 * height, width), jnp.float32),
            ]
            * unroll,
        ),
        input_output_aliases=aliases,
        compiler_params=pltpu.CompilerParams(vmem_limit_bytes=LIMIT),
        cost_estimate=FREE,
        name="sectors",
    )(table, *args)
    return out[:-1], out[-1]


def combine_kernel(share, starts, with_inner, table, kept_ref, vector_ref, diag_ref, *refs):
    arrived_refs, sum_ref = refs[: len(starts)], refs[-2 if with_inner else -1]
    height = vector_ref.shape[0]
    before = refs[len(starts) : -2] if with_inner else ()
    rows = diag_ref.shape[1]
    roots = vector_ref.shape[0] // rows
    step = pl.program_id(0)
    arrived = arrived_refs[0][...]
    for ref, begin in zip(arrived_refs[1:], starts[1:]):
        arrived = jnp.where(step >= begin, ref[...], arrived)
    diag = share * diag_ref[0]
    if with_inner:
        inner_ref = refs[-1]

        @pl.when(step == 0)
        def _():
            inner_ref[...] = sum((ref[...] for ref in before), jnp.zeros_like(inner_ref))

    for r in range(roots):
        at = slice(r * rows, (r + 1) * rows)
        vector = vector_ref[at]
        total = kept_ref[at] + arrived[at] + diag * vector
        if before:
            sum_ref[pl.ds(pl.multiple_of(step * height + r * rows, rows), rows)] = total
        else:
            sum_ref[at] = total
        if with_inner:
            inner_ref[r : r + 1] += jnp.sum(vector * total, axis=0, keepdims=True)
            inner_ref[roots + r : roots + r + 1] += share * jnp.sum(
                vector * vector, axis=0, keepdims=True
            )
    if before:
        sum_ref[sum_ref.shape[0] - TAG :] = inner_ref[...]


def combine(table, pieces, kept, arrived, vector, diag, share, ordered, with_inner, before):
    count, rows, width = diag.shape
    height = kept.shape[0] // count
    starts = [0]
    for _, size in pieces:
        starts.append(starts[-1] + size)

    def slot(i, table):
        return table[count + place_of(i, pieces)]

    def place(i, table):
        return table[2 * count + slot(i, table)]

    def held(i, table):
        return (place(i, table) if ordered else slot(i, table), 0)

    def arrived_spec(begin, end):
        return pl.BlockSpec((height, width), lambda i, t: (jnp.clip(i - begin, 0, end - begin - 1), 0))

    block = (height, width)
    whole = (starts[-1] * height + TAG * bool(before), width)
    out_shape = [jax.ShapeDtypeStruct(whole, jnp.float32)]
    out_specs = [pl.BlockSpec(whole if before else block, lambda i, t: (0 if before else i, 0))]
    if with_inner:
        out_shape.append(jax.ShapeDtypeStruct((TAG, width), jnp.float32))
        out_specs.append(pl.BlockSpec((TAG, width), lambda i, t: (0, 0)))
    out = pl.pallas_call(
        functools.partial(combine_kernel, share, starts[:-1], with_inner),
        out_shape=out_shape,
        grid_spec=pltpu.PrefetchScalarGridSpec(
            num_scalar_prefetch=1,
            grid=(starts[-1],),
            in_specs=[
                pl.BlockSpec(block, lambda i, t: (place(i, t), 0)),
                pl.BlockSpec(block, held),
                pl.BlockSpec((1, rows, width), lambda i, t: (slot(i, t), 0, 0)),
            ]
            + [arrived_spec(begin, end) for begin, end in zip(starts, starts[1:])]
            + [pl.BlockSpec((TAG, width), lambda i, t: (0, 0))] * len(before),
            out_specs=out_specs,
        ),
        compiler_params=pltpu.CompilerParams(vmem_limit_bytes=SMALL),
        cost_estimate=FREE,
        name="combine",
    )(table, kept, vector, diag, *arrived, *before)
    return out if with_inner else (out[0], None)


def correct_kernel(groups, ahead, table, inner_ref, vector_ref, diag_ref, *rest):
    parts, (raw_ref, ahead_ref) = rest[:-2], rest[-2:]
    count, rows, width = diag_ref.shape
    height = vector_ref.shape[0] // count
    roots = height // rows
    inner = jnp.sum(inner_ref[...], axis=1, keepdims=True)
    theta = inner[:roots] / inner[roots : 2 * roots]
    squares = [jnp.zeros((1, width), jnp.float32) for _ in range(roots)]
    for at, pieces in enumerate(groups):
        mine, theirs = parts[2 * at], parts[2 * at + 1]
        row = 0
        for base, size in pieces:
            for i in range(size):
                slot = table[count + base + i]
                held = slot * height
                place = table[2 * count + slot] * height
                diag = diag_ref[slot]
                for r in range(roots):
                    shift = theta[r : r + 1]
                    sigma = mine[row : row + rows] + theirs[row : row + rows]
                    vector = vector_ref[pl.ds(pl.multiple_of(held + r * rows, rows), rows)]
                    raw = (sigma - shift * vector) / jnp.maximum(jnp.abs(diag - shift), 1.0)
                    raw_ref[pl.ds(pl.multiple_of(place + r * rows, rows), rows)] = raw
                    squares[r] = squares[r] + jnp.sum(raw * raw, axis=0, keepdims=True)
                    row += rows
    raw_ref[count * height :] = jnp.concatenate(
        squares + [jnp.zeros((TAG - roots, width), jnp.float32)], axis=0
    )
    ahead_ref[: ahead[1] * height] = raw_ref[ahead[0] * height : (ahead[0] + ahead[1]) * height]
    ahead_ref[ahead[1] * height :] = raw_ref[count * height :]


def correct(table, groups, ahead, inner, vector, diag, parts):
    height, width = vector.shape[0] // diag.shape[0], vector.shape[1]
    return pl.pallas_call(
        functools.partial(correct_kernel, groups, ahead),
        out_shape=[
            jax.ShapeDtypeStruct((vector.shape[0] + TAG, width), jnp.float32),
            jax.ShapeDtypeStruct((ahead[1] * height + TAG, width), jnp.float32),
        ],
        in_specs=[SCALARS] + [WHOLE] * (3 + len(parts)),
        out_specs=[WHOLE, WHOLE],
        compiler_params=pltpu.CompilerParams(vmem_limit_bytes=SMALL),
        cost_estimate=FREE,
        name="correct",
    )(table, inner, vector, diag, *parts)


def scatter(held, out_ref, sems, rows_of):
    height = held.shape[0] // len(rows_of)
    copies = []
    for i, make in enumerate(rows_of):
        at = slice(i * height, (i + 1) * height)
        row = make(at)
        copies.append(
            pltpu.make_async_copy(
                held.at[at], out_ref.at[pl.ds(pl.multiple_of(row, height), height)], sems.at[i]
            )
        )
        copies[-1].start()
    for copy in copies:
        copy.wait()


def scaled_kernel(count, rows, table, scale_ref, raw_ref, out_ref, held, sems):
    height = held.shape[0] // count

    def make(i, at):
        place = pl.multiple_of(table[2 * count + i] * height, height)
        for r in range(height // rows):
            part = raw_ref[pl.ds(place + r * rows, rows)]
            held[at.start + r * rows : at.start + (r + 1) * rows] = part * scale_ref[r : r + 1]
        return i * height

    scatter(held, out_ref, sems, [functools.partial(make, i) for i in range(count)])


def scaled(table, scale, raw, count, rows):
    height, width = raw.shape[0] // count // rows * rows, raw.shape[1]
    return pl.pallas_call(
        functools.partial(scaled_kernel, count, rows),
        out_shape=jax.ShapeDtypeStruct((count * height, width), jnp.float32),
        in_specs=[SCALARS, WHOLE, WHOLE],
        out_specs=ANY,
        scratch_shapes=[
            pltpu.VMEM((count * height, width), jnp.float32),
            pltpu.SemaphoreType.DMA((count,)),
        ],
        compiler_params=pltpu.CompilerParams(vmem_limit_bytes=SMALL),
        cost_estimate=FREE,
        name="scaled",
    )(table, scale, raw)


def finish_kernel(count, rows, places, table, scale_ref, mine_ref, theirs_ref, *rest):
    out_ref, held, sems = rest[-3:]
    height = held.shape[0] // len(places)

    def make(place, at):
        for r in range(height // rows):
            part = slice(at.start + r * rows, at.start + (r + 1) * rows)
            held[part] = (mine_ref[part] + theirs_ref[part]) * scale_ref[r : r + 1]
        return table[count + place] * height

    scatter(held, out_ref, sems, [functools.partial(make, place) for place in places])


def finish(table, pieces, scale, mine, theirs, out, count, rows):
    places = [base + i for base, size in pieces for i in range(size)]
    height, width = mine.shape[0] // len(places), mine.shape[1]
    in_specs = [SCALARS, WHOLE, WHOLE, WHOLE]
    args, aliases = [table, scale, mine, theirs], {}
    if out is not None:
        in_specs.append(ANY)
        args.append(out)
        aliases = {4: 0}
    return pl.pallas_call(
        functools.partial(finish_kernel, count, rows, places),
        out_shape=jax.ShapeDtypeStruct((count * height, width), jnp.float32),
        in_specs=in_specs,
        out_specs=ANY,
        scratch_shapes=[
            pltpu.VMEM(mine.shape, jnp.float32),
            pltpu.SemaphoreType.DMA((len(places),)),
        ],
        input_output_aliases=aliases,
        compiler_params=pltpu.CompilerParams(vmem_limit_bytes=SMALL),
        cost_estimate=FREE,
        name="finish",
    )(*args)


def add_over_term(value):
    size = lax.axis_size("term")
    if size == 1 or not power_of_two(size):
        return lax.psum(value, "term"), jnp.zeros_like(value)
    bit = 1
    while 2 * bit < size:
        value = value + flip(value, "term", bit)
        bit *= 2
    return value, flip(value, "term", bit)


def after(*values):
    return lax.optimization_barrier(values)


def shards(amplitudes, left, right, term_kind, partner, left_diag, right_diag):
    devices, terms_over = lax.axis_size("blk"), lax.axis_size("term")
    slots, rows, roots, width = amplitudes.shape
    per = slots // devices
    elements = slots * devices * rows * lax.axis_size("sub") * width
    vector = jnp.transpose(amplitudes, (0, 2, 1, 3)).reshape(slots * roots * rows, width)
    table = make_table(partner, term_kind, vector)
    diag = left_diag[:, :, None] + right_diag[:, None, :]

    staying = (0, 0, per)
    pairs = [
        [(c, c * per, per), (devices - c, (devices - c) * per, per)]
        for c in range(1, (devices + 1) // 2)
    ]
    opposite = []
    if devices % 2 == 0:
        c = devices // 2
        cuts = [(0, per // 2), (per // 2, per - per // 2)] if per > 1 else [(0, per)]
        opposite = [(c, c * per + start, size) for start, size in cuts]
    moving = [piece for pair in pairs for piece in pair] + opposite
    groups = [[piece] for piece in [staying] + moving]
    batches = [moving[:1], moving[1:] + [staying]]
    late = len(opposite) == 2 and len(pairs) > 0

    def spans(pieces):
        return [piece[1:] for piece in pieces]

    def relay(value, c):
        return lax.ppermute(value, "blk", [(p, (p + c) % devices) for p in range(devices)])

    def swap(value):
        return lax.ppermute(value, "sub", [(0, 1), (1, 0)])

    def partials(own, second, between):
        if second:
            early = (ahead, swap(ahead))
            other = swap(after(own, early[1])[0])
        else:
            other = swap(own)
        kept, outgoing = None, {}
        for batch in batches:
            early_now = second and batch is batches[0]
            pair = early if early_now else (own, other)
            parts, kept = sectors(
                table,
                spans(batch),
                [second and piece[0] > 0 for piece in batch],
                left,
                right,
                *pair,
                kept,
                (batch[0][1] if early_now else 0) if second else None,
                roots,
            )
            outgoing.update(zip(batch, parts))
        arrived, sums, inners, done = {}, [], [], ()
        for at, piece in enumerate(moving):
            value = outgoing[piece]
            if at >= 1:
                value = after(value, arrived[moving[at - 1]])[0]
            arrived[piece] = relay(value, piece[0])
        arrived[staying] = after(outgoing[staying], arrived[moving[0]])[0]
        for group in groups:
            if late and group == groups[-1] and between:
                piece = group[0]
                arrived[piece], *done = after(arrived[piece], *between(sums, arrived, other))
            first, *others = [arrived[piece] for piece in group]
            if sums:
                first = after(first, sums[-2])[0]
            last = group == groups[-1] and len(groups) > 1
            mine, inner = combine(
                table,
                spans(group),
                kept,
                [first] + others,
                own,
                diag,
                1.0 / terms_over,
                second,
                not second,
                (),
            )
            if last:
                mine = after(mine, *sums[1::2][-2:])[0]
            elif len(sums) >= 4:
                mine = after(mine, sums[-3])[0]
            sums += add_over_term(mine)
            inners.append(inner)
        if between and not late:
            done = between(sums, arrived, other)
        return sums, inners, done

    sums, inners, _ = partials(vector, False, None)
    inner = small_sum(small_sum(sum(inners[1:], inners[0]), "sub"), "blk")
    inner = small_sum(after(inner, sums[-1])[0], "term")
    first = spans(batches[0])[0]
    raw, ahead = correct(
        table, [spans(group) for group in groups], first, inner, vector, diag, sums
    )

    def add_finished(sigma, scale, sums, at):
        return finish(
            table, spans(groups[at]), scale, sums[2 * at], sums[2 * at + 1], sigma, slots, rows
        )

    def correction_and_more(sums, arrived, other):
        squares = raw[-TAG:] + other[-TAG:]
        first_of = {piece[0]: piece for piece in reversed(moving)}
        for c in sorted(first_of):
            squares = squares + arrived[first_of[c]][-TAG:]
        scale = lax.rsqrt(jnp.sum(squares, axis=1, keepdims=True) / elements + 1e-06)
        scale = jnp.broadcast_to(scale, squares.shape)
        return scaled(table, scale, raw, slots, rows), scale, add_finished(None, scale, sums, 0)

    sums, _, (correction, scale, sigma) = partials(raw, True, correction_and_more)
    for at in range(1, len(groups)):
        sigma = add_finished(sigma, scale, sums, at)
    return tuple(
        jnp.transpose(value.reshape(slots, roots, rows, width), (0, 2, 1, 3))
        for value in (sigma, correction)
    )


def solution(mesh):
    return jax.shard_map(
        shards,
        mesh=mesh,
        in_specs=(
            P(("grp", "blk"), "sub", None, None),
            P(("grp", "term"), "blk", "sub", None),
            P(("grp", "term"), "blk", None, None),
            P(("grp", "term")),
            P(("grp", "blk")),
            P(("grp", "blk"), "sub"),
            P(("grp", "blk"), None),
        ),
        out_specs=(P(("grp", "blk"), "sub", None, None), P(("grp", "blk"), "sub", None, None)),
        check_vma=False,
    )
```

```python
import functools

import jax
import jax.numpy as jnp
from jax import lax
from jax.experimental import pallas as pl
from jax.experimental.pallas import tpu as pltpu
from jax.sharding import PartitionSpec as P

TAG = 8
LIMIT = 48 * 1024 * 1024
SMALL = 24 * 1024 * 1024
FREE = pl.CostEstimate(flops=0, bytes_accessed=0, transcendentals=0)
WHOLE = pl.BlockSpec(memory_space=pltpu.VMEM)
SCALARS = pl.BlockSpec(memory_space=pltpu.SMEM)
ANY = pl.BlockSpec(memory_space=pl.ANY)


def power_of_two(size):
    return size & (size - 1) == 0


def flip(value, axis, bit):
    size = lax.axis_size(axis)
    return lax.ppermute(value, axis, [(i, i ^ bit) for i in range(size)])


def small_sum(value, axis):
    size = lax.axis_size(axis)
    if not power_of_two(size):
        return lax.psum(value, axis)
    bit = 1
    while bit < size:
        value = value + flip(value, axis, bit)
        bit *= 2
    return value


def halves(value):
    high = value.astype(jnp.bfloat16)
    low = (value - high.astype(jnp.float32)).astype(jnp.bfloat16)
    return high, low


def table_kernel(devices, partner_ref, kind_ref, _, table_ref, used):
    count, terms = partner_ref.shape[0], kind_ref.shape[0]
    per = count // devices
    me = lax.axis_index("blk")
    for c in range(devices):
        used[c] = 0

    def place(j, carry):
        where_to = partner_ref[j]
        owner = lax.div(where_to, count)
        offset = lax.rem(owner - me + devices, devices)
        at = offset * per + used[offset]
        used[offset] = used[offset] + 1
        table_ref[at] = j
        table_ref[count + at] = where_to - owner * count
        table_ref[2 * count + j] = at
        return carry

    lax.fori_loop(0, count, place, 0)
    for k in range(terms):
        table_ref[3 * count + k] = kind_ref[k]
    table_ref[3 * count + terms] = lax.axis_index("sub")


def make_table(partner, term_kind, vector):
    devices = lax.axis_size("blk")
    length = 3 * partner.shape[0] + term_kind.shape[0] + 1
    return pl.pallas_call(
        functools.partial(table_kernel, devices),
        out_shape=jax.ShapeDtypeStruct((length,), jnp.int32),
        in_specs=[SCALARS, SCALARS, WHOLE],
        out_specs=SCALARS,
        scratch_shapes=[pltpu.SMEM((devices,), jnp.int32)],
        compiler_params=pltpu.CompilerParams(vmem_limit_bytes=SMALL),
        name="table",
    )(partner, term_kind, vector)


def sector(table, count, terms, deep, l_ref, r_ref, own_ref, other_ref, lhs, high_rhs, low_rhs):
    rows, width = l_ref.shape[2], r_ref.shape[3]
    height = own_ref.shape[0]
    roots = height // rows
    first = table[3 * count + terms] == 0
    own, other = own_ref[...], other_ref[...]
    top = jnp.where(first, own, other)
    bottom = jnp.where(first, other, own)
    vector = jnp.concatenate(
        [
            jnp.concatenate([half[r * rows : (r + 1) * rows] for r in range(roots)], axis=1)
            for half in (top, bottom)
        ],
        axis=0,
    )
    high, low = halves(vector)
    left = l_ref[:, 0].reshape(terms * rows, 2 * rows)
    left = jnp.concatenate(halves(left) * 2, axis=1)
    middle = jnp.dot(
        left,
        jnp.concatenate([high, high, low, low], axis=0),
        preferred_element_type=jnp.float32,
    )
    high, low = halves(middle)
    for k in range(terms):
        lanes = slice(k * width, (k + 1) * width)
        for r in range(roots):
            part = (slice(k * rows, (k + 1) * rows), slice(r * width, (r + 1) * width))
            lhs[r * rows : (r + 1) * rows, lanes] = high[part]
            lhs[(roots + r) * rows : (roots + r + 1) * rows, lanes] = low[part]
    for k in range(terms):
        lanes = slice(k * width, (k + 1) * width)
        kind = table[3 * count + k]
        used = pl.ds(pl.multiple_of((1 - kind) * width, width), width)
        high, low = halves(r_ref[k, 0].T)
        high_rhs[lanes, used] = high
        low_rhs[lanes, used] = low
    if deep:
        high, low = lhs[:height], lhs[height:]
        return jnp.dot(
            jnp.concatenate([high, low, high], axis=1),
            jnp.concatenate([high_rhs[...], high_rhs[...], low_rhs[...]], axis=0),
            preferred_element_type=jnp.float32,
        )
    tall = jnp.dot(lhs[...], high_rhs[...], preferred_element_type=jnp.float32)
    short = jnp.dot(lhs[:height], low_rhs[...], preferred_element_type=jnp.float32)
    return tall[:height] + tall[height:] + short


def sector_kernel(count, terms, unroll, deep, starts, tags, table, *refs):
    inputs, scratch = refs[: 4 * unroll], refs[-3 * unroll :]
    outputs = refs[-3 * unroll - len(starts) : -3 * unroll]
    tag_refs = refs[4 * unroll : 4 * unroll + 2]
    moved_refs, kept_ref = outputs[:-1], outputs[-1]
    width = kept_ref.shape[1]
    height = kept_ref.shape[0] // unroll
    step = pl.program_id(0)

    @pl.when(step == 0)
    def _():
        for at, ref in enumerate(scratch):
            if at % 3:
                ref[...] = jnp.zeros_like(ref)
        if any(tags):
            tag = tag_refs[0][...] + tag_refs[1][...]
            for ref, begin, end, tagged in zip(moved_refs, starts, starts[1:], tags):
                if tagged:
                    ref[(end - begin) * height :] = tag

    results = [
        sector(table, count, terms, deep, *inputs[4 * u : 4 * u + 4], *scratch[3 * u : 3 * u + 3])
        for u in range(unroll)
    ]
    for u in range(unroll):
        kept_ref[u * height : (u + 1) * height] = results[u][:, width:]
    for ref, begin, end in zip(moved_refs, starts, starts[1:]):
        for u in range(unroll):
            at = step * unroll + u - begin

            @pl.when((at >= 0) & (at < end - begin))
            def _(ref=ref, u=u, at=at):
                ref[pl.ds(pl.multiple_of(at * height, height), height)] = results[u][:, :width]


def place_of(i, pieces):
    at, begin = pieces[0][0] + i, 0
    for (_, size), (base, _) in zip(pieces, pieces[1:]):
        begin += size
        at = jnp.where(i >= begin, base + i - begin, at)
    return at


def sectors(table, pieces, tags, left, right, own, other, kept, origin, roots):
    terms, count, rows, width = left.shape
    height = roots * rows
    starts = [0]
    for _, size in pieces:
        starts.append(starts[-1] + size)
    places = [base + i for base, size in pieces for i in range(size)]

    def fits(unroll):
        return len(places) % unroll == 0 and all(
            places[i] % unroll == 0
            and places[i : i + unroll] == list(range(places[i], places[i] + unroll))
            for i in range(0, len(places), unroll)
        )

    unroll = next(unroll for unroll in (2, 1) if fits(unroll))

    def specs(u):
        def source(i, table):
            return table[place_of(unroll * i + u, pieces)]

        def held(i, table):
            at = source(i, table) if origin is None else place_of(unroll * i + u, pieces) - origin
            return (at, 0)

        return [
            pl.BlockSpec((terms, 1, rows, width), lambda i, t: (0, source(i, t), 0, 0)),
            pl.BlockSpec((terms, 1, width, width), lambda i, t: (0, source(i, t), 0, 0)),
            pl.BlockSpec((height, width), held),
            pl.BlockSpec((height, width), held),
        ]

    in_specs = [spec for u in range(unroll) for spec in specs(u)]
    args = [left, right, own, other] * unroll
    if any(tags):
        in_specs += [pl.BlockSpec((TAG, width), lambda i, t: (own.shape[0] // TAG - 1, 0))] * 2
        args += [own, other]
    aliases = {}
    if kept is not None:
        in_specs.append(ANY)
        args.append(kept)
        aliases = {len(args): len(pieces)}
    deep = terms * width
    shapes = [(size * height + TAG * tagged, width) for (_, size), tagged in zip(pieces, tags)]
    out = pl.pallas_call(
        functools.partial(sector_kernel, count, terms, unroll, origin is not None, starts, tags),
        out_shape=[
            jax.ShapeDtypeStruct(shape, jnp.float32)
            for shape in shapes + [(count * height, width)]
        ],
        grid_spec=pltpu.PrefetchScalarGridSpec(
            num_scalar_prefetch=1,
            grid=(starts[-1] // unroll,),
            in_specs=in_specs,
            out_specs=[pl.BlockSpec(shape, lambda i, t: (0, 0)) for shape in shapes]
            + [
                pl.BlockSpec(
                    (unroll * height, width),
                    lambda i, t: (lax.div(place_of(unroll * i, pieces), unroll), 0),
                )
            ],
            scratch_shapes=[
                pltpu.VMEM((2 * height, deep), jnp.bfloat16),
                pltpu.VMEM((deep, 2 * width), jnp.bfloat16),
                pltpu.VMEM((deep, 2 * width), jnp.bfloat16),
            ]
            * unroll,
        ),
        input_output_aliases=aliases,
        compiler_params=pltpu.CompilerParams(vmem_limit_bytes=LIMIT),
        cost_estimate=FREE,
        name="sectors",
    )(table, *args)
    return out[:-1], out[-1]


def combine_kernel(share, starts, with_inner, table, kept_ref, vector_ref, diag_ref, *refs):
    arrived_refs, sum_ref = refs[: len(starts)], refs[-2 if with_inner else -1]
    height = vector_ref.shape[0]
    before = refs[len(starts) : -2] if with_inner else ()
    rows = diag_ref.shape[1]
    roots = vector_ref.shape[0] // rows
    step = pl.program_id(0)
    arrived = arrived_refs[0][...]
    for ref, begin in zip(arrived_refs[1:], starts[1:]):
        arrived = jnp.where(step >= begin, ref[...], arrived)
    diag = share * diag_ref[0]
    if with_inner:
        inner_ref = refs[-1]

        @pl.when(step == 0)
        def _():
            inner_ref[...] = sum((ref[...] for ref in before), jnp.zeros_like(inner_ref))

    for r in range(roots):
        at = slice(r * rows, (r + 1) * rows)
        vector = vector_ref[at]
        total = kept_ref[at] + arrived[at] + diag * vector
        if before:
            sum_ref[pl.ds(pl.multiple_of(step * height + r * rows, rows), rows)] = total
        else:
            sum_ref[at] = total
        if with_inner:
            inner_ref[r : r + 1] += jnp.sum(vector * total, axis=0, keepdims=True)
            inner_ref[roots + r : roots + r + 1] += share * jnp.sum(
                vector * vector, axis=0, keepdims=True
            )
    if before:
        sum_ref[sum_ref.shape[0] - TAG :] = inner_ref[...]


def combine(table, pieces, kept, arrived, vector, diag, share, ordered, with_inner, before):
    count, rows, width = diag.shape
    height = kept.shape[0] // count
    starts = [0]
    for _, size in pieces:
        starts.append(starts[-1] + size)

    def slot(i, table):
        return table[count + place_of(i, pieces)]

    def place(i, table):
        return table[2 * count + slot(i, table)]

    def held(i, table):
        return (place(i, table) if ordered else slot(i, table), 0)

    def arrived_spec(begin, end):
        return pl.BlockSpec((height, width), lambda i, t: (jnp.clip(i - begin, 0, end - begin - 1), 0))

    block = (height, width)
    whole = (starts[-1] * height + TAG * bool(before), width)
    out_shape = [jax.ShapeDtypeStruct(whole, jnp.float32)]
    out_specs = [pl.BlockSpec(whole if before else block, lambda i, t: (0 if before else i, 0))]
    if with_inner:
        out_shape.append(jax.ShapeDtypeStruct((TAG, width), jnp.float32))
        out_specs.append(pl.BlockSpec((TAG, width), lambda i, t: (0, 0)))
    out = pl.pallas_call(
        functools.partial(combine_kernel, share, starts[:-1], with_inner),
        out_shape=out_shape,
        grid_spec=pltpu.PrefetchScalarGridSpec(
            num_scalar_prefetch=1,
            grid=(starts[-1],),
            in_specs=[
                pl.BlockSpec(block, lambda i, t: (place(i, t), 0)),
                pl.BlockSpec(block, held),
                pl.BlockSpec((1, rows, width), lambda i, t: (slot(i, t), 0, 0)),
            ]
            + [arrived_spec(begin, end) for begin, end in zip(starts, starts[1:])]
            + [pl.BlockSpec((TAG, width), lambda i, t: (0, 0))] * len(before),
            out_specs=out_specs,
        ),
        compiler_params=pltpu.CompilerParams(vmem_limit_bytes=SMALL),
        cost_estimate=FREE,
        name="combine",
    )(table, kept, vector, diag, *arrived, *before)
    return out if with_inner else (out[0], None)


def correct_kernel(groups, ahead, table, inner_ref, vector_ref, diag_ref, *rest):
    parts, (raw_ref, ahead_ref) = rest[:-2], rest[-2:]
    count, rows, width = diag_ref.shape
    height = vector_ref.shape[0] // count
    roots = height // rows
    inner = jnp.sum(inner_ref[...], axis=1, keepdims=True)
    theta = inner[:roots] / inner[roots : 2 * roots]
    squares = [jnp.zeros((1, width), jnp.float32) for _ in range(roots)]
    for at, pieces in enumerate(groups):
        mine, theirs = parts[2 * at], parts[2 * at + 1]
        row = 0
        for base, size in pieces:
            for i in range(size):
                slot = table[count + base + i]
                held = slot * height
                place = table[2 * count + slot] * height
                diag = diag_ref[slot]
                for r in range(roots):
                    shift = theta[r : r + 1]
                    sigma = mine[row : row + rows] + theirs[row : row + rows]
                    vector = vector_ref[pl.ds(pl.multiple_of(held + r * rows, rows), rows)]
                    raw = (sigma - shift * vector) / jnp.maximum(jnp.abs(diag - shift), 1.0)
                    raw_ref[pl.ds(pl.multiple_of(place + r * rows, rows), rows)] = raw
                    squares[r] = squares[r] + jnp.sum(raw * raw, axis=0, keepdims=True)
                    row += rows
    raw_ref[count * height :] = jnp.concatenate(
        squares + [jnp.zeros((TAG - roots, width), jnp.float32)], axis=0
    )
    ahead_ref[: ahead[1] * height] = raw_ref[ahead[0] * height : (ahead[0] + ahead[1]) * height]
    ahead_ref[ahead[1] * height :] = raw_ref[count * height :]


def correct(table, groups, ahead, inner, vector, diag, parts):
    height, width = vector.shape[0] // diag.shape[0], vector.shape[1]
    return pl.pallas_call(
        functools.partial(correct_kernel, groups, ahead),
        out_shape=[
            jax.ShapeDtypeStruct((vector.shape[0] + TAG, width), jnp.float32),
            jax.ShapeDtypeStruct((ahead[1] * height + TAG, width), jnp.float32),
        ],
        in_specs=[SCALARS] + [WHOLE] * (3 + len(parts)),
        out_specs=[WHOLE, WHOLE],
        compiler_params=pltpu.CompilerParams(vmem_limit_bytes=SMALL),
        cost_estimate=FREE,
        name="correct",
    )(table, inner, vector, diag, *parts)


def scatter(held, out_ref, sems, rows_of):
    height = held.shape[0] // len(rows_of)
    copies = []
    for i, make in enumerate(rows_of):
        at = slice(i * height, (i + 1) * height)
        row = make(at)
        copies.append(
            pltpu.make_async_copy(
                held.at[at], out_ref.at[pl.ds(pl.multiple_of(row, height), height)], sems.at[i]
            )
        )
        copies[-1].start()
    for copy in copies:
        copy.wait()


def scaled_kernel(count, rows, table, scale_ref, raw_ref, out_ref, held, sems):
    height = held.shape[0] // count

    def make(i, at):
        place = pl.multiple_of(table[2 * count + i] * height, height)
        for r in range(height // rows):
            part = raw_ref[pl.ds(place + r * rows, rows)]
            held[at.start + r * rows : at.start + (r + 1) * rows] = part * scale_ref[r : r + 1]
        return i * height

    scatter(held, out_ref, sems, [functools.partial(make, i) for i in range(count)])


def scaled(table, scale, raw, count, rows):
    height, width = raw.shape[0] // count // rows * rows, raw.shape[1]
    return pl.pallas_call(
        functools.partial(scaled_kernel, count, rows),
        out_shape=jax.ShapeDtypeStruct((count * height, width), jnp.float32),
        in_specs=[SCALARS, WHOLE, WHOLE],
        out_specs=ANY,
        scratch_shapes=[
            pltpu.VMEM((count * height, width), jnp.float32),
            pltpu.SemaphoreType.DMA((count,)),
        ],
        compiler_params=pltpu.CompilerParams(vmem_limit_bytes=SMALL),
        cost_estimate=FREE,
        name="scaled",
    )(table, scale, raw)


def finish_kernel(count, rows, places, table, scale_ref, mine_ref, theirs_ref, *rest):
    out_ref, held, sems = rest[-3:]
    height = held.shape[0] // len(places)

    def make(place, at):
        for r in range(height // rows):
            part = slice(at.start + r * rows, at.start + (r + 1) * rows)
            held[part] = (mine_ref[part] + theirs_ref[part]) * scale_ref[r : r + 1]
        return table[count + place] * height

    scatter(held, out_ref, sems, [functools.partial(make, place) for place in places])


def finish(table, pieces, scale, mine, theirs, out, count, rows):
    places = [base + i for base, size in pieces for i in range(size)]
    height, width = mine.shape[0] // len(places), mine.shape[1]
    in_specs = [SCALARS, WHOLE, WHOLE, WHOLE]
    args, aliases = [table, scale, mine, theirs], {}
    if out is not None:
        in_specs.append(ANY)
        args.append(out)
        aliases = {4: 0}
    return pl.pallas_call(
        functools.partial(finish_kernel, count, rows, places),
        out_shape=jax.ShapeDtypeStruct((count * height, width), jnp.float32),
        in_specs=in_specs,
        out_specs=ANY,
        scratch_shapes=[
            pltpu.VMEM(mine.shape, jnp.float32),
            pltpu.SemaphoreType.DMA((len(places),)),
        ],
        input_output_aliases=aliases,
        compiler_params=pltpu.CompilerParams(vmem_limit_bytes=SMALL),
        cost_estimate=FREE,
        name="finish",
    )(*args)


def add_over_term(value):
    size = lax.axis_size("term")
    if size == 1 or not power_of_two(size):
        return lax.psum(value, "term"), jnp.zeros_like(value)
    bit = 1
    while 2 * bit < size:
        value = value + flip(value, "term", bit)
        bit *= 2
    return value, flip(value, "term", bit)


def after(*values):
    return lax.optimization_barrier(values)


def shards(amplitudes, left, right, term_kind, partner, left_diag, right_diag):
    devices, terms_over = lax.axis_size("blk"), lax.axis_size("term")
    slots, rows, roots, width = amplitudes.shape
    per = slots // devices
    elements = slots * devices * rows * lax.axis_size("sub") * width
    vector = jnp.transpose(amplitudes, (0, 2, 1, 3)).reshape(slots * roots * rows, width)
    table = make_table(partner, term_kind, vector)
    diag = left_diag[:, :, None] + right_diag[:, None, :]

    staying, moving = (0, 0, per), []
    for c in range(1, (devices + 1) // 2):
        moving += [(c, c * per, per), (devices - c, (devices - c) * per, per)]
    if devices % 2 == 0:
        moving.append((devices // 2, devices // 2 * per, per))
    groups = [[piece] for piece in [staying] + moving]
    batches = [moving[:1], moving[1:] + [staying]]

    def spans(pieces):
        return [piece[1:] for piece in pieces]

    def relay(value, c):
        return lax.ppermute(value, "blk", [(p, (p + c) % devices) for p in range(devices)])

    def swap(value):
        return lax.ppermute(value, "sub", [(0, 1), (1, 0)])

    def partials(own, second):
        if second:
            early = (ahead, swap(ahead))
            other = swap(after(own, early[1])[0])
        else:
            other = swap(own)
        kept, outgoing = None, {}
        for batch in batches:
            early_now = second and batch is batches[0]
            pair = early if early_now else (own, other)
            parts, kept = sectors(
                table,
                spans(batch),
                [second and piece[0] > 0 for piece in batch],
                left,
                right,
                *pair,
                kept,
                (batch[0][1] if early_now else 0) if second else None,
                roots,
            )
            outgoing.update(zip(batch, parts))
        arrived, sums, inners = {}, [], []
        for at, piece in enumerate(moving):
            value = outgoing[piece]
            if at >= 1:
                value = after(value, arrived[moving[at - 1]])[0]
            arrived[piece] = relay(value, piece[0])
        arrived[staying] = after(outgoing[staying], arrived[moving[0]])[0]
        for group in groups:
            first, *others = [arrived[piece] for piece in group]
            if sums:
                first = after(first, sums[-2])[0]
            mine, inner = combine(
                table,
                spans(group),
                kept,
                [first] + others,
                own,
                diag,
                1.0 / terms_over,
                second,
                not second,
                (),
            )
            if len(sums) >= 4:
                mine = after(mine, sums[-1])[0]
            sums += add_over_term(mine)
            inners.append(inner)
        return sums, inners, arrived, other

    sums, inners, _, _ = partials(vector, False)
    inner = small_sum(small_sum(sum(inners[1:], inners[0]), "sub"), "blk")
    inner = small_sum(after(inner, sums[-1])[0], "term")
    first = spans(batches[0])[0]
    raw, ahead = correct(
        table, [spans(group) for group in groups], first, inner, vector, diag, sums
    )

    sums, _, arrived, other = partials(raw, True)
    squares = raw[-TAG:] + other[-TAG:]
    for piece in moving:
        squares = squares + arrived[piece][-TAG:]
    scale = lax.rsqrt(jnp.sum(squares, axis=1, keepdims=True) / elements + 1e-06)
    scale = jnp.broadcast_to(scale, squares.shape)
    correction = scaled(table, scale, raw, slots, rows)
    sigma = None
    for at, group in enumerate(groups):
        sigma = finish(
            table, spans(group), scale, sums[2 * at], sums[2 * at + 1], sigma, slots, rows
        )
    return tuple(
        jnp.transpose(value.reshape(slots, roots, rows, width), (0, 2, 1, 3))
        for value in (sigma, correction)
    )


def solution(mesh):
    return jax.shard_map(
        shards,
        mesh=mesh,
        in_specs=(
            P(("grp", "blk"), "sub", None, None),
            P(("grp", "term"), "blk", "sub", None),
            P(("grp", "term"), "blk", None, None),
            P(("grp", "term")),
            P(("grp", "blk")),
            P(("grp", "blk"), "sub"),
            P(("grp", "blk"), None),
        ),
        out_specs=(P(("grp", "blk"), "sub", None, None), P(("grp", "blk"), "sub", None, None)),
        check_vma=False,
    )
```

```python
import functools

import jax
import jax.numpy as jnp
from jax import lax
from jax.experimental import pallas as pl
from jax.experimental.pallas import tpu as pltpu
from jax.sharding import PartitionSpec as P

TAG = 8
LIMIT = 48 * 1024 * 1024
SMALL = 24 * 1024 * 1024
FREE = pl.CostEstimate(flops=0, bytes_accessed=0, transcendentals=0)
WHOLE = pl.BlockSpec(memory_space=pltpu.VMEM)
SCALARS = pl.BlockSpec(memory_space=pltpu.SMEM)
ANY = pl.BlockSpec(memory_space=pl.ANY)


def power_of_two(size):
    return size & (size - 1) == 0


def flip(value, axis, bit):
    size = lax.axis_size(axis)
    return lax.ppermute(value, axis, [(i, i ^ bit) for i in range(size)])


def small_sum(value, axis):
    size = lax.axis_size(axis)
    if not power_of_two(size):
        return lax.psum(value, axis)
    bit = 1
    while bit < size:
        value = value + flip(value, axis, bit)
        bit *= 2
    return value


def halves(value):
    high = value.astype(jnp.bfloat16)
    low = (value - high.astype(jnp.float32)).astype(jnp.bfloat16)
    return high, low


def table_kernel(devices, partner_ref, kind_ref, _, table_ref, used):
    count, terms = partner_ref.shape[0], kind_ref.shape[0]
    per = count // devices
    me = lax.axis_index("blk")
    for c in range(devices):
        used[c] = 0

    def place(j, carry):
        where_to = partner_ref[j]
        owner = lax.div(where_to, count)
        offset = lax.rem(owner - me + devices, devices)
        at = offset * per + used[offset]
        used[offset] = used[offset] + 1
        table_ref[at] = j
        table_ref[count + at] = where_to - owner * count
        table_ref[2 * count + j] = at
        return carry

    lax.fori_loop(0, count, place, 0)
    for k in range(terms):
        table_ref[3 * count + k] = kind_ref[k]
    table_ref[3 * count + terms] = lax.axis_index("sub")


def make_table(partner, term_kind, vector):
    devices = lax.axis_size("blk")
    length = 3 * partner.shape[0] + term_kind.shape[0] + 1
    return pl.pallas_call(
        functools.partial(table_kernel, devices),
        out_shape=jax.ShapeDtypeStruct((length,), jnp.int32),
        in_specs=[SCALARS, SCALARS, WHOLE],
        out_specs=SCALARS,
        scratch_shapes=[pltpu.SMEM((devices,), jnp.int32)],
        compiler_params=pltpu.CompilerParams(vmem_limit_bytes=SMALL),
        name="table",
    )(partner, term_kind, vector)


def sector(table, count, terms, l_ref, r_ref, own_ref, other_ref, lhs, high_rhs, low_rhs):
    rows, width = l_ref.shape[2], r_ref.shape[3]
    height = own_ref.shape[0]
    roots = height // rows
    first = table[3 * count + terms] == 0
    own, other = own_ref[...], other_ref[...]
    top = jnp.where(first, own, other)
    bottom = jnp.where(first, other, own)
    left = l_ref[:, 0].reshape(terms * rows, 2 * rows)
    left = jnp.concatenate(halves(left), axis=1)
    for r in range(roots):
        at = slice(r * rows, (r + 1) * rows)
        wide = jnp.concatenate(halves(jnp.concatenate([top[at], bottom[at]], axis=0)), axis=1)
        both = jnp.dot(
            left, jnp.concatenate([wide, wide], axis=0), preferred_element_type=jnp.float32
        )
        high, low = halves(both[:, :width] + both[:, width:])
        for k in range(terms):
            lanes = slice(k * width, (k + 1) * width)
            part = slice(k * rows, (k + 1) * rows)
            lhs[r * rows : (r + 1) * rows, lanes] = high[part]
            lhs[(roots + r) * rows : (roots + r + 1) * rows, lanes] = low[part]
    for k in range(terms):
        lanes = slice(k * width, (k + 1) * width)
        kind = table[3 * count + k]
        used = pl.ds(pl.multiple_of((1 - kind) * width, width), width)
        high, low = halves(r_ref[k, 0].T)
        high_rhs[lanes, used] = high
        low_rhs[lanes, used] = low
    high, low = lhs[:height], lhs[height:]
    return jnp.dot(
        jnp.concatenate([high, low, high], axis=1),
        jnp.concatenate([high_rhs[...], high_rhs[...], low_rhs[...]], axis=0),
        preferred_element_type=jnp.float32,
    )


def sector_kernel(count, terms, unroll, starts, tags, table, *refs):
    inputs, scratch = refs[: 4 * unroll], refs[-3 * unroll :]
    outputs = refs[-3 * unroll - len(starts) : -3 * unroll]
    tag_refs = refs[4 * unroll : 4 * unroll + 2]
    moved_refs, kept_ref = outputs[:-1], outputs[-1]
    width = kept_ref.shape[1]
    height = kept_ref.shape[0] // unroll
    step = pl.program_id(0)

    @pl.when(step == 0)
    def _():
        for at, ref in enumerate(scratch):
            if at % 3:
                ref[...] = jnp.zeros_like(ref)
        if any(tags):
            tag = tag_refs[0][...] + tag_refs[1][...]
            for ref, begin, end, tagged in zip(moved_refs, starts, starts[1:], tags):
                if tagged:
                    ref[(end - begin) * height :] = tag

    results = [
        sector(table, count, terms, *inputs[4 * u : 4 * u + 4], *scratch[3 * u : 3 * u + 3])
        for u in range(unroll)
    ]
    for u in range(unroll):
        kept_ref[u * height : (u + 1) * height] = results[u][:, width:]
    for ref, begin, end in zip(moved_refs, starts, starts[1:]):
        for u in range(unroll):
            at = step * unroll + u - begin

            @pl.when((at >= 0) & (at < end - begin))
            def _(ref=ref, u=u, at=at):
                ref[pl.ds(pl.multiple_of(at * height, height), height)] = results[u][:, :width]


def place_of(i, pieces):
    at, begin = pieces[0][0] + i, 0
    for (_, size), (base, _) in zip(pieces, pieces[1:]):
        begin += size
        at = jnp.where(i >= begin, base + i - begin, at)
    return at


def sectors(table, pieces, tags, left, right, own, other, kept, origin, roots):
    terms, count, rows, width = left.shape
    height = roots * rows
    starts = [0]
    for _, size in pieces:
        starts.append(starts[-1] + size)
    places = [base + i for base, size in pieces for i in range(size)]

    def fits(unroll):
        return len(places) % unroll == 0 and all(
            places[i] % unroll == 0
            and places[i : i + unroll] == list(range(places[i], places[i] + unroll))
            for i in range(0, len(places), unroll)
        )

    unroll = next(unroll for unroll in (2, 1) if fits(unroll))

    def specs(u):
        def source(i, table):
            return table[place_of(unroll * i + u, pieces)]

        def held(i, table):
            at = source(i, table) if origin is None else place_of(unroll * i + u, pieces) - origin
            return (at, 0)

        return [
            pl.BlockSpec((terms, 1, rows, width), lambda i, t: (0, source(i, t), 0, 0)),
            pl.BlockSpec((terms, 1, width, width), lambda i, t: (0, source(i, t), 0, 0)),
            pl.BlockSpec((height, width), held),
            pl.BlockSpec((height, width), held),
        ]

    in_specs = [spec for u in range(unroll) for spec in specs(u)]
    args = [left, right, own, other] * unroll
    if any(tags):
        in_specs += [pl.BlockSpec((TAG, width), lambda i, t: (own.shape[0] // TAG - 1, 0))] * 2
        args += [own, other]
    aliases = {}
    if kept is not None:
        in_specs.append(ANY)
        args.append(kept)
        aliases = {len(args): len(pieces)}
    deep = terms * width
    shapes = [(size * height + TAG * tagged, width) for (_, size), tagged in zip(pieces, tags)]
    out = pl.pallas_call(
        functools.partial(sector_kernel, count, terms, unroll, starts, tags),
        out_shape=[
            jax.ShapeDtypeStruct(shape, jnp.float32)
            for shape in shapes + [(count * height, width)]
        ],
        grid_spec=pltpu.PrefetchScalarGridSpec(
            num_scalar_prefetch=1,
            grid=(starts[-1] // unroll,),
            in_specs=in_specs,
            out_specs=[pl.BlockSpec(shape, lambda i, t: (0, 0)) for shape in shapes]
            + [
                pl.BlockSpec(
                    (unroll * height, width),
                    lambda i, t: (lax.div(place_of(unroll * i, pieces), unroll), 0),
                )
            ],
            scratch_shapes=[
                pltpu.VMEM((2 * height, deep), jnp.bfloat16),
                pltpu.VMEM((deep, 2 * width), jnp.bfloat16),
                pltpu.VMEM((deep, 2 * width), jnp.bfloat16),
            ]
            * unroll,
        ),
        input_output_aliases=aliases,
        compiler_params=pltpu.CompilerParams(vmem_limit_bytes=LIMIT),
        cost_estimate=FREE,
        name="sectors",
    )(table, *args)
    return out[:-1], out[-1]


def combine_kernel(share, starts, with_inner, table, kept_ref, vector_ref, diag_ref, *refs):
    arrived_refs, sum_ref = refs[: len(starts)], refs[-2 if with_inner else -1]
    height = vector_ref.shape[0]
    before = refs[len(starts) : -2] if with_inner else ()
    rows = diag_ref.shape[1]
    roots = vector_ref.shape[0] // rows
    step = pl.program_id(0)
    arrived = arrived_refs[0][...]
    for ref, begin in zip(arrived_refs[1:], starts[1:]):
        arrived = jnp.where(step >= begin, ref[...], arrived)
    diag = share * diag_ref[0]
    if with_inner:
        inner_ref = refs[-1]

        @pl.when(step == 0)
        def _():
            inner_ref[...] = sum((ref[...] for ref in before), jnp.zeros_like(inner_ref))

    for r in range(roots):
        at = slice(r * rows, (r + 1) * rows)
        vector = vector_ref[at]
        total = kept_ref[at] + arrived[at] + diag * vector
        if before:
            sum_ref[pl.ds(pl.multiple_of(step * height + r * rows, rows), rows)] = total
        else:
            sum_ref[at] = total
        if with_inner:
            inner_ref[r : r + 1] += jnp.sum(vector * total, axis=0, keepdims=True)
            inner_ref[roots + r : roots + r + 1] += share * jnp.sum(
                vector * vector, axis=0, keepdims=True
            )
    if before:
        sum_ref[sum_ref.shape[0] - TAG :] = inner_ref[...]


def combine(table, pieces, kept, arrived, vector, diag, share, ordered, with_inner, before):
    count, rows, width = diag.shape
    height = kept.shape[0] // count
    starts = [0]
    for _, size in pieces:
        starts.append(starts[-1] + size)

    def slot(i, table):
        return table[count + place_of(i, pieces)]

    def place(i, table):
        return table[2 * count + slot(i, table)]

    def held(i, table):
        return (place(i, table) if ordered else slot(i, table), 0)

    def arrived_spec(begin, end):
        return pl.BlockSpec((height, width), lambda i, t: (jnp.clip(i - begin, 0, end - begin - 1), 0))

    block = (height, width)
    whole = (starts[-1] * height + TAG * bool(before), width)
    out_shape = [jax.ShapeDtypeStruct(whole, jnp.float32)]
    out_specs = [pl.BlockSpec(whole if before else block, lambda i, t: (0 if before else i, 0))]
    if with_inner:
        out_shape.append(jax.ShapeDtypeStruct((TAG, width), jnp.float32))
        out_specs.append(pl.BlockSpec((TAG, width), lambda i, t: (0, 0)))
    out = pl.pallas_call(
        functools.partial(combine_kernel, share, starts[:-1], with_inner),
        out_shape=out_shape,
        grid_spec=pltpu.PrefetchScalarGridSpec(
            num_scalar_prefetch=1,
            grid=(starts[-1],),
            in_specs=[
                pl.BlockSpec(block, lambda i, t: (place(i, t), 0)),
                pl.BlockSpec(block, held),
                pl.BlockSpec((1, rows, width), lambda i, t: (slot(i, t), 0, 0)),
            ]
            + [arrived_spec(begin, end) for begin, end in zip(starts, starts[1:])]
            + [pl.BlockSpec((TAG, width), lambda i, t: (0, 0))] * len(before),
            out_specs=out_specs,
        ),
        compiler_params=pltpu.CompilerParams(vmem_limit_bytes=SMALL),
        cost_estimate=FREE,
        name="combine",
    )(table, kept, vector, diag, *arrived, *before)
    return out if with_inner else (out[0], None)


def correct_kernel(groups, ahead, table, inner_ref, vector_ref, diag_ref, *rest):
    parts, (raw_ref, ahead_ref) = rest[:-2], rest[-2:]
    count, rows, width = diag_ref.shape
    height = vector_ref.shape[0] // count
    roots = height // rows
    inner = jnp.sum(inner_ref[...], axis=1, keepdims=True)
    theta = inner[:roots] / inner[roots : 2 * roots]
    squares = [jnp.zeros((1, width), jnp.float32) for _ in range(roots)]
    for at, pieces in enumerate(groups):
        mine, theirs = parts[2 * at], parts[2 * at + 1]
        row = 0
        for base, size in pieces:
            for i in range(size):
                slot = table[count + base + i]
                held = slot * height
                place = table[2 * count + slot] * height
                diag = diag_ref[slot]
                for r in range(roots):
                    shift = theta[r : r + 1]
                    sigma = mine[row : row + rows] + theirs[row : row + rows]
                    vector = vector_ref[pl.ds(pl.multiple_of(held + r * rows, rows), rows)]
                    raw = (sigma - shift * vector) / jnp.maximum(jnp.abs(diag - shift), 1.0)
                    raw_ref[pl.ds(pl.multiple_of(place + r * rows, rows), rows)] = raw
                    squares[r] = squares[r] + jnp.sum(raw * raw, axis=0, keepdims=True)
                    row += rows
    raw_ref[count * height :] = jnp.concatenate(
        squares + [jnp.zeros((TAG - roots, width), jnp.float32)], axis=0
    )
    ahead_ref[: ahead[1] * height] = raw_ref[ahead[0] * height : (ahead[0] + ahead[1]) * height]
    ahead_ref[ahead[1] * height :] = raw_ref[count * height :]


def correct(table, groups, ahead, inner, vector, diag, parts):
    height, width = vector.shape[0] // diag.shape[0], vector.shape[1]
    return pl.pallas_call(
        functools.partial(correct_kernel, groups, ahead),
        out_shape=[
            jax.ShapeDtypeStruct((vector.shape[0] + TAG, width), jnp.float32),
            jax.ShapeDtypeStruct((ahead[1] * height + TAG, width), jnp.float32),
        ],
        in_specs=[SCALARS] + [WHOLE] * (3 + len(parts)),
        out_specs=[WHOLE, WHOLE],
        compiler_params=pltpu.CompilerParams(vmem_limit_bytes=SMALL),
        cost_estimate=FREE,
        name="correct",
    )(table, inner, vector, diag, *parts)


def scatter(held, out_ref, sems, rows_of):
    height = held.shape[0] // len(rows_of)
    copies = []
    for i, make in enumerate(rows_of):
        at = slice(i * height, (i + 1) * height)
        row = make(at)
        copies.append(
            pltpu.make_async_copy(
                held.at[at], out_ref.at[pl.ds(pl.multiple_of(row, height), height)], sems.at[i]
            )
        )
        copies[-1].start()
    for copy in copies:
        copy.wait()


def scaled_kernel(count, rows, table, scale_ref, raw_ref, out_ref, held, sems):
    height = held.shape[0] // count

    def make(i, at):
        place = pl.multiple_of(table[2 * count + i] * height, height)
        for r in range(height // rows):
            part = raw_ref[pl.ds(place + r * rows, rows)]
            held[at.start + r * rows : at.start + (r + 1) * rows] = part * scale_ref[r : r + 1]
        return i * height

    scatter(held, out_ref, sems, [functools.partial(make, i) for i in range(count)])


def scaled(table, scale, raw, count, rows):
    height, width = raw.shape[0] // count // rows * rows, raw.shape[1]
    return pl.pallas_call(
        functools.partial(scaled_kernel, count, rows),
        out_shape=jax.ShapeDtypeStruct((count * height, width), jnp.float32),
        in_specs=[SCALARS, WHOLE, WHOLE],
        out_specs=ANY,
        scratch_shapes=[
            pltpu.VMEM((count * height, width), jnp.float32),
            pltpu.SemaphoreType.DMA((count,)),
        ],
        compiler_params=pltpu.CompilerParams(vmem_limit_bytes=SMALL),
        cost_estimate=FREE,
        name="scaled",
    )(table, scale, raw)


def finish_kernel(count, rows, places, table, scale_ref, mine_ref, theirs_ref, *rest):
    out_ref, held, sems = rest[-3:]
    height = held.shape[0] // len(places)

    def make(place, at):
        for r in range(height // rows):
            part = slice(at.start + r * rows, at.start + (r + 1) * rows)
            held[part] = (mine_ref[part] + theirs_ref[part]) * scale_ref[r : r + 1]
        return table[count + place] * height

    scatter(held, out_ref, sems, [functools.partial(make, place) for place in places])


def finish(table, pieces, scale, mine, theirs, out, count, rows):
    places = [base + i for base, size in pieces for i in range(size)]
    height, width = mine.shape[0] // len(places), mine.shape[1]
    in_specs = [SCALARS, WHOLE, WHOLE, WHOLE]
    args, aliases = [table, scale, mine, theirs], {}
    if out is not None:
        in_specs.append(ANY)
        args.append(out)
        aliases = {4: 0}
    return pl.pallas_call(
        functools.partial(finish_kernel, count, rows, places),
        out_shape=jax.ShapeDtypeStruct((count * height, width), jnp.float32),
        in_specs=in_specs,
        out_specs=ANY,
        scratch_shapes=[
            pltpu.VMEM(mine.shape, jnp.float32),
            pltpu.SemaphoreType.DMA((len(places),)),
        ],
        input_output_aliases=aliases,
        compiler_params=pltpu.CompilerParams(vmem_limit_bytes=SMALL),
        cost_estimate=FREE,
        name="finish",
    )(*args)


def add_over_term(value):
    size = lax.axis_size("term")
    if size == 1 or not power_of_two(size):
        return lax.psum(value, "term"), jnp.zeros_like(value)
    bit = 1
    while 2 * bit < size:
        value = value + flip(value, "term", bit)
        bit *= 2
    return value, flip(value, "term", bit)


def after(*values):
    return lax.optimization_barrier(values)


def shards(amplitudes, left, right, term_kind, partner, left_diag, right_diag):
    devices, terms_over = lax.axis_size("blk"), lax.axis_size("term")
    slots, rows, roots, width = amplitudes.shape
    per = slots // devices
    elements = slots * devices * rows * lax.axis_size("sub") * width
    vector = jnp.transpose(amplitudes, (0, 2, 1, 3)).reshape(slots * roots * rows, width)
    table = make_table(partner, term_kind, vector)
    diag = left_diag[:, :, None] + right_diag[:, None, :]

    staying = (0, 0, per)
    moving = sorted(range(1, devices), key=lambda c: (-min(c, devices - c), c))
    moving = [(c, c * per, per) for c in moving]
    groups = [[piece] for piece in [staying] + moving]
    batches = [moving[:1], moving[1:] + [staying]]

    def spans(pieces):
        return [piece[1:] for piece in pieces]

    def relay(value, c):
        return lax.ppermute(value, "blk", [(p, (p + c) % devices) for p in range(devices)])

    def swap(value):
        return lax.ppermute(value, "sub", [(0, 1), (1, 0)])

    def partials(own, second):
        if second:
            early = (ahead, swap(ahead))
            other = swap(after(own, early[1])[0])
        else:
            other = swap(own)
        kept, outgoing = None, {}
        for batch in batches:
            early_now = second and batch is batches[0]
            pair = early if early_now else (own, other)
            parts, kept = sectors(
                table,
                spans(batch),
                [second and piece[0] > 0 for piece in batch],
                left,
                right,
                *pair,
                kept,
                (batch[0][1] if early_now else 0) if second else None,
                roots,
            )
            outgoing.update(zip(batch, parts))
        arrived, sums, inners = {}, [], []
        for at, piece in enumerate(moving):
            value = outgoing[piece]
            if at >= 1:
                value = after(value, arrived[moving[at - 1]])[0]
            arrived[piece] = relay(value, piece[0])
        arrived[staying] = outgoing[staying]
        for group in groups:
            first, *others = [arrived[piece] for piece in group]
            if sums:
                first = after(first, sums[-2])[0]
            mine, inner = combine(
                table,
                spans(group),
                kept,
                [first] + others,
                own,
                diag,
                1.0 / terms_over,
                second,
                not second,
                (),
            )
            if sums:
                mine = after(mine, sums[-1])[0]
            sums += add_over_term(mine)
            inners.append(inner)
        return sums, inners, arrived, other

    sums, inners, _, _ = partials(vector, False)
    inner = small_sum(small_sum(sum(inners[1:], inners[0]), "sub"), "blk")
    inner = small_sum(after(inner, sums[-1])[0], "term")
    first = spans(batches[0])[0]
    raw, ahead = correct(
        table, [spans(group) for group in groups], first, inner, vector, diag, sums
    )

    sums, _, arrived, other = partials(raw, True)
    squares = raw[-TAG:] + other[-TAG:]
    for piece in moving:
        squares = squares + arrived[piece][-TAG:]
    scale = lax.rsqrt(jnp.sum(squares, axis=1, keepdims=True) / elements + 1e-06)
    scale = jnp.broadcast_to(scale, squares.shape)
    correction = scaled(table, scale, raw, slots, rows)
    sigma = None
    for at, group in enumerate(groups):
        sigma = finish(
            table, spans(group), scale, sums[2 * at], sums[2 * at + 1], sigma, slots, rows
        )
    return tuple(
        jnp.transpose(value.reshape(slots, roots, rows, width), (0, 2, 1, 3))
        for value in (sigma, correction)
    )


def solution(mesh):
    return jax.shard_map(
        shards,
        mesh=mesh,
        in_specs=(
            P(("grp", "blk"), "sub", None, None),
            P(("grp", "term"), "blk", "sub", None),
            P(("grp", "term"), "blk", None, None),
            P(("grp", "term")),
            P(("grp", "blk")),
            P(("grp", "blk"), "sub"),
            P(("grp", "blk"), None),
        ),
        out_specs=(P(("grp", "blk"), "sub", None, None), P(("grp", "blk"), "sub", None, None)),
        check_vma=False,
    )
```

```python
import functools

import jax
import jax.numpy as jnp
from jax import lax
from jax.experimental import pallas as pl
from jax.experimental.pallas import tpu as pltpu
from jax.sharding import PartitionSpec as P

TAG = 8
LIMIT = 48 * 1024 * 1024
SMALL = 24 * 1024 * 1024
FREE = pl.CostEstimate(flops=0, bytes_accessed=0, transcendentals=0)
WHOLE = pl.BlockSpec(memory_space=pltpu.VMEM)
SCALARS = pl.BlockSpec(memory_space=pltpu.SMEM)
ANY = pl.BlockSpec(memory_space=pl.ANY)


def power_of_two(size):
    return size & (size - 1) == 0


def flip(value, axis, bit):
    size = lax.axis_size(axis)
    return lax.ppermute(value, axis, [(i, i ^ bit) for i in range(size)])


def small_sum(value, axis):
    size = lax.axis_size(axis)
    if not power_of_two(size):
        return lax.psum(value, axis)
    if size == 4:
        one, two, three = (flip(value, axis, bit) for bit in (1, 2, 3))
        return (value + one) + (two + three)
    bit = 1
    while bit < size:
        value = value + flip(value, axis, bit)
        bit *= 2
    return value


def halves(value):
    high = value.astype(jnp.bfloat16)
    low = (value - high.astype(jnp.float32)).astype(jnp.bfloat16)
    return high, low


def table_kernel(devices, partner_hbm, kind_hbm, _, table_ref, used, partner_ref, kind_ref, sems):
    copies = [
        pltpu.make_async_copy(partner_hbm, partner_ref, sems.at[0]),
        pltpu.make_async_copy(kind_hbm, kind_ref, sems.at[1]),
    ]
    for copy in copies:
        copy.start()
    for copy in copies:
        copy.wait()
    count, terms = partner_ref.shape[0], kind_ref.shape[0]
    per = count // devices
    me = lax.axis_index("blk")
    for c in range(devices):
        used[c] = 0

    def place(j, carry):
        where_to = partner_ref[j]
        owner = lax.div(where_to, count)
        offset = lax.rem(owner - me + devices, devices)
        at = offset * per + used[offset]
        used[offset] = used[offset] + 1
        table_ref[at] = j
        table_ref[count + at] = where_to - owner * count
        table_ref[2 * count + j] = at
        return carry

    lax.fori_loop(0, count, place, 0)
    for k in range(terms):
        table_ref[3 * count + k] = kind_ref[k]
    table_ref[3 * count + terms] = lax.axis_index("sub")


def make_table(partner, term_kind, vector):
    devices = lax.axis_size("blk")
    length = 3 * partner.shape[0] + term_kind.shape[0] + 1
    return pl.pallas_call(
        functools.partial(table_kernel, devices),
        out_shape=jax.ShapeDtypeStruct((length,), jnp.int32),
        in_specs=[ANY, ANY, WHOLE],
        out_specs=SCALARS,
        scratch_shapes=[
            pltpu.SMEM((devices,), jnp.int32),
            pltpu.SMEM(partner.shape, jnp.int32),
            pltpu.SMEM(term_kind.shape, jnp.int32),
            pltpu.SemaphoreType.DMA((2,)),
        ],
        compiler_params=pltpu.CompilerParams(vmem_limit_bytes=SMALL),
        name="table",
    )(partner, term_kind, vector)


def sector(table, count, terms, l_ref, r_ref, own_ref, other_ref, lhs, high_rhs, low_rhs):
    rows, width = l_ref.shape[2], r_ref.shape[3]
    height = own_ref.shape[0]
    roots = height // rows
    first = table[3 * count + terms] == 0
    own, other = own_ref[...], other_ref[...]
    top = jnp.where(first, own, other)
    bottom = jnp.where(first, other, own)
    left = l_ref[:, 0].reshape(terms * rows, 2 * rows)
    left = jnp.concatenate(halves(left), axis=1)
    for r in range(roots):
        at = slice(r * rows, (r + 1) * rows)
        wide = jnp.concatenate(halves(jnp.concatenate([top[at], bottom[at]], axis=0)), axis=1)
        both = jnp.dot(
            left, jnp.concatenate([wide, wide], axis=0), preferred_element_type=jnp.float32
        )
        high, low = halves(both[:, :width] + both[:, width:])
        for k in range(terms):
            lanes = slice(k * width, (k + 1) * width)
            part = slice(k * rows, (k + 1) * rows)
            lhs[r * rows : (r + 1) * rows, lanes] = high[part]
            lhs[(roots + r) * rows : (roots + r + 1) * rows, lanes] = low[part]
    for k in range(terms):
        lanes = slice(k * width, (k + 1) * width)
        kind = table[3 * count + k]
        used = pl.ds(pl.multiple_of((1 - kind) * width, width), width)
        high, low = halves(r_ref[k, 0].T)
        high_rhs[lanes, used] = high
        low_rhs[lanes, used] = low
    high, low = lhs[:height], lhs[height:]
    return jnp.dot(
        jnp.concatenate([high, low, high], axis=1),
        jnp.concatenate([high_rhs[...], high_rhs[...], low_rhs[...]], axis=0),
        preferred_element_type=jnp.float32,
    )


def sector_kernel(count, terms, unroll, starts, tags, table, *refs):
    inputs, scratch = refs[: 4 * unroll], refs[-3 * unroll :]
    outputs = refs[-3 * unroll - len(starts) : -3 * unroll]
    tag_refs = refs[4 * unroll : 4 * unroll + 2]
    moved_refs, kept_ref = outputs[:-1], outputs[-1]
    width = kept_ref.shape[1]
    height = kept_ref.shape[0] // unroll
    step = pl.program_id(0)

    @pl.when(step == 0)
    def _():
        for at, ref in enumerate(scratch):
            if at % 3:
                ref[...] = jnp.zeros_like(ref)
        if any(tags):
            tag = tag_refs[0][...] + tag_refs[1][...]
            for ref, begin, end, tagged in zip(moved_refs, starts, starts[1:], tags):
                if tagged:
                    ref[(end - begin) * height :] = tag

    results = [
        sector(table, count, terms, *inputs[4 * u : 4 * u + 4], *scratch[3 * u : 3 * u + 3])
        for u in range(unroll)
    ]
    for u in range(unroll):
        kept_ref[u * height : (u + 1) * height] = results[u][:, width:]
    for ref, begin, end in zip(moved_refs, starts, starts[1:]):
        for u in range(unroll):
            at = step * unroll + u - begin

            @pl.when((at >= 0) & (at < end - begin))
            def _(ref=ref, u=u, at=at):
                ref[pl.ds(pl.multiple_of(at * height, height), height)] = results[u][:, :width]


def place_of(i, pieces):
    at, begin = pieces[0][0] + i, 0
    for (_, size), (base, _) in zip(pieces, pieces[1:]):
        begin += size
        at = jnp.where(i >= begin, base + i - begin, at)
    return at


def sectors(table, pieces, tags, left, right, own, other, kept, origin, roots):
    terms, count, rows, width = left.shape
    height = roots * rows
    starts = [0]
    for _, size in pieces:
        starts.append(starts[-1] + size)
    places = [base + i for base, size in pieces for i in range(size)]

    def fits(unroll):
        return len(places) % unroll == 0 and all(
            places[i] % unroll == 0
            and places[i : i + unroll] == list(range(places[i], places[i] + unroll))
            for i in range(0, len(places), unroll)
        )

    unroll = next(unroll for unroll in (2, 1) if fits(unroll))

    def specs(u):
        def source(i, table):
            return table[place_of(unroll * i + u, pieces)]

        def held(i, table):
            at = source(i, table) if origin is None else place_of(unroll * i + u, pieces) - origin
            return (at, 0)

        return [
            pl.BlockSpec((terms, 1, rows, width), lambda i, t: (0, source(i, t), 0, 0)),
            pl.BlockSpec((terms, 1, width, width), lambda i, t: (0, source(i, t), 0, 0)),
            pl.BlockSpec((height, width), held),
            pl.BlockSpec((height, width), held),
        ]

    in_specs = [spec for u in range(unroll) for spec in specs(u)]
    args = [left, right, own, other] * unroll
    if any(tags):
        in_specs += [pl.BlockSpec((TAG, width), lambda i, t: (own.shape[0] // TAG - 1, 0))] * 2
        args += [own, other]
    aliases = {}
    if kept is not None:
        in_specs.append(ANY)
        args.append(kept)
        aliases = {len(args): len(pieces)}
    deep = terms * width
    shapes = [(size * height + TAG * tagged, width) for (_, size), tagged in zip(pieces, tags)]
    out = pl.pallas_call(
        functools.partial(sector_kernel, count, terms, unroll, starts, tags),
        out_shape=[
            jax.ShapeDtypeStruct(shape, jnp.float32)
            for shape in shapes + [(count * height, width)]
        ],
        grid_spec=pltpu.PrefetchScalarGridSpec(
            num_scalar_prefetch=1,
            grid=(starts[-1] // unroll,),
            in_specs=in_specs,
            out_specs=[pl.BlockSpec(shape, lambda i, t: (0, 0)) for shape in shapes]
            + [
                pl.BlockSpec(
                    (unroll * height, width),
                    lambda i, t: (lax.div(place_of(unroll * i, pieces), unroll), 0),
                )
            ],
            scratch_shapes=[
                pltpu.VMEM((2 * height, deep), jnp.bfloat16),
                pltpu.VMEM((deep, 2 * width), jnp.bfloat16),
                pltpu.VMEM((deep, 2 * width), jnp.bfloat16),
            ]
            * unroll,
        ),
        input_output_aliases=aliases,
        compiler_params=pltpu.CompilerParams(vmem_limit_bytes=LIMIT),
        cost_estimate=FREE,
        name="sectors",
    )(table, *args)
    return out[:-1], out[-1]


def combine_kernel(share, with_inner, table, kept_ref, arrived_ref, vector_ref, diag_ref, sum_ref, *refs):
    rows = diag_ref.shape[1]
    roots = vector_ref.shape[0] // rows
    diag = share * diag_ref[0]
    if with_inner:
        inner_ref = refs[0]

        @pl.when(pl.program_id(0) == 0)
        def _():
            inner_ref[...] = jnp.zeros_like(inner_ref)

    for r in range(roots):
        at = slice(r * rows, (r + 1) * rows)
        vector = vector_ref[at]
        total = kept_ref[at] + arrived_ref[at] + diag * vector
        sum_ref[at] = total
        if with_inner:
            inner_ref[r : r + 1] += jnp.sum(vector * total, axis=0, keepdims=True)
            inner_ref[roots + r : roots + r + 1] += share * jnp.sum(
                vector * vector, axis=0, keepdims=True
            )


def combine(table, part, kept, arrived, vector, diag, share, ordered, with_inner):
    count, rows, width = diag.shape
    base, size, skip = part
    block = (kept.shape[0] // count, width)

    def slot(i, table):
        return table[count + base + i]

    def place(i, table):
        return table[2 * count + slot(i, table)]

    def held(i, table):
        return (place(i, table) if ordered else slot(i, table), 0)

    out_shape = [jax.ShapeDtypeStruct((size * block[0], width), jnp.float32)]
    out_specs = [pl.BlockSpec(block, lambda i, t: (i, 0))]
    if with_inner:
        out_shape.append(jax.ShapeDtypeStruct((TAG, width), jnp.float32))
        out_specs.append(pl.BlockSpec((TAG, width), lambda i, t: (0, 0)))
    out = pl.pallas_call(
        functools.partial(combine_kernel, share, with_inner),
        out_shape=out_shape,
        grid_spec=pltpu.PrefetchScalarGridSpec(
            num_scalar_prefetch=1,
            grid=(size,),
            in_specs=[
                pl.BlockSpec(block, lambda i, t: (place(i, t), 0)),
                pl.BlockSpec(block, lambda i, t: (skip + i, 0)),
                pl.BlockSpec(block, held),
                pl.BlockSpec((1, rows, width), lambda i, t: (slot(i, t), 0, 0)),
            ],
            out_specs=out_specs,
        ),
        compiler_params=pltpu.CompilerParams(vmem_limit_bytes=SMALL),
        cost_estimate=FREE,
        name="combine",
    )(table, kept, arrived, vector, diag)
    return out if with_inner else (out[0], None)


def correct_kernel(groups, ahead, table, inner_ref, vector_ref, diag_ref, *rest):
    parts, (raw_ref, ahead_ref) = rest[:-2], rest[-2:]
    count, rows, width = diag_ref.shape
    height = vector_ref.shape[0] // count
    roots = height // rows
    inner = jnp.sum(inner_ref[...], axis=1, keepdims=True)
    theta = inner[:roots] / inner[roots : 2 * roots]
    squares = [jnp.zeros((1, width), jnp.float32) for _ in range(roots)]
    for at, pieces in enumerate(groups):
        mine, theirs = parts[2 * at], parts[2 * at + 1]
        row = 0
        for base, size in pieces:
            for i in range(size):
                slot = table[count + base + i]
                held = slot * height
                place = table[2 * count + slot] * height
                diag = diag_ref[slot]
                for r in range(roots):
                    shift = theta[r : r + 1]
                    sigma = mine[row : row + rows] + theirs[row : row + rows]
                    vector = vector_ref[pl.ds(pl.multiple_of(held + r * rows, rows), rows)]
                    raw = (sigma - shift * vector) / jnp.maximum(jnp.abs(diag - shift), 1.0)
                    raw_ref[pl.ds(pl.multiple_of(place + r * rows, rows), rows)] = raw
                    squares[r] = squares[r] + jnp.sum(raw * raw, axis=0, keepdims=True)
                    row += rows
    raw_ref[count * height :] = jnp.concatenate(
        squares + [jnp.zeros((TAG - roots, width), jnp.float32)], axis=0
    )
    ahead_ref[: ahead[1] * height] = raw_ref[ahead[0] * height : (ahead[0] + ahead[1]) * height]
    ahead_ref[ahead[1] * height :] = raw_ref[count * height :]


def correct(table, groups, ahead, inner, vector, diag, parts):
    height, width = vector.shape[0] // diag.shape[0], vector.shape[1]
    return pl.pallas_call(
        functools.partial(correct_kernel, groups, ahead),
        out_shape=[
            jax.ShapeDtypeStruct((vector.shape[0] + TAG, width), jnp.float32),
            jax.ShapeDtypeStruct((ahead[1] * height + TAG, width), jnp.float32),
        ],
        in_specs=[SCALARS] + [WHOLE] * (3 + len(parts)),
        out_specs=[WHOLE, WHOLE],
        compiler_params=pltpu.CompilerParams(vmem_limit_bytes=SMALL),
        cost_estimate=FREE,
        name="correct",
    )(table, inner, vector, diag, *parts)


def scatter(held, out_ref, sems, rows_of):
    height = held.shape[0] // len(rows_of)
    copies = []
    for i, make in enumerate(rows_of):
        at = slice(i * height, (i + 1) * height)
        row = make(at)
        copies.append(
            pltpu.make_async_copy(
                held.at[at], out_ref.at[pl.ds(pl.multiple_of(row, height), height)], sems.at[i]
            )
        )
        copies[-1].start()
    for copy in copies:
        copy.wait()


def scaled_kernel(count, rows, table, scale_ref, raw_ref, out_ref, held, sems):
    height = held.shape[0] // count

    def make(i, at):
        place = pl.multiple_of(table[2 * count + i] * height, height)
        for r in range(height // rows):
            part = raw_ref[pl.ds(place + r * rows, rows)]
            held[at.start + r * rows : at.start + (r + 1) * rows] = part * scale_ref[r : r + 1]
        return i * height

    scatter(held, out_ref, sems, [functools.partial(make, i) for i in range(count)])


def scaled(table, scale, raw, count, rows):
    height, width = raw.shape[0] // count // rows * rows, raw.shape[1]
    return pl.pallas_call(
        functools.partial(scaled_kernel, count, rows),
        out_shape=jax.ShapeDtypeStruct((count * height, width), jnp.float32),
        in_specs=[SCALARS, WHOLE, WHOLE],
        out_specs=ANY,
        scratch_shapes=[
            pltpu.VMEM((count * height, width), jnp.float32),
            pltpu.SemaphoreType.DMA((count,)),
        ],
        compiler_params=pltpu.CompilerParams(vmem_limit_bytes=SMALL),
        cost_estimate=FREE,
        name="scaled",
    )(table, scale, raw)


def finish_kernel(count, rows, sizes, places, table, scale_ref, *refs):
    parts, (out_ref, held, sems) = refs[: 2 * len(sizes)], refs[-3:]
    height = held.shape[0] // len(places)
    sources = [(part, i) for part, size in enumerate(sizes) for i in range(size)]

    def make(source, place, at):
        part, i = source
        mine, theirs = parts[2 * part], parts[2 * part + 1]
        for r in range(height // rows):
            row = i * height + r * rows
            total = mine[row : row + rows] + theirs[row : row + rows]
            held[at.start + r * rows : at.start + (r + 1) * rows] = total * scale_ref[r : r + 1]
        return table[count + place] * height

    scatter(held, out_ref, sems, [functools.partial(make, *one) for one in zip(sources, places)])


def finish(table, spans, scale, parts, out, count, rows):
    places = [base + i for base, size in spans for i in range(size)]
    height, width = parts[0].shape[0] // spans[0][1], parts[0].shape[1]
    in_specs = [SCALARS] + [WHOLE] * (1 + len(parts))
    args, aliases = [table, scale, *parts], {}
    if out is not None:
        in_specs.append(ANY)
        aliases = {len(args): 0}
        args.append(out)
    return pl.pallas_call(
        functools.partial(finish_kernel, count, rows, [size for _, size in spans], places),
        out_shape=jax.ShapeDtypeStruct((count * height, width), jnp.float32),
        in_specs=in_specs,
        out_specs=ANY,
        scratch_shapes=[
            pltpu.VMEM((len(places) * height, width), jnp.float32),
            pltpu.SemaphoreType.DMA((len(places),)),
        ],
        input_output_aliases=aliases,
        compiler_params=pltpu.CompilerParams(vmem_limit_bytes=SMALL),
        cost_estimate=FREE,
        name="finish",
    )(*args)


def add_over_term(value):
    size = lax.axis_size("term")
    if size == 1 or not power_of_two(size):
        return lax.psum(value, "term"), jnp.zeros_like(value)
    bit = 1
    while 2 * bit < size:
        value = value + flip(value, "term", bit)
        bit *= 2
    return value, flip(value, "term", bit)


def after(*values):
    return lax.optimization_barrier(values)


def shards(amplitudes, left, right, term_kind, partner, left_diag, right_diag):
    devices, terms_over = lax.axis_size("blk"), lax.axis_size("term")
    slots, rows, roots, width = amplitudes.shape
    per = slots // devices
    elements = slots * devices * rows * lax.axis_size("sub") * width
    vector = jnp.transpose(amplitudes, (0, 2, 1, 3)).reshape(slots * roots * rows, width)
    table = make_table(partner, term_kind, vector)
    diag = left_diag[:, :, None] + right_diag[:, None, :]

    staying = (0, 0, per)
    moving = sorted(range(1, devices), key=lambda c: (-min(c, devices - c), c))
    moving = [(c, c * per, per) for c in moving]
    cuts = [(0, per // 2), (per // 2, per - per // 2)] if per > 1 else [(0, per)]
    shares = [
        (piece, piece[1] + start, size, start) for piece in [staying] + moving for start, size in cuts
    ]
    lasting = len(shares) - len(cuts)
    batches = [moving[:1], moving[1:] + [staying]]

    def spans(pieces):
        return [piece[1:] for piece in pieces]

    def relay(value, c):
        return lax.ppermute(value, "blk", [(p, (p + c) % devices) for p in range(devices)])

    def swap(value):
        return lax.ppermute(value, "sub", [(0, 1), (1, 0)])

    def partials(own, second):
        if second:
            early = (ahead, swap(ahead))
            other = swap(after(own, early[1])[0])
        else:
            other = swap(own)
        kept, outgoing = None, {}
        for batch in batches:
            early_now = second and batch is batches[0]
            pair = early if early_now else (own, other)
            parts, kept = sectors(
                table,
                spans(batch),
                [second and piece[0] > 0 for piece in batch],
                left,
                right,
                *pair,
                kept,
                (batch[0][1] if early_now else 0) if second else None,
                roots,
            )
            outgoing.update(zip(batch, parts))
        arrived, sums, inners = {}, [], []
        for at, piece in enumerate(moving):
            value = outgoing[piece]
            if at >= 2:
                value = after(value, arrived[moving[at - 2]])[0]
            arrived[piece] = relay(value, piece[0])
        arrived[staying] = outgoing[staying]
        for piece, *part in shares:
            mine, inner = combine(
                table,
                part,
                kept,
                arrived[piece],
                own,
                diag,
                1.0 / terms_over,
                second,
                not second,
            )
            if len(sums) >= 2 * len(cuts):
                mine = after(mine, sums[1 - 2 * len(cuts)])[0]
            sums += add_over_term(mine)
            inners.append(inner)
        return sums, inners, arrived, other

    sums, inners, _, _ = partials(vector, False)
    inner = small_sum(small_sum(sum(inners[1:], inners[0]), "sub"), "blk")
    inner = small_sum(after(inner, sums[-1])[0], "term")
    first = spans(batches[0])[0]
    raw, ahead = correct(
        table, [[part[1:3]] for part in shares], first, inner, vector, diag, sums
    )

    sums, _, arrived, other = partials(raw, True)
    squares = raw[-TAG:] + other[-TAG:]
    for piece in moving:
        squares = squares + arrived[piece][-TAG:]
    scale = lax.rsqrt(jnp.sum(squares, axis=1, keepdims=True) / elements + 1e-06)
    scale = jnp.broadcast_to(scale, squares.shape)
    correction = scaled(table, scale, raw, slots, rows)
    sigma = None
    for some in (slice(0, lasting), slice(lasting, None)):
        parts = [one for pair in list(zip(sums[::2], sums[1::2]))[some] for one in pair]
        if parts:
            spans_of = [part[1:3] for part in shares[some]]
            sigma = finish(table, spans_of, scale, parts, sigma, slots, rows)
    return tuple(
        jnp.transpose(value.reshape(slots, roots, rows, width), (0, 2, 1, 3))
        for value in (sigma, correction)
    )


def solution(mesh):
    return jax.shard_map(
        shards,
        mesh=mesh,
        in_specs=(
            P(("grp", "blk"), "sub", None, None),
            P(("grp", "term"), "blk", "sub", None),
            P(("grp", "term"), "blk", None, None),
            P(("grp", "term")),
            P(("grp", "blk")),
            P(("grp", "blk"), "sub"),
            P(("grp", "blk"), None),
        ),
        out_specs=(P(("grp", "blk"), "sub", None, None), P(("grp", "blk"), "sub", None, None)),
        check_vma=False,
    )
```

```python
import functools

import jax
import jax.numpy as jnp
from jax import lax
from jax.experimental import pallas as pl
from jax.experimental.pallas import tpu as pltpu
from jax.sharding import PartitionSpec as P

TAG = 8
LIMIT = 48 * 1024 * 1024
SMALL = 24 * 1024 * 1024
FREE = pl.CostEstimate(flops=0, bytes_accessed=0, transcendentals=0)
WHOLE = pl.BlockSpec(memory_space=pltpu.VMEM)
SCALARS = pl.BlockSpec(memory_space=pltpu.SMEM)
ANY = pl.BlockSpec(memory_space=pl.ANY)


def power_of_two(size):
    return size & (size - 1) == 0


def flip(value, axis, bit):
    size = lax.axis_size(axis)
    return lax.ppermute(value, axis, [(i, i ^ bit) for i in range(size)])


def small_sum(value, axis):
    size = lax.axis_size(axis)
    if not power_of_two(size):
        return lax.psum(value, axis)
    if size == 4:
        one, two, three = (flip(value, axis, bit) for bit in (1, 2, 3))
        return (value + one) + (two + three)
    bit = 1
    while bit < size:
        value = value + flip(value, axis, bit)
        bit *= 2
    return value


def halves(value):
    high = value.astype(jnp.bfloat16)
    low = (value - high.astype(jnp.float32)).astype(jnp.bfloat16)
    return high, low


def table_kernel(devices, partner_hbm, kind_hbm, _, table_ref, used, partner_ref, kind_ref, sems):
    copies = [
        pltpu.make_async_copy(partner_hbm, partner_ref, sems.at[0]),
        pltpu.make_async_copy(kind_hbm, kind_ref, sems.at[1]),
    ]
    for copy in copies:
        copy.start()
    for copy in copies:
        copy.wait()
    count, terms = partner_ref.shape[0], kind_ref.shape[0]
    per = count // devices
    me = lax.axis_index("blk")
    for c in range(devices):
        used[c] = 0

    def place(j, carry):
        where_to = partner_ref[j]
        owner = lax.div(where_to, count)
        offset = lax.rem(owner - me + devices, devices)
        at = offset * per + used[offset]
        used[offset] = used[offset] + 1
        table_ref[at] = j
        table_ref[count + at] = where_to - owner * count
        table_ref[2 * count + j] = at
        return carry

    lax.fori_loop(0, count, place, 0)
    for k in range(terms):
        table_ref[3 * count + k] = kind_ref[k]
    table_ref[3 * count + terms] = lax.axis_index("sub")


def make_table(partner, term_kind, vector):
    devices = lax.axis_size("blk")
    length = 3 * partner.shape[0] + term_kind.shape[0] + 1
    return pl.pallas_call(
        functools.partial(table_kernel, devices),
        out_shape=jax.ShapeDtypeStruct((length,), jnp.int32),
        in_specs=[ANY, ANY, WHOLE],
        out_specs=SCALARS,
        scratch_shapes=[
            pltpu.SMEM((devices,), jnp.int32),
            pltpu.SMEM(partner.shape, jnp.int32),
            pltpu.SMEM(term_kind.shape, jnp.int32),
            pltpu.SemaphoreType.DMA((2,)),
        ],
        compiler_params=pltpu.CompilerParams(vmem_limit_bytes=SMALL),
        name="table",
    )(partner, term_kind, vector)


def sector(table, count, terms, l_ref, r_ref, own_ref, other_ref, lhs, high_rhs, low_rhs):
    rows, width = l_ref.shape[2], r_ref.shape[3]
    height = own_ref.shape[0]
    roots = height // rows
    first = table[3 * count + terms] == 0
    own, other = own_ref[...], other_ref[...]
    top = jnp.where(first, own, other)
    bottom = jnp.where(first, other, own)
    left = l_ref[:, 0].reshape(terms * rows, 2 * rows)
    left = jnp.concatenate(halves(left), axis=1)
    for r in range(roots):
        at = slice(r * rows, (r + 1) * rows)
        wide = jnp.concatenate(halves(jnp.concatenate([top[at], bottom[at]], axis=0)), axis=1)
        both = jnp.dot(
            left, jnp.concatenate([wide, wide], axis=0), preferred_element_type=jnp.float32
        )
        high, low = halves(both[:, :width] + both[:, width:])
        for k in range(terms):
            lanes = slice(k * width, (k + 1) * width)
            part = slice(k * rows, (k + 1) * rows)
            lhs[r * rows : (r + 1) * rows, lanes] = high[part]
            lhs[(roots + r) * rows : (roots + r + 1) * rows, lanes] = low[part]
    for k in range(terms):
        lanes = slice(k * width, (k + 1) * width)
        kind = table[3 * count + k]
        used = pl.ds(pl.multiple_of((1 - kind) * width, width), width)
        high, low = halves(r_ref[k, 0].T)
        high_rhs[lanes, used] = high
        low_rhs[lanes, used] = low
    high, low = lhs[:height], lhs[height:]
    return jnp.dot(
        jnp.concatenate([high, low, high], axis=1),
        jnp.concatenate([high_rhs[...], high_rhs[...], low_rhs[...]], axis=0),
        preferred_element_type=jnp.float32,
    )


def sector_kernel(count, terms, unroll, starts, tags, table, *refs):
    inputs, scratch = refs[: 4 * unroll], refs[-3 * unroll :]
    outputs = refs[-3 * unroll - len(starts) : -3 * unroll]
    tag_refs = refs[4 * unroll : 4 * unroll + 2]
    moved_refs, kept_ref = outputs[:-1], outputs[-1]
    width = kept_ref.shape[1]
    height = kept_ref.shape[0] // unroll
    step = pl.program_id(0)

    @pl.when(step == 0)
    def _():
        for at, ref in enumerate(scratch):
            if at % 3:
                ref[...] = jnp.zeros_like(ref)
        if any(tags):
            tag = tag_refs[0][...] + tag_refs[1][...]
            for ref, begin, end, tagged in zip(moved_refs, starts, starts[1:], tags):
                if tagged:
                    ref[(end - begin) * height :] = tag

    results = [
        sector(table, count, terms, *inputs[4 * u : 4 * u + 4], *scratch[3 * u : 3 * u + 3])
        for u in range(unroll)
    ]
    for u in range(unroll):
        kept_ref[u * height : (u + 1) * height] = results[u][:, width:]
    for ref, begin, end in zip(moved_refs, starts, starts[1:]):
        for u in range(unroll):
            at = step * unroll + u - begin

            @pl.when((at >= 0) & (at < end - begin))
            def _(ref=ref, u=u, at=at):
                ref[pl.ds(pl.multiple_of(at * height, height), height)] = results[u][:, :width]


def place_of(i, pieces):
    at, begin = pieces[0][0] + i, 0
    for (_, size), (base, _) in zip(pieces, pieces[1:]):
        begin += size
        at = jnp.where(i >= begin, base + i - begin, at)
    return at


def sectors(table, pieces, tags, left, right, own, other, kept, origin, roots):
    terms, count, rows, width = left.shape
    height = roots * rows
    starts = [0]
    for _, size in pieces:
        starts.append(starts[-1] + size)
    places = [base + i for base, size in pieces for i in range(size)]

    def fits(unroll):
        return len(places) % unroll == 0 and all(
            places[i] % unroll == 0
            and places[i : i + unroll] == list(range(places[i], places[i] + unroll))
            for i in range(0, len(places), unroll)
        )

    unroll = next(unroll for unroll in (2, 1) if fits(unroll))

    def specs(u):
        def source(i, table):
            return table[place_of(unroll * i + u, pieces)]

        def held(i, table):
            at = source(i, table) if origin is None else place_of(unroll * i + u, pieces) - origin
            return (at, 0)

        return [
            pl.BlockSpec((terms, 1, rows, width), lambda i, t: (0, source(i, t), 0, 0)),
            pl.BlockSpec((terms, 1, width, width), lambda i, t: (0, source(i, t), 0, 0)),
            pl.BlockSpec((height, width), held),
            pl.BlockSpec((height, width), held),
        ]

    in_specs = [spec for u in range(unroll) for spec in specs(u)]
    args = [left, right, own, other] * unroll
    if any(tags):
        in_specs += [pl.BlockSpec((TAG, width), lambda i, t: (own.shape[0] // TAG - 1, 0))] * 2
        args += [own, other]
    aliases = {}
    if kept is not None:
        in_specs.append(ANY)
        args.append(kept)
        aliases = {len(args): len(pieces)}
    deep = terms * width
    shapes = [(size * height + TAG * tagged, width) for (_, size), tagged in zip(pieces, tags)]
    out = pl.pallas_call(
        functools.partial(sector_kernel, count, terms, unroll, starts, tags),
        out_shape=[
            jax.ShapeDtypeStruct(shape, jnp.float32)
            for shape in shapes + [(count * height, width)]
        ],
        grid_spec=pltpu.PrefetchScalarGridSpec(
            num_scalar_prefetch=1,
            grid=(starts[-1] // unroll,),
            in_specs=in_specs,
            out_specs=[pl.BlockSpec(shape, lambda i, t: (0, 0)) for shape in shapes]
            + [
                pl.BlockSpec(
                    (unroll * height, width),
                    lambda i, t: (lax.div(place_of(unroll * i, pieces), unroll), 0),
                )
            ],
            scratch_shapes=[
                pltpu.VMEM((2 * height, deep), jnp.bfloat16),
                pltpu.VMEM((deep, 2 * width), jnp.bfloat16),
                pltpu.VMEM((deep, 2 * width), jnp.bfloat16),
            ]
            * unroll,
        ),
        input_output_aliases=aliases,
        compiler_params=pltpu.CompilerParams(vmem_limit_bytes=LIMIT),
        cost_estimate=FREE,
        name="sectors",
    )(table, *args)
    return out[:-1], out[-1]


def combine_kernel(share, with_inner, table, kept_ref, arrived_ref, vector_ref, diag_ref, sum_ref, *refs):
    rows = diag_ref.shape[1]
    roots = vector_ref.shape[0] // rows
    diag = share * diag_ref[0]
    if with_inner:
        inner_ref = refs[0]

        @pl.when(pl.program_id(0) == 0)
        def _():
            inner_ref[...] = jnp.zeros_like(inner_ref)

    for r in range(roots):
        at = slice(r * rows, (r + 1) * rows)
        vector = vector_ref[at]
        total = kept_ref[at] + arrived_ref[at] + diag * vector
        sum_ref[at] = total
        if with_inner:
            inner_ref[r : r + 1] += jnp.sum(vector * total, axis=0, keepdims=True)
            inner_ref[roots + r : roots + r + 1] += share * jnp.sum(
                vector * vector, axis=0, keepdims=True
            )


def combine(table, piece, kept, arrived, vector, diag, share, ordered, with_inner):
    count, rows, width = diag.shape
    base, size = piece
    block = (kept.shape[0] // count, width)

    def slot(i, table):
        return table[count + base + i]

    def place(i, table):
        return table[2 * count + slot(i, table)]

    def held(i, table):
        return (place(i, table) if ordered else slot(i, table), 0)

    out_shape = [jax.ShapeDtypeStruct((size * block[0], width), jnp.float32)]
    out_specs = [pl.BlockSpec(block, lambda i, t: (i, 0))]
    if with_inner:
        out_shape.append(jax.ShapeDtypeStruct((TAG, width), jnp.float32))
        out_specs.append(pl.BlockSpec((TAG, width), lambda i, t: (0, 0)))
    out = pl.pallas_call(
        functools.partial(combine_kernel, share, with_inner),
        out_shape=out_shape,
        grid_spec=pltpu.PrefetchScalarGridSpec(
            num_scalar_prefetch=1,
            grid=(size,),
            in_specs=[
                pl.BlockSpec(block, lambda i, t: (place(i, t), 0)),
                pl.BlockSpec(block, lambda i, t: (i, 0)),
                pl.BlockSpec(block, held),
                pl.BlockSpec((1, rows, width), lambda i, t: (slot(i, t), 0, 0)),
            ],
            out_specs=out_specs,
        ),
        compiler_params=pltpu.CompilerParams(vmem_limit_bytes=SMALL),
        cost_estimate=FREE,
        name="combine",
    )(table, kept, arrived, vector, diag)
    return out if with_inner else (out[0], None)


def correct_kernel(groups, ahead, table, inner_ref, vector_ref, diag_ref, *rest):
    parts, (raw_ref, ahead_ref) = rest[:-2], rest[-2:]
    count, rows, width = diag_ref.shape
    height = vector_ref.shape[0] // count
    roots = height // rows
    inner = jnp.sum(inner_ref[...], axis=1, keepdims=True)
    theta = inner[:roots] / inner[roots : 2 * roots]
    squares = [jnp.zeros((1, width), jnp.float32) for _ in range(roots)]
    for at, pieces in enumerate(groups):
        mine, theirs = parts[2 * at], parts[2 * at + 1]
        row = 0
        for base, size in pieces:
            for i in range(size):
                slot = table[count + base + i]
                held = slot * height
                place = table[2 * count + slot] * height
                diag = diag_ref[slot]
                for r in range(roots):
                    shift = theta[r : r + 1]
                    sigma = mine[row : row + rows] + theirs[row : row + rows]
                    vector = vector_ref[pl.ds(pl.multiple_of(held + r * rows, rows), rows)]
                    raw = (sigma - shift * vector) / jnp.maximum(jnp.abs(diag - shift), 1.0)
                    raw_ref[pl.ds(pl.multiple_of(place + r * rows, rows), rows)] = raw
                    squares[r] = squares[r] + jnp.sum(raw * raw, axis=0, keepdims=True)
                    row += rows
    raw_ref[count * height :] = jnp.concatenate(
        squares + [jnp.zeros((TAG - roots, width), jnp.float32)], axis=0
    )
    ahead_ref[: ahead[1] * height] = raw_ref[ahead[0] * height : (ahead[0] + ahead[1]) * height]
    ahead_ref[ahead[1] * height :] = raw_ref[count * height :]


def correct(table, groups, ahead, inner, vector, diag, parts):
    height, width = vector.shape[0] // diag.shape[0], vector.shape[1]
    return pl.pallas_call(
        functools.partial(correct_kernel, groups, ahead),
        out_shape=[
            jax.ShapeDtypeStruct((vector.shape[0] + TAG, width), jnp.float32),
            jax.ShapeDtypeStruct((ahead[1] * height + TAG, width), jnp.float32),
        ],
        in_specs=[SCALARS] + [WHOLE] * (3 + len(parts)),
        out_specs=[WHOLE, WHOLE],
        compiler_params=pltpu.CompilerParams(vmem_limit_bytes=SMALL),
        cost_estimate=FREE,
        name="correct",
    )(table, inner, vector, diag, *parts)


def scatter(held, out_ref, sems, rows_of):
    height = held.shape[0] // len(rows_of)
    copies = []
    for i, make in enumerate(rows_of):
        at = slice(i * height, (i + 1) * height)
        row = make(at)
        copies.append(
            pltpu.make_async_copy(
                held.at[at], out_ref.at[pl.ds(pl.multiple_of(row, height), height)], sems.at[i]
            )
        )
        copies[-1].start()
    for copy in copies:
        copy.wait()


def scaled_kernel(count, rows, table, scale_ref, raw_ref, out_ref, held, sems):
    height = held.shape[0] // count

    def make(i, at):
        place = pl.multiple_of(table[2 * count + i] * height, height)
        for r in range(height // rows):
            part = raw_ref[pl.ds(place + r * rows, rows)]
            held[at.start + r * rows : at.start + (r + 1) * rows] = part * scale_ref[r : r + 1]
        return i * height

    scatter(held, out_ref, sems, [functools.partial(make, i) for i in range(count)])


def scaled(table, scale, raw, count, rows):
    height, width = raw.shape[0] // count // rows * rows, raw.shape[1]
    return pl.pallas_call(
        functools.partial(scaled_kernel, count, rows),
        out_shape=jax.ShapeDtypeStruct((count * height, width), jnp.float32),
        in_specs=[SCALARS, WHOLE, WHOLE],
        out_specs=ANY,
        scratch_shapes=[
            pltpu.VMEM((count * height, width), jnp.float32),
            pltpu.SemaphoreType.DMA((count,)),
        ],
        compiler_params=pltpu.CompilerParams(vmem_limit_bytes=SMALL),
        cost_estimate=FREE,
        name="scaled",
    )(table, scale, raw)


def finish_kernel(count, rows, sizes, places, table, scale_ref, *refs):
    parts, (out_ref, held, sems) = refs[: 2 * len(sizes)], refs[-3:]
    height = held.shape[0] // len(places)
    sources = [(part, i) for part, size in enumerate(sizes) for i in range(size)]

    def make(source, place, at):
        part, i = source
        mine, theirs = parts[2 * part], parts[2 * part + 1]
        for r in range(height // rows):
            row = i * height + r * rows
            total = mine[row : row + rows] + theirs[row : row + rows]
            held[at.start + r * rows : at.start + (r + 1) * rows] = total * scale_ref[r : r + 1]
        return table[count + place] * height

    scatter(held, out_ref, sems, [functools.partial(make, *one) for one in zip(sources, places)])


def finish(table, spans, scale, parts, out, count, rows):
    places = [base + i for base, size in spans for i in range(size)]
    height, width = parts[0].shape[0] // spans[0][1], parts[0].shape[1]
    in_specs = [SCALARS] + [WHOLE] * (1 + len(parts))
    args, aliases = [table, scale, *parts], {}
    if out is not None:
        in_specs.append(ANY)
        aliases = {len(args): 0}
        args.append(out)
    return pl.pallas_call(
        functools.partial(finish_kernel, count, rows, [size for _, size in spans], places),
        out_shape=jax.ShapeDtypeStruct((count * height, width), jnp.float32),
        in_specs=in_specs,
        out_specs=ANY,
        scratch_shapes=[
            pltpu.VMEM((len(places) * height, width), jnp.float32),
            pltpu.SemaphoreType.DMA((len(places),)),
        ],
        input_output_aliases=aliases,
        compiler_params=pltpu.CompilerParams(vmem_limit_bytes=SMALL),
        cost_estimate=FREE,
        name="finish",
    )(*args)


def add_over_term(value):
    size = lax.axis_size("term")
    if size == 1 or not power_of_two(size):
        return lax.psum(value, "term"), jnp.zeros_like(value)
    bit = 1
    while 2 * bit < size:
        value = value + flip(value, "term", bit)
        bit *= 2
    return value, flip(value, "term", bit)


def after(*values):
    return lax.optimization_barrier(values)


def shards(amplitudes, left, right, term_kind, partner, left_diag, right_diag):
    devices, terms_over = lax.axis_size("blk"), lax.axis_size("term")
    slots, rows, roots, width = amplitudes.shape
    per = slots // devices
    elements = slots * devices * rows * lax.axis_size("sub") * width
    vector = jnp.transpose(amplitudes, (0, 2, 1, 3)).reshape(slots * roots * rows, width)
    table = make_table(partner, term_kind, vector)
    diag = left_diag[:, :, None] + right_diag[:, None, :]

    cuts = [(0, per // 2), (per // 2, per - per // 2)] if per > 1 else [(0, per)]
    offsets = sorted(range(1, devices), key=lambda c: (-min(c, devices - c), c))
    moving = [(c, c * per + start, size) for c in offsets for start, size in cuts]
    staying = [(0, start, size) for start, size in cuts]
    pieces = staying + moving
    ahead_of = len(cuts)
    lasting = len(pieces) - ahead_of
    batches = [moving[:ahead_of], moving[ahead_of:] + staying]

    def spans(pieces):
        return [piece[1:] for piece in pieces]

    def relay(value, c):
        return lax.ppermute(value, "blk", [(p, (p + c) % devices) for p in range(devices)])

    def swap(value):
        return lax.ppermute(value, "sub", [(0, 1), (1, 0)])

    def partials(own, second):
        if second:
            early = (ahead, swap(ahead))
            other = swap(after(own, early[1])[0])
        else:
            other = swap(own)
        kept, outgoing = None, {}
        for batch in batches:
            early_now = second and batch is batches[0]
            pair = early if early_now else (own, other)
            parts, kept = sectors(
                table,
                spans(batch),
                [second and piece[0] > 0 for piece in batch],
                left,
                right,
                *pair,
                kept,
                (batch[0][1] if early_now else 0) if second else None,
                roots,
            )
            outgoing.update(zip(batch, parts))
        arrived, sums, inners = {}, [], []
        for at, piece in enumerate(moving):
            value = outgoing[piece]
            if at >= ahead_of:
                value = after(value, arrived[moving[at - ahead_of]])[0]
            arrived[piece] = relay(value, piece[0])
        for piece in pieces:
            mine, inner = combine(
                table,
                piece[1:],
                kept,
                arrived[piece] if piece[0] else outgoing[piece],
                own,
                diag,
                1.0 / terms_over,
                second,
                not second,
            )
            if len(sums) >= 2 * ahead_of:
                mine = after(mine, sums[1 - 2 * ahead_of])[0]
            sums += add_over_term(mine)
            inners.append(inner)
        return sums, inners, arrived, other

    sums, inners, _, _ = partials(vector, False)
    inner = small_sum(small_sum(sum(inners[1:], inners[0]), "sub"), "blk")
    inner = small_sum(after(inner, sums[-1])[0], "term")
    first = (batches[0][0][1], sum(size for _, _, size in batches[0]))
    raw, ahead = correct(
        table, [[piece[1:]] for piece in pieces], first, inner, vector, diag, sums
    )

    sums, _, arrived, other = partials(raw, True)
    squares = raw[-TAG:] + other[-TAG:]
    for piece in moving[::ahead_of]:
        squares = squares + arrived[piece][-TAG:]
    scale = lax.rsqrt(jnp.sum(squares, axis=1, keepdims=True) / elements + 1e-06)
    scale = jnp.broadcast_to(scale, squares.shape)
    correction = scaled(table, scale, raw, slots, rows)
    sigma = None
    for some in (slice(0, lasting), slice(lasting, None)):
        parts = [one for pair in list(zip(sums[::2], sums[1::2]))[some] for one in pair]
        if parts:
            sigma = finish(table, spans(pieces[some]), scale, parts, sigma, slots, rows)
    return tuple(
        jnp.transpose(value.reshape(slots, roots, rows, width), (0, 2, 1, 3))
        for value in (sigma, correction)
    )


def solution(mesh):
    return jax.shard_map(
        shards,
        mesh=mesh,
        in_specs=(
            P(("grp", "blk"), "sub", None, None),
            P(("grp", "term"), "blk", "sub", None),
            P(("grp", "term"), "blk", None, None),
            P(("grp", "term")),
            P(("grp", "blk")),
            P(("grp", "blk"), "sub"),
            P(("grp", "blk"), None),
        ),
        out_specs=(P(("grp", "blk"), "sub", None, None), P(("grp", "blk"), "sub", None, None)),
        check_vma=False,
    )
```

```python
import functools

import jax
import jax.numpy as jnp
from jax import lax
from jax.experimental import pallas as pl
from jax.experimental.pallas import tpu as pltpu
from jax.sharding import PartitionSpec as P

TAG = 8
LIMIT = 48 * 1024 * 1024
SMALL = 24 * 1024 * 1024
FREE = pl.CostEstimate(flops=0, bytes_accessed=0, transcendentals=0)
WHOLE = pl.BlockSpec(memory_space=pltpu.VMEM)
SCALARS = pl.BlockSpec(memory_space=pltpu.SMEM)
ANY = pl.BlockSpec(memory_space=pl.ANY)


def power_of_two(size):
    return size & (size - 1) == 0


def flip(value, axis, bit):
    size = lax.axis_size(axis)
    return lax.ppermute(value, axis, [(i, i ^ bit) for i in range(size)])


def small_sum(value, axis):
    size = lax.axis_size(axis)
    if not power_of_two(size):
        return lax.psum(value, axis)
    if size == 4:
        one, two, three = (flip(value, axis, bit) for bit in (1, 2, 3))
        return (value + one) + (two + three)
    bit = 1
    while bit < size:
        value = value + flip(value, axis, bit)
        bit *= 2
    return value


def halves(value):
    high = value.astype(jnp.bfloat16)
    low = (value - high.astype(jnp.float32)).astype(jnp.bfloat16)
    return high, low


def table_kernel(devices, count, terms, given_hbm, _, table_ref, used, given_ref, sem):
    copy = pltpu.make_async_copy(given_hbm, given_ref, sem)
    copy.start()
    copy.wait()
    per = count // devices
    me = lax.axis_index("blk")
    for c in range(devices):
        used[c] = 0

    def place(j, carry):
        where_to = given_ref[j]
        owner = lax.div(where_to, count)
        offset = lax.rem(owner - me + devices, devices)
        at = offset * per + used[offset]
        used[offset] = used[offset] + 1
        table_ref[at] = j
        table_ref[count + at] = where_to - owner * count
        table_ref[2 * count + j] = at
        return carry

    lax.fori_loop(0, count, place, 0)
    for k in range(terms):
        table_ref[3 * count + k] = given_ref[count + k]
    table_ref[3 * count + terms] = lax.axis_index("sub")


def make_table(partner, term_kind, vector):
    devices = lax.axis_size("blk")
    count, terms = partner.shape[0], term_kind.shape[0]
    given = jnp.concatenate([partner, term_kind])
    return pl.pallas_call(
        functools.partial(table_kernel, devices, count, terms),
        out_shape=jax.ShapeDtypeStruct((3 * count + terms + 1,), jnp.int32),
        in_specs=[ANY, WHOLE],
        out_specs=SCALARS,
        scratch_shapes=[
            pltpu.SMEM((devices,), jnp.int32),
            pltpu.SMEM(given.shape, jnp.int32),
            pltpu.SemaphoreType.DMA,
        ],
        compiler_params=pltpu.CompilerParams(vmem_limit_bytes=SMALL),
        name="table",
    )(given, vector)


def sector(table, count, terms, height, held, own_ref, other_ref, l_ref, r_ref, lhs, high_rhs, low_rhs):
    rows, width = l_ref.shape[2], r_ref.shape[3]
    roots = height // rows
    first = table[3 * count + terms] == 0
    own, other = own_ref[held], other_ref[held]
    top = jnp.where(first, own, other)
    bottom = jnp.where(first, other, own)
    left = l_ref[:, 0].reshape(terms * rows, 2 * rows)
    left = jnp.concatenate(halves(left), axis=1)
    for r in range(roots):
        at = slice(r * rows, (r + 1) * rows)
        wide = jnp.concatenate(halves(jnp.concatenate([top[at], bottom[at]], axis=0)), axis=1)
        both = jnp.dot(
            left, jnp.concatenate([wide, wide], axis=0), preferred_element_type=jnp.float32
        )
        high, low = halves(both[:, :width] + both[:, width:])
        for k in range(terms):
            lanes = slice(k * width, (k + 1) * width)
            part = slice(k * rows, (k + 1) * rows)
            lhs[r * rows : (r + 1) * rows, lanes] = high[part]
            lhs[(roots + r) * rows : (roots + r + 1) * rows, lanes] = low[part]
    for k in range(terms):
        lanes = slice(k * width, (k + 1) * width)
        kind = table[3 * count + k]
        used = pl.ds(pl.multiple_of((1 - kind) * width, width), width)
        high, low = halves(r_ref[k, 0].T)
        high_rhs[lanes, used] = high
        low_rhs[lanes, used] = low
    high, low = lhs[:height], lhs[height:]
    return jnp.dot(
        jnp.concatenate([high, low, high], axis=1),
        jnp.concatenate([high_rhs[...], high_rhs[...], low_rhs[...]], axis=0),
        preferred_element_type=jnp.float32,
    )


def sector_kernel(count, terms, unroll, height, pieces, origin, starts, tags, table, own_ref, other_ref, *refs):
    inputs, scratch = refs[: 2 * unroll], refs[-3 * unroll :]
    outputs = refs[-3 * unroll - len(starts) : -3 * unroll]
    moved_refs, kept_ref = outputs[:-1], outputs[-1]
    width = kept_ref.shape[1]
    step = pl.program_id(0)

    def sector_at(at):
        return pl.ds(pl.multiple_of(at * height, height), height)

    @pl.when(step == 0)
    def _():
        for k in range(terms):
            kind = table[3 * count + k]
            unused = pl.ds(pl.multiple_of(kind * width, width), width)
            for at, ref in enumerate(scratch):
                if at % 3:
                    ref[k * width : (k + 1) * width, unused] = jnp.zeros((width, width), ref.dtype)
        if any(tags):
            tag = own_ref[own_ref.shape[0] - TAG :] + other_ref[other_ref.shape[0] - TAG :]
            for ref, begin, end, tagged in zip(moved_refs, starts, starts[1:], tags):
                if tagged:
                    ref[(end - begin) * height :] = tag

    places = [place_of(step * unroll + u, pieces) for u in range(unroll)]
    results = [
        sector(
            table,
            count,
            terms,
            height,
            sector_at(table[place] if origin is None else place - origin),
            own_ref,
            other_ref,
            *inputs[2 * u : 2 * u + 2],
            *scratch[3 * u : 3 * u + 3],
        )
        for u, place in enumerate(places)
    ]
    for u, place in enumerate(places):
        kept_ref[sector_at(place)] = results[u][:, width:]
    for ref, begin, end in zip(moved_refs, starts, starts[1:]):
        for u in range(unroll):
            at = step * unroll + u - begin

            @pl.when((at >= 0) & (at < end - begin))
            def _(ref=ref, u=u, at=at):
                ref[sector_at(at)] = results[u][:, :width]


def place_of(i, pieces):
    at, begin = pieces[0][0] + i, 0
    for (_, size), (base, _) in zip(pieces, pieces[1:]):
        begin += size
        at = jnp.where(i >= begin, base + i - begin, at)
    return at


def sectors(table, pieces, tags, left, right, own, other, kept, origin, roots):
    terms, count, rows, width = left.shape
    height = roots * rows
    starts = [0]
    for _, size in pieces:
        starts.append(starts[-1] + size)
    places = [base + i for base, size in pieces for i in range(size)]

    unroll = 2 if len(places) % 2 == 0 else 1

    def specs(u):
        def source(i, table):
            return table[place_of(unroll * i + u, pieces)]

        return [
            pl.BlockSpec((terms, 1, rows, width), lambda i, t: (0, source(i, t), 0, 0)),
            pl.BlockSpec((terms, 1, width, width), lambda i, t: (0, source(i, t), 0, 0)),
        ]

    in_specs = [WHOLE, WHOLE] + [spec for u in range(unroll) for spec in specs(u)]
    args = [own, other] + [left, right] * unroll
    aliases = {}
    if kept is not None:
        in_specs.append(WHOLE)
        args.append(kept)
        aliases = {len(args): len(pieces)}
    deep = terms * width
    shapes = [(size * height + TAG * tagged, width) for (_, size), tagged in zip(pieces, tags)]
    out = pl.pallas_call(
        functools.partial(
            sector_kernel, count, terms, unroll, height, pieces, origin, starts, tags
        ),
        out_shape=[
            jax.ShapeDtypeStruct(shape, jnp.float32)
            for shape in shapes + [(count * height, width)]
        ],
        grid_spec=pltpu.PrefetchScalarGridSpec(
            num_scalar_prefetch=1,
            grid=(starts[-1] // unroll,),
            in_specs=in_specs,
            out_specs=[WHOLE] * (len(shapes) + 1),
            scratch_shapes=[
                pltpu.VMEM((2 * height, deep), jnp.bfloat16),
                pltpu.VMEM((deep, 2 * width), jnp.bfloat16),
                pltpu.VMEM((deep, 2 * width), jnp.bfloat16),
            ]
            * unroll,
        ),
        input_output_aliases=aliases,
        compiler_params=pltpu.CompilerParams(vmem_limit_bytes=LIMIT),
        cost_estimate=FREE,
        name="sectors",
    )(table, *args)
    return out[:-1], out[-1]


def combine_kernel(share, piece, ordered, with_inner, table, kept_ref, arrived_ref, vector_ref, diag_ref, sum_ref, *refs):
    count, rows, width = diag_ref.shape
    height = kept_ref.shape[0] // count
    roots = height // rows
    base, size = piece
    inner = [jnp.zeros((1, width), jnp.float32) for _ in range(2 * roots)]
    for i in range(size):
        slot = table[count + base + i]
        place = table[2 * count + slot]
        held = place if ordered else slot
        diag = share * diag_ref[slot]
        for r in range(roots):

            def at(sector):
                return pl.ds(pl.multiple_of(sector * height + r * rows, rows), rows)

            here = slice(i * height + r * rows, i * height + (r + 1) * rows)
            vector = vector_ref[at(held)]
            total = kept_ref[at(place)] + arrived_ref[here] + diag * vector
            sum_ref[here] = total
            if with_inner:
                inner[r] = inner[r] + jnp.sum(vector * total, axis=0, keepdims=True)
                inner[roots + r] = inner[roots + r] + share * jnp.sum(
                    vector * vector, axis=0, keepdims=True
                )
    if with_inner:
        rest = jnp.zeros((TAG - 2 * roots, width), jnp.float32)
        refs[0][...] = jnp.concatenate(inner + [rest], axis=0)


def combine(table, piece, kept, arrived, vector, diag, share, ordered, with_inner):
    height, width = kept.shape[0] // diag.shape[0], kept.shape[1]
    out_shape = [jax.ShapeDtypeStruct((piece[1] * height, width), jnp.float32)]
    if with_inner:
        out_shape.append(jax.ShapeDtypeStruct((TAG, width), jnp.float32))
    out = pl.pallas_call(
        functools.partial(combine_kernel, share, piece, ordered, with_inner),
        out_shape=out_shape,
        in_specs=[SCALARS] + [WHOLE] * 4,
        out_specs=[WHOLE] * len(out_shape),
        compiler_params=pltpu.CompilerParams(vmem_limit_bytes=SMALL),
        cost_estimate=FREE,
        name="combine",
    )(table, kept, arrived, vector, diag)
    return out if with_inner else (out[0], None)


def correct_kernel(groups, ahead, table, inner_ref, vector_ref, diag_ref, *rest):
    parts, (raw_ref, ahead_ref) = rest[:-2], rest[-2:]
    count, rows, width = diag_ref.shape
    height = vector_ref.shape[0] // count
    roots = height // rows
    inner = jnp.sum(inner_ref[...], axis=1, keepdims=True)
    theta = inner[:roots] / inner[roots : 2 * roots]
    squares = [jnp.zeros((1, width), jnp.float32) for _ in range(roots)]
    for at, pieces in enumerate(groups):
        mine, theirs = parts[2 * at], parts[2 * at + 1]
        row = 0
        for base, size in pieces:
            for i in range(size):
                slot = table[count + base + i]
                held = slot * height
                place = table[2 * count + slot] * height
                diag = diag_ref[slot]
                for r in range(roots):
                    shift = theta[r : r + 1]
                    sigma = mine[row : row + rows] + theirs[row : row + rows]
                    vector = vector_ref[pl.ds(pl.multiple_of(held + r * rows, rows), rows)]
                    raw = (sigma - shift * vector) / jnp.maximum(jnp.abs(diag - shift), 1.0)
                    raw_ref[pl.ds(pl.multiple_of(place + r * rows, rows), rows)] = raw
                    squares[r] = squares[r] + jnp.sum(raw * raw, axis=0, keepdims=True)
                    row += rows
    raw_ref[count * height :] = jnp.concatenate(
        squares + [jnp.zeros((TAG - roots, width), jnp.float32)], axis=0
    )
    ahead_ref[: ahead[1] * height] = raw_ref[ahead[0] * height : (ahead[0] + ahead[1]) * height]
    ahead_ref[ahead[1] * height :] = raw_ref[count * height :]


def correct(table, groups, ahead, inner, vector, diag, parts):
    height, width = vector.shape[0] // diag.shape[0], vector.shape[1]
    return pl.pallas_call(
        functools.partial(correct_kernel, groups, ahead),
        out_shape=[
            jax.ShapeDtypeStruct((vector.shape[0] + TAG, width), jnp.float32),
            jax.ShapeDtypeStruct((ahead[1] * height + TAG, width), jnp.float32),
        ],
        in_specs=[SCALARS] + [WHOLE] * (3 + len(parts)),
        out_specs=[WHOLE, WHOLE],
        compiler_params=pltpu.CompilerParams(vmem_limit_bytes=SMALL),
        cost_estimate=FREE,
        name="correct",
    )(table, inner, vector, diag, *parts)


def scatter(held, out_ref, sems, rows_of):
    height = held.shape[0] // len(rows_of)
    copies = []
    for i, make in enumerate(rows_of):
        at = slice(i * height, (i + 1) * height)
        row = make(at)
        copies.append(
            pltpu.make_async_copy(
                held.at[at], out_ref.at[pl.ds(pl.multiple_of(row, height), height)], sems.at[i]
            )
        )
        copies[-1].start()
    for copy in copies:
        copy.wait()


def scaled_kernel(count, rows, table, scale_ref, raw_ref, out_ref, held, sems):
    height = held.shape[0] // count

    def make(i, at):
        place = pl.multiple_of(table[2 * count + i] * height, height)
        for r in range(height // rows):
            part = raw_ref[pl.ds(place + r * rows, rows)]
            held[at.start + r * rows : at.start + (r + 1) * rows] = part * scale_ref[r : r + 1]
        return i * height

    scatter(held, out_ref, sems, [functools.partial(make, i) for i in range(count)])


def scaled(table, scale, raw, count, rows):
    height, width = raw.shape[0] // count // rows * rows, raw.shape[1]
    return pl.pallas_call(
        functools.partial(scaled_kernel, count, rows),
        out_shape=jax.ShapeDtypeStruct((count * height, width), jnp.float32),
        in_specs=[SCALARS, WHOLE, WHOLE],
        out_specs=ANY,
        scratch_shapes=[
            pltpu.VMEM((count * height, width), jnp.float32),
            pltpu.SemaphoreType.DMA((count,)),
        ],
        compiler_params=pltpu.CompilerParams(vmem_limit_bytes=SMALL),
        cost_estimate=FREE,
        name="scaled",
    )(table, scale, raw)


def finish_kernel(count, rows, sizes, places, table, scale_ref, *refs):
    parts, (out_ref, held, sems) = refs[: 2 * len(sizes)], refs[-3:]
    height = held.shape[0] // len(places)
    sources = [(part, i) for part, size in enumerate(sizes) for i in range(size)]

    def make(source, place, at):
        part, i = source
        mine, theirs = parts[2 * part], parts[2 * part + 1]
        for r in range(height // rows):
            row = i * height + r * rows
            total = mine[row : row + rows] + theirs[row : row + rows]
            held[at.start + r * rows : at.start + (r + 1) * rows] = total * scale_ref[r : r + 1]
        return table[count + place] * height

    scatter(held, out_ref, sems, [functools.partial(make, *one) for one in zip(sources, places)])


def finish(table, spans, scale, parts, out, count, rows):
    places = [base + i for base, size in spans for i in range(size)]
    height, width = parts[0].shape[0] // spans[0][1], parts[0].shape[1]
    in_specs = [SCALARS] + [WHOLE] * (1 + len(parts))
    args, aliases = [table, scale, *parts], {}
    if out is not None:
        in_specs.append(ANY)
        aliases = {len(args): 0}
        args.append(out)
    return pl.pallas_call(
        functools.partial(finish_kernel, count, rows, [size for _, size in spans], places),
        out_shape=jax.ShapeDtypeStruct((count * height, width), jnp.float32),
        in_specs=in_specs,
        out_specs=ANY,
        scratch_shapes=[
            pltpu.VMEM((len(places) * height, width), jnp.float32),
            pltpu.SemaphoreType.DMA((len(places),)),
        ],
        input_output_aliases=aliases,
        compiler_params=pltpu.CompilerParams(vmem_limit_bytes=SMALL),
        cost_estimate=FREE,
        name="finish",
    )(*args)


def add_over_term(value):
    size = lax.axis_size("term")
    if size == 1 or not power_of_two(size):
        return lax.psum(value, "term"), jnp.zeros_like(value)
    bit = 1
    while 2 * bit < size:
        value = value + flip(value, "term", bit)
        bit *= 2
    return value, flip(value, "term", bit)


def after(*values):
    return lax.optimization_barrier(values)


def shards(amplitudes, left, right, term_kind, partner, left_diag, right_diag):
    devices, terms_over = lax.axis_size("blk"), lax.axis_size("term")
    slots, rows, roots, width = amplitudes.shape
    per = slots // devices
    elements = slots * devices * rows * lax.axis_size("sub") * width
    vector = jnp.transpose(amplitudes, (0, 2, 1, 3)).reshape(slots * roots * rows, width)
    table = make_table(partner, term_kind, vector)
    diag = left_diag[:, :, None] + right_diag[:, None, :]

    cuts = [(0, per // 2), (per // 2, per - per // 2)] if per > 1 else [(0, per)]
    offsets = sorted(range(1, devices), key=lambda c: (-min(c, devices - c), c))
    moving = [(c, c * per + start, size) for c in offsets for start, size in cuts]
    staying = [(0, start, size) for start, size in cuts]
    pieces = staying + moving
    ahead_of = len(cuts)
    lasting = len(pieces) - ahead_of
    batches = [moving[:ahead_of], moving[ahead_of:] + staying]

    def spans(pieces):
        return [piece[1:] for piece in pieces]

    def relay(value, c):
        return lax.ppermute(value, "blk", [(p, (p + c) % devices) for p in range(devices)])

    def swap(value):
        return lax.ppermute(value, "sub", [(0, 1), (1, 0)])

    def partials(own, second):
        if second:
            early = (ahead, swap(ahead))
            other = swap(after(own, early[1])[0])
        else:
            other = swap(own)
        kept, outgoing = None, {}
        for batch in batches:
            early_now = second and batch is batches[0]
            pair = early if early_now else (own, other)
            parts, kept = sectors(
                table,
                spans(batch),
                [second and piece[0] > 0 for piece in batch],
                left,
                right,
                *pair,
                kept,
                (batch[0][1] if early_now else 0) if second else None,
                roots,
            )
            outgoing.update(zip(batch, parts))
        arrived, sums, inners = {}, [], []
        for at, piece in enumerate(moving):
            value = outgoing[piece]
            if at >= ahead_of:
                value = after(value, arrived[moving[at - ahead_of]])[0]
            arrived[piece] = relay(value, piece[0])
        for piece in pieces:
            mine, inner = combine(
                table,
                piece[1:],
                kept,
                arrived[piece] if piece[0] else outgoing[piece],
                own,
                diag,
                1.0 / terms_over,
                second,
                not second,
            )
            if len(sums) >= 2 * ahead_of:
                mine = after(mine, sums[1 - 2 * ahead_of])[0]
            sums += add_over_term(mine)
            inners.append(inner)
        return sums, inners, arrived, other

    sums, inners, _, _ = partials(vector, False)
    inner = small_sum(small_sum(sum(inners[1:], inners[0]), "sub"), "blk")
    inner = small_sum(after(inner, sums[-1])[0], "term")
    first = (batches[0][0][1], sum(size for _, _, size in batches[0]))
    raw, ahead = correct(
        table, [[piece[1:]] for piece in pieces], first, inner, vector, diag, sums
    )

    sums, _, arrived, other = partials(raw, True)
    squares = raw[-TAG:] + other[-TAG:]
    for piece in moving[::ahead_of]:
        squares = squares + arrived[piece][-TAG:]
    scale = lax.rsqrt(jnp.sum(squares, axis=1, keepdims=True) / elements + 1e-06)
    scale = jnp.broadcast_to(scale, squares.shape)
    correction = scaled(table, scale, raw, slots, rows)
    sigma = None
    for some in (slice(0, lasting), slice(lasting, None)):
        parts = [one for pair in list(zip(sums[::2], sums[1::2]))[some] for one in pair]
        if parts:
            sigma = finish(table, spans(pieces[some]), scale, parts, sigma, slots, rows)
    return tuple(
        jnp.transpose(value.reshape(slots, roots, rows, width), (0, 2, 1, 3))
        for value in (sigma, correction)
    )


def solution(mesh):
    return jax.shard_map(
        shards,
        mesh=mesh,
        in_specs=(
            P(("grp", "blk"), "sub", None, None),
            P(("grp", "term"), "blk", "sub", None),
            P(("grp", "term"), "blk", None, None),
            P(("grp", "term")),
            P(("grp", "blk")),
            P(("grp", "blk"), "sub"),
            P(("grp", "blk"), None),
        ),
        out_specs=(P(("grp", "blk"), "sub", None, None), P(("grp", "blk"), "sub", None, None)),
        check_vma=False,
    )
```

```python
import functools

import jax
import jax.numpy as jnp
from jax import lax
from jax.experimental import pallas as pl
from jax.experimental.pallas import tpu as pltpu
from jax.sharding import PartitionSpec as P

TAG = 8
LIMIT = 48 * 1024 * 1024
SMALL = 24 * 1024 * 1024
FREE = pl.CostEstimate(flops=0, bytes_accessed=0, transcendentals=0)
WHOLE = pl.BlockSpec(memory_space=pltpu.VMEM)
SCALARS = pl.BlockSpec(memory_space=pltpu.SMEM)
ANY = pl.BlockSpec(memory_space=pl.ANY)


def power_of_two(size):
    return size & (size - 1) == 0


def flip(value, axis, bit):
    size = lax.axis_size(axis)
    return lax.ppermute(value, axis, [(i, i ^ bit) for i in range(size)])


def small_sum(value, axis):
    size = lax.axis_size(axis)
    if not power_of_two(size):
        return lax.psum(value, axis)
    if size == 4:
        one, two, three = (flip(value, axis, bit) for bit in (1, 2, 3))
        return (value + one) + (two + three)
    bit = 1
    while bit < size:
        value = value + flip(value, axis, bit)
        bit *= 2
    return value


def halves(value):
    high = value.astype(jnp.bfloat16)
    low = (value - high.astype(jnp.float32)).astype(jnp.bfloat16)
    return high, low


def table_kernel(devices, count, terms, given_hbm, _, table_ref, used, given_ref, sem):
    copy = pltpu.make_async_copy(given_hbm, given_ref, sem)
    copy.start()
    copy.wait()
    per = count // devices
    me = lax.axis_index("blk")
    for c in range(devices):
        used[c] = 0

    def place(j, carry):
        where_to = given_ref[j]
        owner = lax.div(where_to, count)
        offset = lax.rem(owner - me + devices, devices)
        at = offset * per + used[offset]
        used[offset] = used[offset] + 1
        table_ref[at] = j
        table_ref[count + at] = where_to - owner * count
        table_ref[2 * count + j] = at
        return carry

    lax.fori_loop(0, count, place, 0)
    for k in range(terms):
        table_ref[3 * count + k] = given_ref[count + k]
    table_ref[3 * count + terms] = lax.axis_index("sub")
    order = 3 * count + terms + 1
    far = devices // 2 * per
    for at in range(count):
        used[at] = 0
    for i in range(per):
        table_ref[order + i] = far + i
        used[far + i] = 1
    done = per
    if devices > 1:
        for i in range(per):
            table_ref[order + per + i] = i
            used[i] = 1
        done = 2 * per
    done = jnp.int32(done)

    def add(at, done):
        new = 1 - used[at]

        @pl.when(new == 1)
        def _():
            table_ref[order + done] = at

        used[at] = 1
        return done + new

    done = lax.fori_loop(
        0, per, lambda i, done: add(table_ref[2 * count + table_ref[count + i]], done), done
    )
    lax.fori_loop(0, count, add, done)


def make_table(partner, term_kind, vector):
    devices = lax.axis_size("blk")
    count, terms = partner.shape[0], term_kind.shape[0]
    given = jnp.concatenate([partner, term_kind])
    return pl.pallas_call(
        functools.partial(table_kernel, devices, count, terms),
        out_shape=jax.ShapeDtypeStruct((4 * count + terms + 1,), jnp.int32),
        in_specs=[ANY, WHOLE],
        out_specs=SCALARS,
        scratch_shapes=[
            pltpu.SMEM((max(devices, count),), jnp.int32),
            pltpu.SMEM(given.shape, jnp.int32),
            pltpu.SemaphoreType.DMA,
        ],
        compiler_params=pltpu.CompilerParams(vmem_limit_bytes=SMALL),
        name="table",
    )(given, vector)


def sector(table, count, terms, height, held, own_ref, other_ref, l_ref, r_ref, lhs, high_rhs, low_rhs):
    rows, width = l_ref.shape[2], r_ref.shape[3]
    roots = height // rows
    first = table[3 * count + terms] == 0
    own, other = own_ref[held], other_ref[held]
    top = jnp.where(first, own, other)
    bottom = jnp.where(first, other, own)
    left = l_ref[:, 0].reshape(terms * rows, 2 * rows)
    left = jnp.concatenate(halves(left), axis=1)
    for r in range(roots):
        at = slice(r * rows, (r + 1) * rows)
        wide = jnp.concatenate(halves(jnp.concatenate([top[at], bottom[at]], axis=0)), axis=1)
        both = jnp.dot(
            left, jnp.concatenate([wide, wide], axis=0), preferred_element_type=jnp.float32
        )
        high, low = halves(both[:, :width] + both[:, width:])
        for k in range(terms):
            lanes = slice(k * width, (k + 1) * width)
            part = slice(k * rows, (k + 1) * rows)
            lhs[r * rows : (r + 1) * rows, lanes] = high[part]
            lhs[(roots + r) * rows : (roots + r + 1) * rows, lanes] = low[part]
    for k in range(terms):
        lanes = slice(k * width, (k + 1) * width)
        kind = table[3 * count + k]
        used = pl.ds(pl.multiple_of((1 - kind) * width, width), width)
        high, low = halves(r_ref[k, 0].T)
        high_rhs[lanes, used] = high
        low_rhs[lanes, used] = low
    high, low = lhs[:height], lhs[height:]
    return jnp.dot(
        jnp.concatenate([high, low, high], axis=1),
        jnp.concatenate([high_rhs[...], high_rhs[...], low_rhs[...]], axis=0),
        preferred_element_type=jnp.float32,
    )


def sector_kernel(count, terms, unroll, height, begin, pieces, origin, tags, table, own_ref, other_ref, *refs):
    inputs, scratch = refs[: 2 * unroll], refs[-3 * unroll :]
    outputs = refs[-3 * unroll - len(pieces) - 1 : -3 * unroll]
    moved_refs, kept_ref = outputs[:-1], outputs[-1]
    width = kept_ref.shape[1]
    step = pl.program_id(0)

    def sector_at(at):
        return pl.ds(pl.multiple_of(at * height, height), height)

    @pl.when(step == 0)
    def _():
        for k in range(terms):
            kind = table[3 * count + k]
            unused = pl.ds(pl.multiple_of(kind * width, width), width)
            for at, ref in enumerate(scratch):
                if at % 3:
                    ref[k * width : (k + 1) * width, unused] = jnp.zeros((width, width), ref.dtype)
        if any(tags):
            tag = own_ref[own_ref.shape[0] - TAG :] + other_ref[other_ref.shape[0] - TAG :]
            for ref, (_, size), tagged in zip(moved_refs, pieces, tags):
                if tagged:
                    ref[size * height :] = tag

    places = [table[3 * count + terms + 1 + begin + step * unroll + u] for u in range(unroll)]
    results = [
        sector(
            table,
            count,
            terms,
            height,
            sector_at(table[place] if origin is None else place - origin),
            own_ref,
            other_ref,
            *inputs[2 * u : 2 * u + 2],
            *scratch[3 * u : 3 * u + 3],
        )
        for u, place in enumerate(places)
    ]
    for u, place in enumerate(places):
        kept_ref[sector_at(place)] = results[u][:, width:]
    for ref, (base, size) in zip(moved_refs, pieces):
        for u, place in enumerate(places):

            @pl.when((place >= base) & (place < base + size))
            def _(ref=ref, u=u, at=place - base):
                ref[sector_at(at)] = results[u][:, :width]


def sectors(table, begin, size, pieces, tags, moved, kept, left, right, own, other, origin, roots):
    terms, count, rows, width = left.shape
    height = roots * rows
    unroll = 2 if size % 2 == 0 else 1
    first = 3 * count + terms + 1 + begin

    def specs(u):
        def source(i, table):
            return table[table[first + unroll * i + u]]

        return [
            pl.BlockSpec((terms, 1, rows, width), lambda i, t: (0, source(i, t), 0, 0)),
            pl.BlockSpec((terms, 1, width, width), lambda i, t: (0, source(i, t), 0, 0)),
        ]

    in_specs = [WHOLE, WHOLE] + [spec for u in range(unroll) for spec in specs(u)]
    args = [own, other] + [left, right] * unroll
    aliases = {}
    for at, earlier in enumerate(moved + [kept]):
        if earlier is not None:
            in_specs.append(WHOLE)
            args.append(earlier)
            aliases[len(args)] = at
    deep = terms * width
    shapes = [(size * height + TAG * tagged, width) for (_, size), tagged in zip(pieces, tags)]
    out = pl.pallas_call(
        functools.partial(
            sector_kernel,
            count,
            terms,
            unroll,
            height,
            begin,
            pieces,
            origin,
            [tagged and earlier is None for tagged, earlier in zip(tags, moved)],
        ),
        out_shape=[
            jax.ShapeDtypeStruct(shape, jnp.float32)
            for shape in shapes + [(count * height, width)]
        ],
        grid_spec=pltpu.PrefetchScalarGridSpec(
            num_scalar_prefetch=1,
            grid=(size // unroll,),
            in_specs=in_specs,
            out_specs=[WHOLE] * (len(shapes) + 1),
            scratch_shapes=[
                pltpu.VMEM((2 * height, deep), jnp.bfloat16),
                pltpu.VMEM((deep, 2 * width), jnp.bfloat16),
                pltpu.VMEM((deep, 2 * width), jnp.bfloat16),
            ]
            * unroll,
        ),
        input_output_aliases=aliases,
        compiler_params=pltpu.CompilerParams(vmem_limit_bytes=LIMIT),
        cost_estimate=FREE,
        name="sectors",
    )(table, *args)
    return out[:-1], out[-1]


def combine_kernel(share, piece, ordered, with_inner, table, kept_ref, arrived_ref, vector_ref, diag_ref, sum_ref, *refs):
    count, rows, width = diag_ref.shape
    height = kept_ref.shape[0] // count
    roots = height // rows
    base, size = piece
    inner = [jnp.zeros((1, width), jnp.float32) for _ in range(2 * roots)]
    for i in range(size):
        slot = table[count + base + i]
        place = table[2 * count + slot]
        held = place if ordered else slot
        diag = share * diag_ref[slot]
        for r in range(roots):

            def at(sector):
                return pl.ds(pl.multiple_of(sector * height + r * rows, rows), rows)

            here = slice(i * height + r * rows, i * height + (r + 1) * rows)
            vector = vector_ref[at(held)]
            total = kept_ref[at(place)] + arrived_ref[here] + diag * vector
            sum_ref[here] = total
            if with_inner:
                inner[r] = inner[r] + jnp.sum(vector * total, axis=0, keepdims=True)
                inner[roots + r] = inner[roots + r] + share * jnp.sum(
                    vector * vector, axis=0, keepdims=True
                )
    if with_inner:
        rest = jnp.zeros((TAG - 2 * roots, width), jnp.float32)
        refs[0][...] = jnp.concatenate(inner + [rest], axis=0)


def combine(table, piece, kept, arrived, vector, diag, share, ordered, with_inner):
    height, width = kept.shape[0] // diag.shape[0], kept.shape[1]
    out_shape = [jax.ShapeDtypeStruct((piece[1] * height, width), jnp.float32)]
    if with_inner:
        out_shape.append(jax.ShapeDtypeStruct((TAG, width), jnp.float32))
    out = pl.pallas_call(
        functools.partial(combine_kernel, share, piece, ordered, with_inner),
        out_shape=out_shape,
        in_specs=[SCALARS] + [WHOLE] * 4,
        out_specs=[WHOLE] * len(out_shape),
        compiler_params=pltpu.CompilerParams(vmem_limit_bytes=SMALL),
        cost_estimate=FREE,
        name="combine",
    )(table, kept, arrived, vector, diag)
    return out if with_inner else (out[0], None)


def correct_kernel(groups, ahead, table, inner_ref, vector_ref, diag_ref, *rest):
    parts, (raw_ref, ahead_ref) = rest[:-2], rest[-2:]
    count, rows, width = diag_ref.shape
    height = vector_ref.shape[0] // count
    roots = height // rows
    inner = jnp.sum(inner_ref[...], axis=1, keepdims=True)
    theta = inner[:roots] / inner[roots : 2 * roots]
    squares = [jnp.zeros((1, width), jnp.float32) for _ in range(roots)]
    for at, pieces in enumerate(groups):
        mine, theirs = parts[2 * at], parts[2 * at + 1]
        row = 0
        for base, size in pieces:
            for i in range(size):
                slot = table[count + base + i]
                held = slot * height
                place = table[2 * count + slot] * height
                diag = diag_ref[slot]
                for r in range(roots):
                    shift = theta[r : r + 1]
                    sigma = mine[row : row + rows] + theirs[row : row + rows]
                    vector = vector_ref[pl.ds(pl.multiple_of(held + r * rows, rows), rows)]
                    raw = (sigma - shift * vector) / jnp.maximum(jnp.abs(diag - shift), 1.0)
                    raw_ref[pl.ds(pl.multiple_of(place + r * rows, rows), rows)] = raw
                    squares[r] = squares[r] + jnp.sum(raw * raw, axis=0, keepdims=True)
                    row += rows
    raw_ref[count * height :] = jnp.concatenate(
        squares + [jnp.zeros((TAG - roots, width), jnp.float32)], axis=0
    )
    ahead_ref[: ahead[1] * height] = raw_ref[ahead[0] * height : (ahead[0] + ahead[1]) * height]
    ahead_ref[ahead[1] * height :] = raw_ref[count * height :]


def correct(table, groups, ahead, inner, vector, diag, parts):
    height, width = vector.shape[0] // diag.shape[0], vector.shape[1]
    return pl.pallas_call(
        functools.partial(correct_kernel, groups, ahead),
        out_shape=[
            jax.ShapeDtypeStruct((vector.shape[0] + TAG, width), jnp.float32),
            jax.ShapeDtypeStruct((ahead[1] * height + TAG, width), jnp.float32),
        ],
        in_specs=[SCALARS] + [WHOLE] * (3 + len(parts)),
        out_specs=[WHOLE, WHOLE],
        compiler_params=pltpu.CompilerParams(vmem_limit_bytes=SMALL),
        cost_estimate=FREE,
        name="correct",
    )(table, inner, vector, diag, *parts)


def scatter(held, out_ref, sems, rows_of):
    height = held.shape[0] // len(rows_of)
    copies = []
    for i, make in enumerate(rows_of):
        at = slice(i * height, (i + 1) * height)
        row = make(at)
        copies.append(
            pltpu.make_async_copy(
                held.at[at], out_ref.at[pl.ds(pl.multiple_of(row, height), height)], sems.at[i]
            )
        )
        copies[-1].start()
    for copy in copies:
        copy.wait()


def scaled_kernel(count, rows, table, scale_ref, raw_ref, out_ref, held, sems):
    height = held.shape[0] // count

    def make(i, at):
        place = pl.multiple_of(table[2 * count + i] * height, height)
        for r in range(height // rows):
            part = raw_ref[pl.ds(place + r * rows, rows)]
            held[at.start + r * rows : at.start + (r + 1) * rows] = part * scale_ref[r : r + 1]
        return i * height

    scatter(held, out_ref, sems, [functools.partial(make, i) for i in range(count)])


def scaled(table, scale, raw, count, rows):
    height, width = raw.shape[0] // count // rows * rows, raw.shape[1]
    return pl.pallas_call(
        functools.partial(scaled_kernel, count, rows),
        out_shape=jax.ShapeDtypeStruct((count * height, width), jnp.float32),
        in_specs=[SCALARS, WHOLE, WHOLE],
        out_specs=ANY,
        scratch_shapes=[
            pltpu.VMEM((count * height, width), jnp.float32),
            pltpu.SemaphoreType.DMA((count,)),
        ],
        compiler_params=pltpu.CompilerParams(vmem_limit_bytes=SMALL),
        cost_estimate=FREE,
        name="scaled",
    )(table, scale, raw)


def finish_kernel(count, rows, sizes, places, table, scale_ref, *refs):
    parts, (out_ref, held, sems) = refs[: 2 * len(sizes)], refs[-3:]
    height = held.shape[0] // len(places)
    sources = [(part, i) for part, size in enumerate(sizes) for i in range(size)]

    def make(source, place, at):
        part, i = source
        mine, theirs = parts[2 * part], parts[2 * part + 1]
        for r in range(height // rows):
            row = i * height + r * rows
            total = mine[row : row + rows] + theirs[row : row + rows]
            held[at.start + r * rows : at.start + (r + 1) * rows] = total * scale_ref[r : r + 1]
        return table[count + place] * height

    scatter(held, out_ref, sems, [functools.partial(make, *one) for one in zip(sources, places)])


def finish(table, spans, scale, parts, out, count, rows):
    places = [base + i for base, size in spans for i in range(size)]
    height, width = parts[0].shape[0] // spans[0][1], parts[0].shape[1]
    in_specs = [SCALARS] + [WHOLE] * (1 + len(parts))
    args, aliases = [table, scale, *parts], {}
    if out is not None:
        in_specs.append(ANY)
        aliases = {len(args): 0}
        args.append(out)
    return pl.pallas_call(
        functools.partial(finish_kernel, count, rows, [size for _, size in spans], places),
        out_shape=jax.ShapeDtypeStruct((count * height, width), jnp.float32),
        in_specs=in_specs,
        out_specs=ANY,
        scratch_shapes=[
            pltpu.VMEM((len(places) * height, width), jnp.float32),
            pltpu.SemaphoreType.DMA((len(places),)),
        ],
        input_output_aliases=aliases,
        compiler_params=pltpu.CompilerParams(vmem_limit_bytes=SMALL),
        cost_estimate=FREE,
        name="finish",
    )(*args)


def add_over_term(value):
    size = lax.axis_size("term")
    if size == 1 or not power_of_two(size):
        return lax.psum(value, "term"), jnp.zeros_like(value)
    bit = 1
    while 2 * bit < size:
        value = value + flip(value, "term", bit)
        bit *= 2
    return value, flip(value, "term", bit)


def after(*values):
    return lax.optimization_barrier(values)


def shards(amplitudes, left, right, term_kind, partner, left_diag, right_diag):
    devices, terms_over = lax.axis_size("blk"), lax.axis_size("term")
    slots, rows, roots, width = amplitudes.shape
    per = slots // devices
    elements = slots * devices * rows * lax.axis_size("sub") * width
    vector = jnp.transpose(amplitudes, (0, 2, 1, 3)).reshape(slots * roots * rows, width)
    table = make_table(partner, term_kind, vector)
    diag = left_diag[:, :, None] + right_diag[:, None, :]

    cuts = [(0, per // 2), (per // 2, per - per // 2)] if per > 1 else [(0, per)]
    offsets = sorted(range(1, devices), key=lambda c: (-min(c, devices - c), c))
    moving = [(c, c * per + start, size) for c in offsets for start, size in cuts]
    staying = [(0, start, size) for start, size in cuts]
    pieces = staying + moving
    ahead_of = len(cuts)
    lasting = len(pieces) - ahead_of
    far, others = moving[:ahead_of], moving[ahead_of:]
    calls = [(0, per), (per, min(2 * per, slots - per)), (3 * per, slots - 3 * per)]

    def spans(pieces):
        return [piece[1:] for piece in pieces]

    def relay(value, c):
        return lax.ppermute(value, "blk", [(p, (p + c) % devices) for p in range(devices)])

    def swap(value):
        return lax.ppermute(value, "sub", [(0, 1), (1, 0)])

    def partials(own, second):
        if second:
            early = (ahead, swap(ahead))
            other = swap(after(own, early[1])[0])
        else:
            other = swap(own)
        kept, outgoing = None, {}

        def compute(call, some, kept):
            ahead_now = second and call == calls[0]
            parts, kept = sectors(
                table,
                *call,
                spans(some),
                [second and piece[0] > 0 for piece in some],
                [outgoing.get(piece) for piece in some],
                kept,
                left,
                right,
                *(early if ahead_now else (own, other)),
                (far[0][1] if ahead_now else 0) if second else None,
                roots,
            )
            outgoing.update(zip(some, parts))
            return kept

        def add_up(piece, kept):
            return combine(
                table,
                piece[1:],
                kept,
                arrived[piece] if piece[0] else outgoing[piece],
                own,
                diag,
                1.0 / terms_over,
                second,
                not second,
            )

        arrived, sums, inners = {}, [], []
        kept = compute(calls[0], far, kept)
        kept = compute(calls[1], staying + others, kept)
        totals = {piece: add_up(piece, kept) for piece in staying}
        if calls[2][1] > 0:
            kept = after(kept, *[totals[piece][0] for piece in staying])[0]
            kept = compute(calls[2], others, kept)
        for at, piece in enumerate(moving):
            value = outgoing[piece]
            if at >= ahead_of:
                value = after(value, arrived[moving[at - ahead_of]])[0]
            arrived[piece] = relay(value, piece[0])
        for piece in pieces:
            mine, inner = totals[piece] if piece in totals else add_up(piece, kept)
            if len(sums) >= 2 * ahead_of:
                mine = after(mine, sums[1 - 2 * ahead_of])[0]
            sums += add_over_term(mine)
            inners.append(inner)
        return sums, inners, arrived, other

    sums, inners, _, _ = partials(vector, False)
    inner = small_sum(small_sum(sum(inners[1:], inners[0]), "sub"), "blk")
    inner = small_sum(after(inner, sums[-1])[0], "term")
    first = (far[0][1], per)
    raw, ahead = correct(
        table, [[piece[1:]] for piece in pieces], first, inner, vector, diag, sums
    )

    sums, _, arrived, other = partials(raw, True)
    squares = raw[-TAG:] + other[-TAG:]
    for piece in moving[::ahead_of]:
        squares = squares + arrived[piece][-TAG:]
    scale = lax.rsqrt(jnp.sum(squares, axis=1, keepdims=True) / elements + 1e-06)
    scale = jnp.broadcast_to(scale, squares.shape)
    correction = scaled(table, scale, raw, slots, rows)
    sigma = None
    for some in (slice(0, lasting), slice(lasting, None)):
        parts = [one for pair in list(zip(sums[::2], sums[1::2]))[some] for one in pair]
        if parts:
            sigma = finish(table, spans(pieces[some]), scale, parts, sigma, slots, rows)
    return tuple(
        jnp.transpose(value.reshape(slots, roots, rows, width), (0, 2, 1, 3))
        for value in (sigma, correction)
    )


def solution(mesh):
    return jax.shard_map(
        shards,
        mesh=mesh,
        in_specs=(
            P(("grp", "blk"), "sub", None, None),
            P(("grp", "term"), "blk", "sub", None),
            P(("grp", "term"), "blk", None, None),
            P(("grp", "term")),
            P(("grp", "blk")),
            P(("grp", "blk"), "sub"),
            P(("grp", "blk"), None),
        ),
        out_specs=(P(("grp", "blk"), "sub", None, None), P(("grp", "blk"), "sub", None, None)),
        check_vma=False,
    )
```

```python
import functools

import jax
import jax.numpy as jnp
from jax import lax
from jax.experimental import pallas as pl
from jax.experimental.pallas import tpu as pltpu
from jax.sharding import PartitionSpec as P

TAG = 8
LIMIT = 48 * 1024 * 1024
SMALL = 24 * 1024 * 1024
FREE = pl.CostEstimate(flops=0, bytes_accessed=0, transcendentals=0)
WHOLE = pl.BlockSpec(memory_space=pltpu.VMEM)
SCALARS = pl.BlockSpec(memory_space=pltpu.SMEM)
ANY = pl.BlockSpec(memory_space=pl.ANY)


def power_of_two(size):
    return size & (size - 1) == 0


def flip(value, axis, bit):
    size = lax.axis_size(axis)
    return lax.ppermute(value, axis, [(i, i ^ bit) for i in range(size)])


def small_sum(value, axis):
    size = lax.axis_size(axis)
    if not power_of_two(size):
        return lax.psum(value, axis)
    if size == 4:
        one, two, three = (flip(value, axis, bit) for bit in (1, 2, 3))
        return (value + one) + (two + three)
    bit = 1
    while bit < size:
        value = value + flip(value, axis, bit)
        bit *= 2
    return value


def halves(value):
    high = value.astype(jnp.bfloat16)
    low = (value - high.astype(jnp.float32)).astype(jnp.bfloat16)
    return high, low


def table_kernel(devices, count, terms, given_hbm, _, table_ref, used, given_ref, sem):
    copy = pltpu.make_async_copy(given_hbm, given_ref, sem)
    copy.start()
    copy.wait()
    per = count // devices
    me = lax.axis_index("blk")
    for c in range(devices):
        used[c] = 0

    def place(j, carry):
        where_to = given_ref[j]
        owner = lax.div(where_to, count)
        offset = lax.rem(owner - me + devices, devices)
        at = offset * per + used[offset]
        used[offset] = used[offset] + 1
        table_ref[at] = j
        table_ref[count + at] = where_to - owner * count
        table_ref[2 * count + j] = at
        return carry

    lax.fori_loop(0, count, place, 0)
    for k in range(terms):
        table_ref[3 * count + k] = given_ref[count + k]
    table_ref[3 * count + terms] = lax.axis_index("sub")


def make_table(partner, term_kind, vector):
    devices = lax.axis_size("blk")
    count, terms = partner.shape[0], term_kind.shape[0]
    given = jnp.concatenate([partner, term_kind])
    return pl.pallas_call(
        functools.partial(table_kernel, devices, count, terms),
        out_shape=jax.ShapeDtypeStruct((3 * count + terms + 1,), jnp.int32),
        in_specs=[ANY, WHOLE],
        out_specs=SCALARS,
        scratch_shapes=[
            pltpu.SMEM((devices,), jnp.int32),
            pltpu.SMEM(given.shape, jnp.int32),
            pltpu.SemaphoreType.DMA,
        ],
        compiler_params=pltpu.CompilerParams(vmem_limit_bytes=SMALL),
        name="table",
    )(given, vector)


def sector(table, count, terms, height, held, own_ref, other_ref, l_ref, r_ref, lhs, high_rhs, low_rhs):
    rows, width = l_ref.shape[2], r_ref.shape[3]
    roots = height // rows
    first = table[3 * count + terms] == 0
    own, other = own_ref[held], other_ref[held]
    top = jnp.where(first, own, other)
    bottom = jnp.where(first, other, own)
    left = l_ref[:, 0].reshape(terms * rows, 2 * rows)
    left = jnp.concatenate(halves(left), axis=1)
    for r in range(roots):
        at = slice(r * rows, (r + 1) * rows)
        wide = jnp.concatenate(halves(jnp.concatenate([top[at], bottom[at]], axis=0)), axis=1)
        both = jnp.dot(
            left, jnp.concatenate([wide, wide], axis=0), preferred_element_type=jnp.float32
        )
        high, low = halves(both[:, :width] + both[:, width:])
        for k in range(terms):
            lanes = slice(k * width, (k + 1) * width)
            part = slice(k * rows, (k + 1) * rows)
            lhs[r * rows : (r + 1) * rows, lanes] = high[part]
            lhs[(roots + r) * rows : (roots + r + 1) * rows, lanes] = low[part]
    for k in range(terms):
        lanes = slice(k * width, (k + 1) * width)
        kind = table[3 * count + k]
        used = pl.ds(pl.multiple_of((1 - kind) * width, width), width)
        high, low = halves(r_ref[k, 0].T)
        high_rhs[lanes, used] = high
        low_rhs[lanes, used] = low
    high, low = lhs[:height], lhs[height:]
    return jnp.dot(
        jnp.concatenate([high, low, high], axis=1),
        jnp.concatenate([high_rhs[...], high_rhs[...], low_rhs[...]], axis=0),
        preferred_element_type=jnp.float32,
    )


def sector_kernel(count, terms, unroll, height, pieces, origin, starts, tags, table, own_ref, other_ref, *refs):
    inputs, scratch = refs[: 2 * unroll], refs[-3 * unroll :]
    outputs = refs[-3 * unroll - len(starts) : -3 * unroll]
    moved_refs, kept_ref = outputs[:-1], outputs[-1]
    width = kept_ref.shape[1]
    step = pl.program_id(0)

    def sector_at(at):
        return pl.ds(pl.multiple_of(at * height, height), height)

    @pl.when(step == 0)
    def _():
        for k in range(terms):
            kind = table[3 * count + k]
            unused = pl.ds(pl.multiple_of(kind * width, width), width)
            for at, ref in enumerate(scratch):
                if at % 3:
                    ref[k * width : (k + 1) * width, unused] = jnp.zeros((width, width), ref.dtype)
        if any(tags):
            tag = own_ref[own_ref.shape[0] - TAG :] + other_ref[other_ref.shape[0] - TAG :]
            for ref, begin, end, tagged in zip(moved_refs, starts, starts[1:], tags):
                if tagged:
                    ref[(end - begin) * height :] = tag

    places = [place_of(step * unroll + u, pieces) for u in range(unroll)]
    results = [
        sector(
            table,
            count,
            terms,
            height,
            sector_at(table[place] if origin is None else place - origin),
            own_ref,
            other_ref,
            *inputs[2 * u : 2 * u + 2],
            *scratch[3 * u : 3 * u + 3],
        )
        for u, place in enumerate(places)
    ]
    for u, place in enumerate(places):
        kept_ref[sector_at(place)] = results[u][:, width:]
    for ref, begin, end in zip(moved_refs, starts, starts[1:]):
        for u in range(unroll):
            at = step * unroll + u - begin

            @pl.when((at >= 0) & (at < end - begin))
            def _(ref=ref, u=u, at=at):
                ref[sector_at(at)] = results[u][:, :width]


def place_of(i, pieces):
    at, begin = pieces[0][0] + i, 0
    for (_, size), (base, _) in zip(pieces, pieces[1:]):
        begin += size
        at = jnp.where(i >= begin, base + i - begin, at)
    return at


def sectors(table, pieces, tags, left, right, own, other, kept, origin, roots):
    terms, count, rows, width = left.shape
    height = roots * rows
    starts = [0]
    for _, size in pieces:
        starts.append(starts[-1] + size)
    places = [base + i for base, size in pieces for i in range(size)]

    unroll = 2 if len(places) % 2 == 0 else 1

    def specs(u):
        def source(i, table):
            return table[place_of(unroll * i + u, pieces)]

        return [
            pl.BlockSpec((terms, 1, rows, width), lambda i, t: (0, source(i, t), 0, 0)),
            pl.BlockSpec((terms, 1, width, width), lambda i, t: (0, source(i, t), 0, 0)),
        ]

    in_specs = [WHOLE, WHOLE] + [spec for u in range(unroll) for spec in specs(u)]
    args = [own, other] + [left, right] * unroll
    aliases = {}
    if kept is not None:
        in_specs.append(WHOLE)
        args.append(kept)
        aliases = {len(args): len(pieces)}
    deep = terms * width
    shapes = [(size * height + TAG * tagged, width) for (_, size), tagged in zip(pieces, tags)]
    out = pl.pallas_call(
        functools.partial(
            sector_kernel, count, terms, unroll, height, pieces, origin, starts, tags
        ),
        out_shape=[
            jax.ShapeDtypeStruct(shape, jnp.float32)
            for shape in shapes + [(count * height, width)]
        ],
        grid_spec=pltpu.PrefetchScalarGridSpec(
            num_scalar_prefetch=1,
            grid=(starts[-1] // unroll,),
            in_specs=in_specs,
            out_specs=[WHOLE] * (len(shapes) + 1),
            scratch_shapes=[
                pltpu.VMEM((2 * height, deep), jnp.bfloat16),
                pltpu.VMEM((deep, 2 * width), jnp.bfloat16),
                pltpu.VMEM((deep, 2 * width), jnp.bfloat16),
            ]
            * unroll,
        ),
        input_output_aliases=aliases,
        compiler_params=pltpu.CompilerParams(vmem_limit_bytes=LIMIT),
        cost_estimate=FREE,
        name="sectors",
    )(table, *args)
    return out[:-1], out[-1]


def combine_kernel(share, pieces, ordered, with_inner, table, kept_ref, vector_ref, diag_ref, *refs):
    arrived_refs, sum_ref, refs = refs[: len(pieces)], refs[len(pieces)], refs[len(pieces) + 1 :]
    count, rows, width = diag_ref.shape
    height = kept_ref.shape[0] // count
    roots = height // rows
    inner = [jnp.zeros((1, width), jnp.float32) for _ in range(2 * roots)]
    every = [(ref, base + i, i) for ref, (base, size) in zip(arrived_refs, pieces) for i in range(size)]
    for i, (arrived_ref, at_place, of_piece) in enumerate(every):
        slot = table[count + at_place]
        place = table[2 * count + slot]
        held = place if ordered else slot
        diag = share * diag_ref[slot]
        for r in range(roots):

            def at(sector):
                return pl.ds(pl.multiple_of(sector * height + r * rows, rows), rows)

            here = slice(i * height + r * rows, i * height + (r + 1) * rows)
            there = slice(of_piece * height + r * rows, of_piece * height + (r + 1) * rows)
            vector = vector_ref[at(held)]
            total = kept_ref[at(place)] + arrived_ref[there] + diag * vector
            sum_ref[here] = total
            if with_inner:
                inner[r] = inner[r] + jnp.sum(vector * total, axis=0, keepdims=True)
                inner[roots + r] = inner[roots + r] + share * jnp.sum(
                    vector * vector, axis=0, keepdims=True
                )
    if with_inner:
        rest = jnp.zeros((TAG - 2 * roots, width), jnp.float32)
        refs[0][...] = jnp.concatenate(inner + [rest], axis=0)


def combine(table, pieces, kept, arrived, vector, diag, share, ordered, with_inner):
    height, width = kept.shape[0] // diag.shape[0], kept.shape[1]
    size = sum(size for _, size in pieces)
    out_shape = [jax.ShapeDtypeStruct((size * height, width), jnp.float32)]
    if with_inner:
        out_shape.append(jax.ShapeDtypeStruct((TAG, width), jnp.float32))
    out = pl.pallas_call(
        functools.partial(combine_kernel, share, pieces, ordered, with_inner),
        out_shape=out_shape,
        in_specs=[SCALARS] + [WHOLE] * (3 + len(arrived)),
        out_specs=[WHOLE] * len(out_shape),
        compiler_params=pltpu.CompilerParams(vmem_limit_bytes=SMALL),
        cost_estimate=FREE,
        name="combine",
    )(table, kept, vector, diag, *arrived)
    return out if with_inner else (out[0], None)


def correct_kernel(groups, ahead, table, inner_ref, vector_ref, diag_ref, *rest):
    parts, (raw_ref, ahead_ref) = rest[:-2], rest[-2:]
    count, rows, width = diag_ref.shape
    height = vector_ref.shape[0] // count
    roots = height // rows
    inner = jnp.sum(inner_ref[...], axis=1, keepdims=True)
    theta = inner[:roots] / inner[roots : 2 * roots]
    squares = [jnp.zeros((1, width), jnp.float32) for _ in range(roots)]
    for at, pieces in enumerate(groups):
        mine, theirs = parts[2 * at], parts[2 * at + 1]
        row = 0
        for base, size in pieces:
            for i in range(size):
                slot = table[count + base + i]
                held = slot * height
                place = table[2 * count + slot] * height
                diag = diag_ref[slot]
                for r in range(roots):
                    shift = theta[r : r + 1]
                    sigma = mine[row : row + rows] + theirs[row : row + rows]
                    vector = vector_ref[pl.ds(pl.multiple_of(held + r * rows, rows), rows)]
                    raw = (sigma - shift * vector) / jnp.maximum(jnp.abs(diag - shift), 1.0)
                    raw_ref[pl.ds(pl.multiple_of(place + r * rows, rows), rows)] = raw
                    squares[r] = squares[r] + jnp.sum(raw * raw, axis=0, keepdims=True)
                    row += rows
    raw_ref[count * height :] = jnp.concatenate(
        squares + [jnp.zeros((TAG - roots, width), jnp.float32)], axis=0
    )
    ahead_ref[: ahead[1] * height] = raw_ref[ahead[0] * height : (ahead[0] + ahead[1]) * height]
    ahead_ref[ahead[1] * height :] = raw_ref[count * height :]


def correct(table, groups, ahead, inner, vector, diag, parts):
    height, width = vector.shape[0] // diag.shape[0], vector.shape[1]
    return pl.pallas_call(
        functools.partial(correct_kernel, groups, ahead),
        out_shape=[
            jax.ShapeDtypeStruct((vector.shape[0] + TAG, width), jnp.float32),
            jax.ShapeDtypeStruct((ahead[1] * height + TAG, width), jnp.float32),
        ],
        in_specs=[SCALARS] + [WHOLE] * (3 + len(parts)),
        out_specs=[WHOLE, WHOLE],
        compiler_params=pltpu.CompilerParams(vmem_limit_bytes=SMALL),
        cost_estimate=FREE,
        name="correct",
    )(table, inner, vector, diag, *parts)


def scatter(held, out_ref, sems, rows_of):
    height = held.shape[0] // len(rows_of)
    copies = []
    for i, make in enumerate(rows_of):
        at = slice(i * height, (i + 1) * height)
        row = make(at)
        copies.append(
            pltpu.make_async_copy(
                held.at[at], out_ref.at[pl.ds(pl.multiple_of(row, height), height)], sems.at[i]
            )
        )
        copies[-1].start()
    for copy in copies:
        copy.wait()


def scaled_kernel(count, rows, table, scale_ref, raw_ref, out_ref, held, sems):
    height = held.shape[0] // count

    def make(i, at):
        place = pl.multiple_of(table[2 * count + i] * height, height)
        for r in range(height // rows):
            part = raw_ref[pl.ds(place + r * rows, rows)]
            held[at.start + r * rows : at.start + (r + 1) * rows] = part * scale_ref[r : r + 1]
        return i * height

    scatter(held, out_ref, sems, [functools.partial(make, i) for i in range(count)])


def scaled(table, scale, raw, count, rows):
    height, width = raw.shape[0] // count // rows * rows, raw.shape[1]
    return pl.pallas_call(
        functools.partial(scaled_kernel, count, rows),
        out_shape=jax.ShapeDtypeStruct((count * height, width), jnp.float32),
        in_specs=[SCALARS, WHOLE, WHOLE],
        out_specs=ANY,
        scratch_shapes=[
            pltpu.VMEM((count * height, width), jnp.float32),
            pltpu.SemaphoreType.DMA((count,)),
        ],
        compiler_params=pltpu.CompilerParams(vmem_limit_bytes=SMALL),
        cost_estimate=FREE,
        name="scaled",
    )(table, scale, raw)


def finish_kernel(count, rows, sizes, places, table, scale_ref, *refs):
    parts, (out_ref, held, sems) = refs[: 2 * len(sizes)], refs[-3:]
    height = held.shape[0] // len(places)
    sources = [(part, i) for part, size in enumerate(sizes) for i in range(size)]

    def make(source, place, at):
        part, i = source
        mine, theirs = parts[2 * part], parts[2 * part + 1]
        for r in range(height // rows):
            row = i * height + r * rows
            total = mine[row : row + rows] + theirs[row : row + rows]
            held[at.start + r * rows : at.start + (r + 1) * rows] = total * scale_ref[r : r + 1]
        return table[count + place] * height

    scatter(held, out_ref, sems, [functools.partial(make, *one) for one in zip(sources, places)])


def finish(table, spans, scale, parts, out, count, rows):
    places = [base + i for base, size in spans for i in range(size)]
    height, width = parts[0].shape[0] // spans[0][1], parts[0].shape[1]
    in_specs = [SCALARS] + [WHOLE] * (1 + len(parts))
    args, aliases = [table, scale, *parts], {}
    if out is not None:
        in_specs.append(ANY)
        aliases = {len(args): 0}
        args.append(out)
    return pl.pallas_call(
        functools.partial(finish_kernel, count, rows, [size for _, size in spans], places),
        out_shape=jax.ShapeDtypeStruct((count * height, width), jnp.float32),
        in_specs=in_specs,
        out_specs=ANY,
        scratch_shapes=[
            pltpu.VMEM((len(places) * height, width), jnp.float32),
            pltpu.SemaphoreType.DMA((len(places),)),
        ],
        input_output_aliases=aliases,
        compiler_params=pltpu.CompilerParams(vmem_limit_bytes=SMALL),
        cost_estimate=FREE,
        name="finish",
    )(*args)


def add_over_term(value):
    size = lax.axis_size("term")
    if size == 1 or not power_of_two(size):
        return lax.psum(value, "term"), jnp.zeros_like(value)
    bit = 1
    while 2 * bit < size:
        value = value + flip(value, "term", bit)
        bit *= 2
    return value, flip(value, "term", bit)


def after(*values):
    return lax.optimization_barrier(values)


def shards(amplitudes, left, right, term_kind, partner, left_diag, right_diag):
    devices, terms_over = lax.axis_size("blk"), lax.axis_size("term")
    slots, rows, roots, width = amplitudes.shape
    per = slots // devices
    elements = slots * devices * rows * lax.axis_size("sub") * width
    vector = jnp.transpose(amplitudes, (0, 2, 1, 3)).reshape(slots * roots * rows, width)
    table = make_table(partner, term_kind, vector)
    diag = left_diag[:, :, None] + right_diag[:, None, :]

    cuts = [(0, per // 2), (per // 2, per - per // 2)] if per > 1 else [(0, per)]
    offsets = sorted(range(1, devices), key=lambda c: (-min(c, devices - c), c))
    moving = [(c, c * per + start, size) for c in offsets for start, size in cuts]
    staying = [(0, start, size) for start, size in cuts]
    pieces = staying + moving
    ahead_of = len(cuts)
    whole = [pieces[i : i + ahead_of] for i in range(0, len(pieces), ahead_of)]
    single = [[piece] for piece in pieces]
    batches = [moving[:ahead_of], moving[ahead_of:] + staying]

    def spans(pieces):
        return [piece[1:] for piece in pieces]

    def relay(value, c):
        return lax.ppermute(value, "blk", [(p, (p + c) % devices) for p in range(devices)])

    def swap(value):
        return lax.ppermute(value, "sub", [(0, 1), (1, 0)])

    def partials(own, second):
        if second:
            early = (ahead, swap(ahead))
            other = swap(after(own, early[1])[0])
        else:
            other = swap(own)
        kept, outgoing = None, {}
        for batch in batches:
            early_now = second and batch is batches[0]
            pair = early if early_now else (own, other)
            parts, kept = sectors(
                table,
                spans(batch),
                [second and piece[0] > 0 for piece in batch],
                left,
                right,
                *pair,
                kept,
                (batch[0][1] if early_now else 0) if second else None,
                roots,
            )
            outgoing.update(zip(batch, parts))
        arrived, sums, inners = {}, [], []
        for at, piece in enumerate(moving):
            value = outgoing[piece]
            if at >= ahead_of:
                value = after(value, arrived[moving[at - ahead_of]])[0]
            arrived[piece] = relay(value, piece[0])
        for group in single if second else whole:
            mine, inner = combine(
                table,
                spans(group),
                kept,
                [arrived[piece] if piece[0] else outgoing[piece] for piece in group],
                own,
                diag,
                1.0 / terms_over,
                second,
                not second,
            )
            if len(sums) >= 2 * 2:
                mine = after(mine, sums[1 - 2 * 2])[0]
            sums += add_over_term(mine)
            inners.append(inner)
        return sums, inners, arrived, other

    sums, inners, _, _ = partials(vector, False)
    inner = small_sum(small_sum(sum(inners[1:], inners[0]), "sub"), "blk")
    inner = small_sum(after(inner, sums[-3])[0], "term")
    first = (batches[0][0][1], sum(size for _, _, size in batches[0]))
    raw, ahead = correct(
        table, [spans(group) for group in whole], first, inner, vector, diag, sums
    )

    sums, _, arrived, other = partials(raw, True)
    squares = raw[-TAG:] + other[-TAG:]
    for piece in moving[::ahead_of]:
        squares = squares + arrived[piece][-TAG:]
    scale = lax.rsqrt(jnp.sum(squares, axis=1, keepdims=True) / elements + 1e-06)
    scale = jnp.broadcast_to(scale, squares.shape)
    correction = scaled(table, scale, raw, slots, rows)
    sigma = None
    for some in (slice(0, -ahead_of), slice(-ahead_of, None)):
        parts = [one for pair in list(zip(sums[::2], sums[1::2]))[some] for one in pair]
        if parts:
            sigma = finish(table, spans(pieces[some]), scale, parts, sigma, slots, rows)
    return tuple(
        jnp.transpose(value.reshape(slots, roots, rows, width), (0, 2, 1, 3))
        for value in (sigma, correction)
    )


def solution(mesh):
    return jax.shard_map(
        shards,
        mesh=mesh,
        in_specs=(
            P(("grp", "blk"), "sub", None, None),
            P(("grp", "term"), "blk", "sub", None),
            P(("grp", "term"), "blk", None, None),
            P(("grp", "term")),
            P(("grp", "blk")),
            P(("grp", "blk"), "sub"),
            P(("grp", "blk"), None),
        ),
        out_specs=(P(("grp", "blk"), "sub", None, None), P(("grp", "blk"), "sub", None, None)),
        check_vma=False,
    )
```

```python
import functools

import jax
import jax.numpy as jnp
from jax import lax
from jax.experimental import pallas as pl
from jax.experimental.pallas import tpu as pltpu
from jax.sharding import PartitionSpec as P

TAG = 8
LIMIT = 48 * 1024 * 1024
SMALL = 24 * 1024 * 1024
FREE = pl.CostEstimate(flops=0, bytes_accessed=0, transcendentals=0)
WHOLE = pl.BlockSpec(memory_space=pltpu.VMEM)
SCALARS = pl.BlockSpec(memory_space=pltpu.SMEM)
ANY = pl.BlockSpec(memory_space=pl.ANY)


def power_of_two(size):
    return size & (size - 1) == 0


def flip(value, axis, bit):
    size = lax.axis_size(axis)
    return lax.ppermute(value, axis, [(i, i ^ bit) for i in range(size)])


def small_sum(value, axis):
    size = lax.axis_size(axis)
    if not power_of_two(size):
        return lax.psum(value, axis)
    if size == 4:
        one, two, three = (flip(value, axis, bit) for bit in (1, 2, 3))
        return (value + one) + (two + three)
    bit = 1
    while bit < size:
        value = value + flip(value, axis, bit)
        bit *= 2
    return value


def halves(value):
    high = value.astype(jnp.bfloat16)
    low = (value - high.astype(jnp.float32)).astype(jnp.bfloat16)
    return high, low


def table_kernel(devices, count, terms, given_hbm, _, table_ref, used, given_ref, sem):
    copy = pltpu.make_async_copy(given_hbm, given_ref, sem)
    copy.start()
    copy.wait()
    per = count // devices
    me = lax.axis_index("blk")
    for c in range(devices):
        used[c] = 0

    def place(j, carry):
        where_to = given_ref[j]
        owner = lax.div(where_to, count)
        offset = lax.rem(owner - me + devices, devices)
        at = offset * per + used[offset]
        used[offset] = used[offset] + 1
        table_ref[at] = j
        table_ref[count + at] = where_to - owner * count
        table_ref[2 * count + j] = at
        return carry

    lax.fori_loop(0, count, place, 0)
    for k in range(terms):
        table_ref[3 * count + k] = given_ref[count + k]
    table_ref[3 * count + terms] = lax.axis_index("sub")


def make_table(partner, term_kind, vector):
    devices = lax.axis_size("blk")
    count, terms = partner.shape[0], term_kind.shape[0]
    given = jnp.concatenate([partner, term_kind])
    return pl.pallas_call(
        functools.partial(table_kernel, devices, count, terms),
        out_shape=jax.ShapeDtypeStruct((3 * count + terms + 1,), jnp.int32),
        in_specs=[ANY, WHOLE],
        out_specs=SCALARS,
        scratch_shapes=[
            pltpu.SMEM((devices,), jnp.int32),
            pltpu.SMEM(given.shape, jnp.int32),
            pltpu.SemaphoreType.DMA,
        ],
        compiler_params=pltpu.CompilerParams(vmem_limit_bytes=SMALL),
        name="table",
    )(given, vector)


def sector(table, count, terms, height, source, held, own_ref, other_ref, l_ref, r_ref, lhs, high_rhs, low_rhs):
    rows, width = l_ref.shape[2], r_ref.shape[3]
    roots = height // rows
    first = table[3 * count + terms] == 0
    own, other = own_ref[held], other_ref[held]
    top = jnp.where(first, own, other)
    bottom = jnp.where(first, other, own)
    left = l_ref[:, source].reshape(terms * rows, 2 * rows)
    left = jnp.concatenate(halves(left), axis=1)
    for r in range(roots):
        at = slice(r * rows, (r + 1) * rows)
        wide = jnp.concatenate(halves(jnp.concatenate([top[at], bottom[at]], axis=0)), axis=1)
        both = jnp.dot(
            left, jnp.concatenate([wide, wide], axis=0), preferred_element_type=jnp.float32
        )
        high, low = halves(both[:, :width] + both[:, width:])
        for k in range(terms):
            lanes = slice(k * width, (k + 1) * width)
            part = slice(k * rows, (k + 1) * rows)
            lhs[r * rows : (r + 1) * rows, lanes] = high[part]
            lhs[(roots + r) * rows : (roots + r + 1) * rows, lanes] = low[part]
    for k in range(terms):
        lanes = slice(k * width, (k + 1) * width)
        kind = table[3 * count + k]
        used = pl.ds(pl.multiple_of((1 - kind) * width, width), width)
        high, low = halves(r_ref[k, source].T)
        high_rhs[lanes, used] = high
        low_rhs[lanes, used] = low
    high, low = lhs[:height], lhs[height:]
    return jnp.dot(
        jnp.concatenate([high, low, high], axis=1),
        jnp.concatenate([high_rhs[...], high_rhs[...], low_rhs[...]], axis=0),
        preferred_element_type=jnp.float32,
    )


def sector_kernel(count, terms, unroll, height, pieces, origin, starts, tags, table, own_ref, other_ref, *refs):
    streamed = origin is None
    inputs, scratch = refs[: 2 * unroll if streamed else 2], refs[-3 * unroll :]
    outputs = refs[-3 * unroll - len(starts) : -3 * unroll]
    moved_refs, kept_ref = outputs[:-1], outputs[-1]
    width = kept_ref.shape[1]
    step = pl.program_id(0)

    def sector_at(at):
        return pl.ds(pl.multiple_of(at * height, height), height)

    @pl.when(step == 0)
    def _():
        for k in range(terms):
            kind = table[3 * count + k]
            unused = pl.ds(pl.multiple_of(kind * width, width), width)
            for at, ref in enumerate(scratch):
                if at % 3:
                    ref[k * width : (k + 1) * width, unused] = jnp.zeros((width, width), ref.dtype)
        if any(tags):
            tag = own_ref[own_ref.shape[0] - TAG :] + other_ref[other_ref.shape[0] - TAG :]
            for ref, begin, end, tagged in zip(moved_refs, starts, starts[1:], tags):
                if tagged:
                    ref[(end - begin) * height :] = tag

    places = [place_of(step * unroll + u, pieces) for u in range(unroll)]
    results = [
        sector(
            table,
            count,
            terms,
            height,
            0 if streamed else table[place],
            sector_at(table[place] if streamed else place - origin),
            own_ref,
            other_ref,
            *(inputs[2 * u : 2 * u + 2] if streamed else inputs),
            *scratch[3 * u : 3 * u + 3],
        )
        for u, place in enumerate(places)
    ]
    for u, place in enumerate(places):
        kept_ref[sector_at(place)] = results[u][:, width:]
    for ref, begin, end in zip(moved_refs, starts, starts[1:]):
        for u in range(unroll):
            at = step * unroll + u - begin

            @pl.when((at >= 0) & (at < end - begin))
            def _(ref=ref, u=u, at=at):
                ref[sector_at(at)] = results[u][:, :width]


def place_of(i, pieces):
    at, begin = pieces[0][0] + i, 0
    for (_, size), (base, _) in zip(pieces, pieces[1:]):
        begin += size
        at = jnp.where(i >= begin, base + i - begin, at)
    return at


def sectors(table, pieces, tags, left, right, own, other, kept, origin, roots):
    terms, count, rows, width = left.shape
    height = roots * rows
    starts = [0]
    for _, size in pieces:
        starts.append(starts[-1] + size)
    places = [base + i for base, size in pieces for i in range(size)]

    unroll = 2 if len(places) % 2 == 0 else 1

    def specs(u):
        def source(i, table):
            return table[place_of(unroll * i + u, pieces)]

        return [
            pl.BlockSpec((terms, 1, rows, width), lambda i, t: (0, source(i, t), 0, 0)),
            pl.BlockSpec((terms, 1, width, width), lambda i, t: (0, source(i, t), 0, 0)),
        ]

    if origin is None:
        in_specs = [WHOLE, WHOLE] + [spec for u in range(unroll) for spec in specs(u)]
        args = [own, other] + [left, right] * unroll
    else:
        in_specs = [WHOLE] * 4
        args = [own, other, left, right]
    aliases = {}
    if kept is not None:
        in_specs.append(WHOLE)
        args.append(kept)
        aliases = {len(args): len(pieces)}
    deep = terms * width
    shapes = [(size * height + TAG * tagged, width) for (_, size), tagged in zip(pieces, tags)]
    out = pl.pallas_call(
        functools.partial(
            sector_kernel, count, terms, unroll, height, pieces, origin, starts, tags
        ),
        out_shape=[
            jax.ShapeDtypeStruct(shape, jnp.float32)
            for shape in shapes + [(count * height, width)]
        ],
        grid_spec=pltpu.PrefetchScalarGridSpec(
            num_scalar_prefetch=1,
            grid=(starts[-1] // unroll,),
            in_specs=in_specs,
            out_specs=[WHOLE] * (len(shapes) + 1),
            scratch_shapes=[
                pltpu.VMEM((2 * height, deep), jnp.bfloat16),
                pltpu.VMEM((deep, 2 * width), jnp.bfloat16),
                pltpu.VMEM((deep, 2 * width), jnp.bfloat16),
            ]
            * unroll,
        ),
        input_output_aliases=aliases,
        compiler_params=pltpu.CompilerParams(vmem_limit_bytes=LIMIT if origin is None else SMALL),
        cost_estimate=FREE,
        name="sectors",
    )(table, *args)
    return out[:-1], out[-1]


def combine_kernel(share, pieces, ordered, with_inner, table, kept_ref, vector_ref, diag_ref, *refs):
    arrived_refs, sum_ref, refs = refs[: len(pieces)], refs[len(pieces)], refs[len(pieces) + 1 :]
    count, rows, width = diag_ref.shape
    height = kept_ref.shape[0] // count
    roots = height // rows
    inner = [jnp.zeros((1, width), jnp.float32) for _ in range(2 * roots)]
    every = [(ref, base + i, i) for ref, (base, size) in zip(arrived_refs, pieces) for i in range(size)]
    for i, (arrived_ref, at_place, of_piece) in enumerate(every):
        slot = table[count + at_place]
        place = table[2 * count + slot]
        held = place if ordered else slot
        diag = share * diag_ref[slot]
        for r in range(roots):

            def at(sector):
                return pl.ds(pl.multiple_of(sector * height + r * rows, rows), rows)

            here = slice(i * height + r * rows, i * height + (r + 1) * rows)
            there = slice(of_piece * height + r * rows, of_piece * height + (r + 1) * rows)
            vector = vector_ref[at(held)]
            total = kept_ref[at(place)] + arrived_ref[there] + diag * vector
            sum_ref[here] = total
            if with_inner:
                inner[r] = inner[r] + jnp.sum(vector * total, axis=0, keepdims=True)
                inner[roots + r] = inner[roots + r] + share * jnp.sum(
                    vector * vector, axis=0, keepdims=True
                )
    if with_inner:
        rest = jnp.zeros((TAG - 2 * roots, width), jnp.float32)
        refs[0][...] = jnp.concatenate(inner + [rest], axis=0)


def combine(table, pieces, kept, arrived, vector, diag, share, ordered, with_inner):
    height, width = kept.shape[0] // diag.shape[0], kept.shape[1]
    size = sum(size for _, size in pieces)
    out_shape = [jax.ShapeDtypeStruct((size * height, width), jnp.float32)]
    if with_inner:
        out_shape.append(jax.ShapeDtypeStruct((TAG, width), jnp.float32))
    out = pl.pallas_call(
        functools.partial(combine_kernel, share, pieces, ordered, with_inner),
        out_shape=out_shape,
        in_specs=[SCALARS] + [WHOLE] * (3 + len(arrived)),
        out_specs=[WHOLE] * len(out_shape),
        compiler_params=pltpu.CompilerParams(vmem_limit_bytes=SMALL),
        cost_estimate=FREE,
        name="combine",
    )(table, kept, vector, diag, *arrived)
    return out if with_inner else (out[0], None)


def correct_kernel(groups, ahead, table, inner_ref, vector_ref, diag_ref, *rest):
    parts, (raw_ref, ahead_ref) = rest[:-2], rest[-2:]
    count, rows, width = diag_ref.shape
    height = vector_ref.shape[0] // count
    roots = height // rows
    inner = jnp.sum(inner_ref[...], axis=1, keepdims=True)
    theta = inner[:roots] / inner[roots : 2 * roots]
    squares = [jnp.zeros((1, width), jnp.float32) for _ in range(roots)]
    for at, pieces in enumerate(groups):
        mine, theirs = parts[2 * at], parts[2 * at + 1]
        row = 0
        for base, size in pieces:
            for i in range(size):
                slot = table[count + base + i]
                held = slot * height
                place = table[2 * count + slot] * height
                diag = diag_ref[slot]
                for r in range(roots):
                    shift = theta[r : r + 1]
                    sigma = mine[row : row + rows] + theirs[row : row + rows]
                    vector = vector_ref[pl.ds(pl.multiple_of(held + r * rows, rows), rows)]
                    raw = (sigma - shift * vector) / jnp.maximum(jnp.abs(diag - shift), 1.0)
                    raw_ref[pl.ds(pl.multiple_of(place + r * rows, rows), rows)] = raw
                    squares[r] = squares[r] + jnp.sum(raw * raw, axis=0, keepdims=True)
                    row += rows
    raw_ref[count * height :] = jnp.concatenate(
        squares + [jnp.zeros((TAG - roots, width), jnp.float32)], axis=0
    )
    ahead_ref[: ahead[1] * height] = raw_ref[ahead[0] * height : (ahead[0] + ahead[1]) * height]
    ahead_ref[ahead[1] * height :] = raw_ref[count * height :]


def correct(table, groups, ahead, inner, vector, diag, parts):
    height, width = vector.shape[0] // diag.shape[0], vector.shape[1]
    return pl.pallas_call(
        functools.partial(correct_kernel, groups, ahead),
        out_shape=[
            jax.ShapeDtypeStruct((vector.shape[0] + TAG, width), jnp.float32),
            jax.ShapeDtypeStruct((ahead[1] * height + TAG, width), jnp.float32),
        ],
        in_specs=[SCALARS] + [WHOLE] * (3 + len(parts)),
        out_specs=[WHOLE, WHOLE],
        compiler_params=pltpu.CompilerParams(vmem_limit_bytes=SMALL),
        cost_estimate=FREE,
        name="correct",
    )(table, inner, vector, diag, *parts)


def scatter(held, out_ref, sems, rows_of):
    height = held.shape[0] // len(rows_of)
    copies = []
    for i, make in enumerate(rows_of):
        at = slice(i * height, (i + 1) * height)
        row = make(at)
        copies.append(
            pltpu.make_async_copy(
                held.at[at], out_ref.at[pl.ds(pl.multiple_of(row, height), height)], sems.at[i]
            )
        )
        copies[-1].start()
    for copy in copies:
        copy.wait()


def scaled_kernel(count, rows, table, scale_ref, raw_ref, out_ref, held, sems):
    height = held.shape[0] // count

    def make(i, at):
        place = pl.multiple_of(table[2 * count + i] * height, height)
        for r in range(height // rows):
            part = raw_ref[pl.ds(place + r * rows, rows)]
            held[at.start + r * rows : at.start + (r + 1) * rows] = part * scale_ref[r : r + 1]
        return i * height

    scatter(held, out_ref, sems, [functools.partial(make, i) for i in range(count)])


def scaled(table, scale, raw, count, rows):
    height, width = raw.shape[0] // count // rows * rows, raw.shape[1]
    return pl.pallas_call(
        functools.partial(scaled_kernel, count, rows),
        out_shape=jax.ShapeDtypeStruct((count * height, width), jnp.float32),
        in_specs=[SCALARS, WHOLE, WHOLE],
        out_specs=ANY,
        scratch_shapes=[
            pltpu.VMEM((count * height, width), jnp.float32),
            pltpu.SemaphoreType.DMA((count,)),
        ],
        compiler_params=pltpu.CompilerParams(vmem_limit_bytes=SMALL),
        cost_estimate=FREE,
        name="scaled",
    )(table, scale, raw)


def finish_kernel(count, rows, sizes, places, table, scale_ref, *refs):
    parts, (out_ref, held, sems) = refs[: 2 * len(sizes)], refs[-3:]
    height = held.shape[0] // len(places)
    sources = [(part, i) for part, size in enumerate(sizes) for i in range(size)]

    def make(source, place, at):
        part, i = source
        mine, theirs = parts[2 * part], parts[2 * part + 1]
        for r in range(height // rows):
            row = i * height + r * rows
            total = mine[row : row + rows] + theirs[row : row + rows]
            held[at.start + r * rows : at.start + (r + 1) * rows] = total * scale_ref[r : r + 1]
        return table[count + place] * height

    scatter(held, out_ref, sems, [functools.partial(make, *one) for one in zip(sources, places)])


def finish(table, spans, scale, parts, out, count, rows):
    places = [base + i for base, size in spans for i in range(size)]
    height, width = parts[0].shape[0] // spans[0][1], parts[0].shape[1]
    in_specs = [SCALARS] + [WHOLE] * (1 + len(parts))
    args, aliases = [table, scale, *parts], {}
    if out is not None:
        in_specs.append(ANY)
        aliases = {len(args): 0}
        args.append(out)
    return pl.pallas_call(
        functools.partial(finish_kernel, count, rows, [size for _, size in spans], places),
        out_shape=jax.ShapeDtypeStruct((count * height, width), jnp.float32),
        in_specs=in_specs,
        out_specs=ANY,
        scratch_shapes=[
            pltpu.VMEM((len(places) * height, width), jnp.float32),
            pltpu.SemaphoreType.DMA((len(places),)),
        ],
        input_output_aliases=aliases,
        compiler_params=pltpu.CompilerParams(vmem_limit_bytes=SMALL),
        cost_estimate=FREE,
        name="finish",
    )(*args)


def add_over_term(value):
    size = lax.axis_size("term")
    if size == 1 or not power_of_two(size):
        return lax.psum(value, "term"), jnp.zeros_like(value)
    bit = 1
    while 2 * bit < size:
        value = value + flip(value, "term", bit)
        bit *= 2
    return value, flip(value, "term", bit)


def after(*values):
    return lax.optimization_barrier(values)


def shards(amplitudes, left, right, term_kind, partner, left_diag, right_diag):
    devices, terms_over = lax.axis_size("blk"), lax.axis_size("term")
    slots, rows, roots, width = amplitudes.shape
    per = slots // devices
    elements = slots * devices * rows * lax.axis_size("sub") * width
    vector = jnp.transpose(amplitudes, (0, 2, 1, 3)).reshape(slots * roots * rows, width)
    table = make_table(partner, term_kind, vector)
    diag = left_diag[:, :, None] + right_diag[:, None, :]

    cuts = [(0, per // 2), (per // 2, per - per // 2)] if per > 1 else [(0, per)]
    offsets = sorted(range(1, devices), key=lambda c: (-min(c, devices - c), c))
    moving = [(c, c * per + start, size) for c in offsets for start, size in cuts]
    staying = [(0, start, size) for start, size in cuts]
    pieces = staying + moving
    ahead_of = len(cuts)
    whole = [pieces[i : i + ahead_of] for i in range(0, len(pieces), ahead_of)]
    single = [[piece] for piece in pieces]
    batches = [moving[:ahead_of], moving[ahead_of:] + staying]

    def spans(pieces):
        return [piece[1:] for piece in pieces]

    def relay(value, c):
        return lax.ppermute(value, "blk", [(p, (p + c) % devices) for p in range(devices)])

    def swap(value):
        return lax.ppermute(value, "sub", [(0, 1), (1, 0)])

    def partials(own, second):
        if second:
            early = (ahead, swap(ahead))
            other = swap(after(own, early[1])[0])
        else:
            other = swap(own)
        kept, outgoing = None, {}
        for batch in batches:
            early_now = second and batch is batches[0]
            pair = early if early_now else (own, other)
            parts, kept = sectors(
                table,
                spans(batch),
                [second and piece[0] > 0 for piece in batch],
                left,
                right,
                *pair,
                kept,
                (batch[0][1] if early_now else 0) if second else None,
                roots,
            )
            outgoing.update(zip(batch, parts))
        arrived, sums, inners = {}, [], []
        for at, piece in enumerate(moving):
            value = outgoing[piece]
            if at >= ahead_of:
                value = after(value, arrived[moving[at - ahead_of]])[0]
            arrived[piece] = relay(value, piece[0])
        for group in single if second else whole:
            mine, inner = combine(
                table,
                spans(group),
                kept,
                [arrived[piece] if piece[0] else outgoing[piece] for piece in group],
                own,
                diag,
                1.0 / terms_over,
                second,
                not second,
            )
            if len(sums) >= 2 * 2:
                mine = after(mine, sums[1 - 2 * 2])[0]
            sums += add_over_term(mine)
            inners.append(inner)
        return sums, inners, arrived, other

    sums, inners, _, _ = partials(vector, False)
    inner = small_sum(small_sum(sum(inners[1:], inners[0]), "sub"), "blk")
    inner = small_sum(after(inner, sums[-3])[0], "term")
    first = (batches[0][0][1], sum(size for _, _, size in batches[0]))
    raw, ahead = correct(
        table, [spans(group) for group in whole], first, inner, vector, diag, sums
    )

    sums, _, arrived, other = partials(raw, True)
    squares = raw[-TAG:] + other[-TAG:]
    for piece in moving[::ahead_of]:
        squares = squares + arrived[piece][-TAG:]
    scale = lax.rsqrt(jnp.sum(squares, axis=1, keepdims=True) / elements + 1e-06)
    scale = jnp.broadcast_to(scale, squares.shape)
    correction = scaled(table, scale, raw, slots, rows)
    sigma = None
    for some in (slice(0, -ahead_of), slice(-ahead_of, None)):
        parts = [one for pair in list(zip(sums[::2], sums[1::2]))[some] for one in pair]
        if parts:
            sigma = finish(table, spans(pieces[some]), scale, parts, sigma, slots, rows)
    return tuple(
        jnp.transpose(value.reshape(slots, roots, rows, width), (0, 2, 1, 3))
        for value in (sigma, correction)
    )


def solution(mesh):
    return jax.shard_map(
        shards,
        mesh=mesh,
        in_specs=(
            P(("grp", "blk"), "sub", None, None),
            P(("grp", "term"), "blk", "sub", None),
            P(("grp", "term"), "blk", None, None),
            P(("grp", "term")),
            P(("grp", "blk")),
            P(("grp", "blk"), "sub"),
            P(("grp", "blk"), None),
        ),
        out_specs=(P(("grp", "blk"), "sub", None, None), P(("grp", "blk"), "sub", None, None)),
        check_vma=False,
    )
```

```python
import functools

import jax
import jax.numpy as jnp
from jax import lax
from jax.experimental import pallas as pl
from jax.experimental.pallas import tpu as pltpu
from jax.sharding import PartitionSpec as P

TAG = 8
LIMIT = 48 * 1024 * 1024
SMALL = 24 * 1024 * 1024
FREE = pl.CostEstimate(flops=0, bytes_accessed=0, transcendentals=0)
WHOLE = pl.BlockSpec(memory_space=pltpu.VMEM)
SCALARS = pl.BlockSpec(memory_space=pltpu.SMEM)
ANY = pl.BlockSpec(memory_space=pl.ANY)


def power_of_two(size):
    return size & (size - 1) == 0


def flip(value, axis, bit):
    size = lax.axis_size(axis)
    return lax.ppermute(value, axis, [(i, i ^ bit) for i in range(size)])


def small_sum(value, axis):
    size = lax.axis_size(axis)
    if not power_of_two(size):
        return lax.psum(value, axis)
    if size == 4:
        one, two, three = (flip(value, axis, bit) for bit in (1, 2, 3))
        return (value + one) + (two + three)
    bit = 1
    while bit < size:
        value = value + flip(value, axis, bit)
        bit *= 2
    return value


def halves(value):
    high = value.astype(jnp.bfloat16)
    low = (value - high.astype(jnp.float32)).astype(jnp.bfloat16)
    return high, low


def table_kernel(devices, count, terms, given_hbm, _, table_ref, used, given_ref, sem):
    copy = pltpu.make_async_copy(given_hbm, given_ref, sem)
    copy.start()
    copy.wait()
    per = count // devices
    me = lax.axis_index("blk")
    for c in range(devices):
        used[c] = 0

    def place(j, carry):
        where_to = given_ref[j]
        owner = lax.div(where_to, count)
        offset = lax.rem(owner - me + devices, devices)
        at = offset * per + used[offset]
        used[offset] = used[offset] + 1
        table_ref[at] = j
        table_ref[count + at] = where_to - owner * count
        table_ref[2 * count + j] = at
        return carry

    lax.fori_loop(0, count, place, 0)
    for k in range(terms):
        table_ref[3 * count + k] = given_ref[count + k]
    table_ref[3 * count + terms] = lax.axis_index("sub")


def make_table(partner, term_kind, vector):
    devices = lax.axis_size("blk")
    count, terms = partner.shape[0], term_kind.shape[0]
    given = jnp.concatenate([partner, term_kind])
    return pl.pallas_call(
        functools.partial(table_kernel, devices, count, terms),
        out_shape=jax.ShapeDtypeStruct((3 * count + terms + 1,), jnp.int32),
        in_specs=[ANY, WHOLE],
        out_specs=SCALARS,
        scratch_shapes=[
            pltpu.SMEM((devices,), jnp.int32),
            pltpu.SMEM(given.shape, jnp.int32),
            pltpu.SemaphoreType.DMA,
        ],
        compiler_params=pltpu.CompilerParams(vmem_limit_bytes=SMALL),
        name="table",
    )(given, vector)


def sector(table, count, terms, height, source, held, own_ref, other_ref, l_ref, r_ref, lhs, high_rhs, low_rhs):
    rows, width = l_ref.shape[2], r_ref.shape[3]
    roots = height // rows
    first = table[3 * count + terms] == 0
    own, other = own_ref[held], other_ref[held]
    top = jnp.where(first, own, other)
    bottom = jnp.where(first, other, own)
    left = l_ref[:, source].reshape(terms * rows, 2 * rows)
    left = jnp.concatenate(halves(left), axis=1)
    for r in range(roots):
        at = slice(r * rows, (r + 1) * rows)
        wide = jnp.concatenate(halves(jnp.concatenate([top[at], bottom[at]], axis=0)), axis=1)
        both = jnp.dot(
            left, jnp.concatenate([wide, wide], axis=0), preferred_element_type=jnp.float32
        )
        high, low = halves(both[:, :width] + both[:, width:])
        for k in range(terms):
            lanes = slice(k * width, (k + 1) * width)
            part = slice(k * rows, (k + 1) * rows)
            lhs[r * rows : (r + 1) * rows, lanes] = high[part]
            lhs[(roots + r) * rows : (roots + r + 1) * rows, lanes] = low[part]
    for k in range(terms):
        lanes = slice(k * width, (k + 1) * width)
        kind = table[3 * count + k]
        used = pl.ds(pl.multiple_of((1 - kind) * width, width), width)
        high, low = halves(r_ref[k, source].T)
        high_rhs[lanes, used] = high
        low_rhs[lanes, used] = low
    high, low = lhs[:height], lhs[height:]
    return jnp.dot(
        jnp.concatenate([high, low, high], axis=1),
        jnp.concatenate([high_rhs[...], high_rhs[...], low_rhs[...]], axis=0),
        preferred_element_type=jnp.float32,
    )


def sector_kernel(count, terms, unroll, height, pieces, origin, starts, tags, table, own_ref, other_ref, *refs):
    streamed = origin is None
    inputs, scratch = refs[: 2 * unroll if streamed else 2], refs[-3 * unroll :]
    outputs = refs[-3 * unroll - len(starts) : -3 * unroll]
    moved_refs, kept_ref = outputs[:-1], outputs[-1]
    width = kept_ref.shape[1]
    step = pl.program_id(0)

    def sector_at(at):
        return pl.ds(pl.multiple_of(at * height, height), height)

    @pl.when(step == 0)
    def _():
        for k in range(terms):
            kind = table[3 * count + k]
            unused = pl.ds(pl.multiple_of(kind * width, width), width)
            for at, ref in enumerate(scratch):
                if at % 3:
                    ref[k * width : (k + 1) * width, unused] = jnp.zeros((width, width), ref.dtype)
        if any(tags):
            tag = own_ref[own_ref.shape[0] - TAG :] + other_ref[other_ref.shape[0] - TAG :]
            for ref, begin, end, tagged in zip(moved_refs, starts, starts[1:], tags):
                if tagged:
                    ref[(end - begin) * height :] = tag

    places = [place_of(step * unroll + u, pieces) for u in range(unroll)]
    results = [
        sector(
            table,
            count,
            terms,
            height,
            0 if streamed else table[place],
            sector_at(table[place] if streamed else place - origin),
            own_ref,
            other_ref,
            *(inputs[2 * u : 2 * u + 2] if streamed else inputs),
            *scratch[3 * u : 3 * u + 3],
        )
        for u, place in enumerate(places)
    ]
    for u, place in enumerate(places):
        kept_ref[sector_at(place)] = results[u][:, width:]
    for ref, begin, end in zip(moved_refs, starts, starts[1:]):
        for u in range(unroll):
            at = step * unroll + u - begin

            @pl.when((at >= 0) & (at < end - begin))
            def _(ref=ref, u=u, at=at):
                ref[sector_at(at)] = results[u][:, :width]


def place_of(i, pieces):
    at, begin = pieces[0][0] + i, 0
    for (_, size), (base, _) in zip(pieces, pieces[1:]):
        begin += size
        at = jnp.where(i >= begin, base + i - begin, at)
    return at


def sectors(table, pieces, tags, left, right, own, other, kept, origin, roots):
    terms, count, rows, width = left.shape
    height = roots * rows
    starts = [0]
    for _, size in pieces:
        starts.append(starts[-1] + size)
    places = [base + i for base, size in pieces for i in range(size)]

    unroll = 2 if len(places) % 2 == 0 else 1

    def specs(u):
        def source(i, table):
            return table[place_of(unroll * i + u, pieces)]

        return [
            pl.BlockSpec((terms, 1, rows, width), lambda i, t: (0, source(i, t), 0, 0)),
            pl.BlockSpec((terms, 1, width, width), lambda i, t: (0, source(i, t), 0, 0)),
        ]

    if origin is None:
        in_specs = [WHOLE, WHOLE] + [spec for u in range(unroll) for spec in specs(u)]
        args = [own, other] + [left, right] * unroll
    else:
        in_specs = [WHOLE] * 4
        args = [own, other, left, right]
    aliases = {}
    if kept is not None:
        in_specs.append(WHOLE)
        args.append(kept)
        aliases = {len(args): len(pieces)}
    deep = terms * width
    shapes = [(size * height + TAG * tagged, width) for (_, size), tagged in zip(pieces, tags)]
    out = pl.pallas_call(
        functools.partial(
            sector_kernel, count, terms, unroll, height, pieces, origin, starts, tags
        ),
        out_shape=[
            jax.ShapeDtypeStruct(shape, jnp.float32)
            for shape in shapes + [(count * height, width)]
        ],
        grid_spec=pltpu.PrefetchScalarGridSpec(
            num_scalar_prefetch=1,
            grid=(starts[-1] // unroll,),
            in_specs=in_specs,
            out_specs=[WHOLE] * (len(shapes) + 1),
            scratch_shapes=[
                pltpu.VMEM((2 * height, deep), jnp.bfloat16),
                pltpu.VMEM((deep, 2 * width), jnp.bfloat16),
                pltpu.VMEM((deep, 2 * width), jnp.bfloat16),
            ]
            * unroll,
        ),
        input_output_aliases=aliases,
        compiler_params=pltpu.CompilerParams(vmem_limit_bytes=LIMIT if origin is None else SMALL),
        cost_estimate=FREE,
        name="sectors",
    )(table, *args)
    return out[:-1], out[-1]


def combine_kernel(share, pieces, ordered, with_inner, table, kept_ref, vector_ref, diag_ref, *refs):
    arrived_refs, sum_ref, refs = refs[: len(pieces)], refs[len(pieces)], refs[len(pieces) + 1 :]
    count, rows, width = diag_ref.shape
    height = kept_ref.shape[0] // count
    roots = height // rows
    inner = [jnp.zeros((1, width), jnp.float32) for _ in range(2 * roots)]
    every = [(ref, base + i, i) for ref, (base, size) in zip(arrived_refs, pieces) for i in range(size)]
    for i, (arrived_ref, at_place, of_piece) in enumerate(every):
        slot = table[count + at_place]
        place = table[2 * count + slot]
        held = place if ordered else slot
        diag = share * diag_ref[slot]
        for r in range(roots):

            def at(sector):
                return pl.ds(pl.multiple_of(sector * height + r * rows, rows), rows)

            here = slice(i * height + r * rows, i * height + (r + 1) * rows)
            there = slice(of_piece * height + r * rows, of_piece * height + (r + 1) * rows)
            vector = vector_ref[at(held)]
            total = kept_ref[at(place)] + arrived_ref[there] + diag * vector
            sum_ref[here] = total
            if with_inner:
                inner[r] = inner[r] + jnp.sum(vector * total, axis=0, keepdims=True)
                inner[roots + r] = inner[roots + r] + share * jnp.sum(
                    vector * vector, axis=0, keepdims=True
                )
    if with_inner:
        rest = jnp.zeros((TAG - 2 * roots, width), jnp.float32)
        refs[0][...] = jnp.concatenate(inner + [rest], axis=0)


def combine(table, pieces, kept, arrived, vector, diag, share, ordered, with_inner):
    height, width = kept.shape[0] // diag.shape[0], kept.shape[1]
    size = sum(size for _, size in pieces)
    out_shape = [jax.ShapeDtypeStruct((size * height, width), jnp.float32)]
    if with_inner:
        out_shape.append(jax.ShapeDtypeStruct((TAG, width), jnp.float32))
    out = pl.pallas_call(
        functools.partial(combine_kernel, share, pieces, ordered, with_inner),
        out_shape=out_shape,
        in_specs=[SCALARS] + [WHOLE] * (3 + len(arrived)),
        out_specs=[WHOLE] * len(out_shape),
        compiler_params=pltpu.CompilerParams(vmem_limit_bytes=SMALL),
        cost_estimate=FREE,
        name="combine",
    )(table, kept, vector, diag, *arrived)
    return out if with_inner else (out[0], None)


def correct_kernel(groups, ahead, table, inner_ref, vector_ref, diag_ref, *rest):
    parts, (raw_ref, ahead_ref) = rest[:-2], rest[-2:]
    count, rows, width = diag_ref.shape
    height = vector_ref.shape[0] // count
    roots = height // rows
    inner = jnp.sum(inner_ref[...], axis=1, keepdims=True)
    theta = inner[:roots] / inner[roots : 2 * roots]
    squares = [jnp.zeros((1, width), jnp.float32) for _ in range(roots)]
    for at, pieces in enumerate(groups):
        mine, theirs = parts[2 * at], parts[2 * at + 1]
        row = 0
        for base, size in pieces:
            for i in range(size):
                slot = table[count + base + i]
                held = slot * height
                place = table[2 * count + slot] * height
                diag = diag_ref[slot]
                for r in range(roots):
                    shift = theta[r : r + 1]
                    sigma = mine[row : row + rows] + theirs[row : row + rows]
                    vector = vector_ref[pl.ds(pl.multiple_of(held + r * rows, rows), rows)]
                    raw = (sigma - shift * vector) / jnp.maximum(jnp.abs(diag - shift), 1.0)
                    raw_ref[pl.ds(pl.multiple_of(place + r * rows, rows), rows)] = raw
                    squares[r] = squares[r] + jnp.sum(raw * raw, axis=0, keepdims=True)
                    row += rows
    raw_ref[count * height :] = jnp.concatenate(
        squares + [jnp.zeros((TAG - roots, width), jnp.float32)], axis=0
    )
    ahead_ref[: ahead[1] * height] = raw_ref[ahead[0] * height : (ahead[0] + ahead[1]) * height]
    ahead_ref[ahead[1] * height :] = raw_ref[count * height :]


def correct(table, groups, ahead, inner, vector, diag, parts):
    height, width = vector.shape[0] // diag.shape[0], vector.shape[1]
    return pl.pallas_call(
        functools.partial(correct_kernel, groups, ahead),
        out_shape=[
            jax.ShapeDtypeStruct((vector.shape[0] + TAG, width), jnp.float32),
            jax.ShapeDtypeStruct((ahead[1] * height + TAG, width), jnp.float32),
        ],
        in_specs=[SCALARS] + [WHOLE] * (3 + len(parts)),
        out_specs=[WHOLE, WHOLE],
        compiler_params=pltpu.CompilerParams(vmem_limit_bytes=SMALL),
        cost_estimate=FREE,
        name="correct",
    )(table, inner, vector, diag, *parts)


def scatter(held, out_ref, sems, rows_of):
    height = held.shape[0] // len(rows_of)
    copies = []
    for i, make in enumerate(rows_of):
        at = slice(i * height, (i + 1) * height)
        row = make(at)
        copies.append(
            pltpu.make_async_copy(
                held.at[at], out_ref.at[pl.ds(pl.multiple_of(row, height), height)], sems.at[i]
            )
        )
        copies[-1].start()
    for copy in copies:
        copy.wait()


def scaled_kernel(count, rows, table, scale_ref, raw_ref, out_ref, held, sems):
    height = held.shape[0] // count

    def make(i, at):
        place = pl.multiple_of(table[2 * count + i] * height, height)
        for r in range(height // rows):
            part = raw_ref[pl.ds(place + r * rows, rows)]
            held[at.start + r * rows : at.start + (r + 1) * rows] = part * scale_ref[r : r + 1]
        return i * height

    scatter(held, out_ref, sems, [functools.partial(make, i) for i in range(count)])


def scaled(table, scale, raw, count, rows):
    height, width = raw.shape[0] // count // rows * rows, raw.shape[1]
    return pl.pallas_call(
        functools.partial(scaled_kernel, count, rows),
        out_shape=jax.ShapeDtypeStruct((count * height, width), jnp.float32),
        in_specs=[SCALARS, WHOLE, WHOLE],
        out_specs=ANY,
        scratch_shapes=[
            pltpu.VMEM((count * height, width), jnp.float32),
            pltpu.SemaphoreType.DMA((count,)),
        ],
        compiler_params=pltpu.CompilerParams(vmem_limit_bytes=SMALL),
        cost_estimate=FREE,
        name="scaled",
    )(table, scale, raw)


def finish_kernel(count, rows, sizes, places, table, scale_ref, *refs):
    parts, (out_ref, held, sems) = refs[: 2 * len(sizes)], refs[-3:]
    height = held.shape[0] // len(places)
    sources = [(part, i) for part, size in enumerate(sizes) for i in range(size)]

    def make(source, place, at):
        part, i = source
        mine, theirs = parts[2 * part], parts[2 * part + 1]
        for r in range(height // rows):
            row = i * height + r * rows
            total = mine[row : row + rows] + theirs[row : row + rows]
            held[at.start + r * rows : at.start + (r + 1) * rows] = total * scale_ref[r : r + 1]
        return table[count + place] * height

    scatter(held, out_ref, sems, [functools.partial(make, *one) for one in zip(sources, places)])


def finish(table, spans, scale, parts, out, count, rows):
    places = [base + i for base, size in spans for i in range(size)]
    height, width = parts[0].shape[0] // spans[0][1], parts[0].shape[1]
    in_specs = [SCALARS] + [WHOLE] * (1 + len(parts))
    args, aliases = [table, scale, *parts], {}
    if out is not None:
        in_specs.append(ANY)
        aliases = {len(args): 0}
        args.append(out)
    return pl.pallas_call(
        functools.partial(finish_kernel, count, rows, [size for _, size in spans], places),
        out_shape=jax.ShapeDtypeStruct((count * height, width), jnp.float32),
        in_specs=in_specs,
        out_specs=ANY,
        scratch_shapes=[
            pltpu.VMEM((len(places) * height, width), jnp.float32),
            pltpu.SemaphoreType.DMA((len(places),)),
        ],
        input_output_aliases=aliases,
        compiler_params=pltpu.CompilerParams(vmem_limit_bytes=SMALL),
        cost_estimate=FREE,
        name="finish",
    )(*args)


def add_over_term(value):
    size = lax.axis_size("term")
    if size == 1 or not power_of_two(size):
        return lax.psum(value, "term"), jnp.zeros_like(value)
    bit = 1
    while 2 * bit < size:
        value = value + flip(value, "term", bit)
        bit *= 2
    return value, flip(value, "term", bit)


def after(*values):
    return lax.optimization_barrier(values)


def shards(amplitudes, left, right, term_kind, partner, left_diag, right_diag):
    devices, terms_over = lax.axis_size("blk"), lax.axis_size("term")
    slots, rows, roots, width = amplitudes.shape
    per = slots // devices
    elements = slots * devices * rows * lax.axis_size("sub") * width
    vector = jnp.transpose(amplitudes, (0, 2, 1, 3)).reshape(slots * roots * rows, width)
    table = make_table(partner, term_kind, vector)
    diag = left_diag[:, :, None] + right_diag[:, None, :]

    cuts = [(0, per // 2), (per // 2, per - per // 2)] if per > 1 else [(0, per)]
    offsets = sorted(range(1, devices), key=lambda c: (-min(c, devices - c), c))
    moving = [(c, c * per + start, size) for c in offsets for start, size in cuts]
    staying = [(0, start, size) for start, size in cuts]
    pieces = staying + moving
    ahead_of = len(cuts)
    whole = [pieces[i : i + ahead_of] for i in range(0, len(pieces), ahead_of)]
    mixed = [[piece] for piece in staying] + whole[1:]
    batches = [moving[:ahead_of], moving[ahead_of:] + staying]

    def spans(pieces):
        return [piece[1:] for piece in pieces]

    def relay(value, c):
        return lax.ppermute(value, "blk", [(p, (p + c) % devices) for p in range(devices)])

    def swap(value):
        return lax.ppermute(value, "sub", [(0, 1), (1, 0)])

    def partials(own, second):
        if second:
            early = (ahead, swap(ahead))
            other = swap(after(own, early[1])[0])
        else:
            other = swap(own)
        kept, outgoing = None, {}
        for batch in batches:
            early_now = second and batch is batches[0]
            pair = early if early_now else (own, other)
            parts, kept = sectors(
                table,
                spans(batch),
                [second and piece[0] > 0 for piece in batch],
                left,
                right,
                *pair,
                kept,
                (batch[0][1] if early_now else 0) if second else None,
                roots,
            )
            outgoing.update(zip(batch, parts))
        arrived, sums, inners = {}, [], []
        for at, piece in enumerate(moving):
            value = outgoing[piece]
            if at >= ahead_of:
                value = after(value, arrived[moving[at - ahead_of]])[0]
            arrived[piece] = relay(value, piece[0])
        for group in mixed if second else whole:
            mine, inner = combine(
                table,
                spans(group),
                kept,
                [arrived[piece] if piece[0] else outgoing[piece] for piece in group],
                own,
                diag,
                1.0 / terms_over,
                second,
                not second,
            )
            if second and len(sums) == 2 * ahead_of and ahead_of > 1:
                mine = after(mine, sums[-1], sums[-3])[0]
            elif len(sums) >= 4:
                mine = after(mine, sums[-3])[0]
            sums += add_over_term(mine)
            inners.append(inner)
        return sums, inners, arrived, other

    sums, inners, _, _ = partials(vector, False)
    inner = small_sum(small_sum(sum(inners[1:], inners[0]), "sub"), "blk")
    inner = small_sum(after(inner, sums[-3])[0], "term")
    first = (batches[0][0][1], sum(size for _, _, size in batches[0]))
    raw, ahead = correct(
        table, [spans(group) for group in whole], first, inner, vector, diag, sums
    )

    sums, _, arrived, other = partials(raw, True)
    squares = raw[-TAG:] + other[-TAG:]
    for piece in moving[::ahead_of]:
        squares = squares + arrived[piece][-TAG:]
    scale = lax.rsqrt(jnp.sum(squares, axis=1, keepdims=True) / elements + 1e-06)
    scale = jnp.broadcast_to(scale, squares.shape)
    correction = scaled(table, scale, raw, slots, rows)
    sigma = None
    for some in (slice(0, -1), slice(-1, None)):
        parts = [one for pair in list(zip(sums[::2], sums[1::2]))[some] for one in pair]
        if parts:
            spans_of = [(group[0][1], sum(one[2] for one in group)) for group in mixed[some]]
            sigma = finish(table, spans_of, scale, parts, sigma, slots, rows)
    return tuple(
        jnp.transpose(value.reshape(slots, roots, rows, width), (0, 2, 1, 3))
        for value in (sigma, correction)
    )


def solution(mesh):
    return jax.shard_map(
        shards,
        mesh=mesh,
        in_specs=(
            P(("grp", "blk"), "sub", None, None),
            P(("grp", "term"), "blk", "sub", None),
            P(("grp", "term"), "blk", None, None),
            P(("grp", "term")),
            P(("grp", "blk")),
            P(("grp", "blk"), "sub"),
            P(("grp", "blk"), None),
        ),
        out_specs=(P(("grp", "blk"), "sub", None, None), P(("grp", "blk"), "sub", None, None)),
        check_vma=False,
    )
```

```python
import functools

import jax
import jax.numpy as jnp
from jax import lax
from jax.experimental import pallas as pl
from jax.experimental.pallas import tpu as pltpu
from jax.sharding import PartitionSpec as P

TAG = 8
LIMIT = 48 * 1024 * 1024
SMALL = 24 * 1024 * 1024
FREE = pl.CostEstimate(flops=0, bytes_accessed=0, transcendentals=0)
WHOLE = pl.BlockSpec(memory_space=pltpu.VMEM)
SCALARS = pl.BlockSpec(memory_space=pltpu.SMEM)
ANY = pl.BlockSpec(memory_space=pl.ANY)


def power_of_two(size):
    return size & (size - 1) == 0


def flip(value, axis, bit):
    size = lax.axis_size(axis)
    return lax.ppermute(value, axis, [(i, i ^ bit) for i in range(size)])


def small_sum(value, axis):
    size = lax.axis_size(axis)
    if not power_of_two(size):
        return lax.psum(value, axis)
    if size == 4:
        one, two, three = (flip(value, axis, bit) for bit in (1, 2, 3))
        return (value + one) + (two + three)
    bit = 1
    while bit < size:
        value = value + flip(value, axis, bit)
        bit *= 2
    return value


def halves(value):
    high = value.astype(jnp.bfloat16)
    low = (value - high.astype(jnp.float32)).astype(jnp.bfloat16)
    return high, low


def table_kernel(devices, count, terms, given_hbm, _, table_ref, used, given_ref, sem):
    copy = pltpu.make_async_copy(given_hbm, given_ref, sem)
    copy.start()
    copy.wait()
    per = count // devices
    me = lax.axis_index("blk")
    for c in range(devices):
        used[c] = 0

    def place(j, carry):
        where_to = given_ref[j]
        owner = lax.div(where_to, count)
        offset = lax.rem(owner - me + devices, devices)
        at = offset * per + used[offset]
        used[offset] = used[offset] + 1
        table_ref[at] = j
        table_ref[count + at] = where_to - owner * count
        table_ref[2 * count + j] = at
        return carry

    lax.fori_loop(0, count, place, 0)
    for k in range(terms):
        table_ref[3 * count + k] = given_ref[count + k]
    table_ref[3 * count + terms] = lax.axis_index("sub")


def make_table(partner, term_kind, vector):
    devices = lax.axis_size("blk")
    count, terms = partner.shape[0], term_kind.shape[0]
    given = jnp.concatenate([partner, term_kind])
    return pl.pallas_call(
        functools.partial(table_kernel, devices, count, terms),
        out_shape=jax.ShapeDtypeStruct((3 * count + terms + 1,), jnp.int32),
        in_specs=[ANY, WHOLE],
        out_specs=SCALARS,
        scratch_shapes=[
            pltpu.SMEM((devices,), jnp.int32),
            pltpu.SMEM(given.shape, jnp.int32),
            pltpu.SemaphoreType.DMA,
        ],
        compiler_params=pltpu.CompilerParams(vmem_limit_bytes=SMALL),
        name="table",
    )(given, vector)


def sector(table, count, terms, height, source, held, own_ref, other_ref, l_ref, r_ref, lhs, high_rhs, low_rhs):
    rows, width = l_ref.shape[2], r_ref.shape[3]
    roots = height // rows
    first = table[3 * count + terms] == 0
    own, other = own_ref[held], other_ref[held]
    top = jnp.where(first, own, other)
    bottom = jnp.where(first, other, own)
    left = l_ref[:, source].reshape(terms * rows, 2 * rows)
    left = jnp.concatenate(halves(left), axis=1)
    for r in range(roots):
        at = slice(r * rows, (r + 1) * rows)
        wide = jnp.concatenate(halves(jnp.concatenate([top[at], bottom[at]], axis=0)), axis=1)
        both = jnp.dot(
            left, jnp.concatenate([wide, wide], axis=0), preferred_element_type=jnp.float32
        )
        high, low = halves(both[:, :width] + both[:, width:])
        for k in range(terms):
            lanes = slice(k * width, (k + 1) * width)
            part = slice(k * rows, (k + 1) * rows)
            lhs[r * rows : (r + 1) * rows, lanes] = high[part]
            lhs[(roots + r) * rows : (roots + r + 1) * rows, lanes] = low[part]
    for k in range(terms):
        lanes = slice(k * width, (k + 1) * width)
        kind = table[3 * count + k]
        used = pl.ds(pl.multiple_of((1 - kind) * width, width), width)
        high, low = halves(r_ref[k, source].T)
        high_rhs[lanes, used] = high
        low_rhs[lanes, used] = low
    high, low = lhs[:height], lhs[height:]
    return jnp.dot(
        jnp.concatenate([high, low, high], axis=1),
        jnp.concatenate([high_rhs[...], high_rhs[...], low_rhs[...]], axis=0),
        preferred_element_type=jnp.float32,
    )


def sector_kernel(count, terms, unroll, height, pieces, origin, starts, tags, table, own_ref, other_ref, *refs):
    streamed = origin is None
    inputs, scratch = refs[: 2 * unroll if streamed else 2], refs[-3 * unroll :]
    outputs = refs[-3 * unroll - len(starts) : -3 * unroll]
    moved_refs, kept_ref = outputs[:-1], outputs[-1]
    width = kept_ref.shape[1]
    step = pl.program_id(0)

    def sector_at(at):
        return pl.ds(pl.multiple_of(at * height, height), height)

    @pl.when(step == 0)
    def _():
        for k in range(terms):
            kind = table[3 * count + k]
            unused = pl.ds(pl.multiple_of(kind * width, width), width)
            for at, ref in enumerate(scratch):
                if at % 3:
                    ref[k * width : (k + 1) * width, unused] = jnp.zeros((width, width), ref.dtype)
        if any(tags):
            tag = own_ref[own_ref.shape[0] - TAG :] + other_ref[other_ref.shape[0] - TAG :]
            for ref, begin, end, tagged in zip(moved_refs, starts, starts[1:], tags):
                if tagged:
                    ref[(end - begin) * height :] = tag

    places = [place_of(step * unroll + u, pieces) for u in range(unroll)]
    results = [
        sector(
            table,
            count,
            terms,
            height,
            0 if streamed else table[place],
            sector_at(table[place] if streamed else place - origin),
            own_ref,
            other_ref,
            *(inputs[2 * u : 2 * u + 2] if streamed else inputs),
            *scratch[3 * u : 3 * u + 3],
        )
        for u, place in enumerate(places)
    ]
    for u, place in enumerate(places):
        kept_ref[sector_at(place)] = results[u][:, width:]
    for ref, begin, end in zip(moved_refs, starts, starts[1:]):
        for u in range(unroll):
            at = step * unroll + u - begin

            @pl.when((at >= 0) & (at < end - begin))
            def _(ref=ref, u=u, at=at):
                ref[sector_at(at)] = results[u][:, :width]


def place_of(i, pieces):
    at, begin = pieces[0][0] + i, 0
    for (_, size), (base, _) in zip(pieces, pieces[1:]):
        begin += size
        at = jnp.where(i >= begin, base + i - begin, at)
    return at


def sectors(table, pieces, tags, left, right, own, other, kept, origin, roots):
    terms, count, rows, width = left.shape
    height = roots * rows
    starts = [0]
    for _, size in pieces:
        starts.append(starts[-1] + size)
    places = [base + i for base, size in pieces for i in range(size)]

    unroll = 2 if len(places) % 2 == 0 else 1

    def specs(u):
        def source(i, table):
            return table[place_of(unroll * i + u, pieces)]

        return [
            pl.BlockSpec((terms, 1, rows, width), lambda i, t: (0, source(i, t), 0, 0)),
            pl.BlockSpec((terms, 1, width, width), lambda i, t: (0, source(i, t), 0, 0)),
        ]

    if origin is None:
        in_specs = [WHOLE, WHOLE] + [spec for u in range(unroll) for spec in specs(u)]
        args = [own, other] + [left, right] * unroll
    else:
        in_specs = [WHOLE] * 4
        args = [own, other, left, right]
    aliases = {}
    if kept is not None:
        in_specs.append(WHOLE)
        args.append(kept)
        aliases = {len(args): len(pieces)}
    deep = terms * width
    shapes = [(size * height + TAG * tagged, width) for (_, size), tagged in zip(pieces, tags)]
    out = pl.pallas_call(
        functools.partial(
            sector_kernel, count, terms, unroll, height, pieces, origin, starts, tags
        ),
        out_shape=[
            jax.ShapeDtypeStruct(shape, jnp.float32)
            for shape in shapes + [(count * height, width)]
        ],
        grid_spec=pltpu.PrefetchScalarGridSpec(
            num_scalar_prefetch=1,
            grid=(starts[-1] // unroll,),
            in_specs=in_specs,
            out_specs=[WHOLE] * (len(shapes) + 1),
            scratch_shapes=[
                pltpu.VMEM((2 * height, deep), jnp.bfloat16),
                pltpu.VMEM((deep, 2 * width), jnp.bfloat16),
                pltpu.VMEM((deep, 2 * width), jnp.bfloat16),
            ]
            * unroll,
        ),
        input_output_aliases=aliases,
        compiler_params=pltpu.CompilerParams(vmem_limit_bytes=LIMIT if origin is None else SMALL),
        cost_estimate=FREE,
        name="sectors",
    )(table, *args)
    return out[:-1], out[-1]


def combine_kernel(share, pieces, ordered, with_inner, table, kept_ref, vector_ref, diag_ref, *refs):
    arrived_refs, refs = refs[: len(pieces)], refs[len(pieces) :]
    sum_refs, refs = refs[: len(refs) - with_inner], refs[len(refs) - with_inner :]
    count, rows, width = diag_ref.shape
    height = kept_ref.shape[0] // count
    roots = height // rows
    inner = [jnp.zeros((1, width), jnp.float32) for _ in range(2 * roots)]
    every = [
        (at, base + i, i) for at, (base, size) in enumerate(pieces) for i in range(size)
    ]
    for i, (of_group, at_place, of_piece) in enumerate(every):
        arrived_ref = arrived_refs[of_group]
        slot = table[count + at_place]
        place = table[2 * count + slot]
        held = place if ordered else slot
        diag = share * diag_ref[slot]
        for r in range(roots):

            def at(sector):
                return pl.ds(pl.multiple_of(sector * height + r * rows, rows), rows)

            here = slice(i * height + r * rows, i * height + (r + 1) * rows)
            there = slice(of_piece * height + r * rows, of_piece * height + (r + 1) * rows)
            vector = vector_ref[at(held)]
            total = kept_ref[at(place)] + arrived_ref[there] + diag * vector
            if len(sum_refs) == 1:
                sum_refs[0][here] = total
            else:
                sum_refs[of_group][there] = total
            if with_inner:
                inner[r] = inner[r] + jnp.sum(vector * total, axis=0, keepdims=True)
                inner[roots + r] = inner[roots + r] + share * jnp.sum(
                    vector * vector, axis=0, keepdims=True
                )
    if with_inner:
        rest = jnp.zeros((TAG - 2 * roots, width), jnp.float32)
        refs[0][...] = jnp.concatenate(inner + [rest], axis=0)


def combine(table, pieces, kept, arrived, vector, diag, share, ordered, with_inner, apart=False):
    height, width = kept.shape[0] // diag.shape[0], kept.shape[1]
    sizes = [size for _, size in pieces]
    out_shape = [
        jax.ShapeDtypeStruct((size * height, width), jnp.float32)
        for size in (sizes if apart else [sum(sizes)])
    ]
    if with_inner:
        out_shape.append(jax.ShapeDtypeStruct((TAG, width), jnp.float32))
    out = pl.pallas_call(
        functools.partial(combine_kernel, share, pieces, ordered, with_inner),
        out_shape=out_shape,
        in_specs=[SCALARS] + [WHOLE] * (3 + len(arrived)),
        out_specs=[WHOLE] * len(out_shape),
        compiler_params=pltpu.CompilerParams(vmem_limit_bytes=SMALL),
        cost_estimate=FREE,
        name="combine",
    )(table, kept, vector, diag, *arrived)
    return out if with_inner or apart else (out[0], None)


def correct_kernel(groups, ahead, table, inner_ref, vector_ref, diag_ref, *rest):
    parts, (raw_ref, ahead_ref) = rest[:-2], rest[-2:]
    count, rows, width = diag_ref.shape
    height = vector_ref.shape[0] // count
    roots = height // rows
    inner = jnp.sum(inner_ref[...], axis=1, keepdims=True)
    theta = inner[:roots] / inner[roots : 2 * roots]
    squares = [jnp.zeros((1, width), jnp.float32) for _ in range(roots)]
    for at, pieces in enumerate(groups):
        mine, theirs = parts[2 * at], parts[2 * at + 1]
        row = 0
        for base, size in pieces:
            for i in range(size):
                slot = table[count + base + i]
                held = slot * height
                place = table[2 * count + slot] * height
                diag = diag_ref[slot]
                for r in range(roots):
                    shift = theta[r : r + 1]
                    sigma = mine[row : row + rows] + theirs[row : row + rows]
                    vector = vector_ref[pl.ds(pl.multiple_of(held + r * rows, rows), rows)]
                    raw = (sigma - shift * vector) / jnp.maximum(jnp.abs(diag - shift), 1.0)
                    raw_ref[pl.ds(pl.multiple_of(place + r * rows, rows), rows)] = raw
                    squares[r] = squares[r] + jnp.sum(raw * raw, axis=0, keepdims=True)
                    row += rows
    raw_ref[count * height :] = jnp.concatenate(
        squares + [jnp.zeros((TAG - roots, width), jnp.float32)], axis=0
    )
    ahead_ref[: ahead[1] * height] = raw_ref[ahead[0] * height : (ahead[0] + ahead[1]) * height]
    ahead_ref[ahead[1] * height :] = raw_ref[count * height :]


def correct(table, groups, ahead, inner, vector, diag, parts):
    height, width = vector.shape[0] // diag.shape[0], vector.shape[1]
    return pl.pallas_call(
        functools.partial(correct_kernel, groups, ahead),
        out_shape=[
            jax.ShapeDtypeStruct((vector.shape[0] + TAG, width), jnp.float32),
            jax.ShapeDtypeStruct((ahead[1] * height + TAG, width), jnp.float32),
        ],
        in_specs=[SCALARS] + [WHOLE] * (3 + len(parts)),
        out_specs=[WHOLE, WHOLE],
        compiler_params=pltpu.CompilerParams(vmem_limit_bytes=SMALL),
        cost_estimate=FREE,
        name="correct",
    )(table, inner, vector, diag, *parts)


def scatter(held, out_ref, sems, rows_of):
    height = held.shape[0] // len(rows_of)
    copies = []
    for i, make in enumerate(rows_of):
        at = slice(i * height, (i + 1) * height)
        row = make(at)
        copies.append(
            pltpu.make_async_copy(
                held.at[at], out_ref.at[pl.ds(pl.multiple_of(row, height), height)], sems.at[i]
            )
        )
        copies[-1].start()
    for copy in copies:
        copy.wait()


def scaled_kernel(count, rows, table, scale_ref, raw_ref, out_ref, held, sems):
    height = held.shape[0] // count

    def make(i, at):
        place = pl.multiple_of(table[2 * count + i] * height, height)
        for r in range(height // rows):
            part = raw_ref[pl.ds(place + r * rows, rows)]
            held[at.start + r * rows : at.start + (r + 1) * rows] = part * scale_ref[r : r + 1]
        return i * height

    scatter(held, out_ref, sems, [functools.partial(make, i) for i in range(count)])


def scaled(table, scale, raw, count, rows):
    height, width = raw.shape[0] // count // rows * rows, raw.shape[1]
    return pl.pallas_call(
        functools.partial(scaled_kernel, count, rows),
        out_shape=jax.ShapeDtypeStruct((count * height, width), jnp.float32),
        in_specs=[SCALARS, WHOLE, WHOLE],
        out_specs=ANY,
        scratch_shapes=[
            pltpu.VMEM((count * height, width), jnp.float32),
            pltpu.SemaphoreType.DMA((count,)),
        ],
        compiler_params=pltpu.CompilerParams(vmem_limit_bytes=SMALL),
        cost_estimate=FREE,
        name="scaled",
    )(table, scale, raw)


def finish_kernel(count, rows, sizes, places, table, scale_ref, *refs):
    parts, (out_ref, held, sems) = refs[: 2 * len(sizes)], refs[-3:]
    height = held.shape[0] // len(places)
    sources = [(part, i) for part, size in enumerate(sizes) for i in range(size)]

    def make(source, place, at):
        part, i = source
        mine, theirs = parts[2 * part], parts[2 * part + 1]
        for r in range(height // rows):
            row = i * height + r * rows
            total = mine[row : row + rows] + theirs[row : row + rows]
            held[at.start + r * rows : at.start + (r + 1) * rows] = total * scale_ref[r : r + 1]
        return table[count + place] * height

    scatter(held, out_ref, sems, [functools.partial(make, *one) for one in zip(sources, places)])


def finish(table, spans, scale, parts, out, count, rows):
    places = [base + i for base, size in spans for i in range(size)]
    height, width = parts[0].shape[0] // spans[0][1], parts[0].shape[1]
    in_specs = [SCALARS] + [WHOLE] * (1 + len(parts))
    args, aliases = [table, scale, *parts], {}
    if out is not None:
        in_specs.append(ANY)
        aliases = {len(args): 0}
        args.append(out)
    return pl.pallas_call(
        functools.partial(finish_kernel, count, rows, [size for _, size in spans], places),
        out_shape=jax.ShapeDtypeStruct((count * height, width), jnp.float32),
        in_specs=in_specs,
        out_specs=ANY,
        scratch_shapes=[
            pltpu.VMEM((len(places) * height, width), jnp.float32),
            pltpu.SemaphoreType.DMA((len(places),)),
        ],
        input_output_aliases=aliases,
        compiler_params=pltpu.CompilerParams(vmem_limit_bytes=SMALL),
        cost_estimate=FREE,
        name="finish",
    )(*args)


def add_over_term(value):
    size = lax.axis_size("term")
    if size == 1 or not power_of_two(size):
        return lax.psum(value, "term"), jnp.zeros_like(value)
    bit = 1
    while 2 * bit < size:
        value = value + flip(value, "term", bit)
        bit *= 2
    return value, flip(value, "term", bit)


def after(*values):
    return lax.optimization_barrier(values)


def shards(amplitudes, left, right, term_kind, partner, left_diag, right_diag):
    devices, terms_over = lax.axis_size("blk"), lax.axis_size("term")
    slots, rows, roots, width = amplitudes.shape
    per = slots // devices
    elements = slots * devices * rows * lax.axis_size("sub") * width
    vector = jnp.transpose(amplitudes, (0, 2, 1, 3)).reshape(slots * roots * rows, width)
    table = make_table(partner, term_kind, vector)
    diag = left_diag[:, :, None] + right_diag[:, None, :]

    cuts = [(0, per // 2), (per // 2, per - per // 2)] if per > 1 else [(0, per)]
    offsets = sorted(range(1, devices), key=lambda c: (-min(c, devices - c), c))
    moving = [(c, c * per + start, size) for c in offsets for start, size in cuts]
    staying = [(0, start, size) for start, size in cuts]
    pieces = staying + moving
    ahead_of = len(cuts)
    whole = [pieces[i : i + ahead_of] for i in range(0, len(pieces), ahead_of)]
    mixed = [[piece] for piece in staying] + whole[1:]
    batches = [moving[:ahead_of], moving[ahead_of:] + staying]

    def spans(pieces):
        return [piece[1:] for piece in pieces]

    def relay(value, c):
        return lax.ppermute(value, "blk", [(p, (p + c) % devices) for p in range(devices)])

    def swap(value):
        return lax.ppermute(value, "sub", [(0, 1), (1, 0)])

    def partials(own, second):
        if second:
            early = (ahead, swap(ahead))
            other = swap(after(own, early[1])[0])
        else:
            other = swap(own)
        kept, outgoing = None, {}
        for batch in batches:
            early_now = second and batch is batches[0]
            pair = early if early_now else (own, other)
            parts, kept = sectors(
                table,
                spans(batch),
                [second and piece[0] > 0 for piece in batch],
                left,
                right,
                *pair,
                kept,
                (batch[0][1] if early_now else 0) if second else None,
                roots,
            )
            outgoing.update(zip(batch, parts))
        arrived, sums, inners = {}, [], []
        for at, piece in enumerate(moving):
            value = outgoing[piece]
            if at >= ahead_of:
                value = after(value, arrived[moving[at - ahead_of]])[0]
            arrived[piece] = relay(value, piece[0])
        stays = []
        if second:
            stays = combine(
                table,
                spans(staying),
                kept,
                [outgoing[piece] for piece in staying],
                own,
                diag,
                1.0 / terms_over,
                True,
                False,
                True,
            )
        for at, group in enumerate(mixed if second else whole):
            if at < len(stays):
                mine, inner = stays[at], None
            else:
                mine, inner = combine(
                    table,
                    spans(group),
                    kept,
                    [arrived[piece] if piece[0] else outgoing[piece] for piece in group],
                    own,
                    diag,
                    1.0 / terms_over,
                    second,
                    not second,
                )
            if second and len(sums) == 2 * ahead_of and ahead_of > 1:
                mine = after(mine, sums[-1], sums[-3])[0]
            elif len(sums) >= 4:
                mine = after(mine, sums[-3])[0]
            sums += add_over_term(mine)
            inners.append(inner)
        return sums, inners, arrived, other

    sums, inners, _, _ = partials(vector, False)
    inner = small_sum(small_sum(sum(inners[1:], inners[0]), "sub"), "blk")
    inner = small_sum(after(inner, sums[-3])[0], "term")
    first = (batches[0][0][1], sum(size for _, _, size in batches[0]))
    raw, ahead = correct(
        table, [spans(group) for group in whole], first, inner, vector, diag, sums
    )

    sums, _, arrived, other = partials(raw, True)
    squares = raw[-TAG:] + other[-TAG:]
    for piece in moving[::ahead_of]:
        squares = squares + arrived[piece][-TAG:]
    scale = lax.rsqrt(jnp.sum(squares, axis=1, keepdims=True) / elements + 1e-06)
    scale = jnp.broadcast_to(scale, squares.shape)
    correction = scaled(table, scale, raw, slots, rows)
    sigma = None
    for some in (slice(0, -1), slice(-1, None)):
        parts = [one for pair in list(zip(sums[::2], sums[1::2]))[some] for one in pair]
        if parts:
            spans_of = [(group[0][1], sum(one[2] for one in group)) for group in mixed[some]]
            sigma = finish(table, spans_of, scale, parts, sigma, slots, rows)
    return tuple(
        jnp.transpose(value.reshape(slots, roots, rows, width), (0, 2, 1, 3))
        for value in (sigma, correction)
    )


def solution(mesh):
    return jax.shard_map(
        shards,
        mesh=mesh,
        in_specs=(
            P(("grp", "blk"), "sub", None, None),
            P(("grp", "term"), "blk", "sub", None),
            P(("grp", "term"), "blk", None, None),
            P(("grp", "term")),
            P(("grp", "blk")),
            P(("grp", "blk"), "sub"),
            P(("grp", "blk"), None),
        ),
        out_specs=(P(("grp", "blk"), "sub", None, None), P(("grp", "blk"), "sub", None, None)),
        check_vma=False,
    )
```

```python
import functools

import jax
import jax.numpy as jnp
from jax import lax
from jax.experimental import pallas as pl
from jax.experimental.pallas import tpu as pltpu
from jax.sharding import PartitionSpec as P

TAG = 8
LIMIT = 48 * 1024 * 1024
SMALL = 24 * 1024 * 1024
FREE = pl.CostEstimate(flops=0, bytes_accessed=0, transcendentals=0)
WHOLE = pl.BlockSpec(memory_space=pltpu.VMEM)
SCALARS = pl.BlockSpec(memory_space=pltpu.SMEM)
ANY = pl.BlockSpec(memory_space=pl.ANY)


def power_of_two(size):
    return size & (size - 1) == 0


def flip(value, axis, bit):
    size = lax.axis_size(axis)
    return lax.ppermute(value, axis, [(i, i ^ bit) for i in range(size)])


def small_sum(value, axis):
    size = lax.axis_size(axis)
    if not power_of_two(size):
        return lax.psum(value, axis)
    if size == 4:
        one, two, three = (flip(value, axis, bit) for bit in (1, 2, 3))
        return (value + one) + (two + three)
    bit = 1
    while bit < size:
        value = value + flip(value, axis, bit)
        bit *= 2
    return value


def halves(value):
    high = value.astype(jnp.bfloat16)
    low = (value - high.astype(jnp.float32)).astype(jnp.bfloat16)
    return high, low


def table_kernel(devices, count, terms, given_hbm, _, table_ref, used, given_ref, sem):
    copy = pltpu.make_async_copy(given_hbm, given_ref, sem)
    copy.start()
    copy.wait()
    per = count // devices
    me = lax.axis_index("blk")
    for c in range(devices):
        used[c] = 0

    def place(j, carry):
        where_to = given_ref[j]
        owner = lax.div(where_to, count)
        offset = lax.rem(owner - me + devices, devices)
        at = offset * per + used[offset]
        used[offset] = used[offset] + 1
        table_ref[at] = j
        table_ref[count + at] = where_to - owner * count
        table_ref[2 * count + j] = at
        return carry

    lax.fori_loop(0, count, place, 0)
    for k in range(terms):
        table_ref[3 * count + k] = given_ref[count + k]
    table_ref[3 * count + terms] = lax.axis_index("sub")


def make_table(partner, term_kind, vector):
    devices = lax.axis_size("blk")
    count, terms = partner.shape[0], term_kind.shape[0]
    given = jnp.concatenate([partner, term_kind])
    return pl.pallas_call(
        functools.partial(table_kernel, devices, count, terms),
        out_shape=jax.ShapeDtypeStruct((3 * count + terms + 1,), jnp.int32),
        in_specs=[ANY, WHOLE],
        out_specs=SCALARS,
        scratch_shapes=[
            pltpu.SMEM((devices,), jnp.int32),
            pltpu.SMEM(given.shape, jnp.int32),
            pltpu.SemaphoreType.DMA,
        ],
        compiler_params=pltpu.CompilerParams(vmem_limit_bytes=SMALL),
        name="table",
    )(given, vector)


def sector(table, count, terms, height, source, held, own_ref, other_ref, l_ref, r_ref, lhs, high_rhs, low_rhs):
    rows, width = l_ref.shape[2], r_ref.shape[3]
    roots = height // rows
    first = table[3 * count + terms] == 0
    own, other = own_ref[held], other_ref[held]
    top = jnp.where(first, own, other)
    bottom = jnp.where(first, other, own)
    left = l_ref[:, source].reshape(terms * rows, 2 * rows)
    left = jnp.concatenate(halves(left), axis=1)
    for r in range(roots):
        at = slice(r * rows, (r + 1) * rows)
        wide = jnp.concatenate(halves(jnp.concatenate([top[at], bottom[at]], axis=0)), axis=1)
        both = jnp.dot(
            left, jnp.concatenate([wide, wide], axis=0), preferred_element_type=jnp.float32
        )
        high, low = halves(both[:, :width] + both[:, width:])
        for k in range(terms):
            lanes = slice(k * width, (k + 1) * width)
            part = slice(k * rows, (k + 1) * rows)
            lhs[r * rows : (r + 1) * rows, lanes] = high[part]
            lhs[(roots + r) * rows : (roots + r + 1) * rows, lanes] = low[part]
    for k in range(terms):
        lanes = slice(k * width, (k + 1) * width)
        kind = table[3 * count + k]
        used = pl.ds(pl.multiple_of((1 - kind) * width, width), width)
        high, low = halves(r_ref[k, source].T)
        high_rhs[lanes, used] = high
        low_rhs[lanes, used] = low
    high, low = lhs[:height], lhs[height:]
    return jnp.dot(
        jnp.concatenate([high, low, high], axis=1),
        jnp.concatenate([high_rhs[...], high_rhs[...], low_rhs[...]], axis=0),
        preferred_element_type=jnp.float32,
    )


def sector_kernel(count, terms, unroll, height, pieces, origin, starts, tags, table, own_ref, other_ref, *refs):
    streamed = origin is None
    inputs, scratch = refs[: 2 * unroll if streamed else 2], refs[-3 * unroll :]
    outputs = refs[-3 * unroll - len(starts) : -3 * unroll]
    moved_refs, kept_ref = outputs[:-1], outputs[-1]
    width = kept_ref.shape[1]
    step = pl.program_id(0)

    def sector_at(at):
        return pl.ds(pl.multiple_of(at * height, height), height)

    @pl.when(step == 0)
    def _():
        for k in range(terms):
            kind = table[3 * count + k]
            unused = pl.ds(pl.multiple_of(kind * width, width), width)
            for at, ref in enumerate(scratch):
                if at % 3:
                    ref[k * width : (k + 1) * width, unused] = jnp.zeros((width, width), ref.dtype)
        if any(tags):
            tag = own_ref[own_ref.shape[0] - TAG :] + other_ref[other_ref.shape[0] - TAG :]
            for ref, begin, end, tagged in zip(moved_refs, starts, starts[1:], tags):
                if tagged:
                    ref[(end - begin) * height :] = tag

    places = [place_of(step * unroll + u, pieces) for u in range(unroll)]
    results = [
        sector(
            table,
            count,
            terms,
            height,
            0 if streamed else table[place],
            sector_at(table[place] if streamed else place - origin),
            own_ref,
            other_ref,
            *(inputs[2 * u : 2 * u + 2] if streamed else inputs),
            *scratch[3 * u : 3 * u + 3],
        )
        for u, place in enumerate(places)
    ]
    for u, place in enumerate(places):
        kept_ref[sector_at(place)] = results[u][:, width:]
    for ref, begin, end in zip(moved_refs, starts, starts[1:]):
        for u in range(unroll):
            at = step * unroll + u - begin

            @pl.when((at >= 0) & (at < end - begin))
            def _(ref=ref, u=u, at=at):
                ref[sector_at(at)] = results[u][:, :width]


def place_of(i, pieces):
    at, begin = pieces[0][0] + i, 0
    for (_, size), (base, _) in zip(pieces, pieces[1:]):
        begin += size
        at = jnp.where(i >= begin, base + i - begin, at)
    return at


def sectors(table, pieces, tags, left, right, own, other, kept, origin, roots):
    terms, count, rows, width = left.shape
    height = roots * rows
    starts = [0]
    for _, size in pieces:
        starts.append(starts[-1] + size)
    places = [base + i for base, size in pieces for i in range(size)]

    most = 2 if origin is None else 4
    unroll = next(unroll for unroll in (4, 2, 1) if unroll <= most and len(places) % unroll == 0)

    def specs(u):
        def source(i, table):
            return table[place_of(unroll * i + u, pieces)]

        return [
            pl.BlockSpec((terms, 1, rows, width), lambda i, t: (0, source(i, t), 0, 0)),
            pl.BlockSpec((terms, 1, width, width), lambda i, t: (0, source(i, t), 0, 0)),
        ]

    if origin is None:
        in_specs = [WHOLE, WHOLE] + [spec for u in range(unroll) for spec in specs(u)]
        args = [own, other] + [left, right] * unroll
    else:
        in_specs = [WHOLE] * 4
        args = [own, other, left, right]
    aliases = {}
    if kept is not None:
        in_specs.append(WHOLE)
        args.append(kept)
        aliases = {len(args): len(pieces)}
    deep = terms * width
    shapes = [(size * height + TAG * tagged, width) for (_, size), tagged in zip(pieces, tags)]
    out = pl.pallas_call(
        functools.partial(
            sector_kernel, count, terms, unroll, height, pieces, origin, starts, tags
        ),
        out_shape=[
            jax.ShapeDtypeStruct(shape, jnp.float32)
            for shape in shapes + [(count * height, width)]
        ],
        grid_spec=pltpu.PrefetchScalarGridSpec(
            num_scalar_prefetch=1,
            grid=(starts[-1] // unroll,),
            in_specs=in_specs,
            out_specs=[WHOLE] * (len(shapes) + 1),
            scratch_shapes=[
                pltpu.VMEM((2 * height, deep), jnp.bfloat16),
                pltpu.VMEM((deep, 2 * width), jnp.bfloat16),
                pltpu.VMEM((deep, 2 * width), jnp.bfloat16),
            ]
            * unroll,
        ),
        input_output_aliases=aliases,
        compiler_params=pltpu.CompilerParams(vmem_limit_bytes=LIMIT if origin is None else SMALL),
        cost_estimate=FREE,
        name="sectors",
    )(table, *args)
    return out[:-1], out[-1]


def combine_kernel(share, pieces, ordered, with_inner, table, kept_ref, vector_ref, diag_ref, *refs):
    arrived_refs, refs = refs[: len(pieces)], refs[len(pieces) :]
    sum_refs, refs = refs[: len(refs) - with_inner], refs[len(refs) - with_inner :]
    count, rows, width = diag_ref.shape
    height = kept_ref.shape[0] // count
    roots = height // rows
    inner = [jnp.zeros((1, width), jnp.float32) for _ in range(2 * roots)]
    every = [
        (at, base + i, i) for at, (base, size) in enumerate(pieces) for i in range(size)
    ]
    for i, (of_group, at_place, of_piece) in enumerate(every):
        arrived_ref = arrived_refs[of_group]
        slot = table[count + at_place]
        place = table[2 * count + slot]
        held = place if ordered else slot
        diag = share * diag_ref[slot]
        for r in range(roots):

            def at(sector):
                return pl.ds(pl.multiple_of(sector * height + r * rows, rows), rows)

            here = slice(i * height + r * rows, i * height + (r + 1) * rows)
            there = slice(of_piece * height + r * rows, of_piece * height + (r + 1) * rows)
            vector = vector_ref[at(held)]
            total = kept_ref[at(place)] + arrived_ref[there] + diag * vector
            if len(sum_refs) == 1:
                sum_refs[0][here] = total
            else:
                sum_refs[of_group][there] = total
            if with_inner:
                inner[r] = inner[r] + jnp.sum(vector * total, axis=0, keepdims=True)
                inner[roots + r] = inner[roots + r] + share * jnp.sum(
                    vector * vector, axis=0, keepdims=True
                )
    if with_inner:
        rest = jnp.zeros((TAG - 2 * roots, width), jnp.float32)
        refs[0][...] = jnp.concatenate(inner + [rest], axis=0)


def combine(table, pieces, kept, arrived, vector, diag, share, ordered, with_inner, apart=False):
    height, width = kept.shape[0] // diag.shape[0], kept.shape[1]
    sizes = [size for _, size in pieces]
    out_shape = [
        jax.ShapeDtypeStruct((size * height, width), jnp.float32)
        for size in (sizes if apart else [sum(sizes)])
    ]
    if with_inner:
        out_shape.append(jax.ShapeDtypeStruct((TAG, width), jnp.float32))
    out = pl.pallas_call(
        functools.partial(combine_kernel, share, pieces, ordered, with_inner),
        out_shape=out_shape,
        in_specs=[SCALARS] + [WHOLE] * (3 + len(arrived)),
        out_specs=[WHOLE] * len(out_shape),
        compiler_params=pltpu.CompilerParams(vmem_limit_bytes=SMALL),
        cost_estimate=FREE,
        name="combine",
    )(table, kept, vector, diag, *arrived)
    return out if with_inner or apart else (out[0], None)


def correct_kernel(groups, ahead, table, inner_ref, vector_ref, diag_ref, *rest):
    parts, (raw_ref, ahead_ref) = rest[:-2], rest[-2:]
    count, rows, width = diag_ref.shape
    height = vector_ref.shape[0] // count
    roots = height // rows
    inner = jnp.sum(inner_ref[...], axis=1, keepdims=True)
    theta = inner[:roots] / inner[roots : 2 * roots]
    squares = [jnp.zeros((1, width), jnp.float32) for _ in range(roots)]
    for at, pieces in enumerate(groups):
        mine, theirs = parts[2 * at], parts[2 * at + 1]
        row = 0
        for base, size in pieces:
            for i in range(size):
                slot = table[count + base + i]
                held = slot * height
                place = table[2 * count + slot] * height
                diag = diag_ref[slot]
                for r in range(roots):
                    shift = theta[r : r + 1]
                    sigma = mine[row : row + rows] + theirs[row : row + rows]
                    vector = vector_ref[pl.ds(pl.multiple_of(held + r * rows, rows), rows)]
                    raw = (sigma - shift * vector) / jnp.maximum(jnp.abs(diag - shift), 1.0)
                    raw_ref[pl.ds(pl.multiple_of(place + r * rows, rows), rows)] = raw
                    squares[r] = squares[r] + jnp.sum(raw * raw, axis=0, keepdims=True)
                    row += rows
    raw_ref[count * height :] = jnp.concatenate(
        squares + [jnp.zeros((TAG - roots, width), jnp.float32)], axis=0
    )
    ahead_ref[: ahead[1] * height] = raw_ref[ahead[0] * height : (ahead[0] + ahead[1]) * height]
    ahead_ref[ahead[1] * height :] = raw_ref[count * height :]


def correct(table, groups, ahead, inner, vector, diag, parts):
    height, width = vector.shape[0] // diag.shape[0], vector.shape[1]
    return pl.pallas_call(
        functools.partial(correct_kernel, groups, ahead),
        out_shape=[
            jax.ShapeDtypeStruct((vector.shape[0] + TAG, width), jnp.float32),
            jax.ShapeDtypeStruct((ahead[1] * height + TAG, width), jnp.float32),
        ],
        in_specs=[SCALARS] + [WHOLE] * (3 + len(parts)),
        out_specs=[WHOLE, WHOLE],
        compiler_params=pltpu.CompilerParams(vmem_limit_bytes=SMALL),
        cost_estimate=FREE,
        name="correct",
    )(table, inner, vector, diag, *parts)


def scatter(held, out_ref, sems, rows_of):
    height = held.shape[0] // len(rows_of)
    copies = []
    for i, make in enumerate(rows_of):
        at = slice(i * height, (i + 1) * height)
        row = make(at)
        copies.append(
            pltpu.make_async_copy(
                held.at[at], out_ref.at[pl.ds(pl.multiple_of(row, height), height)], sems.at[i]
            )
        )
        copies[-1].start()
    for copy in copies:
        copy.wait()


def scaled_kernel(count, rows, table, scale_ref, raw_ref, out_ref, held, sems):
    height = held.shape[0] // count

    def make(i, at):
        place = pl.multiple_of(table[2 * count + i] * height, height)
        for r in range(height // rows):
            part = raw_ref[pl.ds(place + r * rows, rows)]
            held[at.start + r * rows : at.start + (r + 1) * rows] = part * scale_ref[r : r + 1]
        return i * height

    scatter(held, out_ref, sems, [functools.partial(make, i) for i in range(count)])


def scaled(table, scale, raw, count, rows):
    height, width = raw.shape[0] // count // rows * rows, raw.shape[1]
    return pl.pallas_call(
        functools.partial(scaled_kernel, count, rows),
        out_shape=jax.ShapeDtypeStruct((count * height, width), jnp.float32),
        in_specs=[SCALARS, WHOLE, WHOLE],
        out_specs=ANY,
        scratch_shapes=[
            pltpu.VMEM((count * height, width), jnp.float32),
            pltpu.SemaphoreType.DMA((count,)),
        ],
        compiler_params=pltpu.CompilerParams(vmem_limit_bytes=SMALL),
        cost_estimate=FREE,
        name="scaled",
    )(table, scale, raw)


def finish_kernel(count, rows, sizes, places, table, scale_ref, *refs):
    parts, (out_ref, held, sems) = refs[: 2 * len(sizes)], refs[-3:]
    height = held.shape[0] // len(places)
    sources = [(part, i) for part, size in enumerate(sizes) for i in range(size)]

    def make(source, place, at):
        part, i = source
        mine, theirs = parts[2 * part], parts[2 * part + 1]
        for r in range(height // rows):
            row = i * height + r * rows
            total = mine[row : row + rows] + theirs[row : row + rows]
            held[at.start + r * rows : at.start + (r + 1) * rows] = total * scale_ref[r : r + 1]
        return table[count + place] * height

    scatter(held, out_ref, sems, [functools.partial(make, *one) for one in zip(sources, places)])


def finish(table, spans, scale, parts, out, count, rows):
    places = [base + i for base, size in spans for i in range(size)]
    height, width = parts[0].shape[0] // spans[0][1], parts[0].shape[1]
    in_specs = [SCALARS] + [WHOLE] * (1 + len(parts))
    args, aliases = [table, scale, *parts], {}
    if out is not None:
        in_specs.append(ANY)
        aliases = {len(args): 0}
        args.append(out)
    return pl.pallas_call(
        functools.partial(finish_kernel, count, rows, [size for _, size in spans], places),
        out_shape=jax.ShapeDtypeStruct((count * height, width), jnp.float32),
        in_specs=in_specs,
        out_specs=ANY,
        scratch_shapes=[
            pltpu.VMEM((len(places) * height, width), jnp.float32),
            pltpu.SemaphoreType.DMA((len(places),)),
        ],
        input_output_aliases=aliases,
        compiler_params=pltpu.CompilerParams(vmem_limit_bytes=SMALL),
        cost_estimate=FREE,
        name="finish",
    )(*args)


def add_over_term(value):
    size = lax.axis_size("term")
    if size == 1 or not power_of_two(size):
        return lax.psum(value, "term"), jnp.zeros_like(value)
    bit = 1
    while 2 * bit < size:
        value = value + flip(value, "term", bit)
        bit *= 2
    return value, flip(value, "term", bit)


def after(*values):
    return lax.optimization_barrier(values)


def shards(amplitudes, left, right, term_kind, partner, left_diag, right_diag):
    devices, terms_over = lax.axis_size("blk"), lax.axis_size("term")
    slots, rows, roots, width = amplitudes.shape
    per = slots // devices
    elements = slots * devices * rows * lax.axis_size("sub") * width
    vector = jnp.transpose(amplitudes, (0, 2, 1, 3)).reshape(slots * roots * rows, width)
    table = make_table(partner, term_kind, vector)
    diag = left_diag[:, :, None] + right_diag[:, None, :]

    cuts = [(0, per // 2), (per // 2, per - per // 2)] if per > 1 else [(0, per)]
    offsets = sorted(range(1, devices), key=lambda c: (-min(c, devices - c), c))
    moving = [(c, c * per + start, size) for c in offsets for start, size in cuts]
    staying = [(0, start, size) for start, size in cuts]
    pieces = staying + moving
    ahead_of = len(cuts)
    whole = [pieces[i : i + ahead_of] for i in range(0, len(pieces), ahead_of)]
    mixed = [[piece] for piece in staying] + whole[1:]
    batches = [moving[:ahead_of], moving[ahead_of:] + staying]

    def spans(pieces):
        return [piece[1:] for piece in pieces]

    def relay(value, c):
        return lax.ppermute(value, "blk", [(p, (p + c) % devices) for p in range(devices)])

    def swap(value):
        return lax.ppermute(value, "sub", [(0, 1), (1, 0)])

    def partials(own, second):
        if second:
            early = (ahead, swap(ahead))
            other = swap(after(own, early[1])[0])
        else:
            other = swap(own)
        kept, outgoing = None, {}
        for batch in batches:
            early_now = second and batch is batches[0]
            pair = early if early_now else (own, other)
            parts, kept = sectors(
                table,
                spans(batch),
                [second and piece[0] > 0 for piece in batch],
                left,
                right,
                *pair,
                kept,
                (batch[0][1] if early_now else 0) if second else None,
                roots,
            )
            outgoing.update(zip(batch, parts))
        arrived, sums, inners = {}, [], []
        for at, piece in enumerate(moving):
            value = outgoing[piece]
            if at >= ahead_of:
                value = after(value, arrived[moving[at - ahead_of]])[0]
            arrived[piece] = relay(value, piece[0])
        stays = []
        if second:
            stays = combine(
                table,
                spans(staying),
                kept,
                [outgoing[piece] for piece in staying],
                own,
                diag,
                1.0 / terms_over,
                True,
                False,
                True,
            )
        for at, group in enumerate(mixed if second else whole):
            if at < len(stays):
                mine, inner = stays[at], None
            else:
                mine, inner = combine(
                    table,
                    spans(group),
                    kept,
                    [arrived[piece] if piece[0] else outgoing[piece] for piece in group],
                    own,
                    diag,
                    1.0 / terms_over,
                    second,
                    not second,
                )
            if second and len(sums) == 2 * ahead_of and ahead_of > 1:
                mine = after(mine, sums[-1], sums[-3])[0]
            elif len(sums) >= 4:
                mine = after(mine, sums[-3])[0]
            sums += add_over_term(mine)
            inners.append(inner)
        return sums, inners, arrived, other

    sums, inners, _, _ = partials(vector, False)
    inner = small_sum(small_sum(sum(inners[1:], inners[0]), "sub"), "blk")
    inner = small_sum(after(inner, sums[-3])[0], "term")
    first = (batches[0][0][1], sum(size for _, _, size in batches[0]))
    raw, ahead = correct(
        table, [spans(group) for group in whole], first, inner, vector, diag, sums
    )

    sums, _, arrived, other = partials(raw, True)
    squares = raw[-TAG:] + other[-TAG:]
    for piece in moving[::ahead_of]:
        squares = squares + arrived[piece][-TAG:]
    scale = lax.rsqrt(jnp.sum(squares, axis=1, keepdims=True) / elements + 1e-06)
    scale = jnp.broadcast_to(scale, squares.shape)
    correction = scaled(table, scale, raw, slots, rows)
    sigma = None
    for some in (slice(0, -1), slice(-1, None)):
        parts = [one for pair in list(zip(sums[::2], sums[1::2]))[some] for one in pair]
        if parts:
            spans_of = [(group[0][1], sum(one[2] for one in group)) for group in mixed[some]]
            sigma = finish(table, spans_of, scale, parts, sigma, slots, rows)
    return tuple(
        jnp.transpose(value.reshape(slots, roots, rows, width), (0, 2, 1, 3))
        for value in (sigma, correction)
    )


def solution(mesh):
    return jax.shard_map(
        shards,
        mesh=mesh,
        in_specs=(
            P(("grp", "blk"), "sub", None, None),
            P(("grp", "term"), "blk", "sub", None),
            P(("grp", "term"), "blk", None, None),
            P(("grp", "term")),
            P(("grp", "blk")),
            P(("grp", "blk"), "sub"),
            P(("grp", "blk"), None),
        ),
        out_specs=(P(("grp", "blk"), "sub", None, None), P(("grp", "blk"), "sub", None, None)),
        check_vma=False,
    )
```
